32 devices in a mesh: groups: 2 (over x), gx: 8 (over z, y), gy: 2 (over core).
Axes of the slice: x: 2, y: 2, z: 4, core: 2. Of those that a mesh axis runs over, the one named last changes fastest.
Arguments:
- frames: bfloat16 [16, 384, 1280], P(('groups', 'gx')), parts along dimension 0, may hold values from -6 to 6
- out_grad: bfloat16 [16, 384, 1280], P(('groups', 'gx')), parts along dimension 0, may hold values from -6 to 6
- ln_gain: float32 [1280], replicated, may hold values from 0.1 to 1.9
- w_up: bfloat16 [1280, 2560], P('gx', 'gy'), may hold values from -0.15625 to 0.15625
- w_down: bfloat16 [1280, 2560], P('gx', 'gy'), may hold values from -0.15625 to 0.15625
- lengths: int32 [16], P('groups'), parts along dimension 0, may hold values from 1 to 384, 1024 in all
Outputs:
- input_grad: bfloat16 [16, 384, 1280], P(('groups', 'gx'), None, 'gy'), parts along dimension 0
- up_grad: float32 [2560, 2560], P(('groups', 'gx'), 'gy'), parts along dimension 0
The draws below stay inside these ranges and needn't reach their ends.
There are 2 independent parts, one for each index of `groups`. The reference program is written for one: setup_inputs(seed, part) draws one part's arguments, and reference() takes and returns one part's arrays. A program takes and returns all parts, laid end to end along the dimension named above; an argument that names none is the same for every part. Nothing has to cross between parts.
Inputs may be any that keep to these rules, and one draw needn't show every extreme that they name: The lengths of one replica sum to 1024, and the largest equals 384.
All inputs are finite; a program needn't handle non-finite values.
Results may differ from the reference program's by a relative error of at most 0.0055.
Values may be sent and summed in bfloat16 or wider, within the bound.
No kernel may reach another device: no remote copies, remote signals or barrier semaphores. Data moves between devices by JAX's collectives and lax.ppermute only.
A program may use at most 64 MiB of HBM per device.

```python
import math
import jax
import jax.numpy as jnp
import numpy as np
from jax import lax

D = 1280
HIDDEN_UNITS = 2560
FRAMES = 384
WINDOWS = 8
TOTAL = 1024


def strengthened(array, rng, source, target, blocks, factor):
    owner, partner = [(jnp.arange(array.shape[axis_at]) // (array.shape[axis_at] // blocks)).reshape([-1 if axis == axis_at else 1 for axis in range(array.ndim)]) for axis_at in (source, target)]
    chosen = jax.random.permutation(rng, blocks)[partner]
    strong = (owner == chosen) | (owner == (partner + blocks // 2) % blocks)
    return jnp.where(strong, factor * array, array)


def steps_of(stream_key, shape, pieces, low, top_value):
    level = 1.0
    for axis_at, parts in pieces:
        steps = jax.random.uniform(jax.random.fold_in(jax.random.fold_in(stream_key, 6), axis_at), (parts,), jnp.float32, low / len(pieces), top_value / len(pieces))
        level = level * jnp.repeat(jnp.exp(steps), shape[axis_at] // parts).reshape((-1,) + (1,) * (len(shape) - 1 - axis_at))
    return level


def length_profile(amount, total, most, skew):
    loads = [(1 << 20) // math.isqrt(grade ** skew) + 1 for grade in range(2, amount + 1)]
    surplus, given = total - most - (amount - 1), [1] * (amount - 1)
    while surplus > 0:
        movable = [i for i in range(amount - 1) if given[i] < most]
        whole, budget = sum([loads[i] for i in movable]), surplus
        for i in movable:
            more = min(most - given[i], max(1, budget * loads[i] // whole), surplus)
            given[i] = given[i] + more
            surplus = surplus - more
    return np.array([most] + given)


def uneven(own_key, count, total, reach, slope):
    if count == 2:
        one = jax.random.randint(own_key, (), max(1, total - reach), min(reach, total - 1) + 1)
        return jnp.stack([one, total - one])
    sizes = jnp.asarray(length_profile(count, total, reach, slope), jnp.int32)
    pairs = (count - 1) // 2
    giver, sink = sizes[1:1 + 2 * pairs:2], sizes[2:2 + 2 * pairs:2]
    margin = jnp.minimum(giver - 1, reach - sink)
    moved = jax.random.randint(jax.random.fold_in(own_key, 1), (pairs,), 0, 1 << 20) % (margin + 1)
    sizes = sizes.at[1:1 + 2 * pairs:2].set(giver - moved).at[2:2 + 2 * pairs:2].set(sink + moved)
    return sizes[jax.random.permutation(jax.random.fold_in(own_key, 2), count)]


def scatter_about(own_key, extent, spread, bound, pieces=(), held_as=jnp.bfloat16):
    array = spread * jax.random.normal(own_key, extent, jnp.float32)
    if pieces:
        array = array * steps_of(own_key, extent, pieces, -0.22, 0.18)
    return jnp.clip(array, -bound, bound).astype(held_as)


def bell_draw_with(own_key, shape, spread, limit, shards, heavy, kind=jnp.bfloat16):
    values = spread * jax.random.normal(own_key, shape, jnp.float32)
    if shards:
        values = values * steps_of(own_key, shape, shards, -0.22, 0.18)
    return jnp.clip(strengthened(values, jax.random.fold_in(own_key, 3), *heavy), -limit, limit).astype(kind)


def setup_inputs(seed: int = 0, part: int = 0) -> dict:
    keys = jax.random.split(jax.random.key(seed), 7)
    own_keys = jax.random.split(jax.random.fold_in(keys[6], part), 7)
    return {
        "frames": bell_draw_with(own_keys[0], (WINDOWS, FRAMES, D), 1.0, 6.0, ((0, 8),), (0, 2, 8, 2.0)),
        "out_grad": bell_draw_with(own_keys[1], (WINDOWS, FRAMES, D), 1.0, 6.0, ((0, 8),), (0, 2, 8, 2.0)),
        "ln_gain": jnp.clip(1.0 + 0.18 * jax.random.normal(keys[2], (D,), jnp.float32), 0.1, 1.9),
        "w_up": scatter_about(keys[3], (D, HIDDEN_UNITS), D ** -0.5, 0.15625, ((0, 8), (1, 2))),
        "w_down": scatter_about(keys[4], (D, HIDDEN_UNITS), D ** -0.5, 0.15625, ((0, 8), (1, 2))),
        "lengths": uneven(own_keys[5], WINDOWS, WINDOWS * FRAMES // 3, FRAMES, 2).astype(jnp.int32),
    }


def norm_rows(rows, gain):
    values = rows.astype(jnp.float32)
    centre = lax.optimization_barrier(jnp.mean(values, axis=-1, keepdims=True))
    shifted = values - centre
    variance = lax.optimization_barrier(jnp.mean(shifted * shifted, axis=-1, keepdims=True))
    inv_std = lax.rsqrt(variance + 1e-05)
    centred = shifted * inv_std
    normed = (centred * gain).astype(jnp.bfloat16)
    return (centred, inv_std, normed)

def gelu_slope(values):
    return 0.5 * (1.0 + lax.erf(values * 0.7071067811865476)) + values * jnp.exp(-0.5 * values * values) * 0.3989422804014327

def reference(frames, out_grad, ln_gain, w_up, w_down, lengths):
    flat_frames = frames.reshape(WINDOWS * FRAMES, D)
    flat_grads = out_grad.reshape(WINDOWS * FRAMES, D)
    valid_frames = (jnp.arange(FRAMES, dtype=jnp.int32)[None, :] < lengths[:, None]).reshape(-1).astype(jnp.int32)
    running = jnp.cumsum(valid_frames).astype(jnp.int32)
    targets = jnp.arange(TOTAL, dtype=jnp.int32) + 1
    pick_rows = jnp.searchsorted(running, targets, side='left').astype(jnp.int32)
    own_frames = jnp.take(flat_frames, pick_rows, axis=0)
    own_grads = jnp.take(flat_grads, pick_rows, axis=0)
    centred, inv_std, normed = norm_rows(own_frames, ln_gain)
    pre_act = jnp.dot(normed, w_up, preferred_element_type=jnp.float32)
    d_act = jnp.dot(own_grads, w_down, preferred_element_type=jnp.float32)
    d_pre = (d_act * gelu_slope(pre_act)).astype(jnp.bfloat16)
    up_grad = jnp.dot(normed.T, d_pre, preferred_element_type=jnp.float32)
    d_norm = jnp.dot(d_pre, w_up.T, preferred_element_type=jnp.float32)
    scaled = d_norm * ln_gain
    first_mean = lax.optimization_barrier(jnp.mean(scaled, axis=-1, keepdims=True))
    second_mean = lax.optimization_barrier(jnp.mean(scaled * centred, axis=-1, keepdims=True))
    input_rows = (own_grads.astype(jnp.float32) + inv_std * (scaled - first_mean - centred * second_mean)).astype(jnp.bfloat16)
    result = jnp.zeros((WINDOWS * FRAMES, D), jnp.bfloat16).at[pick_rows].set(input_rows)
    return (result.reshape(WINDOWS, FRAMES, D), up_grad)
```

```python
import jax
import jax.numpy as jnp
from jax import lax
from jax.sharding import PartitionSpec as P


def norm_rows(rows):
    values = rows.astype(jnp.float32)
    centre = jnp.mean(values, axis=-1, keepdims=True)
    shifted = values - centre
    variance = jnp.mean(shifted * shifted, axis=-1, keepdims=True)
    inv_std = lax.rsqrt(variance + 1e-05)
    return shifted * inv_std, inv_std


def gelu_slope(values):
    return (
        0.5 * (1.0 + lax.erf(values * 0.7071067811865476))
        + values * jnp.exp(-0.5 * values * values) * 0.3989422804014327
    )


def ring_member(place, count):
    place = place % count
    return jnp.where(place < count // 2, 2 * place, 2 * (count - 1 - place) + 1)


def shards(frames, out_grad, ln_gain, w_up, w_down, lengths):
    peers = lax.axis_size("gx")
    half = peers // 2
    own = lax.axis_index("gx")
    side = lax.axis_index("groups")
    core = lax.axis_index("gy")
    frame_len, width = frames.shape[1:]
    depth, hidden = w_up.shape
    quarter = hidden // 2
    half_width = width // 2
    bf16, f32 = jnp.bfloat16, jnp.float32

    order = list(range(0, peers, 2)) + list(range(peers - 1, 0, -2))
    ahead = [(order[i], order[(i + 1) % peers]) for i in range(peers)]
    behind = [(b, a) for a, b in ahead]
    place = jnp.where(own % 2 == 0, own // 2, peers - 1 - own // 2)
    swap = [(0, 1), (1, 0)]
    wire = bf16 if half <= 8 else f32

    mine = jnp.stack(
        [lax.dynamic_slice_in_dim(w, side * quarter, quarter, 1) for w in (w_up, w_down)]
    )

    centred, inv_std = norm_rows(frames[0])
    normed = (centred * ln_gain).astype(bf16)
    length = lax.dynamic_index_in_dim(lengths, own, 0, keepdims=False)
    keep = (jnp.arange(frame_len, dtype=jnp.int32) < length)[:, None]
    grads = jnp.where(keep, out_grad[0], 0)
    first = core == 0
    fetched = lax.ppermute(jnp.where(first, normed, grads), "groups", swap)
    sibling = lax.ppermute(fetched, "gy", swap)
    other_normed = jnp.where(first, fetched, sibling)
    other_grads = jnp.where(first, sibling, fetched)

    full = jnp.zeros((2, depth * peers, quarter), bf16)

    def put(full, block, step, at=0):
        row = ring_member(place + step + peers, peers) * depth
        return lax.dynamic_update_slice(full, block, (at, row, 0))

    full = put(full, mine, 0)
    up, down = mine, mine
    for step in range(1, half):
        up = lax.ppermute(up, "gx", ahead)
        down = lax.ppermute(down, "gx", behind)
        full = put(full, up, -step)
        full = put(full, down, step)
    full = put(full, lax.ppermute(up[:1], "gx", ahead), half)
    full = put(full, lax.ppermute(down[1:], "gx", behind), half, 1)
    full_up, full_down = full[0], full[1]

    normed_all = jnp.concatenate([normed, other_normed])
    grads_all = jnp.concatenate([grads, other_grads])
    pre_act = jnp.dot(normed_all, full_up, preferred_element_type=f32)
    d_act = jnp.dot(grads_all, full_down, preferred_element_type=f32)
    d_pre = (d_act * gelu_slope(pre_act)).astype(bf16)

    partial = jnp.stack(
        [
            lax.dot_general(
                normed_all[i * frame_len : (i + 1) * frame_len],
                d_pre[i * frame_len : (i + 1) * frame_len],
                (((0,), (0,)), ((), ())),
                preferred_element_type=f32,
            )
            for i in range(2)
        ]
    )

    def term(step):
        row = ring_member(place + step + peers, peers) * depth
        return lax.dynamic_slice_in_dim(partial, row, depth, 1)

    far = term(half)
    up = lax.ppermute(far[0].astype(wire), "gx", ahead)
    down = lax.ppermute(far[1].astype(wire), "gx", behind)
    for step in range(half - 1, 0, -1):
        up_term, down_term = term(step), term(-step)
        if step == half - 1:
            up = jnp.stack([up_term[0] + up.astype(f32), up_term[1]])
            down = jnp.stack([down_term[0], down_term[1] + down.astype(f32)])
        else:
            up = up_term + up.astype(f32)
            down = down_term + down.astype(f32)
        up = lax.ppermute(up.astype(wire), "gx", ahead)
        down = lax.ppermute(down.astype(wire), "gx", behind)
    total = term(0) + up.astype(f32) + down.astype(f32)
    passed = lax.ppermute(total[1].astype(wire), "groups", swap).astype(f32)
    low = jnp.where(side == 0, total[0], passed)
    high = jnp.where(side == 0, passed, total[0])
    up_grad = jnp.concatenate([low, high], axis=1)

    d_norm = lax.dot_general(
        d_pre, full_up, (((1,), (1,)), ((), ())), preferred_element_type=f32
    )
    first_sum = jnp.sum(d_norm * ln_gain, axis=-1)
    second_sum = jnp.sum(d_pre.astype(f32) * pre_act, axis=-1)
    sums = jnp.stack([first_sum, second_sum])
    sums = sums + lax.ppermute(sums, "gy", swap)
    sums = sums[:, :frame_len] + lax.ppermute(sums[:, frame_len:], "groups", swap)
    means = (sums / width)[:, :, None]
    keep_cols = lax.dynamic_slice_in_dim(d_norm, core * half_width, half_width, 1)
    send_cols = lax.dynamic_slice_in_dim(d_norm, (1 - core) * half_width, half_width, 1)
    cols = keep_cols + lax.ppermute(send_cols.astype(bf16), "gy", swap).astype(f32)
    back = lax.ppermute(cols[frame_len:].astype(bf16), "groups", swap)
    d_norm = cols[:frame_len] + back.astype(f32)

    def own_cols(array):
        return lax.dynamic_slice_in_dim(array, core * half_width, half_width, array.ndim - 1)

    scaled = d_norm * own_cols(ln_gain)
    input_grad = own_cols(grads).astype(f32) + inv_std * (
        scaled - means[0] - own_cols(centred) * means[1]
    )
    return (input_grad.astype(bf16)[None], up_grad)


def solution(mesh):
    placed = (
        P(("groups", "gx"), None, None),
        P(("groups", "gx"), None, None),
        P(),
        P("gx", "gy"),
        P("gx", "gy"),
        P("groups"),
    )
    return jax.shard_map(
        shards,
        mesh=mesh,
        in_specs=placed,
        out_specs=(P(("groups", "gx"), None, "gy"), P(("groups", "gx"), "gy")),
        check_vma=False,
    )
```

```python
import jax
import jax.numpy as jnp
from jax import lax
from jax.sharding import PartitionSpec as P


def norm_rows(rows):
    values = rows.astype(jnp.float32)
    centre = jnp.mean(values, axis=-1, keepdims=True)
    shifted = values - centre
    variance = jnp.mean(shifted * shifted, axis=-1, keepdims=True)
    inv_std = lax.rsqrt(variance + 1e-05)
    return shifted * inv_std, inv_std


def gelu_slope(values):
    return (
        0.5 * (1.0 + lax.erf(values * 0.7071067811865476))
        + values * jnp.exp(-0.5 * values * values) * 0.3989422804014327
    )


def ring_member(place, count):
    place = place % count
    return jnp.where(place < count // 2, 2 * place, 2 * (count - 1 - place) + 1)


def shards(frames, out_grad, ln_gain, w_up, w_down, lengths):
    peers = lax.axis_size("gx")
    half = peers // 2
    own = lax.axis_index("gx")
    side = lax.axis_index("groups")
    core = lax.axis_index("gy")
    frame_len, width = frames.shape[1:]
    depth, hidden = w_up.shape
    quarter = hidden // 2
    half_width = width // 2
    bf16, f32 = jnp.bfloat16, jnp.float32

    order = list(range(0, peers, 2)) + list(range(peers - 1, 0, -2))
    ahead = [(order[i], order[(i + 1) % peers]) for i in range(peers)]
    behind = [(b, a) for a, b in ahead]
    place = jnp.where(own % 2 == 0, own // 2, peers - 1 - own // 2)
    swap = [(0, 1), (1, 0)]
    wire = bf16 if half <= 8 else f32

    mine = [lax.dynamic_slice_in_dim(w, side * quarter, quarter, 1) for w in (w_up, w_down)]
    mine, frames, out_grad = lax.optimization_barrier((mine, frames, out_grad))

    half_rows = frame_len // 2

    def fetch(rows):
        part = lax.dynamic_slice_in_dim(rows, core * half_rows, half_rows, 0)
        part = lax.ppermute(part, "groups", swap)
        return jnp.concatenate([part, lax.ppermute(part, "gy", swap)])

    length = lax.dynamic_index_in_dim(lengths, own, 0, keepdims=False)
    keep = (jnp.arange(frame_len, dtype=jnp.int32) < length)[:, None]
    grads = jnp.where(keep, out_grad[0], 0)
    other_grads = fetch(grads)
    centred, inv_std = norm_rows(frames[0])
    normed = (centred * ln_gain).astype(bf16)
    other_normed = fetch(normed)

    def put(full, block, step):
        row = ring_member(place + step + peers, peers) * depth
        return lax.dynamic_update_slice(full, block, (row, 0))

    blank = jnp.zeros((depth * peers, quarter), bf16)
    full = [put(blank, block, 0) for block in mine]
    up, down = list(mine), list(mine)
    for step in range(1, half):
        for i in range(2):
            up[i] = lax.ppermute(up[i], "gx", ahead)
            down[i] = lax.ppermute(down[i], "gx", behind)
        for i in range(2):
            full[i] = put(put(full[i], up[i], -step), down[i], step)
    full_up = put(full[0], lax.ppermute(up[0], "gx", ahead), half)
    full_down = put(full[1], lax.ppermute(down[1], "gx", behind), half)

    rows = [(normed, grads), (other_normed, other_grads)]
    d_pre, partial, second_sum = [None] * 2, [None] * 2, [None] * 2
    for i in (1, 0):
        pre_act = jnp.dot(rows[i][0], full_up, preferred_element_type=f32)
        d_act = jnp.dot(rows[i][1], full_down, preferred_element_type=f32)
        d_pre[i] = (d_act * gelu_slope(pre_act)).astype(bf16)
        second_sum[i] = jnp.sum(d_pre[i].astype(f32) * pre_act, axis=-1)
        partial[i] = lax.dot_general(
            rows[i][0], d_pre[i], (((0,), (0,)), ((), ())), preferred_element_type=f32
        )

    def term(i, step):
        row = ring_member(place + step + peers, peers) * depth
        return lax.dynamic_slice_in_dim(partial[i], row, depth, 0)

    up, down = [None] * 2, [None] * 2
    down[1] = lax.ppermute(term(1, half).astype(wire), "gx", behind)
    up[0] = lax.ppermute(term(0, half).astype(wire), "gx", ahead)
    for step in range(half - 1, 0, -1):
        for i in (1, 0):
            for way, at, pairs in ((up, step, ahead), (down, -step, behind)):
                value = term(i, at)
                if way[i] is not None:
                    value = value + way[i].astype(f32)
                way[i] = lax.ppermute(value.astype(wire), "gx", pairs)
    total = [term(i, 0) + up[i].astype(f32) + down[i].astype(f32) for i in range(2)]
    passed = lax.ppermute(total[1].astype(wire), "groups", swap).astype(f32)
    low = jnp.where(side == 0, total[0], passed)
    high = jnp.where(side == 0, passed, total[0])
    up_grad = jnp.concatenate([low, high], axis=1)

    def swap_halves(array):
        return jnp.concatenate([array[half_rows:], array[:half_rows]])

    cols, sums = [None] * 2, [None] * 2
    for i in (1, 0):
        d_norm = lax.dot_general(
            d_pre[i], full_up, (((1,), (1,)), ((), ())), preferred_element_type=f32
        )
        first_sum = jnp.sum(d_norm * ln_gain, axis=-1)
        sums[i] = jnp.stack([first_sum, second_sum[i]], axis=1)
        mine_cols = lax.dynamic_slice_in_dim(d_norm, core * half_width, half_width, 1)
        send = lax.dynamic_slice_in_dim(d_norm, (1 - core) * half_width, half_width, 1)
        came = lax.ppermute(send.astype(bf16), "gy", swap)
        came_sums = lax.ppermute(sums[i], "gy", swap)
        if i == 1:
            came, came_sums = swap_halves(came), swap_halves(came_sums)
        cols[i] = mine_cols + came.astype(f32)
        sums[i] = sums[i] + came_sums

    def in_order(array):
        return jnp.where(core == 0, array, swap_halves(array))

    back = lax.ppermute(in_order(cols[1].astype(bf16)), "groups", swap)
    means = (sums[0] + lax.ppermute(in_order(sums[1]), "groups", swap)) / width

    def own_cols(array):
        return lax.dynamic_slice_in_dim(array, core * half_width, half_width, array.ndim - 1)

    scaled = (cols[0] + back.astype(f32)) * own_cols(ln_gain)
    input_grad = own_cols(grads).astype(f32) + inv_std * (
        scaled - means[:, :1] - own_cols(centred) * means[:, 1:]
    )
    return (input_grad.astype(bf16)[None], up_grad)


def solution(mesh):
    placed = (
        P(("groups", "gx"), None, None),
        P(("groups", "gx"), None, None),
        P(),
        P("gx", "gy"),
        P("gx", "gy"),
        P("groups"),
    )
    return jax.shard_map(
        shards,
        mesh=mesh,
        in_specs=placed,
        out_specs=(P(("groups", "gx"), None, "gy"), P(("groups", "gx"), "gy")),
        check_vma=False,
    )
```

```python
import functools

import jax
import jax.numpy as jnp
from jax import lax
from jax.experimental import pallas as pl
from jax.experimental.pallas import tpu as pltpu
from jax.sharding import PartitionSpec as P

BF16, F32 = jnp.bfloat16, jnp.float32
VMEM = pl.BlockSpec(memory_space=pltpu.VMEM)
SMEM = pl.BlockSpec(memory_space=pltpu.SMEM)


def shape(dims, kind):
    return jax.ShapeDtypeStruct(dims, kind)


def call(kernel, ins, out_shape, flops, scratch=(), vmem=32, aliases=None):
    outs = jax.tree.leaves(out_shape)
    moved = sum(x.size * x.dtype.itemsize for x in list(ins) + outs)
    return pl.pallas_call(
        kernel,
        out_shape=out_shape,
        in_specs=[SMEM if x.dtype == jnp.int32 else VMEM for x in ins],
        out_specs=jax.tree.map(lambda _: VMEM, out_shape),
        scratch_shapes=list(scratch),
        input_output_aliases=aliases or {},
        compiler_params=pltpu.CompilerParams(vmem_limit_bytes=vmem << 20),
        cost_estimate=pl.CostEstimate(flops=flops, bytes_accessed=moved, transcendentals=0),
    )(*ins)


def dot(left, right, left_dim=1, right_dim=0):
    return lax.dot_general(
        left, right, (((left_dim,), (right_dim,)), ((), ())), preferred_element_type=F32
    )


def gelu_slope(values):
    return (
        0.5 * (1.0 + lax.erf(values * 0.7071067811865476))
        + values * jnp.exp(-0.5 * values * values) * 0.3989422804014327
    )


def norm_kernel(meta, frames, out_grad, gain, normed, grads, share, stats):
    length, core = meta[0], meta[1]
    values = frames[...].astype(F32)
    centre = jnp.mean(values, axis=-1, keepdims=True)
    shifted = values - centre
    variance = jnp.mean(shifted * shifted, axis=-1, keepdims=True)
    inv_std = lax.rsqrt(variance + 1e-05)
    stats[:, 0:1] = centre
    stats[:, 1:2] = inv_std
    normed[...] = (shifted * inv_std * gain[...]).astype(BF16)
    keep = lax.broadcasted_iota(jnp.int32, (frames.shape[0], 1), 0) < length
    grads[...] = jnp.where(keep, out_grad[...].astype(F32), 0.0).astype(BF16)
    half = share.shape[1]
    rows = pl.ds(pl.multiple_of(core * half, half), half)
    share[0] = normed[rows, :]
    share[1] = grads[rows, :]


def back_through(normed, grads, up, down, d_pre, partial):
    pre_act = dot(normed[...], up[...])
    d_act = dot(grads[...], down[...])
    d_pre[...] = (d_act * gelu_slope(pre_act)).astype(BF16)
    partial[...] = dot(normed[...], d_pre[...], 0, 0)


def other_kernel(count, meta, first, second, *refs):
    blocks, refs = refs[: 2 * count], refs[2 * count :]
    d_pre, partial, up, down, normed, grads = refs
    half, depth = first.shape[1], blocks[0].shape[0]
    for i in range(count):
        rows = pl.ds(pl.multiple_of(meta[i] * depth, depth), depth)
        up[rows, :] = blocks[i][...]
        down[rows, :] = blocks[count + i][...]
    for at, part in ((0, first), (half, second)):
        normed[at : at + half, :] = part[0]
        grads[at : at + half, :] = part[1]
    back_through(normed, grads, up, down, d_pre, partial)


def own_kernel(normed, grads, up, down, d_pre, partial):
    back_through(normed, grads, up, down, d_pre, partial)


def d_norm_kernel(meta, d_pre_own, d_pre_other, up, keep, send):
    core = meta[1]
    rows, width = keep.shape[1:]
    mine = up[pl.ds(pl.multiple_of(core * width, width), width), :]
    theirs = up[pl.ds(pl.multiple_of((1 - core) * width, width), width), :]
    keep[0] = dot(d_pre_own[...], mine, 1, 1)
    keep[1] = dot(d_pre_other[...], mine, 1, 1)
    send[0] = dot(d_pre_own[...], theirs, 1, 1).astype(BF16)
    sent = dot(d_pre_other[...], theirs, 1, 1).astype(BF16)
    send[1, rows // 2 :, :] = sent[: rows // 2]
    send[1, : rows // 2, :] = sent[rows // 2 :]


def over_kernel(meta, keep, came, over):
    half = over.shape[0] // 2
    for i in range(2):
        at = lax.rem(i + meta[1], 2) * half
        rows = slice(i * half, (i + 1) * half)
        value = keep[1, rows, :] + came[1, rows, :].astype(F32)
        over[pl.ds(pl.multiple_of(at, half), half), :] = value.astype(BF16)


def own_columns(meta, ref, width):
    return ref[:, pl.ds(pl.multiple_of(meta[1] * width, width), width)]


def scale_kernel(meta, keep, came, back, frames, gain, stats, scaled, sums):
    width = scaled.shape[1]
    d_norm = keep[0] + came[0].astype(F32) + back[...].astype(F32)
    value = d_norm * own_columns(meta, gain, width)
    scaled[...] = value
    rows = own_columns(meta, frames, width).astype(F32)
    centred = (rows - stats[:, 0:1]) * stats[:, 1:2]
    sums[:, 0:1] = jnp.sum(value, axis=-1, keepdims=True)
    sums[:, 1:2] = jnp.sum(value * centred, axis=-1, keepdims=True)


def input_kernel(meta, scaled, sums, came, frames, grads, stats, out):
    width = scaled.shape[1]
    means = (sums[...] + came[...]) * (0.5 / width)
    rows = own_columns(meta, frames, width).astype(F32)
    inv_std = stats[:, 1:2]
    centred = (rows - stats[:, 0:1]) * inv_std
    value = inv_std * (scaled[...] - means[:, 0:1] - centred * means[:, 1:2])
    out[...] = (own_columns(meta, grads, width).astype(F32) + value).astype(BF16)


def ring_member(place, count):
    place = place % count
    return jnp.where(place < count // 2, 2 * place, 2 * (count - 1 - place) + 1)


def shards(frames, out_grad, ln_gain, w_up, w_down, lengths):
    peers = lax.axis_size("gx")
    half = peers // 2
    own = lax.axis_index("gx")
    side = lax.axis_index("groups")
    core = lax.axis_index("gy")
    frame_len, width = frames.shape[1:]
    depth, hidden = w_up.shape
    quarter = hidden // 2
    half_width = width // 2
    half_rows = frame_len // 2
    ringed = peers <= 16 and peers % 2 == 0 and depth % 16 == 0

    order = list(range(0, peers, 2)) + list(range(peers - 1, 0, -2))
    ahead = [(order[i], order[(i + 1) % peers]) for i in range(peers)]
    behind = [(b, a) for a, b in ahead]
    place = jnp.where(own % 2 == 0, own // 2, peers - 1 - own // 2)
    swap = [(0, 1), (1, 0)]

    mine = [lax.dynamic_slice_in_dim(w, side * quarter, quarter, 1) for w in (w_up, w_down)]
    mine, frames, out_grad = lax.optimization_barrier((mine, frames, out_grad))

    length = lax.dynamic_index_in_dim(lengths, own, 0, keepdims=False)
    meta = jnp.stack([length, core]).astype(jnp.int32)
    gain = ln_gain[None]
    frames, out_grad = frames[0], out_grad[0]
    rows_of = shape((frame_len, width), BF16)
    normed, grads, share, stats = call(
        norm_kernel,
        (meta, frames, out_grad, gain),
        (rows_of, rows_of, shape((2, half_rows, width), BF16), shape((frame_len, 2), F32)),
        10 * frame_len * width,
    )
    first = lax.ppermute(share, "groups", swap)
    second = lax.ppermute(first, "gy", swap)

    if ringed:
        blocks = {0: tuple(mine)}
        up, down = list(mine), list(mine)
        for step in range(1, half):
            for i in range(2):
                up[i] = lax.ppermute(up[i], "gx", ahead)
                down[i] = lax.ppermute(down[i], "gx", behind)
            blocks[-step], blocks[step] = tuple(up), tuple(down)
        blocks[half] = (lax.ppermute(up[0], "gx", ahead), lax.ppermute(down[1], "gx", behind))
        steps = list(blocks)
        index = jnp.stack([ring_member(place + step + peers, peers) for step in steps])
        blocks = [blocks[step][i] for i in range(2) for step in steps]
    else:
        blocks = [lax.all_gather(block, "gx", axis=0, tiled=True) for block in mine]
        index = jnp.zeros((1,), jnp.int32)

    weight = shape((depth * peers, quarter), BF16)
    d_pre_of, partial_of = shape((frame_len, quarter), BF16), shape((width, quarter), F32)
    flops = 6 * frame_len * width * quarter
    d_pre_other, partial_other, full_up, full_down = call(
        functools.partial(other_kernel, len(blocks) // 2),
        (index.astype(jnp.int32), first, second, *blocks),
        (d_pre_of, partial_of, weight, weight),
        flops,
        [pltpu.VMEM((frame_len, width), BF16)] * 2,
    )
    d_pre_own, partial_own = call(
        own_kernel, (normed, grads, full_up, full_down), (d_pre_of, partial_of), flops
    )
    partial = [partial_own, partial_other]

    if ringed:

        def term(i, step):
            row = ring_member(place + step + peers, peers) * depth
            return lax.dynamic_slice_in_dim(partial[i], row, depth, 0)

        up, down = [None] * 2, [None] * 2
        down[1] = lax.ppermute(term(1, half).astype(BF16), "gx", behind)
        up[0] = lax.ppermute(term(0, half).astype(BF16), "gx", ahead)
        for step in range(half - 1, 0, -1):
            for i in (1, 0):
                for way, at, pairs in ((up, step, ahead), (down, -step, behind)):
                    value = term(i, at)
                    if way[i] is not None:
                        value = value + way[i].astype(F32)
                    way[i] = lax.ppermute(value.astype(BF16), "gx", pairs)
        total = [term(i, 0) + up[i].astype(F32) + down[i].astype(F32) for i in range(2)]
    else:
        total = [lax.psum_scatter(p, "gx", scatter_dimension=0, tiled=True) for p in partial]
    passed = lax.ppermute(total[1].astype(BF16), "groups", swap).astype(F32)
    low = jnp.where(side == 0, total[0], passed)
    high = jnp.where(side == 0, passed, total[0])
    up_grad = jnp.concatenate([low, high], axis=1)

    keep, send = call(
        d_norm_kernel,
        (meta, d_pre_own, d_pre_other, full_up),
        (shape((2, frame_len, half_width), F32), shape((2, frame_len, half_width), BF16)),
        4 * frame_len * width * quarter,
    )
    came = lax.ppermute(send, "gy", swap)
    over = call(
        over_kernel, (meta, keep, came), shape((frame_len, half_width), BF16), frame_len * width
    )
    back = lax.ppermute(over, "groups", swap)
    scaled, sums = call(
        scale_kernel,
        (meta, keep, came, back, frames, gain, stats),
        (shape((frame_len, half_width), F32), shape((frame_len, 2), F32)),
        4 * frame_len * width,
    )
    input_grad = call(
        input_kernel,
        (meta, scaled, sums, lax.ppermute(sums, "gy", swap), frames, grads, stats),
        shape((frame_len, half_width), BF16),
        4 * frame_len * width,
    )
    return (input_grad[None], up_grad)


def solution(mesh):
    placed = (
        P(("groups", "gx"), None, None),
        P(("groups", "gx"), None, None),
        P(),
        P("gx", "gy"),
        P("gx", "gy"),
        P("groups"),
    )
    return jax.shard_map(
        shards,
        mesh=mesh,
        in_specs=placed,
        out_specs=(P(("groups", "gx"), None, "gy"), P(("groups", "gx"), "gy")),
        check_vma=False,
    )
```

```python
import functools

import jax
import jax.numpy as jnp
from jax import lax
from jax.experimental import pallas as pl
from jax.experimental.pallas import tpu as pltpu
from jax.sharding import PartitionSpec as P

BF16, F32 = jnp.bfloat16, jnp.float32
VMEM = pl.BlockSpec(memory_space=pltpu.VMEM)
SMEM = pl.BlockSpec(memory_space=pltpu.SMEM)


def shape(dims, kind):
    return jax.ShapeDtypeStruct(dims, kind)


def call(kernel, ins, out_shape, flops, scratch=(), vmem=16, aliases=None):
    outs = jax.tree.leaves(out_shape)
    moved = sum(x.size * x.dtype.itemsize for x in list(ins) + outs)
    return pl.pallas_call(
        kernel,
        out_shape=out_shape,
        in_specs=[SMEM if x.dtype == jnp.int32 else VMEM for x in ins],
        out_specs=jax.tree.map(lambda _: VMEM, out_shape),
        scratch_shapes=list(scratch),
        input_output_aliases=aliases or {},
        compiler_params=pltpu.CompilerParams(vmem_limit_bytes=vmem << 20),
        cost_estimate=pl.CostEstimate(flops=flops, bytes_accessed=moved, transcendentals=0),
    )(*ins)


def dot(left, right, left_dim=1, right_dim=0):
    return lax.dot_general(
        left, right, (((left_dim,), (right_dim,)), ((), ())), preferred_element_type=F32
    )


def gelu_slope(values):
    return (
        0.5 * (1.0 + lax.erf(values * 0.7071067811865476))
        + values * jnp.exp(-0.5 * values * values) * 0.3989422804014327
    )


def norm_kernel(meta, frames, out_grad, gain, normed, grads, share, stats):
    length, core = meta[0], meta[1]
    values = frames[...].astype(F32)
    centre = jnp.mean(values, axis=-1, keepdims=True)
    shifted = values - centre
    variance = jnp.mean(shifted * shifted, axis=-1, keepdims=True)
    inv_std = lax.rsqrt(variance + 1e-05)
    stats[:, 0:1] = centre
    stats[:, 1:2] = inv_std
    normed[...] = (shifted * inv_std * gain[...]).astype(BF16)
    keep = lax.broadcasted_iota(jnp.int32, (frames.shape[0], 1), 0) < length
    grads[...] = jnp.where(keep, out_grad[...].astype(F32), 0.0).astype(BF16)
    half = share.shape[1]
    rows = pl.ds(pl.multiple_of(core * half, half), half)
    share[0] = normed[rows, :]
    share[1] = grads[rows, :]


def back_through(normed, grads, up, down, d_pre, partial):
    pre_act = dot(normed[...], up[...])
    d_act = dot(grads[...], down[...])
    d_pre[...] = (d_act * gelu_slope(pre_act)).astype(BF16)
    partial[...] = dot(normed[...], d_pre[...], 0, 0)


def place_kernel(index, *refs):
    blocks, (up, down) = refs[:-2], refs[-2:]
    depth = blocks[0].shape[1]
    for i, block in enumerate(blocks):
        rows = pl.ds(pl.multiple_of(index[i] * depth, depth), depth)
        up[rows, :] = block[0]
        down[rows, :] = block[1]


def other_kernel(index, first, second, _, __, *refs):
    d_pre, partial, up, down, normed, grads = refs[-6:]
    half = first.shape[1]
    for ref, block in zip((up, down), refs[:-6]):
        depth = block.shape[0]
        rows = pl.ds(pl.multiple_of(index[index.shape[0] - 1] * depth, depth), depth)
        ref[rows, :] = block[...]
    for at, part in ((0, first), (half, second)):
        normed[at : at + half, :] = part[0]
        grads[at : at + half, :] = part[1]
    back_through(normed, grads, up, down, d_pre, partial)


def own_kernel(normed, grads, up, down, d_pre, partial):
    back_through(normed, grads, up, down, d_pre, partial)


def d_norm_kernel(meta, d_pre_own, d_pre_other, up, keep, send):
    core = meta[1]
    rows, width = keep.shape[1:]
    mine = up[pl.ds(pl.multiple_of(core * width, width), width), :]
    theirs = up[pl.ds(pl.multiple_of((1 - core) * width, width), width), :]
    keep[0] = dot(d_pre_own[...], mine, 1, 1)
    keep[1] = dot(d_pre_other[...], mine, 1, 1)
    send[0] = dot(d_pre_own[...], theirs, 1, 1).astype(BF16)
    sent = dot(d_pre_other[...], theirs, 1, 1).astype(BF16)
    send[1, rows // 2 :, :] = sent[: rows // 2]
    send[1, : rows // 2, :] = sent[rows // 2 :]


def over_kernel(meta, keep, came, over):
    half = over.shape[0] // 2
    for i in range(2):
        at = lax.rem(i + meta[1], 2) * half
        rows = slice(i * half, (i + 1) * half)
        value = keep[1, rows, :] + came[1, rows, :].astype(F32)
        over[pl.ds(pl.multiple_of(at, half), half), :] = value.astype(BF16)


def own_columns(meta, ref, width):
    return ref[:, pl.ds(pl.multiple_of(meta[1] * width, width), width)]


def scale_kernel(meta, keep, came, back, frames, gain, stats, scaled, sums):
    width = scaled.shape[1]
    d_norm = keep[0] + came[0].astype(F32) + back[...].astype(F32)
    value = d_norm * own_columns(meta, gain, width)
    scaled[...] = value
    rows = own_columns(meta, frames, width).astype(F32)
    centred = (rows - stats[:, 0:1]) * stats[:, 1:2]
    sums[:, 0:1] = jnp.sum(value, axis=-1, keepdims=True)
    sums[:, 1:2] = jnp.sum(value * centred, axis=-1, keepdims=True)


def input_kernel(meta, scaled, sums, came, frames, grads, stats, out):
    width = scaled.shape[1]
    means = (sums[...] + came[...]) * (0.5 / width)
    rows = own_columns(meta, frames, width).astype(F32)
    inv_std = stats[:, 1:2]
    centred = (rows - stats[:, 0:1]) * inv_std
    value = inv_std * (scaled[...] - means[:, 0:1] - centred * means[:, 1:2])
    out[...] = (own_columns(meta, grads, width).astype(F32) + value).astype(BF16)


def hop_kernel(at, given, index, *refs):
    partial, came, out = refs[:2], refs[2:-1], refs[-1]
    depth = out.shape[-2]
    rows = pl.ds(pl.multiple_of(index[at] * depth, depth), depth)
    for i in range(2):
        value = partial[i][rows, :]
        if i in given:
            for ref in came:
                value = value + (ref[i] if len(ref.shape) == 3 else ref[...]).astype(F32)
        out[i] = value.astype(out.dtype)


def total_kernel(index, own, other, up, down, total, passing):
    depth = total.shape[0]
    rows = pl.ds(pl.multiple_of(index[0] * depth, depth), depth)
    total[...] = own[rows, :] + up[0].astype(F32) + down[0].astype(F32)
    passing[...] = (other[rows, :] + up[1].astype(F32) + down[1].astype(F32)).astype(BF16)


def join_kernel(meta, own, passed, out):
    width = own.shape[1]
    side = meta[2]
    out[:, pl.ds(pl.multiple_of(side * width, width), width)] = own[...]
    other = pl.ds(pl.multiple_of((1 - side) * width, width), width)
    out[:, other] = passed[...].astype(F32)


def ring_member(place, count):
    place = place % count
    return jnp.where(place < count // 2, 2 * place, 2 * (count - 1 - place) + 1)


def shards(frames, out_grad, ln_gain, w_up, w_down, lengths):
    peers = lax.axis_size("gx")
    half = peers // 2
    own = lax.axis_index("gx")
    side = lax.axis_index("groups")
    core = lax.axis_index("gy")
    frame_len, width = frames.shape[1:]
    depth, hidden = w_up.shape
    quarter = hidden // 2
    half_width = width // 2
    half_rows = frame_len // 2
    ringed = peers <= 16 and peers % 2 == 0 and depth % 16 == 0

    order = list(range(0, peers, 2)) + list(range(peers - 1, 0, -2))
    ahead = [(order[i], order[(i + 1) % peers]) for i in range(peers)]
    behind = [(b, a) for a, b in ahead]
    place = jnp.where(own % 2 == 0, own // 2, peers - 1 - own // 2)
    swap = [(0, 1), (1, 0)]
    after = lax.optimization_barrier

    mine = [lax.dynamic_slice_in_dim(w, side * quarter, quarter, 1) for w in (w_up, w_down)]
    mine, frames, out_grad, ln_gain, lengths = after(
        (mine, frames, out_grad, ln_gain, lengths)
    )

    length = lax.dynamic_index_in_dim(lengths, own, 0, keepdims=False)
    meta = jnp.stack([length, core, side]).astype(jnp.int32)
    gain = ln_gain[None]
    frames, out_grad = frames[0], out_grad[0]
    rows_of = shape((frame_len, width), BF16)
    normed, grads, share, stats = call(
        norm_kernel,
        (meta, frames, out_grad, gain),
        (rows_of, rows_of, shape((2, half_rows, width), BF16), shape((frame_len, 2), F32)),
        10 * frame_len * width,
    )
    first = lax.ppermute(share, "groups", swap)

    weight = shape((depth * peers, quarter), BF16)
    if ringed:
        pair = jnp.stack(mine)
        blocks = {0: pair}
        up, down = pair, pair
        for step in range(1, half):
            up, down = lax.ppermute(up, "gx", ahead), lax.ppermute(down, "gx", behind)
            if step == 1:
                up, down, share = after((up, down, share))
            else:
                up, down = after((up, down))
            blocks[-step], blocks[step] = up, down
        far = lax.ppermute(up[0], "gx", ahead), lax.ppermute(down[1], "gx", behind)
        steps = list(blocks)
        index = jnp.stack([ring_member(place + step + peers, peers) for step in steps + [half]])
        index = index.astype(jnp.int32)
        first, up = after((first, up))
        near = [blocks[step] for step in steps]
        full_up, full_down = call(place_kernel, (index, *near), (weight, weight), 0)
    else:
        full_up, full_down = [lax.all_gather(w, "gx", axis=0, tiled=True) for w in mine]
        index = own[None].astype(jnp.int32)
        far = ()
    second = lax.ppermute(first, "gy", swap)

    d_pre_of, partial_of = shape((frame_len, quarter), BF16), shape((width, quarter), F32)
    flops = 6 * frame_len * width * quarter
    d_pre_other, partial_other, full_up, full_down = call(
        other_kernel,
        (index, first, second, full_up, full_down, *far),
        (d_pre_of, partial_of, weight, weight),
        flops,
        [pltpu.VMEM((frame_len, width), BF16)] * 2,
        aliases={3: 2, 4: 3},
    )
    d_pre_own, partial_own = call(
        own_kernel, (normed, grads, full_up, full_down), (d_pre_of, partial_of), flops
    )
    partial = [partial_own, partial_other]

    keep, send = call(
        d_norm_kernel,
        (meta, d_pre_own, d_pre_other, full_up),
        (shape((2, frame_len, half_width), F32), shape((2, frame_len, half_width), BF16)),
        4 * frame_len * width * quarter,
    )

    def sum_cores(send):
        came = lax.ppermute(send, "gy", swap)
        over = call(
            over_kernel, (meta, keep, came), shape((frame_len, half_width), BF16), frame_len * width
        )
        return came, over

    if ringed:

        pair_of = shape((2, depth, quarter), BF16)
        place_of = {step: i for i, step in enumerate(steps + [half])}

        def hop(step, given, *came):
            kernel = functools.partial(hop_kernel, place_of[step], given)
            return call(kernel, (index, *partial, *came), pair_of, 2 * depth * quarter)

        far_row = ring_member(place + half, peers) * depth
        far = [lax.dynamic_slice_in_dim(p, far_row, depth, 0).astype(BF16) for p in partial]
        down = lax.ppermute(far[1], "gx", behind)
        up = lax.ppermute(far[0], "gx", ahead)
        for step in range(half - 1, 0, -1):
            if step == half - 1:
                up, down, send = after((up, down, send))
            elif step == half - 2:
                up, down, over = after((up, down, over))
            else:
                up, down, back = after((up, down, back))
            up = hop(step, (0,) if step == half - 1 else (0, 1), up)
            down = hop(-step, (1,) if step == half - 1 else (0, 1), down)
            up, down = lax.ppermute(up, "gx", ahead), lax.ppermute(down, "gx", behind)
            if step == half - 1:
                came, over = sum_cores(send)
            if step == half - 2:
                back = lax.ppermute(over, "groups", swap)
        total, passing = call(
            total_kernel,
            (index, *partial, up, down),
            (shape((depth, quarter), F32), shape((depth, quarter), BF16)),
            4 * depth * quarter,
        )
    else:
        total, passing = [
            lax.psum_scatter(p, "gx", scatter_dimension=0, tiled=True) for p in partial
        ]
        passing = passing.astype(BF16)
        came, over = sum_cores(send)
        back = lax.ppermute(over, "groups", swap)
    passed = lax.ppermute(passing, "groups", swap)
    up_grad = call(join_kernel, (meta, total, passed), shape((depth, hidden), F32), 0)

    scaled, sums = call(
        scale_kernel,
        (meta, keep, came, back, frames, gain, stats),
        (shape((frame_len, half_width), F32), shape((frame_len, 2), F32)),
        4 * frame_len * width,
    )
    input_grad = call(
        input_kernel,
        (meta, scaled, sums, lax.ppermute(sums, "gy", swap), frames, grads, stats),
        shape((frame_len, half_width), BF16),
        4 * frame_len * width,
    )
    return (input_grad[None], up_grad)


def solution(mesh):
    placed = (
        P(("groups", "gx"), None, None),
        P(("groups", "gx"), None, None),
        P(),
        P("gx", "gy"),
        P("gx", "gy"),
        P("groups"),
    )
    return jax.shard_map(
        shards,
        mesh=mesh,
        in_specs=placed,
        out_specs=(P(("groups", "gx"), None, "gy"), P(("groups", "gx"), "gy")),
        check_vma=False,
    )
```

```python
import functools

import jax
import jax.numpy as jnp
from jax import lax
from jax.experimental import pallas as pl
from jax.experimental.pallas import tpu as pltpu
from jax.sharding import PartitionSpec as P

BF16, F32 = jnp.bfloat16, jnp.float32
VMEM = pl.BlockSpec(memory_space=pltpu.VMEM)
ANY = pl.BlockSpec(memory_space=pl.ANY)
SMEM = pl.BlockSpec(memory_space=pltpu.SMEM)


def shape(dims, kind):
    return jax.ShapeDtypeStruct(dims, kind)


def call(kernel, ins, out_shape, flops, scratch=(), vmem=16, aliases=None, left=(), out=VMEM):
    outs = jax.tree.leaves(out_shape)
    moved = sum(x.size * x.dtype.itemsize for x in list(ins) + outs)
    return pl.pallas_call(
        kernel,
        out_shape=out_shape,
        in_specs=[
            SMEM if x.dtype == jnp.int32 else ANY if i in left else VMEM
            for i, x in enumerate(ins)
        ],
        out_specs=jax.tree.map(lambda _: out, out_shape),
        scratch_shapes=list(scratch),
        input_output_aliases=aliases or {},
        compiler_params=pltpu.CompilerParams(vmem_limit_bytes=vmem << 20),
        cost_estimate=pl.CostEstimate(flops=flops, bytes_accessed=moved, transcendentals=0),
    )(*ins)


def dot(left, right, left_dim=1, right_dim=0):
    return lax.dot_general(
        left, right, (((left_dim,), (right_dim,)), ((), ())), preferred_element_type=F32
    )


def gelu_slope(values):
    return (
        0.5 * (1.0 + lax.erf(values * 0.7071067811865476))
        + values * jnp.exp(-0.5 * values * values) * 0.3989422804014327
    )


def norm_kernel(turn, lengths, frames_from, grads_from, gain, *refs):
    outs, (frames, out_grad, normed, grads, stats, sems) = refs[-10:-6], refs[-6:]
    normed_to, grads_to, share, stats_to = outs
    core = lax.axis_index("gy")

    @pl.when(core == turn)
    def _():
        def start(source, target, at):
            copy = pltpu.make_async_copy(source, target, sems.at[at])
            copy.start()
            return copy

        come = [start(frames_from, frames, 0), start(grads_from, out_grad, 1)]
        half = share.shape[1]
        rows = pl.ds(pl.multiple_of(core * half, half), half)
        come[1].wait()
        length = lengths[lax.axis_index("gx")]
        keep = lax.broadcasted_iota(jnp.int32, (frames.shape[0], 1), 0) < length
        grads[...] = jnp.where(keep, out_grad[...].astype(F32), 0.0).astype(BF16)
        go = [start(grads.at[rows], share.at[1], 2), start(grads, grads_to, 3)]
        come[0].wait()
        values = frames[...].astype(F32)
        centre = jnp.mean(values, axis=-1, keepdims=True)
        shifted = values - centre
        variance = jnp.mean(shifted * shifted, axis=-1, keepdims=True)
        inv_std = lax.rsqrt(variance + 1e-05)
        normed[...] = (shifted * inv_std * gain[...][None]).astype(BF16)
        go += [start(normed.at[rows], share.at[0], 4), start(normed, normed_to, 5)]
        stats[...] = jnp.concatenate(
            [jnp.broadcast_to(centre, (len(centre), 128)), jnp.broadcast_to(inv_std, (len(centre), 128))],
            axis=1,
        )
        go += [start(stats, stats_to, 6)]
        for copy in go:
            copy.wait()


def back_through(normed, grads, up, down, d_pre, partial):
    pre_act = dot(normed[...], up[...])
    d_act = dot(grads[...], down[...])
    d_pre[...] = (d_act * gelu_slope(pre_act)).astype(BF16)
    partial[...] = dot(normed[...], d_pre[...], 0, 0)


def other_kernel(index, first, second, up_far, down_far, *refs):
    blocks, (d_pre, partial, up, down, normed, grads) = refs[:-6], refs[-6:]
    half, depth = first.shape[1], up_far.shape[0]

    def rows(i):
        return pl.ds(pl.multiple_of(index[i] * depth, depth), depth)

    for i, block in enumerate(blocks):
        up[rows(i), :] = block[0]
        down[rows(i), :] = block[1]
    up[rows(len(blocks)), :] = up_far[...]
    down[rows(len(blocks)), :] = down_far[...]
    for at, part in ((0, first), (half, second)):
        normed[at : at + half, :] = part[0]
        grads[at : at + half, :] = part[1]
    back_through(normed, grads, up, down, d_pre, partial)


def own_kernel(normed, grads, up, down, d_pre, partial):
    back_through(normed, grads, up, down, d_pre, partial)


def d_norm_kernel(meta, d_pre_own, d_pre_other, up, keep, send):
    core = meta[1]
    rows, width = keep.shape[1:]
    mine = up[pl.ds(pl.multiple_of(core * width, width), width), :]
    theirs = up[pl.ds(pl.multiple_of((1 - core) * width, width), width), :]
    keep[0] = dot(d_pre_own[...], mine, 1, 1)
    keep[1] = dot(d_pre_other[...], mine, 1, 1)
    send[0] = dot(d_pre_own[...], theirs, 1, 1).astype(BF16)
    sent = dot(d_pre_other[...], theirs, 1, 1).astype(BF16)
    send[1, rows // 2 :, :] = sent[: rows // 2]
    send[1, : rows // 2, :] = sent[rows // 2 :]


def over_kernel(meta, keep, came, over):
    half = over.shape[0] // 2
    for i in range(2):
        at = lax.rem(i + meta[1], 2) * half
        rows = slice(i * half, (i + 1) * half)
        value = keep[1, rows, :] + came[1, rows, :].astype(F32)
        over[pl.ds(pl.multiple_of(at, half), half), :] = value.astype(BF16)


def own_columns(meta, ref, width):
    return ref[:, pl.ds(pl.multiple_of(meta[1] * width, width), width)]


def scale_kernel(meta, keep, came, back, frames, gain, stats, scaled, sums):
    width = scaled.shape[1]
    d_norm = keep[0] + came[0].astype(F32) + back[...].astype(F32)
    value = d_norm * own_columns(meta, gain, width)
    scaled[...] = value
    rows = own_columns(meta, frames, width).astype(F32)
    centred = (rows - stats[:, 0:1]) * stats[:, 128:129]
    sums[:, 0:1] = jnp.sum(value, axis=-1, keepdims=True)
    sums[:, 1:2] = jnp.sum(value * centred, axis=-1, keepdims=True)


def input_kernel(meta, scaled, sums, came, frames, grads, stats, out):
    width = scaled.shape[1]
    means = (sums[...] + came[...]) * (0.5 / width)
    rows = own_columns(meta, frames, width).astype(F32)
    inv_std = stats[:, 128:129]
    centred = (rows - stats[:, 0:1]) * inv_std
    value = inv_std * (scaled[...] - means[:, 0:1] - centred * means[:, 1:2])
    out[...] = (own_columns(meta, grads, width).astype(F32) + value).astype(BF16)


def hop_kernel(at, given, index, *refs):
    partial, came, out = refs[:2], refs[2:-1], refs[-1]
    depth = out.shape[-2]
    rows = pl.ds(pl.multiple_of(index[at] * depth, depth), depth)
    for i in range(2):
        value = partial[i][rows, :]
        if i in given:
            for ref in came:
                value = value + (ref[i] if len(ref.shape) == 3 else ref[...]).astype(F32)
        out[i] = value.astype(out.dtype)


def total_kernel(index, own, other, up, down, total, passing):
    depth = total.shape[0]
    rows = pl.ds(pl.multiple_of(index[0] * depth, depth), depth)
    total[...] = own[rows, :] + up[0].astype(F32) + down[0].astype(F32)
    passing[...] = (other[rows, :] + up[1].astype(F32) + down[1].astype(F32)).astype(BF16)


def join_kernel(meta, own, passed, out):
    width = own.shape[1]
    side = meta[2]
    out[:, pl.ds(pl.multiple_of(side * width, width), width)] = own[...]
    other = pl.ds(pl.multiple_of((1 - side) * width, width), width)
    out[:, other] = passed[...].astype(F32)


def ring_member(place, count):
    place = place % count
    return jnp.where(place < count // 2, 2 * place, 2 * (count - 1 - place) + 1)


def shards(frames, out_grad, ln_gain, w_up, w_down, lengths):
    peers = lax.axis_size("gx")
    half = peers // 2
    own = lax.axis_index("gx")
    side = lax.axis_index("groups")
    core = lax.axis_index("gy")
    frame_len, width = frames.shape[1:]
    depth, hidden = w_up.shape
    quarter = hidden // 2
    half_width = width // 2
    half_rows = frame_len // 2
    ringed = peers <= 16 and peers % 2 == 0 and depth % 16 == 0

    order = list(range(0, peers, 2)) + list(range(peers - 1, 0, -2))
    ahead = [(order[i], order[(i + 1) % peers]) for i in range(peers)]
    behind = [(b, a) for a, b in ahead]
    place = jnp.where(own % 2 == 0, own // 2, peers - 1 - own // 2)
    swap = [(0, 1), (1, 0)]
    after = lax.optimization_barrier

    mine = [lax.dynamic_slice_in_dim(w, side * quarter, quarter, 1) for w in (w_up, w_down)]
    meta = jnp.stack([own, core, side]).astype(jnp.int32)
    frames, out_grad = frames[0], out_grad[0]

    rows_of = shape((frame_len, width), BF16)
    halves_of = shape((2, half_rows, width), BF16)
    results = (rows_of, rows_of, halves_of, shape((frame_len, 256), F32))

    def norm(turn, *given):
        return call(
            functools.partial(norm_kernel, turn),
            (lengths, frames, out_grad, ln_gain, *given),
            results,
            10 * frame_len * width,
            [pltpu.VMEM((frame_len, width), BF16)] * 4
            + [pltpu.VMEM((frame_len, 256), F32), pltpu.SemaphoreType.DMA((7,))],
            aliases={4 + i: i for i in range(len(given))},
            vmem=56,
            left=(1, 2, 4, 5, 6, 7),
            out=ANY,
        )

    results_one = norm(1)
    if ringed:
        pair, results_one = after((jnp.stack(mine), results_one))
    normed, grads, share, stats = norm(0, *results_one)

    first = lax.ppermute(share, "groups", swap)

    weight = shape((depth * peers, quarter), BF16)
    if ringed:
        blocks = {0: pair}
        up, down = pair, pair
        for step in range(1, half):
            up, down = lax.ppermute(up, "gx", ahead), lax.ppermute(down, "gx", behind)
            if step == 1:
                up, down, share = after((up, down, share))
            else:
                up, down = after((up, down))
            blocks[-step], blocks[step] = up, down
        far = lax.ppermute(up[0], "gx", ahead), lax.ppermute(down[1], "gx", behind)
        steps = list(blocks)
        index = jnp.stack([ring_member(place + step + peers, peers) for step in steps + [half]])
        index = index.astype(jnp.int32)
        first, up = after((first, up))
        near = [blocks[step] for step in steps]
    else:
        far = [lax.all_gather(w, "gx", axis=0, tiled=True) for w in mine]
        index, near = jnp.zeros((1,), jnp.int32), ()
    second = lax.ppermute(first, "gy", swap)

    d_pre_of, partial_of = shape((frame_len, quarter), BF16), shape((width, quarter), F32)
    flops = 6 * frame_len * width * quarter
    d_pre_other, partial_other, full_up, full_down = call(
        other_kernel,
        (index, first, second, *far, *near),
        (d_pre_of, partial_of, weight, weight),
        flops,
        [pltpu.VMEM((frame_len, width), BF16)] * 2,
    )
    d_pre_own, partial_own = call(
        own_kernel, (normed, grads, full_up, full_down), (d_pre_of, partial_of), flops
    )
    partial = [partial_own, partial_other]

    keep, send = call(
        d_norm_kernel,
        (meta, d_pre_own, d_pre_other, full_up),
        (shape((2, frame_len, half_width), F32), shape((2, frame_len, half_width), BF16)),
        4 * frame_len * width * quarter,
    )

    def sum_cores(send):
        came = lax.ppermute(send, "gy", swap)
        over = call(
            over_kernel, (meta, keep, came), shape((frame_len, half_width), BF16), frame_len * width
        )
        return came, over

    if ringed:

        pair_of = shape((2, depth, quarter), BF16)
        place_of = {step: i for i, step in enumerate(steps + [half])}

        def hop(step, given, *came):
            kernel = functools.partial(hop_kernel, place_of[step], given)
            return call(kernel, (index, *partial, *came), pair_of, 2 * depth * quarter)

        far_row = ring_member(place + half, peers) * depth
        far = [lax.dynamic_slice_in_dim(p, far_row, depth, 0).astype(BF16) for p in partial]
        down = lax.ppermute(far[1], "gx", behind)
        up = lax.ppermute(far[0], "gx", ahead)
        for step in range(half - 1, 0, -1):
            if step == half - 1:
                up, down, send = after((up, down, send))
            elif step == half - 2:
                up, down, over = after((up, down, over))
            else:
                up, down, back = after((up, down, back))
            up = hop(step, (0,) if step == half - 1 else (0, 1), up)
            down = hop(-step, (1,) if step == half - 1 else (0, 1), down)
            up, down = lax.ppermute(up, "gx", ahead), lax.ppermute(down, "gx", behind)
            if step == half - 1:
                came, over = sum_cores(send)
            if step == half - 2:
                back = lax.ppermute(over, "groups", swap)
        total, passing = call(
            total_kernel,
            (index, *partial, up, down),
            (shape((depth, quarter), F32), shape((depth, quarter), BF16)),
            4 * depth * quarter,
        )
    else:
        total, passing = [
            lax.psum_scatter(p, "gx", scatter_dimension=0, tiled=True) for p in partial
        ]
        passing = passing.astype(BF16)
        came, over = sum_cores(send)
        back = lax.ppermute(over, "groups", swap)
    passed = lax.ppermute(passing, "groups", swap)
    up_grad = call(join_kernel, (meta, total, passed), shape((depth, hidden), F32), 0)

    gain = ln_gain[None]
    scaled, sums = call(
        scale_kernel,
        (meta, keep, came, back, frames, gain, stats),
        (shape((frame_len, half_width), F32), shape((frame_len, 2), F32)),
        4 * frame_len * width,
    )
    input_grad = call(
        input_kernel,
        (meta, scaled, sums, lax.ppermute(sums, "gy", swap), frames, grads, stats),
        shape((frame_len, half_width), BF16),
        4 * frame_len * width,
    )
    return (input_grad[None], up_grad)


def solution(mesh):
    placed = (
        P(("groups", "gx"), None, None),
        P(("groups", "gx"), None, None),
        P(),
        P("gx", "gy"),
        P("gx", "gy"),
        P("groups"),
    )
    return jax.shard_map(
        shards,
        mesh=mesh,
        in_specs=placed,
        out_specs=(P(("groups", "gx"), None, "gy"), P(("groups", "gx"), "gy")),
        check_vma=False,
    )
```

```python
import functools

import jax
import jax.numpy as jnp
from jax import lax
from jax.experimental import pallas as pl
from jax.experimental.pallas import tpu as pltpu
from jax.sharding import PartitionSpec as P

BF16, F32 = jnp.bfloat16, jnp.float32
VMEM = pl.BlockSpec(memory_space=pltpu.VMEM)
ANY = pl.BlockSpec(memory_space=pl.ANY)
SMEM = pl.BlockSpec(memory_space=pltpu.SMEM)


def shape(dims, kind):
    return jax.ShapeDtypeStruct(dims, kind)


def call(kernel, ins, out_shape, scratch=(), vmem=16, left=(), cost=1, ties=()):
    count = len(ins)

    def body(*refs):
        kernel(*refs[:count], *refs[count + len(ties) :])

    return pl.pallas_call(
        body if ties else kernel,
        out_shape=out_shape,
        in_specs=[
            SMEM if x.dtype == jnp.int32 else ANY if i in left else VMEM
            for i, x in enumerate(ins)
        ]
        + [ANY] * len(ties),
        out_specs=jax.tree.map(lambda _: VMEM, out_shape),
        scratch_shapes=list(scratch),
        compiler_params=pltpu.CompilerParams(vmem_limit_bytes=vmem << 20),
        cost_estimate=pl.CostEstimate(flops=1, bytes_accessed=cost, transcendentals=0),
    )(*ins, *ties)


def hold(array, *ties):
    return pl.pallas_call(
        lambda *refs: None,
        out_shape=shape(array.shape, array.dtype),
        in_specs=[ANY] * (1 + len(ties)),
        out_specs=ANY,
        input_output_aliases={0: 0},
        cost_estimate=pl.CostEstimate(flops=1, bytes_accessed=1, transcendentals=0),
    )(array, *ties)


def dot(left, right, left_dim=1, right_dim=0):
    return lax.dot_general(
        left, right, (((left_dim,), (right_dim,)), ((), ())), preferred_element_type=F32
    )


def gelu_slope(values):
    return (
        0.5 * (1.0 + lax.erf(values * 0.7071067811865476))
        + values * jnp.exp(-0.5 * values * values) * 0.3989422804014327
    )


def norm_kernel(meta, lengths, frames_from, grads_from, gain, *refs):
    normed, grads, pass_normed, pass_grads, stats, frames, out_grad, sems = refs
    copies = [
        pltpu.make_async_copy(grads_from, out_grad, sems.at[0]),
        pltpu.make_async_copy(frames_from, frames, sems.at[1]),
    ]
    for copy in copies:
        copy.start()
    half = pass_normed.shape[0]
    rows = pl.ds(pl.multiple_of(meta[1] * half, half), half)
    keep = lax.broadcasted_iota(jnp.int32, (frames.shape[0], 1), 0) < lengths[meta[0]]
    copies[0].wait()
    grads[...] = jnp.where(keep, out_grad[...].astype(F32), 0.0).astype(BF16)
    pass_grads[...] = grads[rows, :]
    copies[1].wait()
    values = frames[...].astype(F32)
    centre = jnp.mean(values, axis=-1, keepdims=True)
    shifted = values - centre
    variance = jnp.mean(shifted * shifted, axis=-1, keepdims=True)
    inv_std = lax.rsqrt(variance + 1e-05)
    normed[...] = (shifted * inv_std * gain[...][None]).astype(BF16)
    pass_normed[...] = normed[rows, :]
    stats[:, 0:1] = centre
    stats[:, 1:2] = inv_std


def back_through(normed, grads, up, down, d_pre, partial):
    pre_act = dot(normed[...], up[...])
    d_act = dot(grads[...], down[...])
    d_pre[...] = (d_act * gelu_slope(pre_act)).astype(BF16)
    partial[...] = dot(normed[...], d_pre[...], 0, 0)


def other_kernel(index, *refs):
    d_pre, partial, up, down, normed, grads, sems = refs[-7:]
    halves, blocks = refs[:4], refs[4:-7]
    half, depth = halves[0].shape[0], blocks[-1].shape[0]
    count = len(blocks) - 1
    copies = []

    def start(source, target):
        copies.append(pltpu.make_async_copy(source, target, sems.at[len(copies)]))
        copies[-1].start()

    for i in range(count):
        rows = pl.ds(pl.multiple_of(index[i] * depth, depth), depth)
        pair = (blocks[i].at[0], blocks[i].at[1]) if i < count - 1 else blocks[-2:]
        start(pair[0], up.at[rows])
        start(pair[1], down.at[rows])
    for i in range(2):
        start(halves[2 * i], normed.at[pl.ds(i * half, half)])
        start(halves[2 * i + 1], grads.at[pl.ds(i * half, half)])
    for copy in copies:
        copy.wait()
    back_through(normed, grads, up, down, d_pre, partial)


def halves_kernel(up, down, up_half, down_half, sems):
    copies = [
        pltpu.make_async_copy(up.at[0], up_half, sems.at[0]),
        pltpu.make_async_copy(down.at[1], down_half, sems.at[1]),
    ]
    for copy in copies:
        copy.start()
    for copy in copies:
        copy.wait()


def own_kernel(normed, grads, up, down, d_pre, partial):
    back_through(normed, grads, up, down, d_pre, partial)


def d_norm_kernel(meta, d_pre_own, d_pre_other, up, keep, send_own, send_other):
    core = meta[1]
    rows, width = keep.shape[1:]
    mine = up[pl.ds(pl.multiple_of(core * width, width), width), :]
    theirs = up[pl.ds(pl.multiple_of((1 - core) * width, width), width), :]
    keep[0] = dot(d_pre_own[...], mine, 1, 1)
    keep[1] = dot(d_pre_other[...], mine, 1, 1)
    send_own[...] = dot(d_pre_own[...], theirs, 1, 1).astype(BF16)
    sent = dot(d_pre_other[...], theirs, 1, 1).astype(BF16)
    send_other[rows // 2 :, :] = sent[: rows // 2]
    send_other[: rows // 2, :] = sent[rows // 2 :]


def over_kernel(meta, keep, came, over):
    half = over.shape[0] // 2
    for i in range(2):
        at = lax.rem(i + meta[1], 2) * half
        rows = slice(i * half, (i + 1) * half)
        value = keep[1, rows, :] + came[rows, :].astype(F32)
        over[pl.ds(pl.multiple_of(at, half), half), :] = value.astype(BF16)


def own_columns(meta, ref, width):
    return ref[:, pl.ds(pl.multiple_of(meta[1] * width, width), width)]


def scale_kernel(meta, keep, came, back, frames, gain, stats, scaled, sums):
    width = scaled.shape[1]
    d_norm = keep[0] + came[...].astype(F32) + back[...].astype(F32)
    value = d_norm * own_columns(meta, gain, width)
    scaled[...] = value
    rows = own_columns(meta, frames, width).astype(F32)
    centred = (rows - stats[:, 0:1]) * stats[:, 1:2]
    sums[:, 0:1] = jnp.sum(value, axis=-1, keepdims=True)
    sums[:, 1:2] = jnp.sum(value * centred, axis=-1, keepdims=True)


def input_kernel(meta, scaled, sums, came, frames, grads, stats, out):
    width = scaled.shape[1]
    means = (sums[...] + came[...]) * (0.5 / width)
    rows = own_columns(meta, frames, width).astype(F32)
    inv_std = stats[:, 1:2]
    centred = (rows - stats[:, 0:1]) * inv_std
    value = inv_std * (scaled[...] - means[:, 0:1] - centred * means[:, 1:2])
    out[...] = (own_columns(meta, grads, width).astype(F32) + value).astype(BF16)


def hop_kernel(places, index, partial, *refs):
    outs = refs[len(refs) - len(places) :]
    came = iter(refs)
    depth = outs[0].shape[0]
    for (at, summed), out in zip(places, outs):
        value = partial[pl.ds(pl.multiple_of(index[at] * depth, depth), depth), :]
        if summed:
            value = value + next(came)[...].astype(F32)
        out[...] = value.astype(BF16)


def total_kernel(index, partial, up, down, total):
    depth = total.shape[0]
    rows = pl.ds(pl.multiple_of(index[0] * depth, depth), depth)
    value = partial[rows, :] + up[...].astype(F32) + down[...].astype(F32)
    total[...] = value.astype(total.dtype)


def join_kernel(meta, index, partial, up, down, passed, out):
    depth, width = up.shape
    side = meta[2]
    rows = pl.ds(pl.multiple_of(index[0] * depth, depth), depth)
    value = partial[rows, :] + up[...].astype(F32) + down[...].astype(F32)
    out[:, pl.ds(pl.multiple_of(side * width, width), width)] = value
    other = pl.ds(pl.multiple_of((1 - side) * width, width), width)
    out[:, other] = passed[...].astype(F32)


def place_kernel(meta, own, passed, out):
    width = own.shape[1]
    side = meta[2]
    out[:, pl.ds(pl.multiple_of(side * width, width), width)] = own[...]
    other = pl.ds(pl.multiple_of((1 - side) * width, width), width)
    out[:, other] = passed[...].astype(F32)


def ring_member(place, count):
    place = place % count
    return jnp.where(place < count // 2, 2 * place, 2 * (count - 1 - place) + 1)


def shards(frames, out_grad, ln_gain, w_up, w_down, lengths):
    peers = lax.axis_size("gx")
    half = peers // 2
    own = lax.axis_index("gx")
    side = lax.axis_index("groups")
    core = lax.axis_index("gy")
    frame_len, width = frames.shape[1:]
    depth, hidden = w_up.shape
    quarter = hidden // 2
    half_width = width // 2
    half_rows = frame_len // 2
    ringed = peers <= 16 and peers % 2 == 0 and depth % 16 == 0

    order = list(range(0, peers, 2)) + list(range(peers - 1, 0, -2))
    ahead = [(order[i], order[(i + 1) % peers]) for i in range(peers)]
    behind = [(b, a) for a, b in ahead]
    place = jnp.where(own % 2 == 0, own // 2, peers - 1 - own // 2)
    swap = [(0, 1), (1, 0)]

    mine = [lax.dynamic_slice_in_dim(w, side * quarter, quarter, 1) for w in (w_up, w_down)]
    meta = jnp.stack([own, core, side]).astype(jnp.int32)
    frames, out_grad = frames[0], out_grad[0]

    rows_of, half_of = shape((frame_len, width), BF16), shape((half_rows, width), BF16)
    def norm(*ties):
        normed, grads, *passing, stats = call(
            norm_kernel,
            (meta, lengths, frames, out_grad, ln_gain),
            (rows_of, rows_of, half_of, half_of, shape((frame_len, 2), F32)),
            [pltpu.VMEM((frame_len, width), BF16)] * 2 + [pltpu.SemaphoreType.DMA((2,))],
            left=(2, 3),
            vmem=40,
            ties=ties,
        )
        return normed, grads, [lax.ppermute(part, "groups", swap) for part in passing], stats

    if ringed:
        pair = jnp.stack(mine)
        blocks = {0: pair}
        up, down = pair, pair
        for step in range(1, half):
            up, down = lax.ppermute(up, "gx", ahead), lax.ppermute(down, "gx", behind)
            blocks[-step], blocks[step] = up, down
            if step == 1:
                normed, grads, first, stats = norm(up)
        block_of = shape((depth, quarter), BF16)
        up, down = call(
            halves_kernel,
            (up, down),
            (block_of, block_of),
            [pltpu.SemaphoreType.DMA((2,))],
            left=(0, 1),
        )
        steps = list(blocks) + [half]
        index = jnp.stack([ring_member(place + step + peers, peers) for step in steps])
        blocks = [*blocks.values(), lax.ppermute(up, "gx", ahead), lax.ppermute(down, "gx", behind)]
    else:
        normed, grads, first, stats = norm()
        blocks = [lax.all_gather(w, "gx", axis=0, tiled=True) for w in mine]
        index = jnp.zeros((1,), jnp.int32)
    index = index.astype(jnp.int32)
    second = [lax.ppermute(part, "gy", swap) for part in first]

    d_pre_of, partial_of = shape((frame_len, quarter), BF16), shape((width, quarter), F32)
    weight = shape((width, quarter), BF16)
    d_pre_other, partial_other, full_up, full_down = call(
        other_kernel,
        (index, *first, *second, *blocks),
        (d_pre_of, partial_of, weight, weight),
        [pltpu.VMEM((frame_len, width), BF16)] * 2
        + [pltpu.SemaphoreType.DMA((2 * len(blocks) + 4,))],
        left=range(1, len(blocks) + 5),
    )
    d_pre_own, partial_own = call(
        own_kernel, (normed, grads, full_up, full_down), (d_pre_of, partial_of)
    )
    partial = [partial_own, partial_other]

    half_rows_of = shape((frame_len, half_width), BF16)

    def own_d_norm(*ties):
        return call(
            d_norm_kernel,
            (meta, d_pre_own, d_pre_other, full_up),
            (shape((2, frame_len, half_width), F32), half_rows_of, half_rows_of),
            ties=ties,
        )

    def over_cores(keep, came, *ties):
        return call(over_kernel, (meta, keep, came), half_rows_of, ties=ties)

    if ringed:
        place_of = {step: i for i, step in enumerate(steps)}
        place_of[-half] = place_of[half]
        came = [{}, {}]

        def hop(i, turn, *ties):
            ways = [(half - turn - (i == 1), ahead), (turn + (i == 0) - half, behind)]
            ways = [way for way in ways if way[0] != 0]
            kept = [came[i][pairs[0]] for _, pairs in ways if pairs[0] in came[i]]
            places = [(place_of[step], pairs[0] in came[i]) for step, pairs in ways]
            blocks = call(
                functools.partial(hop_kernel, tuple(places)),
                (index, partial[i], *kept),
                [block_of] * len(ways),
                ties=ties,
            )
            for block, (_, pairs) in zip(blocks, ways):
                came[i][pairs[0]] = lax.ppermute(block, "gx", pairs)
            return blocks[0]

        hop(1, 0)
        tie = hop(0, 0)
        tie = hop(1, 1, tie)
        keep, send_own, send_other = own_d_norm(tie)
        tie = hop(0, 1, tie)
        send_other = hold(send_other, tie)
        tie = hop(1, 2, tie)
        over = over_cores(keep, lax.ppermute(send_other, "gy", swap), tie)
        tie = hop(0, 2, over)
        back = lax.ppermute(over, "groups", swap)
        send_own = hold(send_own, tie)
        for turn in range(3, half):
            tie = hop(0, turn, hop(1, turn, tie))
        tail = (tie,)
        one, two = ([came[i][pairs[0]] for pairs in (ahead, behind)] for i in range(2))
        passing = call(total_kernel, (index, partial[1], *two), block_of, ties=tail)
        tail = (passing,)
        passed = lax.ppermute(passing, "groups", swap)
        up_grad = call(
            join_kernel,
            (meta, index, partial[0], *one, passed),
            shape((depth, hidden), F32),
        )
    else:
        tail = ()
        keep, send_own, send_other = own_d_norm()
        over = over_cores(keep, lax.ppermute(send_other, "gy", swap))
        back = lax.ppermute(over, "groups", swap)
        total = [lax.psum_scatter(p, "gx", scatter_dimension=0, tiled=True) for p in partial]
        passed = lax.ppermute(total[1].astype(BF16), "groups", swap)
        up_grad = call(place_kernel, (meta, total[0], passed), shape((depth, hidden), F32))
    came = lax.ppermute(send_own, "gy", swap)

    gain = ln_gain[None]
    scaled, sums = call(
        scale_kernel,
        (meta, keep, came, back, frames, gain, stats),
        (shape((frame_len, half_width), F32), shape((frame_len, 2), F32)),
        ties=tail,
    )
    input_grad = call(
        input_kernel,
        (meta, scaled, sums, lax.ppermute(sums, "gy", swap), frames, grads, stats),
        shape((frame_len, half_width), BF16),
    )
    return (input_grad[None], up_grad)


def solution(mesh):
    placed = (
        P(("groups", "gx"), None, None),
        P(("groups", "gx"), None, None),
        P(),
        P("gx", "gy"),
        P("gx", "gy"),
        P("groups"),
    )
    return jax.shard_map(
        shards,
        mesh=mesh,
        in_specs=placed,
        out_specs=(P(("groups", "gx"), None, "gy"), P(("groups", "gx"), "gy")),
        check_vma=False,
    )
```

```python
import functools

import jax
import jax.numpy as jnp
from jax import lax
from jax.experimental import pallas as pl
from jax.experimental.pallas import tpu as pltpu
from jax.sharding import PartitionSpec as P

BF16, F32 = jnp.bfloat16, jnp.float32
VMEM = pl.BlockSpec(memory_space=pltpu.VMEM)
ANY = pl.BlockSpec(memory_space=pl.ANY)
SMEM = pl.BlockSpec(memory_space=pltpu.SMEM)


def shape(dims, kind):
    return jax.ShapeDtypeStruct(dims, kind)


def call(kernel, ins, out_shape, scratch=(), vmem=4, left=(), cost=1, ties=()):
    count = len(ins)

    def body(*refs):
        kernel(*refs[:count], *refs[count + len(ties) :])

    return pl.pallas_call(
        body if ties else kernel,
        out_shape=out_shape,
        in_specs=[
            SMEM if x.dtype == jnp.int32 else ANY if i in left else VMEM
            for i, x in enumerate(ins)
        ]
        + [ANY] * len(ties),
        out_specs=jax.tree.map(lambda _: VMEM, out_shape),
        scratch_shapes=list(scratch),
        compiler_params=pltpu.CompilerParams(vmem_limit_bytes=vmem << 20),
        cost_estimate=pl.CostEstimate(flops=1, bytes_accessed=cost, transcendentals=0),
    )(*ins, *ties)


def hold(array, *ties):
    return pl.pallas_call(
        lambda *refs: None,
        out_shape=shape(array.shape, array.dtype),
        in_specs=[ANY] * (1 + len(ties)),
        out_specs=ANY,
        input_output_aliases={0: 0},
        cost_estimate=pl.CostEstimate(flops=1, bytes_accessed=1, transcendentals=0),
    )(array, *ties)


def dot(left, right, left_dim=1, right_dim=0):
    return lax.dot_general(
        left, right, (((left_dim,), (right_dim,)), ((), ())), preferred_element_type=F32
    )


def gelu_slope(values):
    return (
        0.5 * (1.0 + lax.erf(values * 0.7071067811865476))
        + values * jnp.exp(-0.5 * values * values) * 0.3989422804014327
    )


def norm_kernel(meta, lengths, frames, out_grad, gain, *refs):
    normed, grads, passing, stats = refs
    half = passing.shape[1]
    rows = pl.ds(pl.multiple_of(meta[1] * half, half), half)
    keep = lax.broadcasted_iota(jnp.int32, (frames.shape[0], 1), 0) < lengths[meta[0]]
    grads[...] = jnp.where(keep, out_grad[...].astype(F32), 0.0).astype(BF16)
    passing[1] = grads[rows, :]
    values = frames[...].astype(F32)
    centre = jnp.mean(values, axis=-1, keepdims=True)
    shifted = values - centre
    variance = jnp.mean(shifted * shifted, axis=-1, keepdims=True)
    inv_std = lax.rsqrt(variance + 1e-05)
    normed[...] = (shifted * inv_std * gain[...][None]).astype(BF16)
    passing[0] = normed[rows, :]
    stats[:, 0:1] = centre
    stats[:, 1:2] = inv_std


def back_through(normed, grads, up, down, d_pre, partial):
    pre_act = dot(normed[...], up[...])
    d_act = dot(grads[...], down[...])
    d_pre[...] = (d_act * gelu_slope(pre_act)).astype(BF16)
    partial[...] = dot(normed[...], d_pre[...], 0, 0)


def place_kernel(index, *refs):
    blocks, (up, down, sems) = refs[:-3], refs[-3:]
    depth = blocks[0].shape[1]
    copies = []
    for i, block in enumerate(blocks):
        rows = pl.ds(pl.multiple_of(index[i] * depth, depth), depth)
        copies.append(pltpu.make_async_copy(block.at[0], up.at[rows], sems.at[2 * i]))
        copies.append(pltpu.make_async_copy(block.at[1], down.at[rows], sems.at[2 * i + 1]))
    for copy in copies:
        copy.start()
    for copy in copies:
        copy.wait()


def other_kernel(index, first, second, near_up, near_down, *refs):
    d_pre, partial, up, down, normed, grads = refs[-6:]
    half = first.shape[1]
    for at, part in ((0, first), (half, second)):
        normed[at : at + half, :] = part[0]
        grads[at : at + half, :] = part[1]
    up[...] = near_up[...]
    down[...] = near_down[...]
    for ref, far in zip((up, down), refs[:-6]):
        depth = far.shape[0]
        rows = pl.ds(pl.multiple_of(index[index.shape[0] - 1] * depth, depth), depth)
        ref[rows, :] = far[...]
    back_through(normed, grads, up, down, d_pre, partial)


def own_kernel(normed, grads, up, down, d_pre, partial):
    back_through(normed, grads, up, down, d_pre, partial)


def d_norm_kernel(meta, d_pre_own, d_pre_other, up, keep, send):
    core = meta[1]
    rows, width = keep.shape[1:]
    mine = up[pl.ds(pl.multiple_of(core * width, width), width), :]
    theirs = up[pl.ds(pl.multiple_of((1 - core) * width, width), width), :]
    keep[0] = dot(d_pre_own[...], mine, 1, 1)
    keep[1] = dot(d_pre_other[...], mine, 1, 1)
    send[0] = dot(d_pre_own[...], theirs, 1, 1).astype(BF16)
    sent = dot(d_pre_other[...], theirs, 1, 1).astype(BF16)
    send[1, rows // 2 :, :] = sent[: rows // 2]
    send[1, : rows // 2, :] = sent[rows // 2 :]


def over_kernel(meta, keep, came, over):
    half = over.shape[0] // 2
    for i in range(2):
        at = lax.rem(i + meta[1], 2) * half
        rows = slice(i * half, (i + 1) * half)
        value = keep[1, rows, :] + came[1, rows, :].astype(F32)
        over[pl.ds(pl.multiple_of(at, half), half), :] = value.astype(BF16)


def own_columns(meta, ref, width):
    return ref[:, pl.ds(pl.multiple_of(meta[1] * width, width), width)]


def scale_kernel(meta, keep, came, back, frames, gain, stats, scaled, sums):
    width = scaled.shape[1]
    d_norm = keep[0] + came[0].astype(F32) + back[...].astype(F32)
    value = d_norm * own_columns(meta, gain, width)
    scaled[...] = value
    rows = own_columns(meta, frames, width).astype(F32)
    centred = (rows - stats[:, 0:1]) * stats[:, 1:2]
    sums[:, 0:1] = jnp.sum(value, axis=-1, keepdims=True)
    sums[:, 1:2] = jnp.sum(value * centred, axis=-1, keepdims=True)


def input_kernel(meta, scaled, sums, came, frames, grads, stats, out):
    width = scaled.shape[1]
    means = (sums[...] + came[...]) * (0.5 / width)
    rows = own_columns(meta, frames, width).astype(F32)
    inv_std = stats[:, 1:2]
    centred = (rows - stats[:, 0:1]) * inv_std
    value = inv_std * (scaled[...] - means[:, 0:1] - centred * means[:, 1:2])
    out[...] = (own_columns(meta, grads, width).astype(F32) + value).astype(BF16)


def hop_kernel(at, mode, index, *refs):
    windows = [i for i in range(2) if mode[i] is not None]
    partial, came, out = refs[: len(windows)], refs[len(windows) : -1], refs[-1]
    depth = out.shape[1]
    rows = pl.ds(pl.multiple_of(index[at] * depth, depth), depth)
    for k, i in enumerate(windows):
        value = partial[k][rows, :]
        if mode[i]:
            value = value + came[0][k if came[0].shape[0] == 2 else 0].astype(F32)
        out[k] = value.astype(BF16)


def own_total_kernel(index, own, other, down, total):
    depth = total.shape[1]
    rows = pl.ds(pl.multiple_of(index[0] * depth, depth), depth)
    total[0] = own[rows, :] + down[0].astype(F32)
    total[1] = other[rows, :] + down[1].astype(F32)


def total_kernel(both, up, total, passing):
    total[...] = both[0] + up[0].astype(F32)
    passing[...] = (both[1] + up[1].astype(F32)).astype(BF16)


def join_kernel(meta, own, passed, out):
    width = own.shape[1]
    side = meta[2]
    out[:, pl.ds(pl.multiple_of(side * width, width), width)] = own[...]
    other = pl.ds(pl.multiple_of((1 - side) * width, width), width)
    out[:, other] = passed[...].astype(F32)


def ring_member(place, count):
    place = place % count
    return jnp.where(place < count // 2, 2 * place, 2 * (count - 1 - place) + 1)


def shards(frames, out_grad, ln_gain, w_up, w_down, lengths):
    peers = lax.axis_size("gx")
    half = peers // 2
    own = lax.axis_index("gx")
    side = lax.axis_index("groups")
    core = lax.axis_index("gy")
    frame_len, width = frames.shape[1:]
    depth, hidden = w_up.shape
    quarter = hidden // 2
    half_width = width // 2
    half_rows = frame_len // 2
    ringed = peers <= 16 and peers % 2 == 0 and depth % 16 == 0

    order = list(range(0, peers, 2)) + list(range(peers - 1, 0, -2))
    ahead = [(order[i], order[(i + 1) % peers]) for i in range(peers)]
    behind = [(b, a) for a, b in ahead]
    place = jnp.where(own % 2 == 0, own // 2, peers - 1 - own // 2)
    swap = [(0, 1), (1, 0)]
    after = lax.optimization_barrier

    pair = jnp.stack(
        [lax.dynamic_slice_in_dim(w, side * quarter, quarter, 1) for w in (w_up, w_down)]
    )
    pair, frames, out_grad, ln_gain, lengths = after((pair, frames, out_grad, ln_gain, lengths))
    meta = jnp.stack([own, core, side]).astype(jnp.int32)
    frames, out_grad = frames[0], out_grad[0]

    rows_of = shape((frame_len, width), BF16)
    normed, grads, passing, stats = call(
        norm_kernel,
        (meta, lengths, frames, out_grad, ln_gain),
        (rows_of, rows_of, shape((2, half_rows, width), BF16), shape((frame_len, 2), F32)),
        cost=10 * frame_len * width,
    )

    weight = shape((width, quarter), BF16)
    block_of = shape((depth, quarter), BF16)
    if ringed:
        blocks = {0: pair}
        up, down = pair, pair
        for step in range(1, half):
            up, down = lax.ppermute(up, "gx", ahead), lax.ppermute(down, "gx", behind)
            blocks[-step], blocks[step] = up, down
        first = lax.ppermute(passing, "groups", swap)
        first, up, down = after((first, up, down))
        steps = list(blocks) + [half]
        index = jnp.stack([ring_member(place + step + peers, peers) for step in steps])
        index = index.astype(jnp.int32)
        near = call(
            place_kernel,
            (index, *blocks.values()),
            (weight, weight),
            [pltpu.SemaphoreType.DMA((2 * len(blocks),))],
            left=range(1, len(blocks) + 1),
        )
        far = [lax.ppermute(up[0], "gx", ahead), lax.ppermute(down[1], "gx", behind)]
    else:
        first = lax.ppermute(passing, "groups", swap)
        near = [lax.all_gather(block, "gx", axis=0, tiled=True) for block in (pair[0], pair[1])]
        index, far = jnp.zeros((1,), jnp.int32), []
    second = lax.ppermute(first, "gy", swap)

    d_pre_of, partial_of = shape((frame_len, quarter), BF16), shape((width, quarter), F32)
    d_pre_other, partial_other, full_up, full_down = call(
        other_kernel,
        (index, first, second, *near, *far),
        (d_pre_of, partial_of, weight, weight),
        [pltpu.VMEM((frame_len, width), BF16)] * 2,
        vmem=10,
    )
    d_pre_own, partial_own = call(
        own_kernel, (normed, grads, full_up, full_down), (d_pre_of, partial_of), vmem=10
    )
    partial = [partial_own, partial_other]

    half_rows_of = shape((frame_len, half_width), BF16)

    def own_d_norm(*ties):
        return call(
            d_norm_kernel,
            (meta, d_pre_own, d_pre_other, full_up),
            (shape((2, frame_len, half_width), F32), shape((2, frame_len, half_width), BF16)),
            vmem=10,
            ties=ties,
        )

    def over_cores(keep, came, *ties):
        return call(over_kernel, (meta, keep, came), half_rows_of, ties=ties)

    if ringed:
        place_of = {step: i for i, step in enumerate(steps)}
        place_of[-half] = place_of[half]

        def hop(step, mode, *given, ties=()):
            sums = [partial[i] for i in range(2) if mode[i] is not None]
            kernel = functools.partial(hop_kernel, place_of[step], mode)
            out = shape((len(sums), depth, quarter), BF16)
            block = call(kernel, (index, *sums, *given), out, ties=ties)
            return block, lax.ppermute(block, "gx", ahead if step > 0 else behind)

        _, down = hop(-half, (None, 0))
        tie, up = hop(half, (0, None))
        keep, send = own_d_norm(tie)
        for step in range(half - 1, 0, -1):
            farthest = step == half - 1
            tie, down = hop(-step, (0, 1) if farthest else (1, 1), down, ties=(tie,))
            if farthest:
                send = hold(send, tie, up)
                came = lax.ppermute(send, "gy", swap)
            tie, up = hop(step, (1, 0) if farthest else (1, 1), up, ties=(tie,))
            if step == half - 2:
                over = over_cores(keep, came, tie)
                tie = over
                back = lax.ppermute(over, "groups", swap)
        both = call(own_total_kernel, (index, *partial, down), shape((2, depth, quarter), F32))
        total, passing = call(
            total_kernel, (both, up), (shape((depth, quarter), F32), block_of), ties=(back,)
        )
        tail = (passing,)
    else:
        keep, send = own_d_norm()
        came = lax.ppermute(send, "gy", swap)
        back = lax.ppermute(over_cores(keep, came), "groups", swap)
        total, passing = [
            lax.psum_scatter(p, "gx", scatter_dimension=0, tiled=True) for p in partial
        ]
        passing, tail = passing.astype(BF16), ()
    passed = lax.ppermute(passing, "groups", swap)
    up_grad = call(join_kernel, (meta, total, passed), shape((depth, hidden), F32))

    gain = ln_gain[None]
    scaled, sums = call(
        scale_kernel,
        (meta, keep, came, back, frames, gain, stats),
        (shape((frame_len, half_width), F32), shape((frame_len, 2), F32)),
        ties=tail,
    )
    input_grad = call(
        input_kernel,
        (meta, scaled, sums, lax.ppermute(sums, "gy", swap), frames, grads, stats),
        shape((frame_len, half_width), BF16),
    )
    return (input_grad[None], up_grad)


def solution(mesh):
    placed = (
        P(("groups", "gx"), None, None),
        P(("groups", "gx"), None, None),
        P(),
        P("gx", "gy"),
        P("gx", "gy"),
        P("groups"),
    )
    return jax.shard_map(
        shards,
        mesh=mesh,
        in_specs=placed,
        out_specs=(P(("groups", "gx"), None, "gy"), P(("groups", "gx"), "gy")),
        check_vma=False,
    )
```

```python
import functools

import jax
import jax.numpy as jnp
from jax import lax
from jax.experimental import pallas as pl
from jax.experimental.pallas import tpu as pltpu
from jax.sharding import PartitionSpec as P

BF16, F32 = jnp.bfloat16, jnp.float32
VMEM = pl.BlockSpec(memory_space=pltpu.VMEM)
HBM = pl.BlockSpec(memory_space=pltpu.HBM)
ANY = pl.BlockSpec(memory_space=pl.ANY)
SMEM = pl.BlockSpec(memory_space=pltpu.SMEM)


def shape(dims, kind):
    return jax.ShapeDtypeStruct(dims, kind)


def call(kernel, ins, out_shape, scratch=(), vmem=16, flops=1, pinned=(), ties=()):
    count = len(ins)

    def body(*refs):
        kernel(*refs[:count], *refs[count + len(ties) :])

    moved = sum(x.size * x.dtype.itemsize for x in list(ins) + jax.tree.leaves(out_shape))
    return pl.pallas_call(
        body if ties else kernel,
        out_shape=out_shape,
        in_specs=[
            SMEM if x.dtype == jnp.int32 else HBM if i in pinned else VMEM
            for i, x in enumerate(ins)
        ]
        + [ANY] * len(ties),
        out_specs=jax.tree.map(lambda _: VMEM, out_shape),
        scratch_shapes=list(scratch),
        compiler_params=pltpu.CompilerParams(vmem_limit_bytes=vmem << 20),
        cost_estimate=pl.CostEstimate(flops=flops, bytes_accessed=moved, transcendentals=0),
    )(*ins, *ties)


def hold(array, *ties):
    return pl.pallas_call(
        lambda *refs: None,
        out_shape=shape(array.shape, array.dtype),
        in_specs=[ANY] * (1 + len(ties)),
        out_specs=ANY,
        input_output_aliases={0: 0},
        cost_estimate=pl.CostEstimate(flops=1, bytes_accessed=1, transcendentals=0),
    )(array, *ties)


def dot(left, right, left_dim=1, right_dim=0):
    return lax.dot_general(
        left, right, (((left_dim,), (right_dim,)), ((), ())), preferred_element_type=F32
    )


def gelu_slope(values):
    return (
        0.5 * (1.0 + lax.erf(values * 0.7071067811865476))
        + values * jnp.exp(-0.5 * values * values) * 0.3989422804014327
    )


def norm_kernel(meta, lengths, frames, out_grad, gain, *refs):
    normed, grads, passing, stats = refs
    half = passing.shape[1]
    rows = pl.ds(pl.multiple_of(meta[1] * half, half), half)
    keep = lax.broadcasted_iota(jnp.int32, (frames.shape[0], 1), 0) < lengths[meta[0]]
    grads[...] = jnp.where(keep, out_grad[...].astype(F32), 0.0).astype(BF16)
    passing[1] = grads[rows, :]
    values = frames[...].astype(F32)
    centre = jnp.mean(values, axis=-1, keepdims=True)
    shifted = values - centre
    variance = jnp.mean(shifted * shifted, axis=-1, keepdims=True)
    inv_std = lax.rsqrt(variance + 1e-05)
    normed[...] = (shifted * inv_std * gain[...][None]).astype(BF16)
    passing[0] = normed[rows, :]
    stats[:, 0:1] = centre
    stats[:, 1:2] = inv_std


def back_through(normed, grads, up, down, d_pre, partial):
    pre_act = dot(normed[...], up[...])
    d_act = dot(grads[...], down[...])
    d_pre[...] = (d_act * gelu_slope(pre_act)).astype(BF16)
    partial[...] = dot(normed[...], d_pre[...], 0, 0)


def place_kernel(index, *refs):
    blocks, (up, down, sems) = refs[:-3], refs[-3:]
    depth = blocks[0].shape[0]
    copies = []
    for i, block in enumerate(blocks):
        rows = pl.ds(pl.multiple_of(index[i // 2] * depth, depth), depth)
        target = (up, down)[i % 2].at[rows]
        copies.append(pltpu.make_async_copy(block, target, sems.at[i]))
    for copy in copies:
        copy.start()
    for copy in copies:
        copy.wait()


def other_kernel(index, first, second, near_up, near_down, *refs):
    d_pre, partial, up, down, normed, grads = refs[-6:]
    half = first.shape[1]
    for at, part in ((0, first), (half, second)):
        normed[at : at + half, :] = part[0]
        grads[at : at + half, :] = part[1]
    up[...] = near_up[...]
    down[...] = near_down[...]
    for ref, far in zip((up, down), refs[:-6]):
        depth = far.shape[0]
        rows = pl.ds(pl.multiple_of(index[index.shape[0] - 1] * depth, depth), depth)
        ref[rows, :] = far[...]
    back_through(normed, grads, up, down, d_pre, partial)


def own_kernel(normed, grads, up, down, d_pre, partial):
    back_through(normed, grads, up, down, d_pre, partial)


def d_norm_kernel(meta, d_pre_own, d_pre_other, up, keep, send):
    core = meta[1]
    rows, width = keep.shape[1:]
    mine = up[pl.ds(pl.multiple_of(core * width, width), width), :]
    theirs = up[pl.ds(pl.multiple_of((1 - core) * width, width), width), :]
    keep[0] = dot(d_pre_own[...], mine, 1, 1)
    keep[1] = dot(d_pre_other[...], mine, 1, 1)
    send[0] = dot(d_pre_own[...], theirs, 1, 1).astype(BF16)
    sent = dot(d_pre_other[...], theirs, 1, 1).astype(BF16)
    send[1, rows // 2 :, :] = sent[: rows // 2]
    send[1, : rows // 2, :] = sent[rows // 2 :]


def over_kernel(meta, keep, came, over):
    half = over.shape[0] // 2
    for i in range(2):
        at = lax.rem(i + meta[1], 2) * half
        rows = slice(i * half, (i + 1) * half)
        value = keep[1, rows, :] + came[1, rows, :].astype(F32)
        over[pl.ds(pl.multiple_of(at, half), half), :] = value.astype(BF16)


def own_columns(meta, ref, width):
    return ref[:, pl.ds(pl.multiple_of(meta[1] * width, width), width)]


def scale_kernel(meta, keep, came, back, frames, gain, stats, scaled, sums):
    width = scaled.shape[1]
    d_norm = keep[0] + came[0].astype(F32) + back[...].astype(F32)
    value = d_norm * own_columns(meta, gain, width)
    scaled[...] = value
    rows = own_columns(meta, frames, width).astype(F32)
    centred = (rows - stats[:, 0:1]) * stats[:, 1:2]
    sums[:, 0:1] = jnp.sum(value, axis=-1, keepdims=True)
    sums[:, 1:2] = jnp.sum(value * centred, axis=-1, keepdims=True)


def input_kernel(meta, scaled, sums, came, frames, grads, stats, out):
    width = scaled.shape[1]
    means = (sums[...] + came[...]) * (0.5 / width)
    rows = own_columns(meta, frames, width).astype(F32)
    inv_std = stats[:, 1:2]
    centred = (rows - stats[:, 0:1]) * inv_std
    value = inv_std * (scaled[...] - means[:, 0:1] - centred * means[:, 1:2])
    out[...] = (own_columns(meta, grads, width).astype(F32) + value).astype(BF16)


def hop_kernel(places, index, partial, *refs):
    outs = refs[len(refs) - len(places) :]
    came = iter(refs)
    depth = outs[0].shape[0]
    for (at, summed), out in zip(places, outs):
        value = partial[pl.ds(pl.multiple_of(index[at] * depth, depth), depth), :]
        if summed:
            value = value + next(came)[...].astype(F32)
        out[...] = value.astype(BF16)


def total_kernel(index, partial, up, down, total):
    depth = total.shape[0]
    rows = pl.ds(pl.multiple_of(index[0] * depth, depth), depth)
    value = partial[rows, :] + up[...].astype(F32) + down[...].astype(F32)
    total[...] = value.astype(total.dtype)


def join_kernel(meta, own, passed, out):
    width = own.shape[1]
    side = meta[2]
    out[:, pl.ds(pl.multiple_of(side * width, width), width)] = own[...]
    other = pl.ds(pl.multiple_of((1 - side) * width, width), width)
    out[:, other] = passed[...].astype(F32)


def ring_member(place, count):
    place = place % count
    return jnp.where(place < count // 2, 2 * place, 2 * (count - 1 - place) + 1)


def shards(frames, out_grad, ln_gain, w_up, w_down, lengths):
    peers = lax.axis_size("gx")
    half = peers // 2
    own = lax.axis_index("gx")
    side = lax.axis_index("groups")
    core = lax.axis_index("gy")
    frame_len, width = frames.shape[1:]
    depth, hidden = w_up.shape
    quarter = hidden // 2
    half_width = width // 2
    half_rows = frame_len // 2
    ringed = peers <= 16 and peers % 2 == 0 and depth % 16 == 0

    order = list(range(0, peers, 2)) + list(range(peers - 1, 0, -2))
    ahead = [(order[i], order[(i + 1) % peers]) for i in range(peers)]
    behind = [(b, a) for a, b in ahead]
    place = jnp.where(own % 2 == 0, own // 2, peers - 1 - own // 2)
    swap = [(0, 1), (1, 0)]
    after = lax.optimization_barrier

    mine = [lax.dynamic_slice_in_dim(w, side * quarter, quarter, 1) for w in (w_up, w_down)]
    mine, frames, out_grad, ln_gain, lengths = after((mine, frames, out_grad, ln_gain, lengths))
    meta = jnp.stack([own, core, side]).astype(jnp.int32)
    frames, out_grad = frames[0], out_grad[0]

    rows_of = shape((frame_len, width), BF16)
    normed, grads, passing, stats = call(
        norm_kernel,
        (meta, lengths, frames, out_grad, ln_gain),
        (rows_of, rows_of, shape((2, half_rows, width), BF16), shape((frame_len, 2), F32)),
        flops=10 * frame_len * width,
    )

    weight = shape((width, quarter), BF16)
    block_of = shape((depth, quarter), BF16)
    if ringed:
        blocks = {0: list(mine)}
        up, down = list(mine), list(mine)
        for step in range(1, half):
            up = [lax.ppermute(block, "gx", ahead) for block in up]
            down = [lax.ppermute(block, "gx", behind) for block in down]
            blocks[-step], blocks[step] = up, down
            if step == 1:
                passing = hold(passing, up[0], down[0])
        first = lax.ppermute(passing, "groups", swap)
        first, up, down = after((first, up, down))
        steps = list(blocks) + [half]
        index = jnp.stack([ring_member(place + step + peers, peers) for step in steps])
        index = index.astype(jnp.int32)
        blocks = [block for step in blocks for block in blocks[step]]
        near = call(
            place_kernel,
            (index, *blocks),
            (weight, weight),
            [pltpu.SemaphoreType.DMA((len(blocks),))],
            pinned=range(1, len(blocks) + 1),
        )
        far = [lax.ppermute(up[0], "gx", ahead), lax.ppermute(down[1], "gx", behind)]
    else:
        first = lax.ppermute(passing, "groups", swap)
        near = [lax.all_gather(block, "gx", axis=0, tiled=True) for block in mine]
        index, far = jnp.zeros((1,), jnp.int32), []
    second = lax.ppermute(first, "gy", swap)

    d_pre_of, partial_of = shape((frame_len, quarter), BF16), shape((width, quarter), F32)
    d_pre_other, partial_other, full_up, full_down = call(
        other_kernel,
        (index, first, second, *near, *far),
        (d_pre_of, partial_of, weight, weight),
        [pltpu.VMEM((frame_len, width), BF16)] * 2,
        flops=6 * frame_len * width * quarter,
    )
    d_pre_own, partial_own = call(
        own_kernel, (normed, grads, full_up, full_down), (d_pre_of, partial_of),
        flops=6 * frame_len * width * quarter,
    )
    partial = [partial_own, partial_other]

    half_rows_of = shape((frame_len, half_width), BF16)

    def own_d_norm(*ties):
        return call(
            d_norm_kernel,
            (meta, d_pre_own, d_pre_other, full_up),
            (shape((2, frame_len, half_width), F32), shape((2, frame_len, half_width), BF16)),
            flops=4 * frame_len * width * quarter,
            ties=ties,
        )

    def over_cores(keep, came, *ties):
        return call(over_kernel, (meta, keep, came), half_rows_of, ties=ties)

    if ringed:
        place_of = {step: i for i, step in enumerate(steps)}
        place_of[-half] = place_of[half]

        came = [{}, {}]

        def hop(i, turn, *ties):
            ways = [(half - turn - (i == 1), ahead), (turn + (i == 0) - half, behind)]
            ways = [way for way in ways if way[0] != 0]
            kept = [came[i][pairs[0]] for _, pairs in ways if pairs[0] in came[i]]
            places = [(place_of[step], pairs[0] in came[i]) for step, pairs in ways]
            blocks = call(
                functools.partial(hop_kernel, tuple(places)),
                (index, partial[i], *kept),
                [block_of] * len(ways),
                ties=ties,
            )
            for block, (_, pairs) in zip(blocks, ways):
                came[i][pairs[0]] = lax.ppermute(block, "gx", pairs)
            return blocks[0]

        hop(1, 0)
        tie = hop(0, 0)
        tie = hop(1, 1, tie)
        keep, send = own_d_norm(tie)
        tie = hop(0, 1, send)
        send = hold(send, tie, *came[1].values())
        over_cores_came = lax.ppermute(send, "gy", swap)
        tie = hop(1, 2, tie)
        tie = hop(0, 2, tie)
        over = over_cores(keep, over_cores_came, tie)
        back = lax.ppermute(over, "groups", swap)
        tie = over
        for turn in range(3, half):
            tie = hop(0, turn, hop(1, turn, tie))
        one, two = ([came[i][pairs[0]] for pairs in (ahead, behind)] for i in range(2))
        passing = call(total_kernel, (index, partial[1], *two), block_of, ties=(tie,))
        total = call(total_kernel, (index, partial[0], *one), shape((depth, quarter), F32))
        came = over_cores_came
        tail = (passing,)
    else:
        keep, send = own_d_norm()
        came = lax.ppermute(send, "gy", swap)
        back = lax.ppermute(over_cores(keep, came), "groups", swap)
        total, passing = [
            lax.psum_scatter(p, "gx", scatter_dimension=0, tiled=True) for p in partial
        ]
        passing, tail = passing.astype(BF16), ()
    passed = lax.ppermute(passing, "groups", swap)
    up_grad = call(join_kernel, (meta, total, passed), shape((depth, hidden), F32))

    gain = ln_gain[None]
    scaled, sums = call(
        scale_kernel,
        (meta, keep, came, back, frames, gain, stats),
        (shape((frame_len, half_width), F32), shape((frame_len, 2), F32)),
        ties=tail,
    )
    input_grad = call(
        input_kernel,
        (meta, scaled, sums, lax.ppermute(sums, "gy", swap), frames, grads, stats),
        shape((frame_len, half_width), BF16),
    )
    return (input_grad[None], up_grad)


def solution(mesh):
    placed = (
        P(("groups", "gx"), None, None),
        P(("groups", "gx"), None, None),
        P(),
        P("gx", "gy"),
        P("gx", "gy"),
        P("groups"),
    )
    return jax.shard_map(
        shards,
        mesh=mesh,
        in_specs=placed,
        out_specs=(P(("groups", "gx"), None, "gy"), P(("groups", "gx"), "gy")),
        check_vma=False,
    )
```

```python
import functools

import jax
import jax.numpy as jnp
from jax import lax
from jax.experimental import pallas as pl
from jax.experimental.pallas import tpu as pltpu
from jax.sharding import PartitionSpec as P

BF16, F32 = jnp.bfloat16, jnp.float32
VMEM = pl.BlockSpec(memory_space=pltpu.VMEM)
HBM = pl.BlockSpec(memory_space=pltpu.HBM)
ANY = pl.BlockSpec(memory_space=pl.ANY)
SMEM = pl.BlockSpec(memory_space=pltpu.SMEM)


def shape(dims, kind):
    return jax.ShapeDtypeStruct(dims, kind)


def call(kernel, ins, out_shape, scratch=(), vmem=16, flops=1, pinned=(), ties=()):
    count = len(ins)

    def body(*refs):
        kernel(*refs[:count], *refs[count + len(ties) :])

    moved = sum(x.size * x.dtype.itemsize for x in list(ins) + jax.tree.leaves(out_shape))
    return pl.pallas_call(
        body if ties else kernel,
        out_shape=out_shape,
        in_specs=[
            SMEM if x.dtype == jnp.int32 else HBM if i in pinned else VMEM
            for i, x in enumerate(ins)
        ]
        + [ANY] * len(ties),
        out_specs=jax.tree.map(lambda _: VMEM, out_shape),
        scratch_shapes=list(scratch),
        compiler_params=pltpu.CompilerParams(vmem_limit_bytes=vmem << 20),
        cost_estimate=pl.CostEstimate(flops=flops, bytes_accessed=moved, transcendentals=0),
    )(*ins, *ties)


def hold(array, *ties):
    return pl.pallas_call(
        lambda *refs: None,
        out_shape=shape(array.shape, array.dtype),
        in_specs=[ANY] * (1 + len(ties)),
        out_specs=ANY,
        input_output_aliases={0: 0},
        cost_estimate=pl.CostEstimate(flops=1, bytes_accessed=1, transcendentals=0),
    )(array, *ties)


def dot(left, right, left_dim=1, right_dim=0):
    return lax.dot_general(
        left, right, (((left_dim,), (right_dim,)), ((), ())), preferred_element_type=F32
    )


def gelu_slope(values):
    return (
        0.5 * (1.0 + lax.erf(values * 0.7071067811865476))
        + values * jnp.exp(-0.5 * values * values) * 0.3989422804014327
    )


def norm_rows(rows, gain):
    values = rows.astype(F32)
    centre = jnp.mean(values, axis=-1, keepdims=True)
    shifted = values - centre
    variance = jnp.mean(shifted * shifted, axis=-1, keepdims=True)
    inv_std = lax.rsqrt(variance + 1e-05)
    return (shifted * inv_std * gain[...][None]).astype(BF16), centre, inv_std


def mask_rows(rows, start, length):
    index = start + lax.broadcasted_iota(jnp.int32, (rows.shape[0], 1), 0)
    return jnp.where(index < length, rows.astype(F32), 0.0).astype(BF16)


def pass_kernel(meta, lengths, frames, out_grad, gain, passing, sems, rows, grads):
    half = rows.shape[0]
    start = pl.multiple_of(meta[1] * half, half)
    copies = [
        pltpu.make_async_copy(source.at[pl.ds(start, half)], target, sems.at[i])
        for i, (source, target) in enumerate(((frames, rows), (out_grad, grads)))
    ]
    for copy in copies:
        copy.start()
    copies[0].wait()
    passing[0] = norm_rows(rows[...], gain)[0]
    copies[1].wait()
    passing[1] = mask_rows(grads[...], start, lengths[meta[0]])


def norm_kernel(meta, lengths, frames, out_grad, gain, normed, grads, stats):
    value, centre, inv_std = norm_rows(frames[...], gain)
    normed[...] = value
    stats[:, 0:1] = centre
    stats[:, 1:2] = inv_std
    grads[...] = mask_rows(out_grad[...], 0, lengths[meta[0]])


def back_through(normed, grads, up, down, d_pre, partial):
    pre_act = dot(normed[...], up[...])
    d_act = dot(grads[...], down[...])
    d_pre[...] = (d_act * gelu_slope(pre_act)).astype(BF16)
    partial[...] = dot(normed[...], d_pre[...], 0, 0).astype(BF16)


def place_kernel(index, *refs):
    blocks, (up, down, sems) = refs[:-3], refs[-3:]
    depth = blocks[0].shape[0]
    copies = []
    for i, block in enumerate(blocks):
        rows = pl.ds(pl.multiple_of(index[i // 2] * depth, depth), depth)
        target = (up, down)[i % 2].at[rows]
        copies.append(pltpu.make_async_copy(block, target, sems.at[i]))
    for copy in copies:
        copy.start()
    for copy in copies:
        copy.wait()


def own_kernel(index, normed, grads, near_up, near_down, *refs):
    d_pre, partial, up, down = refs[-4:]
    up[...] = near_up[...]
    down[...] = near_down[...]
    for ref, far in zip((up, down), refs[:-4]):
        depth = far.shape[0]
        rows = pl.ds(pl.multiple_of(index[index.shape[0] - 1] * depth, depth), depth)
        ref[rows, :] = far[...]
    back_through(normed, grads, up, down, d_pre, partial)


def other_kernel(first, second, up, down, d_pre, partial, normed, grads):
    half = first.shape[1]
    for at, part in ((0, first), (half, second)):
        normed[at : at + half, :] = part[0]
        grads[at : at + half, :] = part[1]
    back_through(normed, grads, up, down, d_pre, partial)


def d_norm_kernel(meta, d_pre_own, d_pre_other, up, keep, send):
    core = meta[1]
    rows, width = keep.shape[1:]
    mine = up[pl.ds(pl.multiple_of(core * width, width), width), :]
    theirs = up[pl.ds(pl.multiple_of((1 - core) * width, width), width), :]
    keep[0] = dot(d_pre_own[...], mine, 1, 1).astype(BF16)
    keep[1] = dot(d_pre_other[...], mine, 1, 1).astype(BF16)
    send[0] = dot(d_pre_own[...], theirs, 1, 1).astype(BF16)
    sent = dot(d_pre_other[...], theirs, 1, 1).astype(BF16)
    send[1, rows // 2 :, :] = sent[: rows // 2]
    send[1, : rows // 2, :] = sent[rows // 2 :]


def over_kernel(meta, keep, came, over):
    half = over.shape[0] // 2
    for i in range(2):
        at = lax.rem(i + meta[1], 2) * half
        rows = slice(i * half, (i + 1) * half)
        value = keep[1, rows, :].astype(F32) + came[1, rows, :].astype(F32)
        over[pl.ds(pl.multiple_of(at, half), half), :] = value.astype(BF16)


def own_columns(meta, ref, width):
    return ref[:, pl.ds(pl.multiple_of(meta[1] * width, width), width)]


def scale_kernel(meta, keep, came, back, frames, gain, stats, scaled, sums):
    width = scaled.shape[1]
    d_norm = keep[0].astype(F32) + came[0].astype(F32) + back[...].astype(F32)
    value = d_norm * own_columns(meta, gain, width)
    scaled[...] = value
    rows = own_columns(meta, frames, width).astype(F32)
    centred = (rows - stats[:, 0:1]) * stats[:, 1:2]
    sums[:, 0:1] = jnp.sum(value, axis=-1, keepdims=True)
    sums[:, 1:2] = jnp.sum(value * centred, axis=-1, keepdims=True)


def input_kernel(meta, scaled, sums, came, frames, grads, stats, out):
    width = scaled.shape[1]
    means = (sums[...] + came[...]) * (0.5 / width)
    rows = own_columns(meta, frames, width).astype(F32)
    inv_std = stats[:, 1:2]
    centred = (rows - stats[:, 0:1]) * inv_std
    value = inv_std * (scaled[...] - means[:, 0:1] - centred * means[:, 1:2])
    out[...] = (own_columns(meta, grads, width).astype(F32) + value).astype(BF16)


def hop_kernel(places, index, partial, *refs):
    outs = refs[len(refs) - len(places) :]
    came = iter(refs)
    depth = outs[0].shape[0]
    for (at, summed), out in zip(places, outs):
        value = partial[pl.ds(pl.multiple_of(index[at] * depth, depth), depth), :].astype(F32)
        if summed:
            value = value + next(came)[...].astype(F32)
        out[...] = value.astype(BF16)


def add_kernel(one, two, total):
    total[...] = one[...].astype(F32) + two[...].astype(F32)


def own_total_kernel(index, partial, up, down, total):
    depth = total.shape[0]
    rows = pl.ds(pl.multiple_of(index[0] * depth, depth), depth)
    total[...] = partial[rows, :].astype(F32) + up[...].astype(F32) + down[...].astype(F32)


def join_kernel(meta, own, *refs):
    width, out = own.shape[1], refs[-1]
    side = meta[2]
    out[:, pl.ds(pl.multiple_of(side * width, width), width)] = own[...]
    value = refs[0][...].astype(F32)
    for ref in refs[1:-1]:
        value = value + ref[...].astype(F32)
    out[:, pl.ds(pl.multiple_of((1 - side) * width, width), width)] = value


def ring_member(place, count):
    place = place % count
    return jnp.where(place < count // 2, 2 * place, 2 * (count - 1 - place) + 1)


def shards(frames, out_grad, ln_gain, w_up, w_down, lengths):
    peers = lax.axis_size("gx")
    half = peers // 2
    own = lax.axis_index("gx")
    side = lax.axis_index("groups")
    core = lax.axis_index("gy")
    frame_len, width = frames.shape[1:]
    depth, hidden = w_up.shape
    quarter = hidden // 2
    half_width = width // 2
    half_rows = frame_len // 2
    ringed = peers <= 16 and peers % 2 == 0 and depth % 16 == 0

    order = list(range(0, peers, 2)) + list(range(peers - 1, 0, -2))
    ahead = [(order[i], order[(i + 1) % peers]) for i in range(peers)]
    behind = [(b, a) for a, b in ahead]
    place = jnp.where(own % 2 == 0, own // 2, peers - 1 - own // 2)
    swap = [(0, 1), (1, 0)]
    after = lax.optimization_barrier

    mine = [lax.dynamic_slice_in_dim(w, side * quarter, quarter, 1) for w in (w_up, w_down)]
    mine, frames, out_grad, ln_gain, lengths = after((mine, frames, out_grad, ln_gain, lengths))
    meta = jnp.stack([own, core, side]).astype(jnp.int32)
    frames, out_grad = frames[0], out_grad[0]

    rows_of = shape((frame_len, width), BF16)
    operands = (meta, lengths, frames, out_grad, ln_gain)
    passing = call(
        pass_kernel,
        operands,
        shape((2, half_rows, width), BF16),
        [pltpu.SemaphoreType.DMA((2,))] + [pltpu.VMEM((half_rows, width), BF16)] * 2,
        flops=5 * frame_len * width,
        pinned=(2, 3),
    )
    first = lax.ppermute(passing, "groups", swap)
    normed, grads, stats = call(
        norm_kernel,
        operands,
        (rows_of, rows_of, shape((frame_len, 2), F32)),
        flops=10 * frame_len * width,
    )

    weight = shape((width, quarter), BF16)
    block_of = shape((depth, quarter), BF16)
    if ringed:
        blocks = {0: list(mine)}
        up, down = list(mine), list(mine)
        for step in range(1, half):
            up = [lax.ppermute(block, "gx", ahead) for block in up]
            down = [lax.ppermute(block, "gx", behind) for block in down]
            blocks[-step], blocks[step] = up, down
        first, up, down = after((first, up, down))
        first = hold(first, normed)
        steps = list(blocks) + [half]
        index = jnp.stack([ring_member(place + step + peers, peers) for step in steps])
        index = index.astype(jnp.int32)
        blocks = [block for step in blocks for block in blocks[step]]
        near = call(
            place_kernel,
            (index, *blocks),
            (weight, weight),
            [pltpu.SemaphoreType.DMA((len(blocks),))],
            pinned=range(1, len(blocks) + 1),
        )
        far = [lax.ppermute(up[0], "gx", ahead), lax.ppermute(down[1], "gx", behind)]
    else:
        near = [lax.all_gather(block, "gx", axis=0, tiled=True) for block in mine]
        index, far = jnp.zeros((1,), jnp.int32), []
    second = lax.ppermute(first, "gy", swap)

    d_pre_of, partial_of = shape((frame_len, quarter), BF16), shape((width, quarter), BF16)
    d_pre_own, partial_own, full_up, full_down = call(
        own_kernel,
        (index, normed, grads, *near, *far),
        (d_pre_of, partial_of, weight, weight),
        flops=6 * frame_len * width * quarter,
    )
    d_pre_other, partial_other = call(
        other_kernel,
        (first, second, full_up, full_down),
        (d_pre_of, partial_of),
        [pltpu.VMEM((frame_len, width), BF16)] * 2,
        flops=6 * frame_len * width * quarter,
    )
    partial = [partial_own, partial_other]

    half_rows_of = shape((frame_len, half_width), BF16)

    def own_d_norm(*ties):
        return call(
            d_norm_kernel,
            (meta, d_pre_own, d_pre_other, full_up),
            (shape((2, frame_len, half_width), BF16), shape((2, frame_len, half_width), BF16)),
            flops=4 * frame_len * width * quarter,
            ties=ties,
        )

    def over_cores(keep, came, *ties):
        return call(over_kernel, (meta, keep, came), half_rows_of, ties=ties)

    def scale(keep, came, back, *ties):
        return call(
            scale_kernel,
            (meta, keep, came, back, frames, ln_gain[None], stats),
            (shape((frame_len, half_width), F32), shape((frame_len, 2), F32)),
            ties=ties,
        )

    def input_gradient(scaled, sums, *ties):
        return call(
            input_kernel,
            (meta, scaled, sums, lax.ppermute(sums, "gy", swap), frames, grads, stats),
            half_rows_of,
            ties=ties,
        )

    up_grad_of = shape((depth, hidden), F32)
    if ringed:
        place_of = {step: i for i, step in enumerate(steps)}
        place_of[-half] = place_of[half]
        came = [{}, {}]
        across = {}
        for name, pairs in (("up", ahead), ("down", behind)):
            across[name] = [
                (a + side_at * peers, b + (1 - side_at) * peers)
                for side_at in range(2)
                for a, b in pairs
            ]

        def hop(i, turn, *ties):
            ways = [("up", half - turn - i), ("down", turn + 1 - i - half)]
            ways = [way for way in ways if way[1] != 0]
            kept = [came[i][name] for name, _ in ways if name in came[i]]
            places = [(place_of[step], name in came[i]) for name, step in ways]
            if (i, turn) == (1, 0):
                places.append((0, False))
            blocks = call(
                functools.partial(hop_kernel, tuple(places)),
                (index, partial[i], *kept),
                [block_of] * len(places),
                ties=ties,
            )
            for block, (name, step) in zip(blocks, ways):
                if i == 1 and abs(step) == 1:
                    came[i][name] = lax.ppermute(block, ("groups", "gx"), across[name])
                else:
                    came[i][name] = lax.ppermute(block, "gx", ahead if name == "up" else behind)
            if (i, turn) == (1, 0):
                came[i]["own"] = lax.ppermute(blocks[-1], "groups", swap)
            return blocks[0]

        hop(0, 0)
        tie = hop(1, 0)
        keep, send = own_d_norm(tie)
        send = hold(send, came[0]["up"], came[0]["down"])
        sent = lax.ppermute(send, "gy", swap)
        tie = hop(0, 1, send)
        tie = hop(1, 1, tie)
        over = over_cores(keep, sent, tie)
        over = hold(over, came[0]["up"], came[0]["down"])
        back = lax.ppermute(over, "groups", swap)
        tie = hop(0, 2, over)
        tie = hop(1, 2, tie)
        for turn in range(3, half):
            tie = hop(1, turn, hop(0, turn, tie, came[1]["own"]))
        other = call(
            add_kernel, (came[1]["own"], came[1]["up"]), shape((depth, quarter), F32), ties=(tie,)
        )
        scaled, sums = scale(keep, sent, back, other)
        input_grad = input_gradient(scaled, sums)
        total = call(
            own_total_kernel,
            (index, partial[0], came[0]["up"], came[0]["down"]),
            shape((depth, quarter), F32),
            ties=(input_grad,),
        )
        up_grad = call(join_kernel, (meta, total, other, came[1]["down"]), up_grad_of)
    else:
        keep, send = own_d_norm()
        sent = lax.ppermute(send, "gy", swap)
        back = lax.ppermute(over_cores(keep, sent), "groups", swap)
        input_grad = input_gradient(*scale(keep, sent, back))
        total, passing = [
            lax.psum_scatter(p.astype(F32), "gx", scatter_dimension=0, tiled=True) for p in partial
        ]
        passed = lax.ppermute(passing.astype(BF16), "groups", swap)
        up_grad = call(join_kernel, (meta, total, passed), up_grad_of)
    return (input_grad[None], up_grad)


def solution(mesh):
    placed = (
        P(("groups", "gx"), None, None),
        P(("groups", "gx"), None, None),
        P(),
        P("gx", "gy"),
        P("gx", "gy"),
        P("groups"),
    )
    return jax.shard_map(
        shards,
        mesh=mesh,
        in_specs=placed,
        out_specs=(P(("groups", "gx"), None, "gy"), P(("groups", "gx"), "gy")),
        check_vma=False,
    )
```

```python
import functools

import jax
import jax.numpy as jnp
from jax import lax
from jax.experimental import pallas as pl
from jax.experimental.pallas import tpu as pltpu
from jax.sharding import PartitionSpec as P

BF16, F32 = jnp.bfloat16, jnp.float32
VMEM = pl.BlockSpec(memory_space=pltpu.VMEM)
ANY = pl.BlockSpec(memory_space=pl.ANY)
SMEM = pl.BlockSpec(memory_space=pltpu.SMEM)


def shape(dims, kind):
    return jax.ShapeDtypeStruct(dims, kind)


def call(kernel, ins, out_shape, scratch=(), vmem=16, flops=1, left=(), ties=()):
    count = len(ins)

    def body(*refs):
        kernel(*refs[:count], *refs[count + len(ties) :])

    moved = sum(x.size * x.dtype.itemsize for x in list(ins) + jax.tree.leaves(out_shape))
    return pl.pallas_call(
        body if ties else kernel,
        out_shape=out_shape,
        in_specs=[
            SMEM if x.dtype == jnp.int32 else ANY if i in left else VMEM
            for i, x in enumerate(ins)
        ]
        + [ANY] * len(ties),
        out_specs=jax.tree.map(lambda _: VMEM, out_shape),
        scratch_shapes=list(scratch),
        compiler_params=pltpu.CompilerParams(vmem_limit_bytes=vmem << 20),
        cost_estimate=pl.CostEstimate(flops=flops, bytes_accessed=moved, transcendentals=0),
    )(*ins, *ties)


def hold(array, *ties):
    return pl.pallas_call(
        lambda *refs: None,
        out_shape=shape(array.shape, array.dtype),
        in_specs=[ANY] * (1 + len(ties)),
        out_specs=ANY,
        input_output_aliases={0: 0},
        compiler_params=pltpu.CompilerParams(vmem_limit_bytes=1 << 20),
        cost_estimate=pl.CostEstimate(flops=1, bytes_accessed=1, transcendentals=0),
    )(array, *ties)


def dot(left, right, left_dim=1, right_dim=0):
    return lax.dot_general(
        left, right, (((left_dim,), (right_dim,)), ((), ())), preferred_element_type=F32
    )


def gelu_slope(values):
    return (
        0.5 * (1.0 + lax.erf(values * 0.7071067811865476))
        + values * jnp.exp(-0.5 * values * values) * 0.3989422804014327
    )


def norm_rows(rows, gain):
    values = rows.astype(F32)
    centre = jnp.mean(values, axis=-1, keepdims=True)
    shifted = values - centre
    variance = jnp.mean(shifted * shifted, axis=-1, keepdims=True)
    inv_std = lax.rsqrt(variance + 1e-05)
    return (shifted * inv_std * gain[...][None]).astype(BF16), centre, inv_std


def mask_rows(rows, start, length):
    index = start + lax.broadcasted_iota(jnp.int32, (rows.shape[0], 1), 0)
    return jnp.where(index < length, rows.astype(F32), 0.0).astype(BF16)


def pass_kernel(meta, lengths, frames, out_grad, gain, passing, sems, rows, grads):
    half = rows.shape[0]
    start = pl.multiple_of(meta[1] * half, half)
    copies = [
        pltpu.make_async_copy(source.at[pl.ds(start, half)], target, sems.at[i])
        for i, (source, target) in enumerate(((frames, rows), (out_grad, grads)))
    ]
    for copy in copies:
        copy.start()
    copies[0].wait()
    passing[0] = norm_rows(rows[...], gain)[0]
    copies[1].wait()
    passing[1] = mask_rows(grads[...], start, lengths[meta[0]])


def norm_kernel(meta, lengths, frames, out_grad, gain, normed, grads, stats):
    value, centre, inv_std = norm_rows(frames[...], gain)
    normed[...] = value
    stats[:, 0:1] = centre
    stats[:, 1:2] = inv_std
    grads[...] = mask_rows(out_grad[...], 0, lengths[meta[0]])


def back_through(normed, grads, up, down, d_pre, partial):
    pre_act = dot(normed[...], up[...])
    d_act = dot(grads[...], down[...])
    d_pre[...] = (d_act * gelu_slope(pre_act)).astype(BF16)
    partial[...] = dot(normed[...], d_pre[...], 0, 0).astype(BF16)


def own_kernel(index, normed, grads, *refs):
    blocks, (d_pre, partial, up, down) = refs[:-4], refs[-4:]
    depth = blocks[0].shape[0]
    for i, block in enumerate(blocks):
        rows = pl.ds(pl.multiple_of(index[i // 2] * depth, depth), depth)
        (up, down)[i % 2][rows, :] = block[...]
    back_through(normed, grads, up, down, d_pre, partial)


def other_kernel(first, second, up, down, d_pre, partial, normed, grads):
    half = first.shape[1]
    for at, part in ((0, first), (half, second)):
        normed[at : at + half, :] = part[0]
        grads[at : at + half, :] = part[1]
    back_through(normed, grads, up, down, d_pre, partial)


def d_norm_kernel(meta, d_pre_own, d_pre_other, up, keep, send):
    core = meta[1]
    rows, width = keep.shape[1:]
    mine = up[pl.ds(pl.multiple_of(core * width, width), width), :]
    theirs = up[pl.ds(pl.multiple_of((1 - core) * width, width), width), :]
    keep[0] = dot(d_pre_own[...], mine, 1, 1).astype(BF16)
    keep[1] = dot(d_pre_other[...], mine, 1, 1).astype(BF16)
    send[0] = dot(d_pre_own[...], theirs, 1, 1).astype(BF16)
    sent = dot(d_pre_other[...], theirs, 1, 1).astype(BF16)
    send[1, rows // 2 :, :] = sent[: rows // 2]
    send[1, : rows // 2, :] = sent[rows // 2 :]


def over_kernel(meta, keep, came, over):
    half = over.shape[0] // 2
    for i in range(2):
        at = lax.rem(i + meta[1], 2) * half
        rows = slice(i * half, (i + 1) * half)
        value = keep[1, rows, :].astype(F32) + came[1, rows, :].astype(F32)
        over[pl.ds(pl.multiple_of(at, half), half), :] = value.astype(BF16)


def own_columns(meta, ref, width):
    return ref[:, pl.ds(pl.multiple_of(meta[1] * width, width), width)]


def scale_kernel(meta, keep, came, back, frames, gain, stats, scaled, sums):
    width = scaled.shape[1]
    d_norm = keep[0].astype(F32) + came[0].astype(F32) + back[...].astype(F32)
    value = d_norm * own_columns(meta, gain, width)
    scaled[...] = value
    rows = own_columns(meta, frames, width).astype(F32)
    centred = (rows - stats[:, 0:1]) * stats[:, 1:2]
    sums[:, 0:1] = jnp.sum(value, axis=-1, keepdims=True)
    sums[:, 1:2] = jnp.sum(value * centred, axis=-1, keepdims=True)


def input_kernel(meta, scaled, sums, came, frames, grads, stats, out):
    width = scaled.shape[1]
    means = (sums[...] + came[...]) * (0.5 / width)
    rows = own_columns(meta, frames, width).astype(F32)
    inv_std = stats[:, 1:2]
    centred = (rows - stats[:, 0:1]) * inv_std
    value = inv_std * (scaled[...] - means[:, 0:1] - centred * means[:, 1:2])
    out[...] = (own_columns(meta, grads, width).astype(F32) + value).astype(BF16)


def hop_kernel(places, index, partial, *refs):
    outs = refs[len(refs) - len(places) :]
    came = iter(refs)
    depth = outs[0].shape[0]
    for (at, summed), out in zip(places, outs):
        value = partial[pl.ds(pl.multiple_of(index[at] * depth, depth), depth), :].astype(F32)
        if summed:
            value = value + next(came)[...].astype(F32)
        out[...] = value.astype(BF16)


def add_kernel(one, two, total):
    total[...] = one[...].astype(F32) + two[...].astype(F32)


def own_total_kernel(index, partial, up, down, total):
    depth = total.shape[0]
    rows = pl.ds(pl.multiple_of(index[0] * depth, depth), depth)
    total[...] = partial[rows, :].astype(F32) + up[...].astype(F32) + down[...].astype(F32)


def join_kernel(meta, own, *refs):
    width, out = own.shape[1], refs[-1]
    side = meta[2]
    out[:, pl.ds(pl.multiple_of(side * width, width), width)] = own[...]
    value = refs[0][...].astype(F32)
    for ref in refs[1:-1]:
        value = value + ref[...].astype(F32)
    out[:, pl.ds(pl.multiple_of((1 - side) * width, width), width)] = value


def ring_member(place, count):
    place = place % count
    return jnp.where(place < count // 2, 2 * place, 2 * (count - 1 - place) + 1)


def shards(frames, out_grad, ln_gain, w_up, w_down, lengths):
    peers = lax.axis_size("gx")
    half = peers // 2
    own = lax.axis_index("gx")
    side = lax.axis_index("groups")
    core = lax.axis_index("gy")
    frame_len, width = frames.shape[1:]
    depth, hidden = w_up.shape
    quarter = hidden // 2
    half_width = width // 2
    half_rows = frame_len // 2
    ringed = peers <= 16 and peers % 2 == 0 and depth % 16 == 0

    order = list(range(0, peers, 2)) + list(range(peers - 1, 0, -2))
    ahead = [(order[i], order[(i + 1) % peers]) for i in range(peers)]
    behind = [(b, a) for a, b in ahead]
    place = jnp.where(own % 2 == 0, own // 2, peers - 1 - own // 2)
    swap = [(0, 1), (1, 0)]
    after = lax.optimization_barrier

    mine = [lax.dynamic_slice_in_dim(w, side * quarter, quarter, 1) for w in (w_up, w_down)]
    mine, frames, out_grad, ln_gain, lengths = after((mine, frames, out_grad, ln_gain, lengths))
    meta = jnp.stack([own, core, side]).astype(jnp.int32)
    frames, out_grad = frames[0], out_grad[0]

    rows_of = shape((frame_len, width), BF16)
    operands = (meta, lengths, frames, out_grad, ln_gain)
    passing = call(
        pass_kernel,
        operands,
        shape((2, half_rows, width), BF16),
        [pltpu.SemaphoreType.DMA((2,))] + [pltpu.VMEM((half_rows, width), BF16)] * 2,
        flops=5 * frame_len * width,
        vmem=60,
        left=(2, 3),
    )
    first = lax.ppermute(passing, "groups", swap)
    normed, grads, stats = call(
        norm_kernel,
        operands,
        (rows_of, rows_of, shape((frame_len, 2), F32)),
        flops=10 * frame_len * width,
    )

    weight = shape((width, quarter), BF16)
    block_of = shape((depth, quarter), BF16)
    if ringed:
        blocks = {0: list(mine)}
        up, down = list(mine), list(mine)
        for step in range(1, half):
            up = [lax.ppermute(block, "gx", ahead) for block in up]
            down = [lax.ppermute(block, "gx", behind) for block in down]
            blocks[-step], blocks[step] = up, down
        first, up, down = after((first, up, down))
        first = hold(first, normed)
        steps = list(blocks) + [half]
        index = jnp.stack([ring_member(place + step + peers, peers) for step in steps])
        index = index.astype(jnp.int32)
        blocks = [block for step in blocks for block in blocks[step]]
        blocks += [lax.ppermute(up[0], "gx", ahead), lax.ppermute(down[1], "gx", behind)]
    else:
        blocks = [lax.all_gather(block, "gx", axis=0, tiled=True) for block in mine]
        index = jnp.zeros((1,), jnp.int32)
    second = lax.ppermute(first, "gy", swap)

    d_pre_of, partial_of = shape((frame_len, quarter), BF16), shape((width, quarter), BF16)
    d_pre_own, partial_own, full_up, full_down = call(
        own_kernel,
        (index, normed, grads, *blocks),
        (d_pre_of, partial_of, weight, weight),
        flops=6 * frame_len * width * quarter,
    )
    d_pre_other, partial_other = call(
        other_kernel,
        (first, second, full_up, full_down),
        (d_pre_of, partial_of),
        [pltpu.VMEM((frame_len, width), BF16)] * 2,
        flops=6 * frame_len * width * quarter,
    )
    partial = [partial_own, partial_other]

    half_rows_of = shape((frame_len, half_width), BF16)

    def own_d_norm(*ties):
        return call(
            d_norm_kernel,
            (meta, d_pre_own, d_pre_other, full_up),
            (shape((2, frame_len, half_width), BF16), shape((2, frame_len, half_width), BF16)),
            flops=4 * frame_len * width * quarter,
            ties=ties,
        )

    def over_cores(keep, came, *ties):
        return call(over_kernel, (meta, keep, came), half_rows_of, ties=ties)

    def scale(keep, came, back, *ties):
        return call(
            scale_kernel,
            (meta, keep, came, back, frames, ln_gain[None], stats),
            (shape((frame_len, half_width), F32), shape((frame_len, 2), F32)),
            ties=ties,
        )

    def input_gradient(scaled, sums, *ties):
        return call(
            input_kernel,
            (meta, scaled, sums, lax.ppermute(sums, "gy", swap), frames, grads, stats),
            half_rows_of,
            ties=ties,
        )

    up_grad_of = shape((depth, hidden), F32)
    if ringed:
        place_of = {step: i for i, step in enumerate(steps)}
        place_of[-half] = place_of[half]
        came = [{}, {}]
        across = {}
        for name, pairs in (("up", ahead), ("down", behind)):
            across[name] = [
                (a + side_at * peers, b + (1 - side_at) * peers)
                for side_at in range(2)
                for a, b in pairs
            ]

        def hop(i, turn, *ties):
            ways = [("up", half - turn - i), ("down", turn + 1 - i - half)]
            ways = [way for way in ways if way[1] != 0]
            kept = [came[i][name] for name, _ in ways if name in came[i]]
            places = [(place_of[step], name in came[i]) for name, step in ways]
            if (i, turn) == (1, 0):
                places.append((0, False))
            blocks = call(
                functools.partial(hop_kernel, tuple(places)),
                (index, partial[i], *kept),
                [block_of] * len(places),
                ties=ties,
            )
            for block, (name, step) in zip(blocks, ways):
                if i == 1 and abs(step) == 1:
                    came[i][name] = lax.ppermute(block, ("groups", "gx"), across[name])
                else:
                    came[i][name] = lax.ppermute(block, "gx", ahead if name == "up" else behind)
            if (i, turn) == (1, 0):
                came[i]["own"] = lax.ppermute(blocks[-1], "groups", swap)
            return blocks[0]

        hop(0, 0)
        tie = hop(1, 0)
        keep, send = own_d_norm(tie)
        send = hold(send, came[0]["up"], came[0]["down"])
        sent = lax.ppermute(send, "gy", swap)
        tie = hop(0, 1, send)
        tie = hop(1, 1, tie, came[1]["own"])
        over = over_cores(keep, sent, tie)
        over = hold(over, came[0]["up"], came[0]["down"])
        back = lax.ppermute(over, "groups", swap)
        tie = hop(0, 2, over)
        tie = hop(1, 2, tie)
        for turn in range(3, half):
            tie = hop(1, turn, hop(0, turn, tie))
        other = call(
            add_kernel, (came[1]["own"], came[1]["up"]), shape((depth, quarter), F32), ties=(tie,)
        )
        scaled, sums = scale(keep, sent, back, other)
        input_grad = input_gradient(scaled, sums)
        total = call(
            own_total_kernel,
            (index, partial[0], came[0]["up"], came[0]["down"]),
            shape((depth, quarter), F32),
            ties=(input_grad,),
        )
        up_grad = call(join_kernel, (meta, total, other, came[1]["down"]), up_grad_of)
    else:
        keep, send = own_d_norm()
        sent = lax.ppermute(send, "gy", swap)
        back = lax.ppermute(over_cores(keep, sent), "groups", swap)
        input_grad = input_gradient(*scale(keep, sent, back))
        total, passing = [
            lax.psum_scatter(p.astype(F32), "gx", scatter_dimension=0, tiled=True) for p in partial
        ]
        passed = lax.ppermute(passing.astype(BF16), "groups", swap)
        up_grad = call(join_kernel, (meta, total, passed), up_grad_of)
    return (input_grad[None], up_grad)


def solution(mesh):
    placed = (
        P(("groups", "gx"), None, None),
        P(("groups", "gx"), None, None),
        P(),
        P("gx", "gy"),
        P("gx", "gy"),
        P("groups"),
    )
    return jax.shard_map(
        shards,
        mesh=mesh,
        in_specs=placed,
        out_specs=(P(("groups", "gx"), None, "gy"), P(("groups", "gx"), "gy")),
        check_vma=False,
    )
```

```python
import functools

import jax
import jax.numpy as jnp
from jax import lax
from jax.experimental import pallas as pl
from jax.experimental.pallas import tpu as pltpu
from jax.sharding import PartitionSpec as P

BF16, F32 = jnp.bfloat16, jnp.float32
VMEM = pl.BlockSpec(memory_space=pltpu.VMEM)
ANY = pl.BlockSpec(memory_space=pl.ANY)
SMEM = pl.BlockSpec(memory_space=pltpu.SMEM)


def shape(dims, kind):
    return jax.ShapeDtypeStruct(dims, kind)


def call(kernel, ins, out_shape, scratch=(), vmem=16, flops=1, left=(), ties=()):
    count = len(ins)

    def body(*refs):
        kernel(*refs[:count], *refs[count + len(ties) :])

    moved = sum(x.size * x.dtype.itemsize for x in list(ins) + jax.tree.leaves(out_shape))
    return pl.pallas_call(
        body if ties else kernel,
        out_shape=out_shape,
        in_specs=[
            SMEM if x.dtype == jnp.int32 else ANY if i in left else VMEM
            for i, x in enumerate(ins)
        ]
        + [ANY] * len(ties),
        out_specs=jax.tree.map(lambda _: VMEM, out_shape),
        scratch_shapes=list(scratch),
        compiler_params=pltpu.CompilerParams(vmem_limit_bytes=vmem << 20),
        cost_estimate=pl.CostEstimate(flops=flops, bytes_accessed=moved, transcendentals=0),
    )(*ins, *ties)


def hold(array, *ties):
    return pl.pallas_call(
        lambda *refs: None,
        out_shape=shape(array.shape, array.dtype),
        in_specs=[ANY] * (1 + len(ties)),
        out_specs=ANY,
        input_output_aliases={0: 0},
        compiler_params=pltpu.CompilerParams(vmem_limit_bytes=1 << 20),
        cost_estimate=pl.CostEstimate(flops=1, bytes_accessed=1, transcendentals=0),
    )(array, *ties)


def dot(left, right, left_dim=1, right_dim=0):
    return lax.dot_general(
        left, right, (((left_dim,), (right_dim,)), ((), ())), preferred_element_type=F32
    )


def gelu_slope(values):
    return (
        0.5 * (1.0 + lax.erf(values * 0.7071067811865476))
        + values * jnp.exp(-0.5 * values * values) * 0.3989422804014327
    )


def norm_rows(rows, gain):
    values = rows.astype(F32)
    centre = jnp.mean(values, axis=-1, keepdims=True)
    shifted = values - centre
    variance = jnp.mean(shifted * shifted, axis=-1, keepdims=True)
    inv_std = lax.rsqrt(variance + 1e-05)
    return (shifted * inv_std * gain[...][None]).astype(BF16), centre, inv_std


def mask_rows(rows, start, length):
    index = start + lax.broadcasted_iota(jnp.int32, (rows.shape[0], 1), 0)
    return jnp.where(index < length, rows.astype(F32), 0.0).astype(BF16)


def pass_kernel(meta, lengths, frames, out_grad, gain, passing, sems, rows, grads):
    half = rows.shape[0]
    start = pl.multiple_of(meta[1] * half, half)
    copies = [
        pltpu.make_async_copy(source.at[pl.ds(start, half)], target, sems.at[i])
        for i, (source, target) in enumerate(((frames, rows), (out_grad, grads)))
    ]
    for copy in copies:
        copy.start()
    copies[0].wait()
    passing[0] = norm_rows(rows[...], gain)[0]
    copies[1].wait()
    passing[1] = mask_rows(grads[...], start, lengths[meta[0]])


def norm_kernel(meta, lengths, frames, out_grad, gain, normed, grads, stats):
    value, centre, inv_std = norm_rows(frames[...], gain)
    normed[...] = value
    stats[:, 0:1] = centre
    stats[:, 1:2] = inv_std
    grads[...] = mask_rows(out_grad[...], 0, lengths[meta[0]])


def back_through(normed, grads, up, down, d_pre, partial):
    pre_act = dot(normed[...], up[...])
    d_act = dot(grads[...], down[...])
    d_pre[...] = (d_act * gelu_slope(pre_act)).astype(BF16)
    partial[...] = dot(normed[...], d_pre[...], 0, 0).astype(BF16)


def place_kernel(index, *refs):
    blocks, (up, down, sems) = refs[:-3], refs[-3:]
    depth = blocks[0].shape[0]
    copies = []
    for i, block in enumerate(blocks):
        rows = pl.ds(pl.multiple_of(index[i // 2] * depth, depth), depth)
        target = (up, down)[i % 2].at[rows]
        copies.append(pltpu.make_async_copy(block, target, sems.at[i]))
    for copy in copies:
        copy.start()
    for copy in copies:
        copy.wait()


def other_kernel(index, first, second, near_up, near_down, *refs):
    d_pre, partial, up, down, normed, grads = refs[-6:]
    half = first.shape[1]
    for at, part in ((0, first), (half, second)):
        normed[at : at + half, :] = part[0]
        grads[at : at + half, :] = part[1]
    up[...] = near_up[...]
    down[...] = near_down[...]
    for ref, far in zip((up, down), refs[:-6]):
        depth = far.shape[0]
        rows = pl.ds(pl.multiple_of(index[index.shape[0] - 1] * depth, depth), depth)
        ref[rows, :] = far[...]
    back_through(normed, grads, up, down, d_pre, partial)


def own_kernel(normed, grads, up, down, d_pre, partial):
    back_through(normed, grads, up, down, d_pre, partial)


def d_norm_kernel(meta, d_pre_own, d_pre_other, up, keep, send):
    core = meta[1]
    rows, width = keep.shape[1:]
    mine = up[pl.ds(pl.multiple_of(core * width, width), width), :]
    theirs = up[pl.ds(pl.multiple_of((1 - core) * width, width), width), :]
    keep[0] = dot(d_pre_own[...], mine, 1, 1).astype(BF16)
    keep[1] = dot(d_pre_other[...], mine, 1, 1).astype(BF16)
    send[0] = dot(d_pre_own[...], theirs, 1, 1).astype(BF16)
    sent = dot(d_pre_other[...], theirs, 1, 1).astype(BF16)
    send[1, rows // 2 :, :] = sent[: rows // 2]
    send[1, : rows // 2, :] = sent[rows // 2 :]


def over_kernel(meta, keep, came, over):
    half = over.shape[0] // 2
    for i in range(2):
        at = lax.rem(i + meta[1], 2) * half
        rows = slice(i * half, (i + 1) * half)
        value = keep[1, rows, :].astype(F32) + came[1, rows, :].astype(F32)
        over[pl.ds(pl.multiple_of(at, half), half), :] = value.astype(BF16)


def own_columns(meta, ref, width):
    return ref[:, pl.ds(pl.multiple_of(meta[1] * width, width), width)]


def scale_kernel(meta, keep, came, back, frames, gain, stats, scaled, sums):
    width = scaled.shape[1]
    d_norm = keep[0].astype(F32) + came[0].astype(F32) + back[...].astype(F32)
    value = d_norm * own_columns(meta, gain, width)
    scaled[...] = value
    rows = own_columns(meta, frames, width).astype(F32)
    centred = (rows - stats[:, 0:1]) * stats[:, 1:2]
    sums[:, 0:1] = jnp.sum(value, axis=-1, keepdims=True)
    sums[:, 1:2] = jnp.sum(value * centred, axis=-1, keepdims=True)


def input_kernel(meta, scaled, sums, came, frames, grads, stats, out):
    width = scaled.shape[1]
    means = (sums[...] + came[...]) * (0.5 / width)
    rows = own_columns(meta, frames, width).astype(F32)
    inv_std = stats[:, 1:2]
    centred = (rows - stats[:, 0:1]) * inv_std
    value = inv_std * (scaled[...] - means[:, 0:1] - centred * means[:, 1:2])
    out[...] = (own_columns(meta, grads, width).astype(F32) + value).astype(BF16)


def hop_kernel(places, index, partial, *refs):
    outs = refs[len(refs) - len(places) :]
    came = iter(refs)
    depth = outs[0].shape[0]
    for (at, summed), out in zip(places, outs):
        value = partial[pl.ds(pl.multiple_of(index[at] * depth, depth), depth), :].astype(F32)
        if summed:
            value = value + next(came)[...].astype(F32)
        out[...] = value.astype(BF16)


def total_kernel(index, partial, up, down, total):
    depth = total.shape[0]
    rows = pl.ds(pl.multiple_of(index[0] * depth, depth), depth)
    value = partial[rows, :].astype(F32) + up[...].astype(F32) + down[...].astype(F32)
    total[...] = value.astype(total.dtype)


def join_kernel(meta, own, passed, out):
    width = own.shape[1]
    side = meta[2]
    out[:, pl.ds(pl.multiple_of(side * width, width), width)] = own[...]
    other = pl.ds(pl.multiple_of((1 - side) * width, width), width)
    out[:, other] = passed[...].astype(F32)


def ring_member(place, count):
    place = place % count
    return jnp.where(place < count // 2, 2 * place, 2 * (count - 1 - place) + 1)


def shards(frames, out_grad, ln_gain, w_up, w_down, lengths):
    peers = lax.axis_size("gx")
    half = peers // 2
    own = lax.axis_index("gx")
    side = lax.axis_index("groups")
    core = lax.axis_index("gy")
    frame_len, width = frames.shape[1:]
    depth, hidden = w_up.shape
    quarter = hidden // 2
    half_width = width // 2
    half_rows = frame_len // 2
    ringed = peers <= 16 and peers % 2 == 0 and depth % 16 == 0

    order = list(range(0, peers, 2)) + list(range(peers - 1, 0, -2))
    ahead = [(order[i], order[(i + 1) % peers]) for i in range(peers)]
    behind = [(b, a) for a, b in ahead]
    place = jnp.where(own % 2 == 0, own // 2, peers - 1 - own // 2)
    swap = [(0, 1), (1, 0)]
    after = lax.optimization_barrier

    mine = [lax.dynamic_slice_in_dim(w, side * quarter, quarter, 1) for w in (w_up, w_down)]
    mine, frames, out_grad, ln_gain, lengths = after((mine, frames, out_grad, ln_gain, lengths))
    meta = jnp.stack([own, core, side]).astype(jnp.int32)
    frames, out_grad = frames[0], out_grad[0]

    rows_of = shape((frame_len, width), BF16)
    operands = (meta, lengths, frames, out_grad, ln_gain)
    passing = call(
        pass_kernel,
        operands,
        shape((2, half_rows, width), BF16),
        [pltpu.SemaphoreType.DMA((2,))] + [pltpu.VMEM((half_rows, width), BF16)] * 2,
        flops=5 * frame_len * width,
        vmem=60,
        left=(2, 3),
    )
    first = lax.ppermute(passing, "groups", swap)
    normed, grads, stats = call(
        norm_kernel,
        operands,
        (rows_of, rows_of, shape((frame_len, 2), F32)),
        flops=10 * frame_len * width,
    )

    weight = shape((width, quarter), BF16)
    block_of = shape((depth, quarter), BF16)
    if ringed:
        blocks = {0: list(mine)}
        up, down = list(mine), list(mine)
        for step in range(1, half):
            up = [lax.ppermute(block, "gx", ahead) for block in up]
            down = [lax.ppermute(block, "gx", behind) for block in down]
            if step == 1:
                down[0] = hold(down[0], normed)
            blocks[-step], blocks[step] = up, down
        first, up, down = after((first, up, down))
        steps = list(blocks) + [half]
        index = jnp.stack([ring_member(place + step + peers, peers) for step in steps])
        index = index.astype(jnp.int32)
        blocks = [block for step in blocks for block in blocks[step]]
        near = call(
            place_kernel,
            (index, *blocks),
            (weight, weight),
            [pltpu.SemaphoreType.DMA((len(blocks),))],
            left=range(1, len(blocks) + 1),
        )
        far = [lax.ppermute(up[0], "gx", ahead), lax.ppermute(down[1], "gx", behind)]
    else:
        near = [lax.all_gather(block, "gx", axis=0, tiled=True) for block in mine]
        index, far = jnp.zeros((1,), jnp.int32), []
    second = lax.ppermute(first, "gy", swap)

    d_pre_of, partial_of = shape((frame_len, quarter), BF16), shape((width, quarter), BF16)
    d_pre_other, partial_other, full_up, full_down = call(
        other_kernel,
        (index, first, second, *near, *far),
        (d_pre_of, partial_of, weight, weight),
        [pltpu.VMEM((frame_len, width), BF16)] * 2,
        flops=6 * frame_len * width * quarter,
    )
    d_pre_own, partial_own = call(
        own_kernel,
        (normed, grads, full_up, full_down),
        (d_pre_of, partial_of),
        flops=6 * frame_len * width * quarter,
    )
    partial = [partial_own, partial_other]

    half_rows_of = shape((frame_len, half_width), BF16)

    def own_d_norm(*ties):
        return call(
            d_norm_kernel,
            (meta, d_pre_own, d_pre_other, full_up),
            (shape((2, frame_len, half_width), BF16), shape((2, frame_len, half_width), BF16)),
            flops=4 * frame_len * width * quarter,
            ties=ties,
        )

    def over_cores(keep, came, *ties):
        return call(over_kernel, (meta, keep, came), half_rows_of, ties=ties)

    def scale(keep, came, back, *ties):
        return call(
            scale_kernel,
            (meta, keep, came, back, frames, ln_gain[None], stats),
            (shape((frame_len, half_width), F32), shape((frame_len, 2), F32)),
            ties=ties,
        )

    def input_gradient(scaled, sums, *ties):
        return call(
            input_kernel,
            (meta, scaled, sums, lax.ppermute(sums, "gy", swap), frames, grads, stats),
            half_rows_of,
            ties=ties,
        )

    up_grad_of = shape((depth, hidden), F32)
    if ringed:
        place_of = {step: i for i, step in enumerate(steps)}
        place_of[-half] = place_of[half]
        came = [{}, {}]

        def hop(i, turn, *ties):
            ways = [("up", half - turn - i), ("down", turn + 1 - i - half)]
            ways = [way for way in ways if way[1] != 0]
            kept = [came[i][name] for name, _ in ways if name in came[i]]
            ended = [came[i][name] for name in came[i] if name not in dict(ways)]
            places = [(place_of[step], name in came[i]) for name, step in ways]
            blocks = call(
                functools.partial(hop_kernel, tuple(places)),
                (index, partial[i], *kept),
                [block_of] * len(places),
                ties=(*ended, *ties),
            )
            for block, (name, _) in zip(blocks, ways):
                came[i][name] = lax.ppermute(block, "gx", ahead if name == "up" else behind)
            return blocks[0]

        hop(1, 0)
        tie = hop(0, 0)
        tie = hop(1, 1, tie)
        keep, send = own_d_norm(tie)
        tie = hop(0, 1, send)
        send = hold(send, tie, *came[1].values())
        sent = lax.ppermute(send, "gy", swap)
        tie = hop(1, 2, tie)
        tie = hop(0, 2, tie)
        over = over_cores(keep, sent, tie)
        back = lax.ppermute(over, "groups", swap)
        tie = over
        for turn in range(3, half):
            tie = hop(0, turn, hop(1, turn, tie))
        passing = call(
            total_kernel,
            (index, partial[1], came[1]["up"], came[1]["down"]),
            block_of,
            ties=(tie,),
        )
        passed = lax.ppermute(passing, "groups", swap)
        scaled, sums = scale(keep, sent, back, passing)
        input_grad = input_gradient(scaled, sums)
        total = call(
            total_kernel,
            (index, partial[0], came[0]["up"], came[0]["down"]),
            shape((depth, quarter), F32),
            ties=(input_grad,),
        )
        up_grad = call(join_kernel, (meta, total, passed), up_grad_of)
    else:
        keep, send = own_d_norm()
        sent = lax.ppermute(send, "gy", swap)
        back = lax.ppermute(over_cores(keep, sent), "groups", swap)
        input_grad = input_gradient(*scale(keep, sent, back))
        total, passing = [
            lax.psum_scatter(p.astype(F32), "gx", scatter_dimension=0, tiled=True) for p in partial
        ]
        passed = lax.ppermute(passing.astype(BF16), "groups", swap)
        up_grad = call(join_kernel, (meta, total, passed), up_grad_of)
    return (input_grad[None], up_grad)


def solution(mesh):
    placed = (
        P(("groups", "gx"), None, None),
        P(("groups", "gx"), None, None),
        P(),
        P("gx", "gy"),
        P("gx", "gy"),
        P("groups"),
    )
    return jax.shard_map(
        shards,
        mesh=mesh,
        in_specs=placed,
        out_specs=(P(("groups", "gx"), None, "gy"), P(("groups", "gx"), "gy")),
        check_vma=False,
    )
```

```python
import functools

import jax
import jax.numpy as jnp
from jax import lax
from jax.experimental import pallas as pl
from jax.experimental.pallas import tpu as pltpu
from jax.sharding import PartitionSpec as P

BF16, F32 = jnp.bfloat16, jnp.float32
VMEM = pl.BlockSpec(memory_space=pltpu.VMEM)
HBM = pl.BlockSpec(memory_space=pltpu.HBM)
ANY = pl.BlockSpec(memory_space=pl.ANY)
SMEM = pl.BlockSpec(memory_space=pltpu.SMEM)


def shape(dims, kind):
    return jax.ShapeDtypeStruct(dims, kind)


def call(kernel, ins, out_shape, scratch=(), vmem=16, flops=1, left=(), pinned=(), out=VMEM, ties=()):
    count = len(ins)

    def body(*refs):
        kernel(*refs[:count], *refs[count + len(ties) :])

    moved = sum(x.size * x.dtype.itemsize for x in list(ins) + jax.tree.leaves(out_shape))
    return pl.pallas_call(
        body if ties else kernel,
        out_shape=out_shape,
        in_specs=[
            SMEM if x.dtype == jnp.int32 else ANY if i in left else HBM if i in pinned else VMEM
            for i, x in enumerate(ins)
        ]
        + [ANY] * len(ties),
        out_specs=jax.tree.map(lambda _: out, out_shape),
        scratch_shapes=list(scratch),
        compiler_params=pltpu.CompilerParams(vmem_limit_bytes=vmem << 20),
        cost_estimate=pl.CostEstimate(flops=flops, bytes_accessed=moved, transcendentals=0),
    )(*ins, *ties)


def hold(array, *ties):
    return pl.pallas_call(
        lambda *refs: None,
        out_shape=shape(array.shape, array.dtype),
        in_specs=[ANY] * (1 + len(ties)),
        out_specs=ANY,
        input_output_aliases={0: 0},
        compiler_params=pltpu.CompilerParams(vmem_limit_bytes=1 << 20),
        cost_estimate=pl.CostEstimate(flops=1, bytes_accessed=1, transcendentals=0),
    )(array, *ties)


def dot(left, right, left_dim=1, right_dim=0):
    return lax.dot_general(
        left, right, (((left_dim,), (right_dim,)), ((), ())), preferred_element_type=F32
    )


def gelu_slope(values):
    return (
        0.5 * (1.0 + lax.erf(values * 0.7071067811865476))
        + values * jnp.exp(-0.5 * values * values) * 0.3989422804014327
    )


def norm_rows(rows, gain):
    values = rows.astype(F32)
    centre = jnp.mean(values, axis=-1, keepdims=True)
    shifted = values - centre
    variance = jnp.mean(shifted * shifted, axis=-1, keepdims=True)
    inv_std = lax.rsqrt(variance + 1e-05)
    return (shifted * inv_std * gain[...][None]).astype(BF16), centre, inv_std


def mask_rows(rows, start, length):
    index = start + lax.broadcasted_iota(jnp.int32, (rows.shape[0], 1), 0)
    return jnp.where(index < length, rows.astype(F32), 0.0).astype(BF16)


def pass_kernel(lengths, frames, out_grad, gain, passing, sems, rows, grads):
    half = rows.shape[0]
    start = pl.multiple_of(lax.axis_index("gy") * half, half)
    copies = [
        pltpu.make_async_copy(source.at[pl.ds(start, half)], target, sems.at[i])
        for i, (source, target) in enumerate(((frames, rows), (out_grad, grads)))
    ]
    for copy in copies:
        copy.start()
    copies[0].wait()
    passing[0] = norm_rows(rows[...], gain)[0]
    copies[1].wait()
    passing[1] = mask_rows(grads[...], start, lengths[lax.axis_index("gx")])


def norm_kernel(meta, lengths, frames, out_grad, gain, normed, grads, stats):
    value, centre, inv_std = norm_rows(frames[...], gain)
    normed[...] = value
    stats[:, 0:1] = centre
    stats[:, 1:2] = inv_std
    grads[...] = mask_rows(out_grad[...], 0, lengths[meta[0]])


def back_through(normed, grads, up, down, d_pre, partial):
    pre_act = dot(normed[...], up[...])
    d_act = dot(grads[...], down[...])
    d_pre[...] = (d_act * gelu_slope(pre_act)).astype(BF16)
    partial[...] = dot(normed[...], d_pre[...], 0, 0).astype(BF16)


def place_kernel(index, *refs):
    blocks, (up, down, sems) = refs[:-3], refs[-3:]
    depth = blocks[0].shape[0]
    copies = []
    for i, block in enumerate(blocks):
        rows = pl.ds(pl.multiple_of(index[i // 2] * depth, depth), depth)
        target = (up, down)[i % 2].at[rows]
        copies.append(pltpu.make_async_copy(block, target, sems.at[i]))
    for copy in copies:
        copy.start()
    for copy in copies:
        copy.wait()


def other_kernel(index, first, second, near_up, near_down, *refs):
    d_pre, partial, up, down, normed, grads = refs[-6:]
    half = first.shape[1]
    for at, part in ((0, first), (half, second)):
        normed[at : at + half, :] = part[0]
        grads[at : at + half, :] = part[1]
    up[...] = near_up[...]
    down[...] = near_down[...]
    for ref, far in zip((up, down), refs[:-6]):
        depth = far.shape[0]
        rows = pl.ds(pl.multiple_of(index[index.shape[0] - 1] * depth, depth), depth)
        ref[rows, :] = far[...]
    back_through(normed, grads, up, down, d_pre, partial)


def own_kernel(normed, grads, up, down, d_pre, partial):
    back_through(normed, grads, up, down, d_pre, partial)


def d_norm_kernel(meta, d_pre_own, d_pre_other, up, keep, send):
    core = meta[1]
    rows, width = keep.shape[1:]
    mine = up[pl.ds(pl.multiple_of(core * width, width), width), :]
    theirs = up[pl.ds(pl.multiple_of((1 - core) * width, width), width), :]
    keep[0] = dot(d_pre_own[...], mine, 1, 1).astype(BF16)
    keep[1] = dot(d_pre_other[...], mine, 1, 1).astype(BF16)
    send[0] = dot(d_pre_own[...], theirs, 1, 1).astype(BF16)
    sent = dot(d_pre_other[...], theirs, 1, 1).astype(BF16)
    send[1, rows // 2 :, :] = sent[: rows // 2]
    send[1, : rows // 2, :] = sent[rows // 2 :]


def over_kernel(meta, keep, came, over):
    half = over.shape[0] // 2
    for i in range(2):
        at = lax.rem(i + meta[1], 2) * half
        rows = slice(i * half, (i + 1) * half)
        value = keep[1, rows, :].astype(F32) + came[1, rows, :].astype(F32)
        over[pl.ds(pl.multiple_of(at, half), half), :] = value.astype(BF16)


def own_columns(meta, ref, width):
    return ref[:, pl.ds(pl.multiple_of(meta[1] * width, width), width)]


def scale_kernel(meta, keep, came, back, frames, gain, grads, stats, base, factor, sums):
    width = base.shape[1]
    d_norm = keep[0].astype(F32) + came[0].astype(F32) + back[...].astype(F32)
    scaled = d_norm * own_columns(meta, gain, width)
    rows = own_columns(meta, frames, width).astype(F32)
    inv_std = stats[:, 1:2]
    centred = (rows - stats[:, 0:1]) * inv_std
    sums[:, 0:1] = jnp.sum(scaled, axis=-1, keepdims=True)
    sums[:, 1:2] = jnp.sum(scaled * centred, axis=-1, keepdims=True)
    base[...] = own_columns(meta, grads, width).astype(F32) + inv_std * scaled
    factor[...] = inv_std * centred


def input_kernel(base, factor, sums, came, stats, out, block, sem):
    means = (sums[...] + came[...]) * (0.5 / base.shape[1])
    value = base[...] - stats[:, 1:2] * means[:, 0:1] - factor[...] * means[:, 1:2]
    block[...] = value.astype(BF16)
    copy = pltpu.make_async_copy(block, out, sem)
    copy.start()
    copy.wait()


def hop_kernel(places, index, partial, *refs):
    outs = refs[len(refs) - len(places) :]
    came = iter(refs)
    depth = outs[0].shape[0]
    for (at, summed), out in zip(places, outs):
        value = partial[pl.ds(pl.multiple_of(index[at] * depth, depth), depth), :].astype(F32)
        if summed:
            value = value + next(came)[...].astype(F32)
        out[...] = value.astype(BF16)


def total_kernel(index, partial, up, down, total):
    depth = total.shape[0]
    rows = pl.ds(pl.multiple_of(index[0] * depth, depth), depth)
    value = partial[rows, :].astype(F32) + up[...].astype(F32) + down[...].astype(F32)
    total[...] = value.astype(total.dtype)


def join_kernel(meta, index, partial, up, down, passed, out):
    depth, width = passed.shape
    side = meta[2]
    rows = pl.ds(pl.multiple_of(index[0] * depth, depth), depth)
    value = partial[rows, :].astype(F32) + up[...].astype(F32) + down[...].astype(F32)
    out[:, pl.ds(pl.multiple_of(side * width, width), width)] = value
    other = pl.ds(pl.multiple_of((1 - side) * width, width), width)
    out[:, other] = passed[...].astype(F32)


def place_halves_kernel(meta, own, passed, out):
    width = own.shape[1]
    side = meta[2]
    out[:, pl.ds(pl.multiple_of(side * width, width), width)] = own[...]
    other = pl.ds(pl.multiple_of((1 - side) * width, width), width)
    out[:, other] = passed[...].astype(F32)


def ring_member(place, count):
    place = place % count
    return jnp.where(place < count // 2, 2 * place, 2 * (count - 1 - place) + 1)


def shards(frames, out_grad, ln_gain, w_up, w_down, lengths):
    peers = lax.axis_size("gx")
    half = peers // 2
    own = lax.axis_index("gx")
    side = lax.axis_index("groups")
    core = lax.axis_index("gy")
    frame_len, width = frames.shape[1:]
    depth, hidden = w_up.shape
    quarter = hidden // 2
    half_width = width // 2
    half_rows = frame_len // 2
    ringed = peers <= 16 and peers % 2 == 0 and depth % 16 == 0

    order = list(range(0, peers, 2)) + list(range(peers - 1, 0, -2))
    ahead = [(order[i], order[(i + 1) % peers]) for i in range(peers)]
    behind = [(b, a) for a, b in ahead]
    place = jnp.where(own % 2 == 0, own // 2, peers - 1 - own // 2)
    swap = [(0, 1), (1, 0)]
    after = lax.optimization_barrier

    mine = [lax.dynamic_slice_in_dim(w, side * quarter, quarter, 1) for w in (w_up, w_down)]
    mine, frames, out_grad, ln_gain, lengths = after((mine, frames, out_grad, ln_gain, lengths))
    meta = jnp.stack([own, core, side]).astype(jnp.int32)
    frames, out_grad = frames[0], out_grad[0]

    rows_of = shape((frame_len, width), BF16)
    operands = (lengths, frames, out_grad, ln_gain)
    passing = call(
        pass_kernel,
        operands,
        shape((2, half_rows, width), BF16),
        [pltpu.SemaphoreType.DMA((2,))] + [pltpu.VMEM((half_rows, width), BF16)] * 2,
        flops=5 * frame_len * width,
        vmem=60,
        left=(1, 2),
    )
    first = lax.ppermute(passing, "groups", swap)
    normed, grads, stats = call(
        norm_kernel,
        (meta, *operands),
        (rows_of, rows_of, shape((frame_len, 2), F32)),
        flops=10 * frame_len * width,
    )

    weight = shape((width, quarter), BF16)
    block_of = shape((depth, quarter), BF16)
    if ringed:
        blocks = {0: list(mine)}
        up, down = list(mine), list(mine)
        for step in range(1, half):
            up = [lax.ppermute(block, "gx", ahead) for block in up]
            down = [lax.ppermute(block, "gx", behind) for block in down]
            if step == 1:
                down[0] = hold(down[0], normed)
            blocks[-step], blocks[step] = up, down
        first, up, down = after((first, up, down))
        steps = list(blocks) + [half]
        index = jnp.stack([ring_member(place + step + peers, peers) for step in steps])
        index = index.astype(jnp.int32)
        blocks = [block for step in blocks for block in blocks[step]]
        near = call(
            place_kernel,
            (index, *blocks),
            (weight, weight),
            [pltpu.SemaphoreType.DMA((len(blocks),))],
            pinned=range(1, len(blocks) + 1),
        )
        far = [lax.ppermute(up[0], "gx", ahead), lax.ppermute(down[1], "gx", behind)]
    else:
        near = [lax.all_gather(block, "gx", axis=0, tiled=True) for block in mine]
        index, far = jnp.zeros((1,), jnp.int32), []
    second = lax.ppermute(first, "gy", swap)

    d_pre_of, partial_of = shape((frame_len, quarter), BF16), shape((width, quarter), BF16)
    d_pre_other, partial_other, full_up, full_down = call(
        other_kernel,
        (index, first, second, *near, *far),
        (d_pre_of, partial_of, weight, weight),
        [pltpu.VMEM((frame_len, width), BF16)] * 2,
        flops=6 * frame_len * width * quarter,
    )
    d_pre_own, partial_own = call(
        own_kernel,
        (normed, grads, full_up, full_down),
        (d_pre_of, partial_of),
        flops=6 * frame_len * width * quarter,
    )
    partial = [partial_own, partial_other]

    half_rows_of = shape((frame_len, half_width), BF16)

    def own_d_norm(*ties):
        return call(
            d_norm_kernel,
            (meta, d_pre_own, d_pre_other, full_up),
            (shape((2, frame_len, half_width), BF16), shape((2, frame_len, half_width), BF16)),
            flops=4 * frame_len * width * quarter,
            ties=ties,
        )

    def over_cores(keep, came, *ties):
        return call(over_kernel, (meta, keep, came), half_rows_of, ties=ties)

    def scale(keep, came, back, *ties):
        return call(
            scale_kernel,
            (meta, keep, came, back, frames, ln_gain[None], grads, stats),
            (
                shape((frame_len, half_width), F32),
                shape((frame_len, half_width), F32),
                shape((frame_len, 2), F32),
            ),
            ties=ties,
        )

    def input_gradient(base, factor, sums):
        return call(
            input_kernel,
            (base, factor, sums, lax.ppermute(sums, "gy", swap), stats),
            half_rows_of,
            [pltpu.VMEM((frame_len, half_width), BF16), pltpu.SemaphoreType.DMA],
            out=HBM,
        )

    up_grad_of = shape((depth, hidden), F32)
    if ringed:
        place_of = {step: i for i, step in enumerate(steps)}
        place_of[-half] = place_of[half]
        came = [{}, {}]

        def hop(i, turn, *ties):
            ways = [("up", half - turn - i), ("down", turn + 1 - i - half)]
            ways = [way for way in ways if way[1] != 0]
            kept = [came[i][name] for name, _ in ways if name in came[i]]
            ended = [came[i][name] for name in came[i] if name not in dict(ways)]
            places = [(place_of[step], name in came[i]) for name, step in ways]
            blocks = call(
                functools.partial(hop_kernel, tuple(places)),
                (index, partial[i], *kept),
                [block_of] * len(places),
                ties=(*ended, *ties),
            )
            for block, (name, _) in zip(blocks, ways):
                came[i][name] = lax.ppermute(block, "gx", ahead if name == "up" else behind)
            return blocks[0]

        hop(1, 0)
        tie = hop(0, 0)
        tie = hop(1, 1, tie)
        keep, send = own_d_norm(tie)
        tie = hop(0, 1, send)
        send = hold(send, tie, *came[1].values())
        sent = lax.ppermute(send, "gy", swap)
        tie = hop(1, 2, tie)
        tie = hop(0, 2, tie)
        over = over_cores(keep, sent, tie)
        back = lax.ppermute(over, "groups", swap)
        tie = over
        for turn in range(3, half):
            tie = hop(0, turn, hop(1, turn, tie))
        passing = call(
            total_kernel,
            (index, partial[1], came[1]["up"], came[1]["down"]),
            block_of,
            ties=(tie,),
        )
        passed = lax.ppermute(passing, "groups", swap)
        input_grad = input_gradient(*scale(keep, sent, back, passing))
        up_grad = call(
            join_kernel,
            (meta, index, partial[0], came[0]["up"], came[0]["down"], passed),
            up_grad_of,
            ties=(input_grad,),
        )
    else:
        keep, send = own_d_norm()
        sent = lax.ppermute(send, "gy", swap)
        back = lax.ppermute(over_cores(keep, sent), "groups", swap)
        input_grad = input_gradient(*scale(keep, sent, back))
        total, passing = [
            lax.psum_scatter(p.astype(F32), "gx", scatter_dimension=0, tiled=True) for p in partial
        ]
        passed = lax.ppermute(passing.astype(BF16), "groups", swap)
        up_grad = call(place_halves_kernel, (meta, total, passed), up_grad_of)
    return (input_grad[None], up_grad)


def solution(mesh):
    placed = (
        P(("groups", "gx"), None, None),
        P(("groups", "gx"), None, None),
        P(),
        P("gx", "gy"),
        P("gx", "gy"),
        P("groups"),
    )
    return jax.shard_map(
        shards,
        mesh=mesh,
        in_specs=placed,
        out_specs=(P(("groups", "gx"), None, "gy"), P(("groups", "gx"), "gy")),
        check_vma=False,
    )
```

```python
import functools

import jax
import jax.numpy as jnp
from jax import lax
from jax.experimental import pallas as pl
from jax.experimental.pallas import tpu as pltpu
from jax.sharding import PartitionSpec as P

BF16, F32 = jnp.bfloat16, jnp.float32
VMEM = pl.BlockSpec(memory_space=pltpu.VMEM)
HBM = pl.BlockSpec(memory_space=pltpu.HBM)
ANY = pl.BlockSpec(memory_space=pl.ANY)
SMEM = pl.BlockSpec(memory_space=pltpu.SMEM)


def shape(dims, kind):
    return jax.ShapeDtypeStruct(dims, kind)


def call(kernel, ins, out_shape, scratch=(), vmem=16, flops=1, left=(), pinned=(), out=VMEM, ties=()):
    count = len(ins)

    def body(*refs):
        kernel(*refs[:count], *refs[count + len(ties) :])

    moved = sum(x.size * x.dtype.itemsize for x in list(ins) + jax.tree.leaves(out_shape))
    return pl.pallas_call(
        body if ties else kernel,
        out_shape=out_shape,
        in_specs=[
            SMEM if x.dtype == jnp.int32 else ANY if i in left else HBM if i in pinned else VMEM
            for i, x in enumerate(ins)
        ]
        + [ANY] * len(ties),
        out_specs=jax.tree.map(lambda _: out, out_shape),
        scratch_shapes=list(scratch),
        compiler_params=pltpu.CompilerParams(vmem_limit_bytes=vmem << 20),
        cost_estimate=pl.CostEstimate(flops=flops, bytes_accessed=moved, transcendentals=0),
    )(*ins, *ties)


def hold(array, *ties):
    return pl.pallas_call(
        lambda *refs: None,
        out_shape=shape(array.shape, array.dtype),
        in_specs=[ANY] * (1 + len(ties)),
        out_specs=ANY,
        input_output_aliases={0: 0},
        compiler_params=pltpu.CompilerParams(vmem_limit_bytes=1 << 20),
        cost_estimate=pl.CostEstimate(flops=1, bytes_accessed=1, transcendentals=0),
    )(array, *ties)


def dot(left, right, left_dim=1, right_dim=0):
    return lax.dot_general(
        left, right, (((left_dim,), (right_dim,)), ((), ())), preferred_element_type=F32
    )


def gelu_slope(values):
    return (
        0.5 * (1.0 + lax.erf(values * 0.7071067811865476))
        + values * jnp.exp(-0.5 * values * values) * 0.3989422804014327
    )


def block_rows(step, peers, depth):
    own = lax.axis_index("gx")
    place = jnp.where(lax.rem(own, 2) == 0, lax.div(own, 2), peers - 1 - lax.div(own, 2))
    place = lax.rem(place + (step + peers), peers)
    member = jnp.where(place < peers // 2, 2 * place, 2 * (peers - 1 - place) + 1)
    return pl.ds(pl.multiple_of(member * depth, depth), depth)


def norm_rows(rows, gain):
    values = rows.astype(F32)
    centre = jnp.mean(values, axis=-1, keepdims=True)
    shifted = values - centre
    variance = jnp.mean(shifted * shifted, axis=-1, keepdims=True)
    inv_std = lax.rsqrt(variance + 1e-05)
    return (shifted * inv_std * gain[...][None]).astype(BF16), centre, inv_std


def mask_rows(rows, start, length):
    index = start + lax.broadcasted_iota(jnp.int32, (rows.shape[0], 1), 0)
    return jnp.where(index < length, rows.astype(F32), 0.0).astype(BF16)


def first_kernel(
    lengths, frames, out_grad, gain, w_up, w_down, passing, mine_up, mine_down, sems, rows, grads
):
    half, quarter = rows.shape[0], mine_up.shape[1]
    start = pl.multiple_of(lax.axis_index("gy") * half, half)
    columns = pl.ds(pl.multiple_of(lax.axis_index("groups") * quarter, quarter), quarter)
    moves = (
        (frames.at[pl.ds(start, half)], rows),
        (out_grad.at[pl.ds(start, half)], grads),
        (w_up.at[:, columns], mine_up),
        (w_down.at[:, columns], mine_down),
    )
    copies = [pltpu.make_async_copy(*move, sems.at[i]) for i, move in enumerate(moves)]
    for copy in copies:
        copy.start()
    copies[0].wait()
    passing[0] = norm_rows(rows[...], gain)[0]
    copies[1].wait()
    passing[1] = mask_rows(grads[...], start, lengths[lax.axis_index("gx")])
    copies[2].wait()
    copies[3].wait()


def norm_kernel(lengths, frames, out_grad, gain, normed, grads, stats):
    value, centre, inv_std = norm_rows(frames[...], gain)
    normed[...] = value
    stats[:, 0:1] = centre
    stats[:, 1:2] = inv_std
    grads[...] = mask_rows(out_grad[...], 0, lengths[lax.axis_index("gx")])


def back_through(normed, grads, up, down, d_pre, partial):
    pre_act = dot(normed[...], up[...])
    d_act = dot(grads[...], down[...])
    d_pre[...] = (d_act * gelu_slope(pre_act)).astype(BF16)
    partial[...] = dot(normed[...], d_pre[...], 0, 0).astype(BF16)


def place_kernel(places, peers, *refs):
    blocks, (up, down, sems) = refs[:-3], refs[-3:]
    copies = []
    for i, ((step, which), block) in enumerate(zip(places, blocks)):
        rows = block_rows(step, peers, block.shape[0])
        copies.append(pltpu.make_async_copy(block, (up, down)[which].at[rows], sems.at[i]))
    for copy in copies:
        copy.start()
    for copy in copies:
        copy.wait()


def other_kernel(places, sends, peers, first, second, near_up, near_down, *refs):
    late, refs = refs[: len(places)], refs[len(places) :]
    (d_pre, partial, up, down), blocks, (normed, grads) = refs[:4], refs[4:-2], refs[-2:]
    half = first.shape[1]
    for at, part in ((0, first), (half, second)):
        normed[at : at + half, :] = part[0]
        grads[at : at + half, :] = part[1]
    up[...] = near_up[...]
    down[...] = near_down[...]
    for (step, which), block in zip(places, late):
        (up, down)[which][block_rows(step, peers, block.shape[0]), :] = block[...]
    back_through(normed, grads, up, down, d_pre, partial)
    for step, block in zip(sends, blocks):
        block[...] = partial[block_rows(step, peers, block.shape[0]), :]


def own_kernel(sends, peers, normed, grads, up, down, d_pre, partial, *blocks):
    back_through(normed, grads, up, down, d_pre, partial)
    for step, block in zip(sends, blocks):
        block[...] = partial[block_rows(step, peers, block.shape[0]), :]


def d_norm_kernel(d_pre_own, d_pre_other, up, keep, send):
    core = lax.axis_index("gy")
    rows, width = keep.shape[1:]
    mine = up[pl.ds(pl.multiple_of(core * width, width), width), :]
    theirs = up[pl.ds(pl.multiple_of((1 - core) * width, width), width), :]
    keep[0] = dot(d_pre_own[...], mine, 1, 1).astype(BF16)
    keep[1] = dot(d_pre_other[...], mine, 1, 1).astype(BF16)
    send[0] = dot(d_pre_own[...], theirs, 1, 1).astype(BF16)
    sent = dot(d_pre_other[...], theirs, 1, 1).astype(BF16)
    send[1, rows // 2 :, :] = sent[: rows // 2]
    send[1, : rows // 2, :] = sent[rows // 2 :]


def over_kernel(keep, came, over):
    half = over.shape[0] // 2
    for i in range(2):
        at = lax.rem(i + lax.axis_index("gy"), 2) * half
        rows = slice(i * half, (i + 1) * half)
        value = keep[1, rows, :].astype(F32) + came[1, rows, :].astype(F32)
        over[pl.ds(pl.multiple_of(at, half), half), :] = value.astype(BF16)


def own_columns(ref, width):
    return ref[:, pl.ds(pl.multiple_of(lax.axis_index("gy") * width, width), width)]


def scale_kernel(keep, came, back, frames, gain, grads, stats, base, factor, sums):
    width = base.shape[1]
    d_norm = keep[0].astype(F32) + came[0].astype(F32) + back[...].astype(F32)
    scaled = d_norm * own_columns(gain, width)
    rows = own_columns(frames, width).astype(F32)
    inv_std = stats[:, 1:2]
    centred = (rows - stats[:, 0:1]) * inv_std
    sums[:, 0:1] = jnp.sum(scaled, axis=-1, keepdims=True)
    sums[:, 1:2] = jnp.sum(scaled * centred, axis=-1, keepdims=True)
    base[...] = own_columns(grads, width).astype(F32) + inv_std * scaled
    factor[...] = inv_std * centred


def input_kernel(base, factor, sums, came, stats, out, token):
    means = (sums[...] + came[...]) * (0.5 / base.shape[1])
    value = base[...] - stats[:, 1:2] * means[:, 0:1] - factor[...] * means[:, 1:2]
    out[...] = value.astype(BF16)
    token[...] = jnp.zeros_like(token)


def hop_kernel(places, peers, partial, *refs):
    count = len(places)
    for step, came, out in zip(places, refs[:count], refs[count:]):
        value = partial[block_rows(step, peers, out.shape[0]), :].astype(F32)
        out[...] = (value + came[...].astype(F32)).astype(BF16)


def total_kernel(peers, partial, up, down, total):
    value = partial[block_rows(0, peers, total.shape[0]), :].astype(F32)
    total[...] = (value + up[...].astype(F32) + down[...].astype(F32)).astype(BF16)


def join_kernel(peers, partial, up, down, passed, out):
    depth, width = passed.shape
    side = lax.axis_index("groups")
    value = partial[block_rows(0, peers, depth), :].astype(F32)
    value = value + up[...].astype(F32) + down[...].astype(F32)
    out[:, pl.ds(pl.multiple_of(side * width, width), width)] = value
    other = pl.ds(pl.multiple_of((1 - side) * width, width), width)
    out[:, other] = passed[...].astype(F32)


def place_halves_kernel(own, passed, out):
    width = own.shape[1]
    side = lax.axis_index("groups")
    out[:, pl.ds(pl.multiple_of(side * width, width), width)] = own[...]
    other = pl.ds(pl.multiple_of((1 - side) * width, width), width)
    out[:, other] = passed[...].astype(F32)


def shards(frames, out_grad, ln_gain, w_up, w_down, lengths):
    peers = lax.axis_size("gx")
    half = peers // 2
    frame_len, width = frames.shape[1:]
    depth, hidden = w_up.shape
    quarter = hidden // 2
    half_width = width // 2
    half_rows = frame_len // 2
    ringed = peers <= 16 and peers % 2 == 0 and depth % 16 == 0

    order = list(range(0, peers, 2)) + list(range(peers - 1, 0, -2))
    ahead = [(order[i], order[(i + 1) % peers]) for i in range(peers)]
    behind = [(b, a) for a, b in ahead]
    swap = [(0, 1), (1, 0)]

    frames, out_grad = frames[0], out_grad[0]
    rows_of = shape((frame_len, width), BF16)
    block_of = shape((depth, quarter), BF16)
    passing, *mine = call(
        first_kernel,
        (lengths, frames, out_grad, ln_gain, w_up, w_down),
        (shape((2, half_rows, width), BF16), block_of, block_of),
        [pltpu.SemaphoreType.DMA((4,))] + [pltpu.VMEM((half_rows, width), BF16)] * 2,
        flops=5 * frame_len * width,
        vmem=60,
        left=(1, 2, 4, 5),
    )
    first = lax.ppermute(passing, "groups", swap)
    normed, grads, stats = call(
        norm_kernel,
        (lengths, frames, out_grad, ln_gain),
        (rows_of, rows_of, shape((frame_len, 2), F32)),
        flops=10 * frame_len * width,
    )

    weight = shape((width, quarter), BF16)
    if ringed:
        blocks = {(0, 0): mine[0], (0, 1): mine[1]}
        up, down = list(mine), list(mine)
        for step in range(1, half):
            for i in range(2):
                up[i] = lax.ppermute(up[i], "gx", ahead)
                down[i] = lax.ppermute(down[i], "gx", behind)
            if step == 1:
                up[0] = hold(up[0], normed)
            for i in range(2):
                blocks[-step, i], blocks[step, i] = up[i], down[i]
        first = hold(first, *up, *down)
        late = {
            (half - 1, 0): blocks.pop((half - 1, 0)),
            (1 - half, 1): blocks.pop((1 - half, 1)),
            (half, 0): lax.ppermute(up[0], "gx", ahead),
            (half, 1): lax.ppermute(down[1], "gx", behind),
        }
        near = call(
            functools.partial(place_kernel, tuple(blocks), peers),
            list(blocks.values()),
            (weight, weight),
            [pltpu.SemaphoreType.DMA((len(blocks),))],
            pinned=range(len(blocks)),
        )
        sends = ((half - 1, -half), (half, 1 - half))
    else:
        near = [lax.all_gather(block, "gx", axis=0, tiled=True) for block in mine]
        late, sends = {}, ((), ())
    second = lax.ppermute(first, "gy", swap)

    d_pre_of, partial_of = shape((frame_len, quarter), BF16), shape((width, quarter), BF16)
    d_pre_other, partial_other, full_up, full_down, *blocks_other = call(
        functools.partial(other_kernel, tuple(late), sends[0], peers),
        (first, second, *near, *late.values()),
        (d_pre_of, partial_of, weight, weight, *[block_of] * len(sends[0])),
        [pltpu.VMEM((frame_len, width), BF16)] * 2,
        flops=6 * frame_len * width * quarter,
    )
    d_pre_own, partial_own, *blocks_own = call(
        functools.partial(own_kernel, sends[1], peers),
        (normed, grads, full_up, full_down),
        (d_pre_of, partial_of, *[block_of] * len(sends[1])),
        flops=6 * frame_len * width * quarter,
    )
    partial = [partial_own, partial_other]

    half_rows_of = shape((frame_len, half_width), BF16)

    def own_d_norm(*ties):
        return call(
            d_norm_kernel,
            (d_pre_own, d_pre_other, full_up),
            (shape((2, frame_len, half_width), BF16), shape((2, frame_len, half_width), BF16)),
            flops=4 * frame_len * width * quarter,
            ties=ties,
        )

    def over_cores(keep, came, *ties):
        return call(over_kernel, (keep, came), half_rows_of, ties=ties)

    def scale(keep, came, back, *ties):
        return call(
            scale_kernel,
            (keep, came, back, frames, ln_gain[None], grads, stats),
            (
                shape((frame_len, half_width), F32),
                shape((frame_len, half_width), F32),
                shape((frame_len, 2), F32),
            ),
            ties=ties,
        )

    def input_gradient(base, factor, sums):
        return call(
            input_kernel,
            (base, factor, sums, lax.ppermute(sums, "gy", swap), stats),
            (half_rows_of, shape((8, 128), F32)),
        )

    up_grad_of = shape((depth, hidden), F32)
    if ringed:
        came = [{}, {}]

        def send_on(i, blocks, names):
            for block, name in zip(blocks, names):
                came[i][name] = lax.ppermute(block, "gx", ahead if name == "up" else behind)

        def hop(i, turn, *ties):
            ways = [("up", half - turn - i), ("down", turn + 1 - i - half)]
            ways = [way for way in ways if way[1] != 0]
            names = [name for name, _ in ways]
            if i == 1:
                ties += tuple(came[i][name] for name in came[i] if name not in names)
            blocks = call(
                functools.partial(hop_kernel, tuple(step for _, step in ways), peers),
                (partial[i], *[came[i][name] for name in names]),
                [block_of] * len(ways),
                ties=ties,
            )
            send_on(i, blocks, names)
            return blocks[0]

        send_on(1, blocks_other, ("up", "down"))
        send_on(0, blocks_own, ("up", "down"))
        tie = hop(1, 1, partial_own)
        keep, send = own_d_norm(tie)
        tie = hop(0, 1, send)
        send = hold(send, tie, *came[1].values())
        sent = lax.ppermute(send, "gy", swap)
        tie = hop(1, 2, tie)
        tie = hop(0, 2, tie)
        over = over_cores(keep, sent, tie)
        back = lax.ppermute(over, "groups", swap)
        tie = over
        for turn in range(3, half):
            tie = hop(0, turn, hop(1, turn, tie))
        passing = call(
            functools.partial(total_kernel, peers),
            (partial[1], came[1]["up"], came[1]["down"]),
            block_of,
            ties=(tie,),
        )
        passed = lax.ppermute(passing, "groups", swap)
        input_grad, token = input_gradient(*scale(keep, sent, back, passing))
        up_grad = call(
            functools.partial(join_kernel, peers),
            (partial[0], came[0]["up"], came[0]["down"], passed),
            up_grad_of,
            ties=(token,),
        )
    else:
        keep, send = own_d_norm()
        sent = lax.ppermute(send, "gy", swap)
        back = lax.ppermute(over_cores(keep, sent), "groups", swap)
        input_grad, _ = input_gradient(*scale(keep, sent, back))
        total, passing = [
            lax.psum_scatter(p.astype(F32), "gx", scatter_dimension=0, tiled=True) for p in partial
        ]
        passed = lax.ppermute(passing.astype(BF16), "groups", swap)
        up_grad = call(place_halves_kernel, (total, passed), up_grad_of)
    return (input_grad[None], up_grad)


def solution(mesh):
    placed = (
        P(("groups", "gx"), None, None),
        P(("groups", "gx"), None, None),
        P(),
        P("gx", "gy"),
        P("gx", "gy"),
        P("groups"),
    )
    return jax.shard_map(
        shards,
        mesh=mesh,
        in_specs=placed,
        out_specs=(P(("groups", "gx"), None, "gy"), P(("groups", "gx"), "gy")),
        check_vma=False,
    )
```

```python
import functools

import jax
import jax.numpy as jnp
from jax import lax
from jax.experimental import pallas as pl
from jax.experimental.pallas import tpu as pltpu
from jax.sharding import PartitionSpec as P

BF16, F32 = jnp.bfloat16, jnp.float32
VMEM = pl.BlockSpec(memory_space=pltpu.VMEM)
HBM = pl.BlockSpec(memory_space=pltpu.HBM)
ANY = pl.BlockSpec(memory_space=pl.ANY)
SMEM = pl.BlockSpec(memory_space=pltpu.SMEM)


def shape(dims, kind):
    return jax.ShapeDtypeStruct(dims, kind)


def call(kernel, ins, out_shape, scratch=(), vmem=16, flops=1, left=(), pinned=(), out=VMEM, ties=()):
    count = len(ins)

    def body(*refs):
        kernel(*refs[:count], *refs[count + len(ties) :])

    moved = sum(x.size * x.dtype.itemsize for x in list(ins) + jax.tree.leaves(out_shape))
    return pl.pallas_call(
        body if ties else kernel,
        out_shape=out_shape,
        in_specs=[
            SMEM if x.dtype == jnp.int32 else ANY if i in left else HBM if i in pinned else VMEM
            for i, x in enumerate(ins)
        ]
        + [ANY] * len(ties),
        out_specs=jax.tree.map(lambda _: out, out_shape),
        scratch_shapes=list(scratch),
        compiler_params=pltpu.CompilerParams(vmem_limit_bytes=vmem << 20),
        cost_estimate=pl.CostEstimate(flops=flops, bytes_accessed=moved, transcendentals=0),
    )(*ins, *ties)


def hold(array, *ties):
    return pl.pallas_call(
        lambda *refs: None,
        out_shape=shape(array.shape, array.dtype),
        in_specs=[ANY] * (1 + len(ties)),
        out_specs=ANY,
        input_output_aliases={0: 0},
        compiler_params=pltpu.CompilerParams(vmem_limit_bytes=1 << 20),
        cost_estimate=pl.CostEstimate(flops=1, bytes_accessed=1, transcendentals=0),
    )(array, *ties)


def dot(left, right, left_dim=1, right_dim=0):
    return lax.dot_general(
        left, right, (((left_dim,), (right_dim,)), ((), ())), preferred_element_type=F32
    )


def gelu_slope(values):
    return (
        0.5 * (1.0 + lax.erf(values * 0.7071067811865476))
        + values * jnp.exp(-0.5 * values * values) * 0.3989422804014327
    )


def block_rows(step, peers, depth):
    own = lax.axis_index("gx")
    place = jnp.where(lax.rem(own, 2) == 0, lax.div(own, 2), peers - 1 - lax.div(own, 2))
    place = lax.rem(place + (step + peers), peers)
    member = jnp.where(place < peers // 2, 2 * place, 2 * (peers - 1 - place) + 1)
    return pl.ds(pl.multiple_of(member * depth, depth), depth)


def norm_rows(rows, gain):
    values = rows.astype(F32)
    centre = jnp.mean(values, axis=-1, keepdims=True)
    shifted = values - centre
    variance = jnp.mean(shifted * shifted, axis=-1, keepdims=True)
    inv_std = lax.rsqrt(variance + 1e-05)
    return (shifted * inv_std * gain[...][None]).astype(BF16), centre, inv_std


def mask_rows(rows, start, length):
    index = start + lax.broadcasted_iota(jnp.int32, (rows.shape[0], 1), 0)
    return jnp.where(index < length, rows.astype(F32), 0.0).astype(BF16)


def first_kernel(
    lengths, frames, out_grad, gain, w_up, w_down, passing, mine_up, mine_down, sems, rows, grads
):
    half, quarter = rows.shape[0], mine_up.shape[1]
    start = pl.multiple_of(lax.axis_index("gy") * half, half)
    columns = pl.ds(pl.multiple_of(lax.axis_index("groups") * quarter, quarter), quarter)
    moves = (
        (frames.at[pl.ds(start, half)], rows),
        (out_grad.at[pl.ds(start, half)], grads),
        (w_up.at[:, columns], mine_up),
        (w_down.at[:, columns], mine_down),
    )
    copies = [pltpu.make_async_copy(*move, sems.at[i]) for i, move in enumerate(moves)]
    for copy in copies:
        copy.start()
    copies[0].wait()
    passing[0] = norm_rows(rows[...], gain)[0]
    copies[1].wait()
    passing[1] = mask_rows(grads[...], start, lengths[lax.axis_index("gx")])
    copies[2].wait()
    copies[3].wait()


def norm_kernel(lengths, frames, out_grad, gain, normed, grads, stats):
    value, centre, inv_std = norm_rows(frames[...], gain)
    normed[...] = value
    stats[:, 0:1] = centre
    stats[:, 1:2] = inv_std
    grads[...] = mask_rows(out_grad[...], 0, lengths[lax.axis_index("gx")])


def back_through(normed, grads, up, down, d_pre, partial):
    pre_act = dot(normed[...], up[...])
    d_act = dot(grads[...], down[...])
    d_pre[...] = (d_act * gelu_slope(pre_act)).astype(BF16)
    partial[...] = dot(normed[...], d_pre[...], 0, 0).astype(BF16)


def place_kernel(places, peers, *refs):
    blocks, (up, down, sems) = refs[:-3], refs[-3:]
    copies = []
    for i, ((step, which), block) in enumerate(zip(places, blocks)):
        rows = block_rows(step, peers, block.shape[0])
        copies.append(pltpu.make_async_copy(block, (up, down)[which].at[rows], sems.at[i]))
    for copy in copies:
        copy.start()
    for copy in copies:
        copy.wait()


def own_kernel(places, sends, peers, normed, grads, near_up, near_down, *refs):
    late, refs = refs[: len(places)], refs[len(places) :]
    (d_pre, partial, up, down), blocks = refs[:4], refs[4:]
    up[...] = near_up[...]
    down[...] = near_down[...]
    for (step, which), block in zip(places, late):
        (up, down)[which][block_rows(step, peers, block.shape[0]), :] = block[...]
    back_through(normed, grads, up, down, d_pre, partial)
    for step, block in zip(sends, blocks):
        block[...] = partial[block_rows(step, peers, block.shape[0]), :]


def other_kernel(sends, peers, first, second, up, down, d_pre, partial, *refs):
    blocks, (normed, grads) = refs[:-2], refs[-2:]
    half = first.shape[1]
    for at, part in ((0, first), (half, second)):
        normed[at : at + half, :] = part[0]
        grads[at : at + half, :] = part[1]
    back_through(normed, grads, up, down, d_pre, partial)
    for step, block in zip(sends, blocks):
        block[...] = partial[block_rows(step, peers, block.shape[0]), :]


def d_norm_kernel(d_pre_own, d_pre_other, up, keep, send_own, *sends):
    core = lax.axis_index("gy")
    rows, width = keep.shape[1:]
    mine = up[pl.ds(pl.multiple_of(core * width, width), width), :]
    theirs = up[pl.ds(pl.multiple_of((1 - core) * width, width), width), :]
    keep[0] = dot(d_pre_own[...], mine, 1, 1).astype(BF16)
    keep[1] = dot(d_pre_other[...], mine, 1, 1).astype(BF16)
    send_own[...] = dot(d_pre_own[...], theirs, 1, 1).astype(BF16)
    sent = dot(d_pre_other[...], theirs, 1, 1).astype(BF16)
    sent = jnp.concatenate([sent[rows // 2 :], sent[: rows // 2]])
    step = rows // len(sends)
    for i, send in enumerate(sends):
        send[...] = sent[i * step : (i + 1) * step]


def over_kernel(keep, *refs):
    parts, over = refs[:-1], refs[-1]
    half = over.shape[0] // 2
    value = jnp.concatenate([part[...].astype(F32) for part in parts])
    value = (keep[1].astype(F32) + value).astype(BF16)
    for i in range(2):
        at = lax.rem(i + lax.axis_index("gy"), 2) * half
        over[pl.ds(pl.multiple_of(at, half), half), :] = value[i * half : (i + 1) * half]


def own_columns(ref, width):
    return ref[:, pl.ds(pl.multiple_of(lax.axis_index("gy") * width, width), width)]


def scale_kernel(keep, came, back, frames, gain, grads, stats, base, factor, sums):
    width = base.shape[1]
    d_norm = keep[0].astype(F32) + came[...].astype(F32) + back[...].astype(F32)
    scaled = d_norm * own_columns(gain, width)
    rows = own_columns(frames, width).astype(F32)
    inv_std = stats[:, 1:2]
    centred = (rows - stats[:, 0:1]) * inv_std
    sums[:, 0:1] = jnp.sum(scaled, axis=-1, keepdims=True)
    sums[:, 1:2] = jnp.sum(scaled * centred, axis=-1, keepdims=True)
    base[...] = own_columns(grads, width).astype(F32) + inv_std * scaled
    factor[...] = inv_std * centred


def input_kernel(base, factor, sums, came, stats, out, token):
    means = (sums[...] + came[...]) * (0.5 / base.shape[1])
    value = base[...] - stats[:, 1:2] * means[:, 0:1] - factor[...] * means[:, 1:2]
    out[...] = value.astype(BF16)
    token[...] = jnp.zeros_like(token)


def hop_kernel(places, peers, partial, *refs):
    count = len(places)
    for step, came, out in zip(places, refs[:count], refs[count:]):
        value = partial[block_rows(step, peers, out.shape[0]), :].astype(F32)
        out[...] = (value + came[...].astype(F32)).astype(BF16)


def total_kernel(peers, partial, up, down, total):
    value = partial[block_rows(0, peers, total.shape[0]), :].astype(F32)
    total[...] = (value + up[...].astype(F32) + down[...].astype(F32)).astype(BF16)


def join_kernel(peers, partial, up, down, passed, out):
    depth, width = passed.shape
    side = lax.axis_index("groups")
    value = partial[block_rows(0, peers, depth), :].astype(F32)
    value = value + up[...].astype(F32) + down[...].astype(F32)
    out[:, pl.ds(pl.multiple_of(side * width, width), width)] = value
    other = pl.ds(pl.multiple_of((1 - side) * width, width), width)
    out[:, other] = passed[...].astype(F32)


def place_halves_kernel(own, passed, out):
    width = own.shape[1]
    side = lax.axis_index("groups")
    out[:, pl.ds(pl.multiple_of(side * width, width), width)] = own[...]
    other = pl.ds(pl.multiple_of((1 - side) * width, width), width)
    out[:, other] = passed[...].astype(F32)


def shards(frames, out_grad, ln_gain, w_up, w_down, lengths):
    peers = lax.axis_size("gx")
    half = peers // 2
    frame_len, width = frames.shape[1:]
    depth, hidden = w_up.shape
    quarter = hidden // 2
    half_width = width // 2
    half_rows = frame_len // 2
    ringed = peers <= 16 and peers % 2 == 0 and depth % 16 == 0

    order = list(range(0, peers, 2)) + list(range(peers - 1, 0, -2))
    ahead = [(order[i], order[(i + 1) % peers]) for i in range(peers)]
    behind = [(b, a) for a, b in ahead]
    swap = [(0, 1), (1, 0)]

    frames, out_grad = frames[0], out_grad[0]
    rows_of = shape((frame_len, width), BF16)
    block_of = shape((depth, quarter), BF16)
    passing, *mine = call(
        first_kernel,
        (lengths, frames, out_grad, ln_gain, w_up, w_down),
        (shape((2, half_rows, width), BF16), block_of, block_of),
        [pltpu.SemaphoreType.DMA((4,))] + [pltpu.VMEM((half_rows, width), BF16)] * 2,
        flops=5 * frame_len * width,
        vmem=60,
        left=(1, 2, 4, 5),
    )
    first = lax.ppermute(passing, "groups", swap)
    normed, grads, stats = call(
        norm_kernel,
        (lengths, frames, out_grad, ln_gain),
        (rows_of, rows_of, shape((frame_len, 2), F32)),
        flops=10 * frame_len * width,
    )

    weight = shape((width, quarter), BF16)
    if ringed:
        blocks = {(0, 0): mine[0], (0, 1): mine[1]}
        up, down = list(mine), list(mine)
        for step in range(1, half):
            for i in range(2):
                up[i] = lax.ppermute(up[i], "gx", ahead)
                down[i] = lax.ppermute(down[i], "gx", behind)
            if step == 1:
                up[0] = hold(up[0], normed)
            for i in range(2):
                blocks[-step, i], blocks[step, i] = up[i], down[i]
        late = {
            (half - 1, 0): blocks.pop((half - 1, 0)),
            (1 - half, 1): blocks.pop((1 - half, 1)),
            (half, 0): lax.ppermute(up[0], "gx", ahead),
            (half, 1): lax.ppermute(down[1], "gx", behind),
        }
        near = call(
            functools.partial(place_kernel, tuple(blocks), peers),
            list(blocks.values()),
            (weight, weight),
            [pltpu.SemaphoreType.DMA((len(blocks),))],
            pinned=range(len(blocks)),
        )
        first = hold(first, *late.values())
        sends = ((half - 1, -half), (half, 1 - half))
    else:
        near = [lax.all_gather(block, "gx", axis=0, tiled=True) for block in mine]
        late, sends = {}, ((), ())
    second = lax.ppermute(first, "gy", swap)

    d_pre_of, partial_of = shape((frame_len, quarter), BF16), shape((width, quarter), BF16)
    d_pre_own, partial_own, full_up, full_down, *blocks_own = call(
        functools.partial(own_kernel, tuple(late), sends[1], peers),
        (normed, grads, *near, *late.values()),
        (d_pre_of, partial_of, weight, weight, *[block_of] * len(sends[1])),
        flops=6 * frame_len * width * quarter,
    )
    d_pre_other, partial_other, *blocks_other = call(
        functools.partial(other_kernel, sends[0], peers),
        (first, second, full_up, full_down),
        (d_pre_of, partial_of, *[block_of] * len(sends[0])),
        [pltpu.VMEM((frame_len, width), BF16)] * 2,
        flops=6 * frame_len * width * quarter,
    )
    partial = [partial_own, partial_other]

    half_rows_of = shape((frame_len, half_width), BF16)
    parts_of = [shape((frame_len // 3, half_width), BF16)] * 3

    def own_d_norm(*ties):
        keep, send, *parts = call(
            d_norm_kernel,
            (d_pre_own, d_pre_other, full_up),
            (shape((2, frame_len, half_width), BF16), half_rows_of, *parts_of),
            flops=4 * frame_len * width * quarter,
            ties=ties,
        )
        return keep, send, [lax.ppermute(part, "gy", swap) for part in parts]

    def over_cores(keep, parts, *ties):
        over = call(over_kernel, (keep, *parts), half_rows_of, ties=ties)
        return over, lax.ppermute(over, "groups", swap)

    def scale(keep, came, back, *ties):
        return call(
            scale_kernel,
            (keep, came, back, frames, ln_gain[None], grads, stats),
            (
                shape((frame_len, half_width), F32),
                shape((frame_len, half_width), F32),
                shape((frame_len, 2), F32),
            ),
            ties=ties,
        )

    def input_gradient(base, factor, sums):
        return call(
            input_kernel,
            (base, factor, sums, lax.ppermute(sums, "gy", swap), stats),
            (half_rows_of, shape((8, 128), F32)),
        )

    up_grad_of = shape((depth, hidden), F32)
    if ringed:
        came = [{}, {}]

        def send_on(i, blocks, names):
            for block, name in zip(blocks, names):
                came[i][name] = lax.ppermute(block, "gx", ahead if name == "up" else behind)

        def hop(i, turn, *ties):
            ways = [("up", half - turn - i), ("down", turn + 1 - i - half)]
            ways = [way for way in ways if way[1] != 0]
            names = [name for name, _ in ways]
            ties += tuple(came[i][name] for name in came[i] if name not in names)
            blocks = call(
                functools.partial(hop_kernel, tuple(step for _, step in ways), peers),
                (partial[i], *[came[i][name] for name in names]),
                [block_of] * len(ways),
                ties=ties,
            )
            send_on(i, blocks, names)
            return blocks[0]

        send_on(0, blocks_own, ("up", "down"))
        send_on(1, blocks_other, ("up", "down"))
        tie = hop(0, 1, partial_other)
        keep, send, parts = own_d_norm(tie)
        tie = hop(1, 1, keep)
        tie = hop(0, 2, tie)
        over, back = over_cores(keep, parts, tie)
        tie = hop(1, 2, over)
        for turn in range(3, half):
            tie = hop(1, turn, hop(0, turn, tie))
        sent = lax.ppermute(hold(send, tie), "gy", swap)
        passing = call(
            functools.partial(total_kernel, peers),
            (partial[1], came[1]["up"], came[1]["down"]),
            block_of,
            ties=(tie,),
        )
        passed = lax.ppermute(passing, "groups", swap)
        input_grad, token = input_gradient(*scale(keep, sent, back, passing))
        up_grad = call(
            functools.partial(join_kernel, peers),
            (partial[0], came[0]["up"], came[0]["down"], passed),
            up_grad_of,
            ties=(token,),
        )
    else:
        keep, send, parts = own_d_norm()
        sent = lax.ppermute(send, "gy", swap)
        _, back = over_cores(keep, parts)
        input_grad, _ = input_gradient(*scale(keep, sent, back))
        total, passing = [
            lax.psum_scatter(p.astype(F32), "gx", scatter_dimension=0, tiled=True) for p in partial
        ]
        passed = lax.ppermute(passing.astype(BF16), "groups", swap)
        up_grad = call(place_halves_kernel, (total, passed), up_grad_of)
    return (input_grad[None], up_grad)


def solution(mesh):
    placed = (
        P(("groups", "gx"), None, None),
        P(("groups", "gx"), None, None),
        P(),
        P("gx", "gy"),
        P("gx", "gy"),
        P("groups"),
    )
    return jax.shard_map(
        shards,
        mesh=mesh,
        in_specs=placed,
        out_specs=(P(("groups", "gx"), None, "gy"), P(("groups", "gx"), "gy")),
        check_vma=False,
    )
```

```python
import functools

import jax
import jax.numpy as jnp
from jax import lax
from jax.experimental import pallas as pl
from jax.experimental.pallas import tpu as pltpu
from jax.sharding import PartitionSpec as P

BF16, F32 = jnp.bfloat16, jnp.float32
VMEM = pl.BlockSpec(memory_space=pltpu.VMEM)
HBM = pl.BlockSpec(memory_space=pltpu.HBM)
ANY = pl.BlockSpec(memory_space=pl.ANY)
SMEM = pl.BlockSpec(memory_space=pltpu.SMEM)


def shape(dims, kind):
    return jax.ShapeDtypeStruct(dims, kind)


def call(kernel, ins, out_shape, scratch=(), vmem=16, flops=1, left=(), pinned=(), out=VMEM, ties=()):
    count = len(ins)

    def body(*refs):
        kernel(*refs[:count], *refs[count + len(ties) :])

    moved = sum(x.size * x.dtype.itemsize for x in list(ins) + jax.tree.leaves(out_shape))
    return pl.pallas_call(
        body if ties else kernel,
        out_shape=out_shape,
        in_specs=[
            SMEM if x.dtype == jnp.int32 else ANY if i in left else HBM if i in pinned else VMEM
            for i, x in enumerate(ins)
        ]
        + [ANY] * len(ties),
        out_specs=jax.tree.map(lambda _: out, out_shape),
        scratch_shapes=list(scratch),
        compiler_params=pltpu.CompilerParams(vmem_limit_bytes=vmem << 20),
        cost_estimate=pl.CostEstimate(flops=flops, bytes_accessed=moved, transcendentals=0),
    )(*ins, *ties)


def hold(array, *ties):
    return pl.pallas_call(
        lambda *refs: None,
        out_shape=shape(array.shape, array.dtype),
        in_specs=[ANY] * (1 + len(ties)),
        out_specs=ANY,
        input_output_aliases={0: 0},
        compiler_params=pltpu.CompilerParams(vmem_limit_bytes=1 << 20),
        cost_estimate=pl.CostEstimate(flops=1, bytes_accessed=1, transcendentals=0),
    )(array, *ties)


def dot(left, right, left_dim=1, right_dim=0):
    return lax.dot_general(
        left, right, (((left_dim,), (right_dim,)), ((), ())), preferred_element_type=F32
    )


def gelu_slope(values):
    return (
        0.5 * (1.0 + lax.erf(values * 0.7071067811865476))
        + values * jnp.exp(-0.5 * values * values) * 0.3989422804014327
    )


def block_rows(step, peers, depth):
    own = lax.axis_index("gx")
    place = jnp.where(lax.rem(own, 2) == 0, lax.div(own, 2), peers - 1 - lax.div(own, 2))
    place = lax.rem(place + (step + peers), peers)
    member = jnp.where(place < peers // 2, 2 * place, 2 * (peers - 1 - place) + 1)
    return pl.ds(pl.multiple_of(member * depth, depth), depth)


def norm_rows(rows, gain):
    values = rows.astype(F32)
    centre = jnp.mean(values, axis=-1, keepdims=True)
    shifted = values - centre
    variance = jnp.mean(shifted * shifted, axis=-1, keepdims=True)
    inv_std = lax.rsqrt(variance + 1e-05)
    return (shifted * inv_std * gain[...][None]).astype(BF16), centre, inv_std


def mask_rows(rows, start, length):
    index = start + lax.broadcasted_iota(jnp.int32, (rows.shape[0], 1), 0)
    return jnp.where(index < length, rows.astype(F32), 0.0).astype(BF16)


def first_kernel(
    lengths, frames, out_grad, gain, w_up, w_down, passing, mine_up, mine_down, sems, rows, grads
):
    half, quarter = rows.shape[0], mine_up.shape[1]
    start = pl.multiple_of(lax.axis_index("gy") * half, half)
    columns = pl.ds(pl.multiple_of(lax.axis_index("groups") * quarter, quarter), quarter)
    moves = (
        (frames.at[pl.ds(start, half)], rows),
        (out_grad.at[pl.ds(start, half)], grads),
        (w_up.at[:, columns], mine_up),
        (w_down.at[:, columns], mine_down),
    )
    copies = [pltpu.make_async_copy(*move, sems.at[i]) for i, move in enumerate(moves)]
    for copy in copies:
        copy.start()
    copies[0].wait()
    passing[0] = norm_rows(rows[...], gain)[0]
    copies[1].wait()
    passing[1] = mask_rows(grads[...], start, lengths[lax.axis_index("gx")])
    copies[2].wait()
    copies[3].wait()


def norm_kernel(lengths, frames, out_grad, gain, normed, grads, stats):
    value, centre, inv_std = norm_rows(frames[...], gain)
    normed[...] = value
    stats[:, 0:1] = centre
    stats[:, 1:2] = inv_std
    grads[...] = mask_rows(out_grad[...], 0, lengths[lax.axis_index("gx")])


def back_through(normed, grads, up, down, d_pre, partial):
    pre_act = dot(normed[...], up[...])
    d_act = dot(grads[...], down[...])
    d_pre[...] = (d_act * gelu_slope(pre_act)).astype(BF16)
    partial[...] = dot(normed[...], d_pre[...], 0, 0).astype(BF16)


def place_kernel(places, peers, *refs):
    blocks, (up, down, sems) = refs[:-3], refs[-3:]
    copies = []
    for i, ((step, which), block) in enumerate(zip(places, blocks)):
        rows = block_rows(step, peers, block.shape[0])
        copies.append(pltpu.make_async_copy(block, (up, down)[which].at[rows], sems.at[i]))
    for copy in copies:
        copy.start()
    for copy in copies:
        copy.wait()


def own_kernel(places, sends, peers, normed, grads, near_up, near_down, *refs):
    late, refs = refs[: len(places)], refs[len(places) :]
    (d_pre, partial, up, down), blocks = refs[:4], refs[4:]
    up[...] = near_up[...]
    down[...] = near_down[...]
    for (step, which), block in zip(places, late):
        (up, down)[which][block_rows(step, peers, block.shape[0]), :] = block[...]
    back_through(normed, grads, up, down, d_pre, partial)
    for step, block in zip(sends, blocks):
        block[...] = partial[block_rows(step, peers, block.shape[0]), :]


def other_kernel(sends, peers, first, second, up, down, d_pre, partial, *refs):
    blocks, (normed, grads) = refs[:-2], refs[-2:]
    half = first.shape[1]
    for at, part in ((0, first), (half, second)):
        normed[at : at + half, :] = part[0]
        grads[at : at + half, :] = part[1]
    back_through(normed, grads, up, down, d_pre, partial)
    for step, block in zip(sends, blocks):
        block[...] = partial[block_rows(step, peers, block.shape[0]), :]


def d_norm_kernel(d_pre_own, d_pre_other, up, keep, send_own, *sends):
    core = lax.axis_index("gy")
    rows, width = keep.shape[1:]
    mine = up[pl.ds(pl.multiple_of(core * width, width), width), :]
    theirs = up[pl.ds(pl.multiple_of((1 - core) * width, width), width), :]
    keep[0] = dot(d_pre_own[...], mine, 1, 1).astype(BF16)
    keep[1] = dot(d_pre_other[...], mine, 1, 1).astype(BF16)
    send_own[...] = dot(d_pre_own[...], theirs, 1, 1).astype(BF16)
    sent = dot(d_pre_other[...], theirs, 1, 1).astype(BF16)
    sent = jnp.concatenate([sent[rows // 2 :], sent[: rows // 2]])
    step = rows // len(sends)
    for i, send in enumerate(sends):
        send[...] = sent[i * step : (i + 1) * step]


def over_kernel(keep, *refs):
    parts, over = refs[:-1], refs[-1]
    half = over.shape[0] // 2
    value = jnp.concatenate([part[...].astype(F32) for part in parts])
    value = (keep[1].astype(F32) + value).astype(BF16)
    for i in range(2):
        at = lax.rem(i + lax.axis_index("gy"), 2) * half
        over[pl.ds(pl.multiple_of(at, half), half), :] = value[i * half : (i + 1) * half]


def own_columns(ref, width):
    return ref[:, pl.ds(pl.multiple_of(lax.axis_index("gy") * width, width), width)]


def scale_kernel(keep, came, back, frames, gain, grads, stats, base, factor, sums):
    width = base.shape[1]
    d_norm = keep[0].astype(F32) + came[...].astype(F32) + back[...].astype(F32)
    scaled = d_norm * own_columns(gain, width)
    rows = own_columns(frames, width).astype(F32)
    inv_std = stats[:, 1:2]
    centred = (rows - stats[:, 0:1]) * inv_std
    sums[:, 0:1] = jnp.sum(scaled, axis=-1, keepdims=True)
    sums[:, 1:2] = jnp.sum(scaled * centred, axis=-1, keepdims=True)
    base[...] = own_columns(grads, width).astype(F32) + inv_std * scaled
    factor[...] = inv_std * centred


def input_kernel(base, factor, sums, came, stats, out, token):
    means = (sums[...] + came[...]) * (0.5 / base.shape[1])
    value = base[...] - stats[:, 1:2] * means[:, 0:1] - factor[...] * means[:, 1:2]
    out[...] = value.astype(BF16)
    token[...] = jnp.zeros_like(token)


def hop_kernel(places, peers, partial, *refs):
    count = len(places)
    for step, came, out in zip(places, refs[:count], refs[count:]):
        value = partial[block_rows(step, peers, out.shape[0]), :].astype(F32)
        out[...] = (value + came[...].astype(F32)).astype(BF16)


def total_kernel(peers, partial, up, total):
    value = partial[block_rows(0, peers, total.shape[0]), :].astype(F32)
    total[...] = (value + up[...].astype(F32)).astype(BF16)


def add_kernel(one, two, total):
    total[...] = one[...].astype(F32) + two[...].astype(F32)


def join_kernel(peers, partial, up, down, passed, out):
    depth, width = passed.shape
    side = lax.axis_index("groups")
    value = partial[block_rows(0, peers, depth), :].astype(F32)
    value = value + up[...].astype(F32) + down[...].astype(F32)
    out[:, pl.ds(pl.multiple_of(side * width, width), width)] = value
    other = pl.ds(pl.multiple_of((1 - side) * width, width), width)
    out[:, other] = passed[...]


def place_halves_kernel(own, passed, out):
    width = own.shape[1]
    side = lax.axis_index("groups")
    out[:, pl.ds(pl.multiple_of(side * width, width), width)] = own[...]
    other = pl.ds(pl.multiple_of((1 - side) * width, width), width)
    out[:, other] = passed[...].astype(F32)


def shards(frames, out_grad, ln_gain, w_up, w_down, lengths):
    peers = lax.axis_size("gx")
    half = peers // 2
    frame_len, width = frames.shape[1:]
    depth, hidden = w_up.shape
    quarter = hidden // 2
    half_width = width // 2
    half_rows = frame_len // 2
    ringed = peers <= 16 and peers % 2 == 0 and depth % 16 == 0

    order = list(range(0, peers, 2)) + list(range(peers - 1, 0, -2))
    ahead = [(order[i], order[(i + 1) % peers]) for i in range(peers)]
    behind = [(b, a) for a, b in ahead]
    swap = [(0, 1), (1, 0)]

    frames, out_grad = frames[0], out_grad[0]
    rows_of = shape((frame_len, width), BF16)
    block_of = shape((depth, quarter), BF16)
    passing, *mine = call(
        first_kernel,
        (lengths, frames, out_grad, ln_gain, w_up, w_down),
        (shape((2, half_rows, width), BF16), block_of, block_of),
        [pltpu.SemaphoreType.DMA((4,))] + [pltpu.VMEM((half_rows, width), BF16)] * 2,
        flops=5 * frame_len * width,
        vmem=60,
        left=(1, 2, 4, 5),
    )
    first = lax.ppermute(passing, "groups", swap)
    normed, grads, stats = call(
        norm_kernel,
        (lengths, frames, out_grad, ln_gain),
        (rows_of, rows_of, shape((frame_len, 2), F32)),
        flops=10 * frame_len * width,
    )

    weight = shape((width, quarter), BF16)
    if ringed:
        blocks = {(0, 0): mine[0], (0, 1): mine[1]}
        up, down = list(mine), list(mine)
        for step in range(1, half):
            for i in range(2):
                up[i] = lax.ppermute(up[i], "gx", ahead)
                down[i] = lax.ppermute(down[i], "gx", behind)
            if step == 1:
                up[0] = hold(up[0], normed)
            for i in range(2):
                blocks[-step, i], blocks[step, i] = up[i], down[i]
        late = {
            (half - 1, 0): blocks.pop((half - 1, 0)),
            (1 - half, 1): blocks.pop((1 - half, 1)),
            (half, 0): lax.ppermute(up[0], "gx", ahead),
            (half, 1): lax.ppermute(down[1], "gx", behind),
        }
        near = call(
            functools.partial(place_kernel, tuple(blocks), peers),
            list(blocks.values()),
            (weight, weight),
            [pltpu.SemaphoreType.DMA((len(blocks),))],
            pinned=range(len(blocks)),
        )
        first = hold(first, *late.values(), near[0])
        sends = ((half - 1, -half), (half, 1 - half))
    else:
        near = [lax.all_gather(block, "gx", axis=0, tiled=True) for block in mine]
        late, sends = {}, ((), ())
    second = lax.ppermute(first, "gy", swap)

    d_pre_of, partial_of = shape((frame_len, quarter), BF16), shape((width, quarter), BF16)
    d_pre_own, partial_own, full_up, full_down, *blocks_own = call(
        functools.partial(own_kernel, tuple(late), sends[1], peers),
        (normed, grads, *near, *late.values()),
        (d_pre_of, partial_of, weight, weight, *[block_of] * len(sends[1])),
        flops=6 * frame_len * width * quarter,
    )
    d_pre_other, partial_other, *blocks_other = call(
        functools.partial(other_kernel, sends[0], peers),
        (first, second, full_up, full_down),
        (d_pre_of, partial_of, *[block_of] * len(sends[0])),
        [pltpu.VMEM((frame_len, width), BF16)] * 2,
        flops=6 * frame_len * width * quarter,
    )
    partial = [partial_own, partial_other]

    half_rows_of = shape((frame_len, half_width), BF16)
    parts_of = [shape((frame_len // 3, half_width), BF16)] * 3

    def own_d_norm(*ties):
        keep, send, *parts = call(
            d_norm_kernel,
            (d_pre_own, d_pre_other, full_up),
            (shape((2, frame_len, half_width), BF16), half_rows_of, *parts_of),
            flops=4 * frame_len * width * quarter,
            ties=ties,
        )
        return keep, send, [lax.ppermute(part, "gy", swap) for part in parts]

    def over_cores(keep, parts, *ties):
        over = call(over_kernel, (keep, *parts), half_rows_of, ties=ties)
        return over, lax.ppermute(over, "groups", swap)

    def scale(keep, came, back, *ties):
        return call(
            scale_kernel,
            (keep, came, back, frames, ln_gain[None], grads, stats),
            (
                shape((frame_len, half_width), F32),
                shape((frame_len, half_width), F32),
                shape((frame_len, 2), F32),
            ),
            ties=ties,
        )

    def input_gradient(base, factor, sums):
        return call(
            input_kernel,
            (base, factor, sums, lax.ppermute(sums, "gy", swap), stats),
            (half_rows_of, shape((8, 128), F32)),
        )

    up_grad_of = shape((depth, hidden), F32)
    if ringed:
        came = [{}, {}]

        across = [
            (a + k * peers, b + (1 - k) * peers) for k in range(2) for a, b in behind
        ]

        def send_on(i, blocks, names, last=False):
            for block, name in zip(blocks, names):
                if last and i == 1:
                    came[i][name] = lax.ppermute(block, ("groups", "gx"), across)
                else:
                    came[i][name] = lax.ppermute(block, "gx", ahead if name == "up" else behind)

        def hop(i, turn, *ties):
            ways = [("up", half - turn - i), ("down", turn + 1 - i - half)]
            ways = [way for way in ways if way[1] != 0]
            names = [name for name, _ in ways]
            ties += tuple(came[i][name] for name in came[i] if name not in names)
            blocks = call(
                functools.partial(hop_kernel, tuple(step for _, step in ways), peers),
                (partial[i], *[came[i][name] for name in names]),
                [block_of] * len(ways),
                ties=ties,
            )
            send_on(i, blocks, names, turn == half - 1)
            return blocks[0]

        send_on(0, blocks_own, ("up", "down"))
        send_on(1, blocks_other, ("up", "down"))
        tie = hop(0, 1, partial_other)
        keep, send, parts = own_d_norm(tie)
        tie = hop(1, 1, keep)
        tie = hop(0, 2, tie)
        over, back = over_cores(keep, parts, tie)
        tie = hop(1, 2, over)
        for turn in range(3, half):
            tie = hop(1, turn, hop(0, turn, tie))
        sent = lax.ppermute(hold(send, tie), "gy", swap)
        passing = call(
            functools.partial(total_kernel, peers),
            (partial[1], came[1]["up"]),
            block_of,
            ties=(tie,),
        )
        passed = lax.ppermute(passing, "groups", swap)
        input_grad, token = input_gradient(*scale(keep, sent, back, passing))
        passed = call(
            add_kernel, (passed, came[1]["down"]), shape((depth, quarter), F32), ties=(token,)
        )
        up_grad = call(
            functools.partial(join_kernel, peers),
            (partial[0], came[0]["up"], came[0]["down"], passed),
            up_grad_of,
        )
    else:
        keep, send, parts = own_d_norm()
        sent = lax.ppermute(send, "gy", swap)
        _, back = over_cores(keep, parts)
        input_grad, _ = input_gradient(*scale(keep, sent, back))
        total, passing = [
            lax.psum_scatter(p.astype(F32), "gx", scatter_dimension=0, tiled=True) for p in partial
        ]
        passed = lax.ppermute(passing.astype(BF16), "groups", swap)
        up_grad = call(place_halves_kernel, (total, passed), up_grad_of)
    return (input_grad[None], up_grad)


def solution(mesh):
    placed = (
        P(("groups", "gx"), None, None),
        P(("groups", "gx"), None, None),
        P(),
        P("gx", "gy"),
        P("gx", "gy"),
        P("groups"),
    )
    return jax.shard_map(
        shards,
        mesh=mesh,
        in_specs=placed,
        out_specs=(P(("groups", "gx"), None, "gy"), P(("groups", "gx"), "gy")),
        check_vma=False,
    )
```

```python
import functools

import jax
import jax.numpy as jnp
from jax import lax
from jax.experimental import pallas as pl
from jax.experimental.pallas import tpu as pltpu
from jax.sharding import PartitionSpec as P

BF16, F32 = jnp.bfloat16, jnp.float32
VMEM = pl.BlockSpec(memory_space=pltpu.VMEM)
HBM = pl.BlockSpec(memory_space=pltpu.HBM)
ANY = pl.BlockSpec(memory_space=pl.ANY)
SMEM = pl.BlockSpec(memory_space=pltpu.SMEM)


def shape(dims, kind):
    return jax.ShapeDtypeStruct(dims, kind)


def call(kernel, ins, out_shape, scratch=(), vmem=16, flops=1, left=(), pinned=(), out=VMEM, ties=()):
    count = len(ins)

    def body(*refs):
        kernel(*refs[:count], *refs[count + len(ties) :])

    moved = sum(x.size * x.dtype.itemsize for x in list(ins) + jax.tree.leaves(out_shape))
    return pl.pallas_call(
        body if ties else kernel,
        out_shape=out_shape,
        in_specs=[
            SMEM if x.dtype == jnp.int32 else ANY if i in left else HBM if i in pinned else VMEM
            for i, x in enumerate(ins)
        ]
        + [ANY] * len(ties),
        out_specs=jax.tree.map(lambda _: out, out_shape),
        scratch_shapes=list(scratch),
        compiler_params=pltpu.CompilerParams(vmem_limit_bytes=vmem << 20),
        cost_estimate=pl.CostEstimate(flops=flops, bytes_accessed=moved, transcendentals=0),
    )(*ins, *ties)


def hold(array, *ties):
    return pl.pallas_call(
        lambda *refs: None,
        out_shape=shape(array.shape, array.dtype),
        in_specs=[ANY] * (1 + len(ties)),
        out_specs=ANY,
        input_output_aliases={0: 0},
        compiler_params=pltpu.CompilerParams(vmem_limit_bytes=1 << 20),
        cost_estimate=pl.CostEstimate(flops=1, bytes_accessed=1, transcendentals=0),
    )(array, *ties)


def dot(left, right, left_dim=1, right_dim=0):
    return lax.dot_general(
        left, right, (((left_dim,), (right_dim,)), ((), ())), preferred_element_type=F32
    )


def gelu_slope(values):
    return (
        0.5 * (1.0 + lax.erf(values * 0.7071067811865476))
        + values * jnp.exp(-0.5 * values * values) * 0.3989422804014327
    )


def block_rows(step, peers, depth):
    own = lax.axis_index("gx")
    place = jnp.where(lax.rem(own, 2) == 0, lax.div(own, 2), peers - 1 - lax.div(own, 2))
    place = lax.rem(place + (step + peers), peers)
    member = jnp.where(place < peers // 2, 2 * place, 2 * (peers - 1 - place) + 1)
    return pl.ds(pl.multiple_of(member * depth, depth), depth)


def norm_rows(rows, gain):
    values = rows.astype(F32)
    centre = jnp.mean(values, axis=-1, keepdims=True)
    shifted = values - centre
    variance = jnp.mean(shifted * shifted, axis=-1, keepdims=True)
    inv_std = lax.rsqrt(variance + 1e-05)
    return (shifted * inv_std * gain[...][None]).astype(BF16), centre, inv_std


def mask_rows(rows, start, length):
    index = start + lax.broadcasted_iota(jnp.int32, (rows.shape[0], 1), 0)
    return jnp.where(index < length, rows.astype(F32), 0.0).astype(BF16)


def cut_kernel(w_up, w_down, mine_up, mine_down, sems):
    quarter = mine_up.shape[1]
    columns = pl.ds(pl.multiple_of(lax.axis_index("groups") * quarter, quarter), quarter)
    copies = [
        pltpu.make_async_copy(w_up.at[:, columns], mine_up, sems.at[0]),
        pltpu.make_async_copy(w_down.at[:, columns], mine_down, sems.at[1]),
    ]
    for copy in copies:
        copy.start()
    for copy in copies:
        copy.wait()


def pass_kernel(lengths, frames, out_grad, gain, passing, sems, rows, grads):
    half = rows.shape[0]
    start = pl.multiple_of(lax.axis_index("gy") * half, half)
    copies = [
        pltpu.make_async_copy(source.at[pl.ds(start, half)], target, sems.at[i])
        for i, (source, target) in enumerate(((frames, rows), (out_grad, grads)))
    ]
    for copy in copies:
        copy.start()
    copies[0].wait()
    passing[0] = norm_rows(rows[...], gain)[0]
    copies[1].wait()
    passing[1] = mask_rows(grads[...], start, lengths[lax.axis_index("gx")])


def norm_kernel(lengths, frames, out_grad, gain, normed, grads, stats):
    value, centre, inv_std = norm_rows(frames[...], gain)
    normed[...] = value
    stats[:, 0:1] = centre
    stats[:, 1:2] = inv_std
    grads[...] = mask_rows(out_grad[...], 0, lengths[lax.axis_index("gx")])


def back_through(normed, grads, up, down, d_pre, partial):
    pre_act = dot(normed[...], up[...])
    d_act = dot(grads[...], down[...])
    d_pre[...] = (d_act * gelu_slope(pre_act)).astype(BF16)
    partial[...] = dot(normed[...], d_pre[...], 0, 0).astype(BF16)


def place_kernel(places, peers, *refs):
    blocks, (up, down, sems) = refs[:-3], refs[-3:]
    copies = []
    for i, ((step, which), block) in enumerate(zip(places, blocks)):
        rows = block_rows(step, peers, block.shape[0])
        copies.append(pltpu.make_async_copy(block, (up, down)[which].at[rows], sems.at[i]))
    for copy in copies:
        copy.start()
    for copy in copies:
        copy.wait()


def own_kernel(places, sends, peers, normed, grads, near_up, near_down, *refs):
    late, refs = refs[: len(places)], refs[len(places) :]
    (d_pre, partial, up, down), blocks = refs[:4], refs[4:]
    up[...] = near_up[...]
    down[...] = near_down[...]
    for (step, which), block in zip(places, late):
        (up, down)[which][block_rows(step, peers, block.shape[0]), :] = block[...]
    back_through(normed, grads, up, down, d_pre, partial)
    for step, block in zip(sends, blocks):
        block[...] = partial[block_rows(step, peers, block.shape[0]), :]


def other_kernel(sends, peers, first, second, up, down, d_pre, partial, *refs):
    blocks, (normed, grads) = refs[:-2], refs[-2:]
    half = first.shape[1]
    for at, part in ((0, first), (half, second)):
        normed[at : at + half, :] = part[0]
        grads[at : at + half, :] = part[1]
    back_through(normed, grads, up, down, d_pre, partial)
    for step, block in zip(sends, blocks):
        block[...] = partial[block_rows(step, peers, block.shape[0]), :]


def d_norm_kernel(d_pre_own, d_pre_other, up, keep, send_own, *sends):
    core = lax.axis_index("gy")
    rows, width = keep.shape[1:]
    mine = up[pl.ds(pl.multiple_of(core * width, width), width), :]
    theirs = up[pl.ds(pl.multiple_of((1 - core) * width, width), width), :]
    keep[0] = dot(d_pre_own[...], mine, 1, 1).astype(BF16)
    keep[1] = dot(d_pre_other[...], mine, 1, 1).astype(BF16)
    send_own[...] = dot(d_pre_own[...], theirs, 1, 1).astype(BF16)
    sent = dot(d_pre_other[...], theirs, 1, 1).astype(BF16)
    sent = jnp.concatenate([sent[rows // 2 :], sent[: rows // 2]])
    step = rows // len(sends)
    for i, send in enumerate(sends):
        send[...] = sent[i * step : (i + 1) * step]


def over_kernel(keep, *refs):
    parts, over = refs[:-1], refs[-1]
    half = over.shape[0] // 2
    value = jnp.concatenate([part[...].astype(F32) for part in parts])
    value = (keep[1].astype(F32) + value).astype(BF16)
    for i in range(2):
        at = lax.rem(i + lax.axis_index("gy"), 2) * half
        over[pl.ds(pl.multiple_of(at, half), half), :] = value[i * half : (i + 1) * half]


def own_columns(ref, width):
    return ref[:, pl.ds(pl.multiple_of(lax.axis_index("gy") * width, width), width)]


def scale_kernel(keep, came, back, frames, gain, grads, stats, base, factor, sums):
    width = base.shape[1]
    d_norm = keep[0].astype(F32) + came[...].astype(F32) + back[...].astype(F32)
    scaled = d_norm * own_columns(gain, width)
    rows = own_columns(frames, width).astype(F32)
    inv_std = stats[:, 1:2]
    centred = (rows - stats[:, 0:1]) * inv_std
    sums[:, 0:1] = jnp.sum(scaled, axis=-1, keepdims=True)
    sums[:, 1:2] = jnp.sum(scaled * centred, axis=-1, keepdims=True)
    base[...] = own_columns(grads, width).astype(F32) + inv_std * scaled
    factor[...] = inv_std * centred


def input_kernel(base, factor, sums, came, stats, out, token):
    means = (sums[...] + came[...]) * (0.5 / base.shape[1])
    value = base[...] - stats[:, 1:2] * means[:, 0:1] - factor[...] * means[:, 1:2]
    out[...] = value.astype(BF16)
    token[...] = jnp.zeros_like(token)


def hop_kernel(places, peers, partial, *refs):
    count = len(places)
    for step, came, out in zip(places, refs[:count], refs[count:]):
        value = partial[block_rows(step, peers, out.shape[0]), :].astype(F32)
        out[...] = (value + came[...].astype(F32)).astype(BF16)


def total_kernel(peers, partial, up, down, total):
    value = partial[block_rows(0, peers, total.shape[0]), :].astype(F32)
    total[...] = (value + up[...].astype(F32) + down[...].astype(F32)).astype(BF16)


def join_kernel(peers, partial, up, down, passed, out):
    depth, width = passed.shape
    side = lax.axis_index("groups")
    value = partial[block_rows(0, peers, depth), :].astype(F32)
    value = value + up[...].astype(F32) + down[...].astype(F32)
    out[:, pl.ds(pl.multiple_of(side * width, width), width)] = value
    other = pl.ds(pl.multiple_of((1 - side) * width, width), width)
    out[:, other] = passed[...].astype(F32)


def place_halves_kernel(own, passed, out):
    width = own.shape[1]
    side = lax.axis_index("groups")
    out[:, pl.ds(pl.multiple_of(side * width, width), width)] = own[...]
    other = pl.ds(pl.multiple_of((1 - side) * width, width), width)
    out[:, other] = passed[...].astype(F32)


def shards(frames, out_grad, ln_gain, w_up, w_down, lengths):
    peers = lax.axis_size("gx")
    half = peers // 2
    frame_len, width = frames.shape[1:]
    depth, hidden = w_up.shape
    quarter = hidden // 2
    half_width = width // 2
    half_rows = frame_len // 2
    ringed = peers <= 16 and peers % 2 == 0 and depth % 16 == 0

    order = list(range(0, peers, 2)) + list(range(peers - 1, 0, -2))
    ahead = [(order[i], order[(i + 1) % peers]) for i in range(peers)]
    behind = [(b, a) for a, b in ahead]
    swap = [(0, 1), (1, 0)]

    frames, out_grad = frames[0], out_grad[0]
    rows_of = shape((frame_len, width), BF16)
    block_of = shape((depth, quarter), BF16)
    mine = call(
        cut_kernel,
        (w_up, w_down),
        (block_of, block_of),
        [pltpu.SemaphoreType.DMA((2,))],
        vmem=60,
        left=(0, 1),
    )
    passing = call(
        pass_kernel,
        (lengths, frames, out_grad, ln_gain),
        shape((2, half_rows, width), BF16),
        [pltpu.SemaphoreType.DMA((2,))] + [pltpu.VMEM((half_rows, width), BF16)] * 2,
        flops=5 * frame_len * width,
        left=(1, 2),
    )
    normed, grads, stats = call(
        norm_kernel,
        (lengths, frames, out_grad, ln_gain),
        (rows_of, rows_of, shape((frame_len, 2), F32)),
        flops=10 * frame_len * width,
    )

    weight = shape((width, quarter), BF16)
    if ringed:
        blocks = {(0, 0): mine[0], (0, 1): mine[1]}
        up, down = list(mine), list(mine)
        for step in range(1, half):
            for i in range(2):
                up[i] = lax.ppermute(up[i], "gx", ahead)
                down[i] = lax.ppermute(down[i], "gx", behind)
            if step == 1:
                first = lax.ppermute(hold(passing, up[0], down[1]), "groups", swap)
            if step == 2:
                up[0] = hold(up[0], normed)
            for i in range(2):
                blocks[-step, i], blocks[step, i] = up[i], down[i]
        late = {
            (half - 1, 0): blocks.pop((half - 1, 0)),
            (1 - half, 1): blocks.pop((1 - half, 1)),
            (half, 0): lax.ppermute(up[0], "gx", ahead),
            (half, 1): lax.ppermute(down[1], "gx", behind),
        }
        near = call(
            functools.partial(place_kernel, tuple(blocks), peers),
            list(blocks.values()),
            (weight, weight),
            [pltpu.SemaphoreType.DMA((len(blocks),))],
            pinned=range(len(blocks)),
        )
        first = hold(first, *late.values(), near[0])
        sends = ((half - 1, -half), (half, 1 - half))
    else:
        first = lax.ppermute(passing, "groups", swap)
        near = [lax.all_gather(block, "gx", axis=0, tiled=True) for block in mine]
        late, sends = {}, ((), ())
    second = lax.ppermute(first, "gy", swap)

    d_pre_of, partial_of = shape((frame_len, quarter), BF16), shape((width, quarter), BF16)
    d_pre_own, partial_own, full_up, full_down, *blocks_own = call(
        functools.partial(own_kernel, tuple(late), sends[1], peers),
        (normed, grads, *near, *late.values()),
        (d_pre_of, partial_of, weight, weight, *[block_of] * len(sends[1])),
        flops=6 * frame_len * width * quarter,
    )
    d_pre_other, partial_other, *blocks_other = call(
        functools.partial(other_kernel, sends[0], peers),
        (first, second, full_up, full_down),
        (d_pre_of, partial_of, *[block_of] * len(sends[0])),
        [pltpu.VMEM((frame_len, width), BF16)] * 2,
        flops=6 * frame_len * width * quarter,
    )
    partial = [partial_own, partial_other]

    half_rows_of = shape((frame_len, half_width), BF16)
    parts_of = [shape((frame_len // 3, half_width), BF16)] * 3

    def own_d_norm(*ties):
        keep, send, *parts = call(
            d_norm_kernel,
            (d_pre_own, d_pre_other, full_up),
            (shape((2, frame_len, half_width), BF16), half_rows_of, *parts_of),
            flops=4 * frame_len * width * quarter,
            ties=ties,
        )
        return keep, send, [lax.ppermute(part, "gy", swap) for part in parts]

    def over_cores(keep, parts, *ties):
        over = call(over_kernel, (keep, *parts), half_rows_of, ties=ties)
        return over, lax.ppermute(over, "groups", swap)

    def scale(keep, came, back, *ties):
        return call(
            scale_kernel,
            (keep, came, back, frames, ln_gain[None], grads, stats),
            (
                shape((frame_len, half_width), F32),
                shape((frame_len, half_width), F32),
                shape((frame_len, 2), F32),
            ),
            ties=ties,
        )

    def input_gradient(base, factor, sums):
        return call(
            input_kernel,
            (base, factor, sums, lax.ppermute(sums, "gy", swap), stats),
            (half_rows_of, shape((8, 128), F32)),
        )

    up_grad_of = shape((depth, hidden), F32)
    if ringed:
        came = [{}, {}]

        def send_on(i, blocks, names):
            for block, name in zip(blocks, names):
                came[i][name] = lax.ppermute(block, "gx", ahead if name == "up" else behind)

        def hop(i, turn, *ties):
            ways = [("up", half - turn - i), ("down", turn + 1 - i - half)]
            ways = [way for way in ways if way[1] != 0]
            names = [name for name, _ in ways]
            ties += tuple(came[i][name] for name in came[i] if name not in names)
            blocks = call(
                functools.partial(hop_kernel, tuple(step for _, step in ways), peers),
                (partial[i], *[came[i][name] for name in names]),
                [block_of] * len(ways),
                ties=ties,
            )
            send_on(i, blocks, names)
            return blocks[0]

        send_on(0, blocks_own, ("up", "down"))
        send_on(1, blocks_other, ("up", "down"))
        keep, send, parts = own_d_norm(*came[0].values())
        tie = hop(1, 1, keep)
        tie = hop(0, 1, tie)
        over, back = over_cores(keep, parts, tie)
        tie = hop(1, 2, over)
        tie = hop(0, 2, tie)
        for turn in range(3, half):
            tie = hop(0, turn, hop(1, turn, tie))
        sent = lax.ppermute(hold(send, tie), "gy", swap)
        passing = call(
            functools.partial(total_kernel, peers),
            (partial[1], came[1]["up"], came[1]["down"]),
            block_of,
            ties=(tie,),
        )
        passed = lax.ppermute(passing, "groups", swap)
        input_grad, token = input_gradient(*scale(keep, sent, back, passing))
        up_grad = call(
            functools.partial(join_kernel, peers),
            (partial[0], came[0]["up"], came[0]["down"], passed),
            up_grad_of,
            ties=(token,),
        )
    else:
        keep, send, parts = own_d_norm()
        sent = lax.ppermute(send, "gy", swap)
        _, back = over_cores(keep, parts)
        input_grad, _ = input_gradient(*scale(keep, sent, back))
        total, passing = [
            lax.psum_scatter(p.astype(F32), "gx", scatter_dimension=0, tiled=True) for p in partial
        ]
        passed = lax.ppermute(passing.astype(BF16), "groups", swap)
        up_grad = call(place_halves_kernel, (total, passed), up_grad_of)
    return (input_grad[None], up_grad)


def solution(mesh):
    placed = (
        P(("groups", "gx"), None, None),
        P(("groups", "gx"), None, None),
        P(),
        P("gx", "gy"),
        P("gx", "gy"),
        P("groups"),
    )
    return jax.shard_map(
        shards,
        mesh=mesh,
        in_specs=placed,
        out_specs=(P(("groups", "gx"), None, "gy"), P(("groups", "gx"), "gy")),
        check_vma=False,
    )
```

```python
import functools

import jax
import jax.numpy as jnp
from jax import lax
from jax.experimental import pallas as pl
from jax.experimental.pallas import tpu as pltpu
from jax.sharding import PartitionSpec as P

BF16, F32 = jnp.bfloat16, jnp.float32
VMEM = pl.BlockSpec(memory_space=pltpu.VMEM)
HBM = pl.BlockSpec(memory_space=pltpu.HBM)
ANY = pl.BlockSpec(memory_space=pl.ANY)
SMEM = pl.BlockSpec(memory_space=pltpu.SMEM)


def shape(dims, kind):
    return jax.ShapeDtypeStruct(dims, kind)


def call(kernel, ins, out_shape, scratch=(), vmem=16, flops=1, left=(), pinned=(), out=VMEM, ties=()):
    count = len(ins)

    def body(*refs):
        kernel(*refs[:count], *refs[count + len(ties) :])

    moved = sum(x.size * x.dtype.itemsize for x in list(ins) + jax.tree.leaves(out_shape))
    return pl.pallas_call(
        body if ties else kernel,
        out_shape=out_shape,
        in_specs=[
            SMEM if x.dtype == jnp.int32 else ANY if i in left else HBM if i in pinned else VMEM
            for i, x in enumerate(ins)
        ]
        + [ANY] * len(ties),
        out_specs=jax.tree.map(lambda _: out, out_shape),
        scratch_shapes=list(scratch),
        compiler_params=pltpu.CompilerParams(vmem_limit_bytes=vmem << 20),
        cost_estimate=pl.CostEstimate(flops=flops, bytes_accessed=moved, transcendentals=0),
    )(*ins, *ties)


def hold(array, *ties):
    return pl.pallas_call(
        lambda *refs: None,
        out_shape=shape(array.shape, array.dtype),
        in_specs=[ANY] * (1 + len(ties)),
        out_specs=ANY,
        input_output_aliases={0: 0},
        compiler_params=pltpu.CompilerParams(vmem_limit_bytes=1 << 20),
        cost_estimate=pl.CostEstimate(flops=1, bytes_accessed=1, transcendentals=0),
    )(array, *ties)


def dot(left, right, left_dim=1, right_dim=0):
    return lax.dot_general(
        left, right, (((left_dim,), (right_dim,)), ((), ())), preferred_element_type=F32
    )


def gelu_slope(values):
    return (
        0.5 * (1.0 + lax.erf(values * 0.7071067811865476))
        + values * jnp.exp(-0.5 * values * values) * 0.3989422804014327
    )


def block_rows(step, peers, depth):
    own = lax.axis_index("gx")
    place = jnp.where(lax.rem(own, 2) == 0, lax.div(own, 2), peers - 1 - lax.div(own, 2))
    place = lax.rem(place + (step + peers), peers)
    member = jnp.where(place < peers // 2, 2 * place, 2 * (peers - 1 - place) + 1)
    return pl.ds(pl.multiple_of(member * depth, depth), depth)


def norm_rows(rows, gain):
    values = rows.astype(F32)
    centre = jnp.mean(values, axis=-1, keepdims=True)
    shifted = values - centre
    variance = jnp.mean(shifted * shifted, axis=-1, keepdims=True)
    inv_std = lax.rsqrt(variance + 1e-05)
    return (shifted * inv_std * gain[...][None]).astype(BF16), centre, inv_std


def mask_rows(rows, start, length):
    index = start + lax.broadcasted_iota(jnp.int32, (rows.shape[0], 1), 0)
    return jnp.where(index < length, rows.astype(F32), 0.0).astype(BF16)


def first_kernel(
    lengths, frames, out_grad, gain, w_up, w_down, passing, mine_up, mine_down, sems, rows, grads
):
    half, quarter = rows.shape[0], mine_up.shape[1]
    start = pl.multiple_of(lax.axis_index("gy") * half, half)
    columns = pl.ds(pl.multiple_of(lax.axis_index("groups") * quarter, quarter), quarter)
    moves = (
        (frames.at[pl.ds(start, half)], rows),
        (out_grad.at[pl.ds(start, half)], grads),
        (w_up.at[:, columns], mine_up),
        (w_down.at[:, columns], mine_down),
    )
    copies = [pltpu.make_async_copy(*move, sems.at[i]) for i, move in enumerate(moves)]
    for copy in copies:
        copy.start()
    copies[0].wait()
    passing[0] = norm_rows(rows[...], gain)[0]
    copies[1].wait()
    passing[1] = mask_rows(grads[...], start, lengths[lax.axis_index("gx")])
    copies[2].wait()
    copies[3].wait()


def norm_kernel(lengths, frames, out_grad, gain, normed, grads, stats):
    value, centre, inv_std = norm_rows(frames[...], gain)
    normed[...] = value
    stats[:, 0:1] = centre
    stats[:, 1:2] = inv_std
    grads[...] = mask_rows(out_grad[...], 0, lengths[lax.axis_index("gx")])


def back_through(normed, grads, up, down, d_pre, partial):
    pre_act = dot(normed[...], up[...])
    d_act = dot(grads[...], down[...])
    d_pre[...] = (d_act * gelu_slope(pre_act)).astype(BF16)
    partial[...] = dot(normed[...], d_pre[...], 0, 0).astype(BF16)


def place_kernel(places, peers, *refs):
    blocks, (up, down, sems) = refs[:-3], refs[-3:]
    copies = []
    for i, ((step, which), block) in enumerate(zip(places, blocks)):
        rows = block_rows(step, peers, block.shape[0])
        copies.append(pltpu.make_async_copy(block, (up, down)[which].at[rows], sems.at[i]))
    for copy in copies:
        copy.start()
    for copy in copies:
        copy.wait()


def own_kernel(places, sends, peers, normed, grads, near_up, near_down, *refs):
    late, refs = refs[: len(places)], refs[len(places) :]
    (d_pre, partial, up, down), blocks = refs[:4], refs[4:]
    up[...] = near_up[...]
    down[...] = near_down[...]
    for (step, which), block in zip(places, late):
        (up, down)[which][block_rows(step, peers, block.shape[0]), :] = block[...]
    back_through(normed, grads, up, down, d_pre, partial)
    for step, block in zip(sends, blocks):
        block[...] = partial[block_rows(step, peers, block.shape[0]), :]


def other_kernel(sends, peers, first, second, up, down, d_pre, partial, *refs):
    blocks, (normed, grads) = refs[:-2], refs[-2:]
    half = first.shape[1]
    for at, part in ((0, first), (half, second)):
        normed[at : at + half, :] = part[0]
        grads[at : at + half, :] = part[1]
    back_through(normed, grads, up, down, d_pre, partial)
    for step, block in zip(sends, blocks):
        block[...] = partial[block_rows(step, peers, block.shape[0]), :]


def d_norm_kernel(d_pre_own, d_pre_other, up, keep, send_own, *sends):
    core = lax.axis_index("gy")
    rows, width = keep.shape[1:]
    mine = up[pl.ds(pl.multiple_of(core * width, width), width), :]
    theirs = up[pl.ds(pl.multiple_of((1 - core) * width, width), width), :]
    keep[0] = dot(d_pre_own[...], mine, 1, 1).astype(BF16)
    keep[1] = dot(d_pre_other[...], mine, 1, 1).astype(BF16)
    send_own[...] = dot(d_pre_own[...], theirs, 1, 1).astype(BF16)
    sent = dot(d_pre_other[...], theirs, 1, 1).astype(BF16)
    sent = jnp.concatenate([sent[rows // 2 :], sent[: rows // 2]])
    step = rows // len(sends)
    for i, send in enumerate(sends):
        send[...] = sent[i * step : (i + 1) * step]


def over_kernel(keep, *refs):
    parts, over = refs[:-1], refs[-1]
    half = over.shape[0] // 2
    value = jnp.concatenate([part[...].astype(F32) for part in parts])
    value = (keep[1].astype(F32) + value).astype(BF16)
    for i in range(2):
        at = lax.rem(i + lax.axis_index("gy"), 2) * half
        over[pl.ds(pl.multiple_of(at, half), half), :] = value[i * half : (i + 1) * half]


def own_columns(ref, width):
    return ref[:, pl.ds(pl.multiple_of(lax.axis_index("gy") * width, width), width)]


def scale_kernel(keep, came, back, frames, gain, grads, stats, base, factor, sums):
    width = base.shape[1]
    d_norm = keep[0].astype(F32) + came[...].astype(F32) + back[...].astype(F32)
    scaled = d_norm * own_columns(gain, width)
    rows = own_columns(frames, width).astype(F32)
    inv_std = stats[:, 1:2]
    centred = (rows - stats[:, 0:1]) * inv_std
    sums[:, 0:1] = jnp.sum(scaled, axis=-1, keepdims=True)
    sums[:, 1:2] = jnp.sum(scaled * centred, axis=-1, keepdims=True)
    base[...] = own_columns(grads, width).astype(F32) + inv_std * scaled
    factor[...] = inv_std * centred


def input_kernel(base, factor, sums, came, stats, out, token):
    means = (sums[...] + came[...]) * (0.5 / base.shape[1])
    value = base[...] - stats[:, 1:2] * means[:, 0:1] - factor[...] * means[:, 1:2]
    out[...] = value.astype(BF16)
    token[...] = jnp.zeros_like(token)


def hop_kernel(places, peers, partial, *refs):
    count = len(places)
    for step, came, out in zip(places, refs[:count], refs[count:]):
        value = partial[block_rows(step, peers, out.shape[0]), :].astype(F32)
        out[...] = (value + came[...].astype(F32)).astype(BF16)


def total_kernel(peers, partial, up, down, total):
    value = partial[block_rows(0, peers, total.shape[0]), :].astype(F32)
    total[...] = (value + up[...].astype(F32) + down[...].astype(F32)).astype(BF16)


def join_kernel(peers, partial, up, down, passed, out):
    depth, width = passed.shape
    side = lax.axis_index("groups")
    value = partial[block_rows(0, peers, depth), :].astype(F32)
    value = value + up[...].astype(F32) + down[...].astype(F32)
    out[:, pl.ds(pl.multiple_of(side * width, width), width)] = value
    other = pl.ds(pl.multiple_of((1 - side) * width, width), width)
    out[:, other] = passed[...].astype(F32)


def place_halves_kernel(own, passed, out):
    width = own.shape[1]
    side = lax.axis_index("groups")
    out[:, pl.ds(pl.multiple_of(side * width, width), width)] = own[...]
    other = pl.ds(pl.multiple_of((1 - side) * width, width), width)
    out[:, other] = passed[...].astype(F32)


def shards(frames, out_grad, ln_gain, w_up, w_down, lengths):
    peers = lax.axis_size("gx")
    half = peers // 2
    frame_len, width = frames.shape[1:]
    depth, hidden = w_up.shape
    quarter = hidden // 2
    half_width = width // 2
    half_rows = frame_len // 2
    ringed = peers <= 16 and peers % 2 == 0 and depth % 16 == 0

    order = list(range(0, peers, 2)) + list(range(peers - 1, 0, -2))
    ahead = [(order[i], order[(i + 1) % peers]) for i in range(peers)]
    behind = [(b, a) for a, b in ahead]
    swap = [(0, 1), (1, 0)]

    frames, out_grad = frames[0], out_grad[0]
    rows_of = shape((frame_len, width), BF16)
    block_of = shape((depth, quarter), BF16)
    passing, *mine = call(
        first_kernel,
        (lengths, frames, out_grad, ln_gain, w_up, w_down),
        (shape((2, half_rows, width), BF16), block_of, block_of),
        [pltpu.SemaphoreType.DMA((4,))] + [pltpu.VMEM((half_rows, width), BF16)] * 2,
        flops=5 * frame_len * width,
        vmem=60,
        left=(1, 2, 4, 5),
    )
    first = lax.ppermute(passing, "groups", swap)
    normed, grads, stats = call(
        norm_kernel,
        (lengths, frames, out_grad, ln_gain),
        (rows_of, rows_of, shape((frame_len, 2), F32)),
        flops=10 * frame_len * width,
    )

    weight = shape((width, quarter), BF16)
    if ringed:
        blocks = {(0, 0): mine[0], (0, 1): mine[1]}
        up, down = list(mine), list(mine)
        for step in range(1, half):
            for i in range(2):
                up[i] = lax.ppermute(up[i], "gx", ahead)
                down[i] = lax.ppermute(down[i], "gx", behind)
            if step == 1:
                up[0] = hold(up[0], normed)
            for i in range(2):
                blocks[-step, i], blocks[step, i] = up[i], down[i]
        late = {
            (half - 1, 0): blocks.pop((half - 1, 0)),
            (1 - half, 1): blocks.pop((1 - half, 1)),
            (half, 0): lax.ppermute(up[0], "gx", ahead),
            (half, 1): lax.ppermute(down[1], "gx", behind),
        }
        near = call(
            functools.partial(place_kernel, tuple(blocks), peers),
            list(blocks.values()),
            (weight, weight),
            [pltpu.SemaphoreType.DMA((len(blocks),))],
            pinned=range(len(blocks)),
        )
        first = hold(first, *late.values(), near[0])
        sends = ((half - 1, -half), (half, 1 - half))
    else:
        near = [lax.all_gather(block, "gx", axis=0, tiled=True) for block in mine]
        late, sends = {}, ((), ())
    second = lax.ppermute(first, "gy", swap)

    d_pre_of, partial_of = shape((frame_len, quarter), BF16), shape((width, quarter), BF16)
    d_pre_own, partial_own, full_up, full_down, *blocks_own = call(
        functools.partial(own_kernel, tuple(late), sends[1], peers),
        (normed, grads, *near, *late.values()),
        (d_pre_of, partial_of, weight, weight, *[block_of] * len(sends[1])),
        flops=6 * frame_len * width * quarter,
    )
    d_pre_other, partial_other, *blocks_other = call(
        functools.partial(other_kernel, sends[0], peers),
        (first, second, full_up, full_down),
        (d_pre_of, partial_of, *[block_of] * len(sends[0])),
        [pltpu.VMEM((frame_len, width), BF16)] * 2,
        flops=6 * frame_len * width * quarter,
    )
    partial = [partial_own, partial_other]

    half_rows_of = shape((frame_len, half_width), BF16)
    parts_of = [half_rows_of]

    def own_d_norm(*ties):
        keep, send, *parts = call(
            d_norm_kernel,
            (d_pre_own, d_pre_other, full_up),
            (shape((2, frame_len, half_width), BF16), half_rows_of, *parts_of),
            flops=4 * frame_len * width * quarter,
            ties=ties,
        )
        return keep, send, [lax.ppermute(part, "gy", swap) for part in parts]

    def over_cores(keep, parts, *ties):
        over = call(over_kernel, (keep, *parts), half_rows_of, ties=ties)
        return over, lax.ppermute(over, "groups", swap)

    def scale(keep, came, back, *ties):
        return call(
            scale_kernel,
            (keep, came, back, frames, ln_gain[None], grads, stats),
            (
                shape((frame_len, half_width), F32),
                shape((frame_len, half_width), F32),
                shape((frame_len, 2), F32),
            ),
            ties=ties,
        )

    def input_gradient(base, factor, sums):
        return call(
            input_kernel,
            (base, factor, sums, lax.ppermute(sums, "gy", swap), stats),
            (half_rows_of, shape((8, 128), F32)),
        )

    up_grad_of = shape((depth, hidden), F32)
    if ringed:
        came = [{}, {}]

        def send_on(i, blocks, names):
            for block, name in zip(blocks, names):
                came[i][name] = lax.ppermute(block, "gx", ahead if name == "up" else behind)

        def hop(i, turn, *ties):
            ways = [("up", half - turn - i), ("down", turn + 1 - i - half)]
            ways = [way for way in ways if way[1] != 0]
            names = [name for name, _ in ways]
            ties += tuple(came[i][name] for name in came[i] if name not in names)
            blocks = call(
                functools.partial(hop_kernel, tuple(step for _, step in ways), peers),
                (partial[i], *[came[i][name] for name in names]),
                [block_of] * len(ways),
                ties=ties,
            )
            send_on(i, blocks, names)
            return blocks[0]

        send_on(0, blocks_own, ("up", "down"))
        send_on(1, blocks_other, ("up", "down"))
        keep, send, parts = own_d_norm(*came[0].values())
        tie = hop(1, 1, keep)
        tie = hop(0, 1, tie)
        tie = hop(1, 2, tie)
        tie = hop(0, 2, tie)
        tie, back = over_cores(keep, parts, tie)
        for turn in range(3, half):
            tie = hop(0, turn, hop(1, turn, tie))
        sent = lax.ppermute(send, "gy", swap)
        passing = call(
            functools.partial(total_kernel, peers),
            (partial[1], came[1]["up"], came[1]["down"]),
            block_of,
            ties=(tie,),
        )
        passed = lax.ppermute(passing, "groups", swap)
        input_grad, token = input_gradient(*scale(keep, sent, back, passing))
        up_grad = call(
            functools.partial(join_kernel, peers),
            (partial[0], came[0]["up"], came[0]["down"], passed),
            up_grad_of,
            ties=(token,),
        )
    else:
        keep, send, parts = own_d_norm()
        sent = lax.ppermute(send, "gy", swap)
        _, back = over_cores(keep, parts)
        input_grad, _ = input_gradient(*scale(keep, sent, back))
        total, passing = [
            lax.psum_scatter(p.astype(F32), "gx", scatter_dimension=0, tiled=True) for p in partial
        ]
        passed = lax.ppermute(passing.astype(BF16), "groups", swap)
        up_grad = call(place_halves_kernel, (total, passed), up_grad_of)
    return (input_grad[None], up_grad)


def solution(mesh):
    placed = (
        P(("groups", "gx"), None, None),
        P(("groups", "gx"), None, None),
        P(),
        P("gx", "gy"),
        P("gx", "gy"),
        P("groups"),
    )
    return jax.shard_map(
        shards,
        mesh=mesh,
        in_specs=placed,
        out_specs=(P(("groups", "gx"), None, "gy"), P(("groups", "gx"), "gy")),
        check_vma=False,
    )
```

```python
import functools

import jax
import jax.numpy as jnp
from jax import lax
from jax.experimental import pallas as pl
from jax.experimental.pallas import tpu as pltpu
from jax.sharding import PartitionSpec as P

BF16, F32 = jnp.bfloat16, jnp.float32
VMEM = pl.BlockSpec(memory_space=pltpu.VMEM)
HBM = pl.BlockSpec(memory_space=pltpu.HBM)
ANY = pl.BlockSpec(memory_space=pl.ANY)
SMEM = pl.BlockSpec(memory_space=pltpu.SMEM)


def shape(dims, kind):
    return jax.ShapeDtypeStruct(dims, kind)


def call(kernel, ins, out_shape, scratch=(), vmem=16, flops=1, left=(), pinned=(), out=VMEM, ties=()):
    count = len(ins)

    def body(*refs):
        kernel(*refs[:count], *refs[count + len(ties) :])

    moved = sum(x.size * x.dtype.itemsize for x in list(ins) + jax.tree.leaves(out_shape))
    return pl.pallas_call(
        body if ties else kernel,
        out_shape=out_shape,
        in_specs=[
            SMEM if x.dtype == jnp.int32 else ANY if i in left else HBM if i in pinned else VMEM
            for i, x in enumerate(ins)
        ]
        + [ANY] * len(ties),
        out_specs=jax.tree.map(lambda _: out, out_shape),
        scratch_shapes=list(scratch),
        compiler_params=pltpu.CompilerParams(vmem_limit_bytes=vmem << 20),
        cost_estimate=pl.CostEstimate(flops=flops, bytes_accessed=moved, transcendentals=0),
    )(*ins, *ties)


def hold(array, *ties):
    return pl.pallas_call(
        lambda *refs: None,
        out_shape=shape(array.shape, array.dtype),
        in_specs=[ANY] * (1 + len(ties)),
        out_specs=ANY,
        input_output_aliases={0: 0},
        compiler_params=pltpu.CompilerParams(vmem_limit_bytes=1 << 20),
        cost_estimate=pl.CostEstimate(flops=1, bytes_accessed=1, transcendentals=0),
    )(array, *ties)


def dot(left, right, left_dim=1, right_dim=0):
    return lax.dot_general(
        left, right, (((left_dim,), (right_dim,)), ((), ())), preferred_element_type=F32
    )


def gelu_slope(values):
    return (
        0.5 * (1.0 + lax.erf(values * 0.7071067811865476))
        + values * jnp.exp(-0.5 * values * values) * 0.3989422804014327
    )


def block_rows(step, peers, depth):
    own = lax.axis_index("gx")
    place = jnp.where(lax.rem(own, 2) == 0, lax.div(own, 2), peers - 1 - lax.div(own, 2))
    place = lax.rem(place + (step + peers), peers)
    member = jnp.where(place < peers // 2, 2 * place, 2 * (peers - 1 - place) + 1)
    return pl.ds(pl.multiple_of(member * depth, depth), depth)


def norm_rows(rows, gain):
    values = rows.astype(F32)
    centre = jnp.mean(values, axis=-1, keepdims=True)
    shifted = values - centre
    variance = jnp.mean(shifted * shifted, axis=-1, keepdims=True)
    inv_std = lax.rsqrt(variance + 1e-05)
    return (shifted * inv_std * gain[...][None]).astype(BF16), centre, inv_std


def mask_rows(rows, start, length):
    index = start + lax.broadcasted_iota(jnp.int32, (rows.shape[0], 1), 0)
    return jnp.where(index < length, rows.astype(F32), 0.0).astype(BF16)


def first_kernel(
    lengths, frames, out_grad, gain, w_up, w_down, passing, mine_up, mine_down, sems, rows, grads
):
    half, quarter = rows.shape[0], mine_up.shape[1]
    start = pl.multiple_of(lax.axis_index("gy") * half, half)
    columns = pl.ds(pl.multiple_of(lax.axis_index("groups") * quarter, quarter), quarter)
    moves = (
        (frames.at[pl.ds(start, half)], rows),
        (out_grad.at[pl.ds(start, half)], grads),
        (w_up.at[:, columns], mine_up),
        (w_down.at[:, columns], mine_down),
    )
    copies = [pltpu.make_async_copy(*move, sems.at[i]) for i, move in enumerate(moves)]
    for copy in copies:
        copy.start()
    copies[0].wait()
    passing[0] = norm_rows(rows[...], gain)[0]
    copies[1].wait()
    passing[1] = mask_rows(grads[...], start, lengths[lax.axis_index("gx")])
    copies[2].wait()
    copies[3].wait()


def norm_kernel(lengths, frames, out_grad, gain, normed, grads, stats):
    value, centre, inv_std = norm_rows(frames[...], gain)
    normed[...] = value
    stats[:, 0:1] = centre
    stats[:, 1:2] = inv_std
    grads[...] = mask_rows(out_grad[...], 0, lengths[lax.axis_index("gx")])


def back_through(normed, grads, up, down, d_pre, partial):
    pre_act = dot(normed[...], up[...])
    d_act = dot(grads[...], down[...])
    d_pre[...] = (d_act * gelu_slope(pre_act)).astype(BF16)
    partial[...] = dot(normed[...], d_pre[...], 0, 0).astype(BF16)


def place_kernel(places, peers, *refs):
    blocks, (up, down, sems) = refs[:-3], refs[-3:]
    copies = []
    for i, ((step, which), block) in enumerate(zip(places, blocks)):
        rows = block_rows(step, peers, block.shape[0])
        copies.append(pltpu.make_async_copy(block, (up, down)[which].at[rows], sems.at[i]))
    for copy in copies:
        copy.start()
    for copy in copies:
        copy.wait()


def own_kernel(places, sends, peers, normed, grads, near_up, near_down, *refs):
    late, refs = refs[: len(places)], refs[len(places) :]
    (d_pre, partial, up, down), blocks = refs[:4], refs[4:]
    up[...] = near_up[...]
    down[...] = near_down[...]
    for (step, which), block in zip(places, late):
        (up, down)[which][block_rows(step, peers, block.shape[0]), :] = block[...]
    back_through(normed, grads, up, down, d_pre, partial)
    for step, block in zip(sends, blocks):
        block[...] = partial[block_rows(step, peers, block.shape[0]), :]


def other_kernel(sends, peers, first, second, up, down, d_pre, partial, *refs):
    blocks, (normed, grads) = refs[:-2], refs[-2:]
    half = first.shape[1]
    for at, part in ((0, first), (half, second)):
        normed[at : at + half, :] = part[0]
        grads[at : at + half, :] = part[1]
    back_through(normed, grads, up, down, d_pre, partial)
    for step, block in zip(sends, blocks):
        block[...] = partial[block_rows(step, peers, block.shape[0]), :]


def d_norm_kernel(d_pre_own, d_pre_other, up, keep, send_own, *sends):
    core = lax.axis_index("gy")
    rows, width = keep.shape[1:]
    mine = up[pl.ds(pl.multiple_of(core * width, width), width), :]
    theirs = up[pl.ds(pl.multiple_of((1 - core) * width, width), width), :]
    keep[0] = dot(d_pre_own[...], mine, 1, 1).astype(BF16)
    keep[1] = dot(d_pre_other[...], mine, 1, 1).astype(BF16)
    send_own[...] = dot(d_pre_own[...], theirs, 1, 1).astype(BF16)
    sent = dot(d_pre_other[...], theirs, 1, 1).astype(BF16)
    sent = jnp.concatenate([sent[rows // 2 :], sent[: rows // 2]])
    step = rows // len(sends)
    for i, send in enumerate(sends):
        send[...] = sent[i * step : (i + 1) * step]


def over_kernel(keep, *refs):
    parts, over = refs[:-1], refs[-1]
    half = over.shape[0] // 2
    value = jnp.concatenate([part[...].astype(F32) for part in parts])
    value = (keep[1].astype(F32) + value).astype(BF16)
    for i in range(2):
        at = lax.rem(i + lax.axis_index("gy"), 2) * half
        over[pl.ds(pl.multiple_of(at, half), half), :] = value[i * half : (i + 1) * half]


def own_columns(ref, width):
    return ref[:, pl.ds(pl.multiple_of(lax.axis_index("gy") * width, width), width)]


def scale_kernel(keep, came, back, frames, gain, grads, stats, base, factor, sums):
    width = base.shape[1]
    d_norm = keep[0].astype(F32) + came[...].astype(F32) + back[...].astype(F32)
    scaled = d_norm * own_columns(gain, width)
    rows = own_columns(frames, width).astype(F32)
    inv_std = stats[:, 1:2]
    centred = (rows - stats[:, 0:1]) * inv_std
    sums[:, 0:1] = jnp.sum(scaled, axis=-1, keepdims=True)
    sums[:, 1:2] = jnp.sum(scaled * centred, axis=-1, keepdims=True)
    base[...] = own_columns(grads, width).astype(F32) + inv_std * scaled
    factor[...] = inv_std * centred


def input_kernel(base, factor, sums, came, stats, out, token):
    means = (sums[...] + came[...]) * (0.5 / base.shape[1])
    value = base[...] - stats[:, 1:2] * means[:, 0:1] - factor[...] * means[:, 1:2]
    out[...] = value.astype(BF16)
    token[...] = jnp.zeros_like(token)


def hop_kernel(places, peers, partial, *refs):
    count = len(places)
    for step, came, out in zip(places, refs[:count], refs[count:]):
        value = partial[block_rows(step, peers, out.shape[0]), :].astype(F32)
        out[...] = (value + came[...].astype(F32)).astype(BF16)


def total_kernel(peers, partial, up, down, total):
    value = partial[block_rows(0, peers, total.shape[0]), :].astype(F32)
    total[...] = (value + up[...].astype(F32) + down[...].astype(F32)).astype(BF16)


def join_kernel(peers, partial, up, down, passed, out):
    depth, width = passed.shape
    side = lax.axis_index("groups")
    value = partial[block_rows(0, peers, depth), :].astype(F32)
    value = value + up[...].astype(F32) + down[...].astype(F32)
    out[:, pl.ds(pl.multiple_of(side * width, width), width)] = value
    other = pl.ds(pl.multiple_of((1 - side) * width, width), width)
    out[:, other] = passed[...].astype(F32)


def place_halves_kernel(own, passed, out):
    width = own.shape[1]
    side = lax.axis_index("groups")
    out[:, pl.ds(pl.multiple_of(side * width, width), width)] = own[...]
    other = pl.ds(pl.multiple_of((1 - side) * width, width), width)
    out[:, other] = passed[...].astype(F32)


def shards(frames, out_grad, ln_gain, w_up, w_down, lengths):
    peers = lax.axis_size("gx")
    half = peers // 2
    frame_len, width = frames.shape[1:]
    depth, hidden = w_up.shape
    quarter = hidden // 2
    half_width = width // 2
    half_rows = frame_len // 2
    ringed = peers <= 16 and peers % 2 == 0 and depth % 16 == 0

    order = list(range(0, peers, 2)) + list(range(peers - 1, 0, -2))
    ahead = [(order[i], order[(i + 1) % peers]) for i in range(peers)]
    behind = [(b, a) for a, b in ahead]
    swap = [(0, 1), (1, 0)]

    frames, out_grad = frames[0], out_grad[0]
    rows_of = shape((frame_len, width), BF16)
    block_of = shape((depth, quarter), BF16)
    passing, *mine = call(
        first_kernel,
        (lengths, frames, out_grad, ln_gain, w_up, w_down),
        (shape((2, half_rows, width), BF16), block_of, block_of),
        [pltpu.SemaphoreType.DMA((4,))] + [pltpu.VMEM((half_rows, width), BF16)] * 2,
        flops=5 * frame_len * width,
        vmem=60,
        left=(1, 2, 4, 5),
    )
    first = lax.ppermute(passing, "groups", swap)
    normed, grads, stats = call(
        norm_kernel,
        (lengths, frames, out_grad, ln_gain),
        (rows_of, rows_of, shape((frame_len, 2), F32)),
        flops=10 * frame_len * width,
    )

    weight = shape((width, quarter), BF16)
    if ringed:
        blocks = {(0, 0): mine[0], (0, 1): mine[1]}
        up, down = list(mine), list(mine)
        for step in range(1, half):
            for i in range(2):
                up[i] = lax.ppermute(up[i], "gx", ahead)
                down[i] = lax.ppermute(down[i], "gx", behind)
            if step == 1:
                up[0] = hold(up[0], normed)
            for i in range(2):
                blocks[-step, i], blocks[step, i] = up[i], down[i]
        late = {
            (half - 1, 0): blocks.pop((half - 1, 0)),
            (1 - half, 1): blocks.pop((1 - half, 1)),
            (half, 0): lax.ppermute(up[0], "gx", ahead),
            (half, 1): lax.ppermute(down[1], "gx", behind),
        }
        near = call(
            functools.partial(place_kernel, tuple(blocks), peers),
            list(blocks.values()),
            (weight, weight),
            [pltpu.SemaphoreType.DMA((len(blocks),))],
            pinned=range(len(blocks)),
        )
        first = hold(first, *late.values(), near[0])
        sends = ((half - 1, -half), (half, 1 - half))
    else:
        near = [lax.all_gather(block, "gx", axis=0, tiled=True) for block in mine]
        late, sends = {}, ((), ())
    second = lax.ppermute(first, "gy", swap)

    d_pre_of, partial_of = shape((frame_len, quarter), BF16), shape((width, quarter), BF16)
    d_pre_own, partial_own, full_up, full_down, *blocks_own = call(
        functools.partial(own_kernel, tuple(late), sends[1], peers),
        (normed, grads, *near, *late.values()),
        (d_pre_of, partial_of, weight, weight, *[block_of] * len(sends[1])),
        flops=6 * frame_len * width * quarter,
    )
    d_pre_other, partial_other, *blocks_other = call(
        functools.partial(other_kernel, sends[0], peers),
        (first, second, full_up, full_down),
        (d_pre_of, partial_of, *[block_of] * len(sends[0])),
        [pltpu.VMEM((frame_len, width), BF16)] * 2,
        flops=6 * frame_len * width * quarter,
    )
    partial = [partial_own, partial_other]

    half_rows_of = shape((frame_len, half_width), BF16)
    parts_of = [half_rows_of]

    def own_d_norm(*ties):
        keep, send, *parts = call(
            d_norm_kernel,
            (d_pre_own, d_pre_other, full_up),
            (shape((2, frame_len, half_width), BF16), half_rows_of, *parts_of),
            flops=4 * frame_len * width * quarter,
            ties=ties,
        )
        return keep, send, [lax.ppermute(part, "gy", swap) for part in parts]

    def over_cores(keep, parts, *ties):
        over = call(over_kernel, (keep, *parts), half_rows_of, ties=ties)
        return over, lax.ppermute(over, "groups", swap)

    def scale(keep, came, back, *ties):
        return call(
            scale_kernel,
            (keep, came, back, frames, ln_gain[None], grads, stats),
            (
                shape((frame_len, half_width), F32),
                shape((frame_len, half_width), F32),
                shape((frame_len, 2), F32),
            ),
            ties=ties,
        )

    def input_gradient(base, factor, sums):
        return call(
            input_kernel,
            (base, factor, sums, lax.ppermute(sums, "gy", swap), stats),
            (half_rows_of, shape((8, 128), F32)),
        )

    up_grad_of = shape((depth, hidden), F32)
    if ringed:
        came = [{}, {}]

        def send_on(i, blocks, names):
            for block, name in zip(blocks, names):
                came[i][name] = lax.ppermute(block, "gx", ahead if name == "up" else behind)

        def hop(i, turn, *ties):
            ways = [("up", half - turn - i), ("down", turn + 1 - i - half)]
            ways = [way for way in ways if way[1] != 0]
            names = [name for name, _ in ways]
            ties += tuple(came[i][name] for name in came[i] if name not in names)
            blocks = call(
                functools.partial(hop_kernel, tuple(step for _, step in ways), peers),
                (partial[i], *[came[i][name] for name in names]),
                [block_of] * len(ways),
                ties=ties,
            )
            send_on(i, blocks, names)
            return blocks[0]

        send_on(0, blocks_own, ("up", "down"))
        send_on(1, blocks_other, ("up", "down"))
        tie = hop(0, 1, partial_other)
        keep, send, parts = own_d_norm(tie)
        tie = hop(1, 1, keep)
        tie = hop(0, 2, tie)
        tie = hop(1, 2, tie)
        tie, back = over_cores(keep, parts, tie)
        for turn in range(3, half):
            tie = hop(0, turn, hop(1, turn, tie))
        sent = lax.ppermute(send, "gy", swap)
        passing = call(
            functools.partial(total_kernel, peers),
            (partial[1], came[1]["up"], came[1]["down"]),
            block_of,
            ties=(tie,),
        )
        passed = lax.ppermute(passing, "groups", swap)
        input_grad, token = input_gradient(*scale(keep, sent, back, passing))
        up_grad = call(
            functools.partial(join_kernel, peers),
            (partial[0], came[0]["up"], came[0]["down"], passed),
            up_grad_of,
            ties=(token,),
        )
    else:
        keep, send, parts = own_d_norm()
        sent = lax.ppermute(send, "gy", swap)
        _, back = over_cores(keep, parts)
        input_grad, _ = input_gradient(*scale(keep, sent, back))
        total, passing = [
            lax.psum_scatter(p.astype(F32), "gx", scatter_dimension=0, tiled=True) for p in partial
        ]
        passed = lax.ppermute(passing.astype(BF16), "groups", swap)
        up_grad = call(place_halves_kernel, (total, passed), up_grad_of)
    return (input_grad[None], up_grad)


def solution(mesh):
    placed = (
        P(("groups", "gx"), None, None),
        P(("groups", "gx"), None, None),
        P(),
        P("gx", "gy"),
        P("gx", "gy"),
        P("groups"),
    )
    return jax.shard_map(
        shards,
        mesh=mesh,
        in_specs=placed,
        out_specs=(P(("groups", "gx"), None, "gy"), P(("groups", "gx"), "gy")),
        check_vma=False,
    )
```

```python
import functools

import jax
import jax.numpy as jnp
from jax import lax
from jax.experimental import pallas as pl
from jax.experimental.pallas import tpu as pltpu
from jax.sharding import PartitionSpec as P

BF16, F32 = jnp.bfloat16, jnp.float32
VMEM = pl.BlockSpec(memory_space=pltpu.VMEM)
HBM = pl.BlockSpec(memory_space=pltpu.HBM)
ANY = pl.BlockSpec(memory_space=pl.ANY)
SMEM = pl.BlockSpec(memory_space=pltpu.SMEM)


def shape(dims, kind):
    return jax.ShapeDtypeStruct(dims, kind)


def call(kernel, ins, out_shape, scratch=(), vmem=16, flops=1, left=(), pinned=(), out=VMEM, ties=()):
    count = len(ins)

    def body(*refs):
        kernel(*refs[:count], *refs[count + len(ties) :])

    moved = sum(x.size * x.dtype.itemsize for x in list(ins) + jax.tree.leaves(out_shape))
    return pl.pallas_call(
        body if ties else kernel,
        out_shape=out_shape,
        in_specs=[
            SMEM if x.dtype == jnp.int32 else ANY if i in left else HBM if i in pinned else VMEM
            for i, x in enumerate(ins)
        ]
        + [ANY] * len(ties),
        out_specs=jax.tree.map(lambda _: out, out_shape),
        scratch_shapes=list(scratch),
        compiler_params=pltpu.CompilerParams(vmem_limit_bytes=vmem << 20),
        cost_estimate=pl.CostEstimate(flops=flops, bytes_accessed=moved, transcendentals=0),
    )(*ins, *ties)


def hold(array, *ties):
    return pl.pallas_call(
        lambda *refs: None,
        out_shape=shape(array.shape, array.dtype),
        in_specs=[ANY] * (1 + len(ties)),
        out_specs=ANY,
        input_output_aliases={0: 0},
        compiler_params=pltpu.CompilerParams(vmem_limit_bytes=1 << 20),
        cost_estimate=pl.CostEstimate(flops=1, bytes_accessed=1, transcendentals=0),
    )(array, *ties)


def dot(left, right, left_dim=1, right_dim=0):
    return lax.dot_general(
        left, right, (((left_dim,), (right_dim,)), ((), ())), preferred_element_type=F32
    )


def gelu_slope(values):
    return (
        0.5 * (1.0 + lax.erf(values * 0.7071067811865476))
        + values * jnp.exp(-0.5 * values * values) * 0.3989422804014327
    )


def block_rows(step, peers, depth):
    own = lax.axis_index("gx")
    place = jnp.where(lax.rem(own, 2) == 0, lax.div(own, 2), peers - 1 - lax.div(own, 2))
    place = lax.rem(place + (step + peers), peers)
    member = jnp.where(place < peers // 2, 2 * place, 2 * (peers - 1 - place) + 1)
    return pl.ds(pl.multiple_of(member * depth, depth), depth)


def norm_rows(rows, gain):
    values = rows.astype(F32)
    centre = jnp.mean(values, axis=-1, keepdims=True)
    shifted = values - centre
    variance = jnp.mean(shifted * shifted, axis=-1, keepdims=True)
    inv_std = lax.rsqrt(variance + 1e-05)
    return (shifted * inv_std * gain[...][None]).astype(BF16), centre, inv_std


def mask_rows(rows, start, length):
    index = start + lax.broadcasted_iota(jnp.int32, (rows.shape[0], 1), 0)
    return jnp.where(index < length, rows.astype(F32), 0.0).astype(BF16)


def first_kernel(
    lengths, frames, out_grad, gain, w_up, w_down, passing, mine_up, mine_down, sems, rows, grads
):
    half, quarter = rows.shape[0], mine_up.shape[1]
    start = pl.multiple_of(lax.axis_index("gy") * half, half)
    columns = pl.ds(pl.multiple_of(lax.axis_index("groups") * quarter, quarter), quarter)
    moves = (
        (frames.at[pl.ds(start, half)], rows),
        (out_grad.at[pl.ds(start, half)], grads),
        (w_up.at[:, columns], mine_up),
        (w_down.at[:, columns], mine_down),
    )
    copies = [pltpu.make_async_copy(*move, sems.at[i]) for i, move in enumerate(moves)]
    for copy in copies:
        copy.start()
    copies[0].wait()
    passing[0] = norm_rows(rows[...], gain)[0]
    copies[1].wait()
    passing[1] = mask_rows(grads[...], start, lengths[lax.axis_index("gx")])
    copies[2].wait()
    copies[3].wait()


def norm_kernel(lengths, frames, out_grad, gain, normed, grads, stats):
    value, centre, inv_std = norm_rows(frames[...], gain)
    normed[...] = value
    stats[:, 0:1] = centre
    stats[:, 1:2] = inv_std
    grads[...] = mask_rows(out_grad[...], 0, lengths[lax.axis_index("gx")])


def back_through(normed, grads, up, down, d_pre, partial):
    pre_act = dot(normed[...], up[...])
    d_act = dot(grads[...], down[...])
    d_pre[...] = (d_act * gelu_slope(pre_act)).astype(BF16)
    partial[...] = dot(normed[...], d_pre[...], 0, 0).astype(BF16)


def place_kernel(places, peers, *refs):
    blocks, (up, down, sems) = refs[:-3], refs[-3:]
    copies = []
    for i, ((step, which), block) in enumerate(zip(places, blocks)):
        rows = block_rows(step, peers, block.shape[0])
        copies.append(pltpu.make_async_copy(block, (up, down)[which].at[rows], sems.at[i]))
    for copy in copies:
        copy.start()
    for copy in copies:
        copy.wait()


def own_kernel(places, sends, peers, normed, grads, near_up, near_down, *refs):
    late, refs = refs[: len(places)], refs[len(places) :]
    (d_pre, partial, up, down), blocks = refs[:4], refs[4:]
    up[...] = near_up[...]
    down[...] = near_down[...]
    for (step, which), block in zip(places, late):
        (up, down)[which][block_rows(step, peers, block.shape[0]), :] = block[...]
    back_through(normed, grads, up, down, d_pre, partial)
    for step, block in zip(sends, blocks):
        block[...] = partial[block_rows(step, peers, block.shape[0]), :]


def other_kernel(sends, peers, first, second, up, down, d_pre, partial, *refs):
    blocks, (normed, grads) = refs[:-2], refs[-2:]
    half = first.shape[1]
    for at, part in ((0, first), (half, second)):
        normed[at : at + half, :] = part[0]
        grads[at : at + half, :] = part[1]
    back_through(normed, grads, up, down, d_pre, partial)
    for step, block in zip(sends, blocks):
        block[...] = partial[block_rows(step, peers, block.shape[0]), :]


def d_norm_kernel(d_pre_own, d_pre_other, up, keep, send_own, *sends):
    core = lax.axis_index("gy")
    rows, width = keep.shape[1:]
    mine = up[pl.ds(pl.multiple_of(core * width, width), width), :]
    theirs = up[pl.ds(pl.multiple_of((1 - core) * width, width), width), :]
    keep[0] = dot(d_pre_own[...], mine, 1, 1).astype(BF16)
    keep[1] = dot(d_pre_other[...], mine, 1, 1).astype(BF16)
    send_own[...] = dot(d_pre_own[...], theirs, 1, 1).astype(BF16)
    sent = dot(d_pre_other[...], theirs, 1, 1).astype(BF16)
    sent = jnp.concatenate([sent[rows // 2 :], sent[: rows // 2]])
    step = rows // len(sends)
    for i, send in enumerate(sends):
        send[...] = sent[i * step : (i + 1) * step]


def over_kernel(keep, *refs):
    parts, over = refs[:-1], refs[-1]
    half = over.shape[0] // 2
    value = jnp.concatenate([part[...].astype(F32) for part in parts])
    value = (keep[1].astype(F32) + value).astype(BF16)
    for i in range(2):
        at = lax.rem(i + lax.axis_index("gy"), 2) * half
        over[pl.ds(pl.multiple_of(at, half), half), :] = value[i * half : (i + 1) * half]


def own_columns(ref, width):
    return ref[:, pl.ds(pl.multiple_of(lax.axis_index("gy") * width, width), width)]


def scale_kernel(keep, came, back, frames, gain, grads, stats, base, factor, sums):
    width = base.shape[1]
    d_norm = keep[0].astype(F32) + came[...].astype(F32) + back[...].astype(F32)
    scaled = d_norm * own_columns(gain, width)
    rows = own_columns(frames, width).astype(F32)
    inv_std = stats[:, 1:2]
    centred = (rows - stats[:, 0:1]) * inv_std
    sums[:, 0:1] = jnp.sum(scaled, axis=-1, keepdims=True)
    sums[:, 1:2] = jnp.sum(scaled * centred, axis=-1, keepdims=True)
    base[...] = own_columns(grads, width).astype(F32) + inv_std * scaled
    factor[...] = inv_std * centred


def input_kernel(base, factor, sums, came, stats, out, token):
    means = (sums[...] + came[...]) * (0.5 / base.shape[1])
    value = base[...] - stats[:, 1:2] * means[:, 0:1] - factor[...] * means[:, 1:2]
    out[...] = value.astype(BF16)
    token[...] = jnp.zeros_like(token)


def hop_kernel(places, peers, partial, *refs):
    count = len(places)
    for step, came, out in zip(places, refs[:count], refs[count:]):
        value = partial[block_rows(step, peers, out.shape[0]), :].astype(F32)
        out[...] = (value + came[...].astype(F32)).astype(BF16)


def total_kernel(peers, partial, up, down, total):
    value = partial[block_rows(0, peers, total.shape[0]), :].astype(F32)
    total[...] = (value + up[...].astype(F32) + down[...].astype(F32)).astype(BF16)


def join_kernel(peers, partial, up, down, passed, out):
    depth, width = passed.shape
    side = lax.axis_index("groups")
    value = partial[block_rows(0, peers, depth), :].astype(F32)
    value = value + up[...].astype(F32) + down[...].astype(F32)
    out[:, pl.ds(pl.multiple_of(side * width, width), width)] = value
    other = pl.ds(pl.multiple_of((1 - side) * width, width), width)
    out[:, other] = passed[...].astype(F32)


def place_halves_kernel(own, passed, out):
    width = own.shape[1]
    side = lax.axis_index("groups")
    out[:, pl.ds(pl.multiple_of(side * width, width), width)] = own[...]
    other = pl.ds(pl.multiple_of((1 - side) * width, width), width)
    out[:, other] = passed[...].astype(F32)


def shards(frames, out_grad, ln_gain, w_up, w_down, lengths):
    peers = lax.axis_size("gx")
    half = peers // 2
    frame_len, width = frames.shape[1:]
    depth, hidden = w_up.shape
    quarter = hidden // 2
    half_width = width // 2
    half_rows = frame_len // 2
    ringed = peers <= 16 and peers % 2 == 0 and depth % 16 == 0

    order = list(range(0, peers, 2)) + list(range(peers - 1, 0, -2))
    ahead = [(order[i], order[(i + 1) % peers]) for i in range(peers)]
    behind = [(b, a) for a, b in ahead]
    swap = [(0, 1), (1, 0)]

    frames, out_grad = frames[0], out_grad[0]
    rows_of = shape((frame_len, width), BF16)
    block_of = shape((depth, quarter), BF16)
    passing, *mine = call(
        first_kernel,
        (lengths, frames, out_grad, ln_gain, w_up, w_down),
        (shape((2, half_rows, width), BF16), block_of, block_of),
        [pltpu.SemaphoreType.DMA((4,))] + [pltpu.VMEM((half_rows, width), BF16)] * 2,
        flops=5 * frame_len * width,
        vmem=60,
        left=(1, 2, 4, 5),
    )
    first = lax.ppermute(passing, "groups", swap)
    normed, grads, stats = call(
        norm_kernel,
        (lengths, frames, out_grad, ln_gain),
        (rows_of, rows_of, shape((frame_len, 2), F32)),
        flops=10 * frame_len * width,
    )

    weight = shape((width, quarter), BF16)
    if ringed:
        blocks = {(0, 0): mine[0], (0, 1): mine[1]}
        up, down = list(mine), list(mine)
        for step in range(1, half):
            for i in range(2):
                up[i] = lax.ppermute(up[i], "gx", ahead)
                down[i] = lax.ppermute(down[i], "gx", behind)
            if step == 1:
                up[0] = hold(up[0], normed)
            for i in range(2):
                blocks[-step, i], blocks[step, i] = up[i], down[i]
        late = {
            (half - 1, 0): blocks.pop((half - 1, 0)),
            (1 - half, 1): blocks.pop((1 - half, 1)),
            (half, 0): lax.ppermute(up[0], "gx", ahead),
            (half, 1): lax.ppermute(down[1], "gx", behind),
        }
        near = call(
            functools.partial(place_kernel, tuple(blocks), peers),
            list(blocks.values()),
            (weight, weight),
            [pltpu.SemaphoreType.DMA((len(blocks),))],
            pinned=range(len(blocks)),
        )
        first = hold(first, *late.values(), near[0])
        sends = ((half - 1, -half), (half, 1 - half))
    else:
        near = [lax.all_gather(block, "gx", axis=0, tiled=True) for block in mine]
        late, sends = {}, ((), ())
    second = lax.ppermute(first, "gy", swap)

    d_pre_of, partial_of = shape((frame_len, quarter), BF16), shape((width, quarter), BF16)
    d_pre_own, partial_own, full_up, full_down, *blocks_own = call(
        functools.partial(own_kernel, tuple(late), sends[1], peers),
        (normed, grads, *near, *late.values()),
        (d_pre_of, partial_of, weight, weight, *[block_of] * len(sends[1])),
        flops=6 * frame_len * width * quarter,
    )
    d_pre_other, partial_other, *blocks_other = call(
        functools.partial(other_kernel, sends[0], peers),
        (first, second, full_up, full_down),
        (d_pre_of, partial_of, *[block_of] * len(sends[0])),
        [pltpu.VMEM((frame_len, width), BF16)] * 2,
        flops=6 * frame_len * width * quarter,
    )
    partial = [partial_own, partial_other]

    half_rows_of = shape((frame_len, half_width), BF16)
    parts_of = [half_rows_of]

    def own_d_norm(*ties):
        keep, send, *parts = call(
            d_norm_kernel,
            (d_pre_own, d_pre_other, full_up),
            (shape((2, frame_len, half_width), BF16), half_rows_of, *parts_of),
            flops=4 * frame_len * width * quarter,
            ties=ties,
        )
        return keep, send, [lax.ppermute(part, "gy", swap) for part in parts]

    def over_cores(keep, parts, *ties):
        over = call(over_kernel, (keep, *parts), half_rows_of, ties=ties)
        return over, lax.ppermute(over, "groups", swap)

    def scale(keep, came, back, *ties):
        return call(
            scale_kernel,
            (keep, came, back, frames, ln_gain[None], grads, stats),
            (
                shape((frame_len, half_width), F32),
                shape((frame_len, half_width), F32),
                shape((frame_len, 2), F32),
            ),
            ties=ties,
        )

    def input_gradient(base, factor, sums):
        return call(
            input_kernel,
            (base, factor, sums, lax.ppermute(sums, "gy", swap), stats),
            (half_rows_of, shape((8, 128), F32)),
        )

    up_grad_of = shape((depth, hidden), F32)
    if ringed:
        came, kept = [{}, {}], []

        def send_on(i, blocks, names):
            for block, name in zip(blocks, names):
                came[i][name] = lax.ppermute(block, "gx", ahead if name == "up" else behind)

        def hop(i, turn, *ties):
            ways = [("up", half - turn - i), ("down", turn + 1 - i - half)]
            ways = [way for way in ways if way[1] != 0]
            names = [name for name, _ in ways]
            ties += tuple(came[i][name] for name in came[i] if name not in names)
            blocks = call(
                functools.partial(hop_kernel, tuple(step for _, step in ways), peers),
                (partial[i], *[came[i][name] for name in names]),
                [block_of] * len(ways),
                ties=ties,
            )
            if (i, turn) == (0, half - 2):
                kept.append(blocks[1])
                blocks, names = blocks[:1], names[:1]
            send_on(i, blocks, names)
            return blocks[0]

        send_on(0, blocks_own, ("up", "down"))
        send_on(1, blocks_other, ("up", "down"))
        keep, send, parts = own_d_norm(*came[0].values())
        tie = hop(1, 1, keep)
        tie = hop(0, 1, tie)
        tie = hop(1, 2, tie)
        tie = hop(0, 2, tie)
        tie, back = over_cores(keep, parts, tie)
        for turn in range(3, half):
            tie = hop(0, turn, hop(1, turn, tie))
        sent = lax.ppermute(send, "gy", swap)
        passing = call(
            functools.partial(total_kernel, peers),
            (partial[1], came[1]["up"], came[1]["down"]),
            block_of,
            ties=(tie,),
        )
        passed = lax.ppermute(passing, "groups", swap)
        send_on(0, [hold(kept[0], passing)], ["down"])
        input_grad, token = input_gradient(*scale(keep, sent, back, passing))
        up_grad = call(
            functools.partial(join_kernel, peers),
            (partial[0], came[0]["up"], came[0]["down"], passed),
            up_grad_of,
            ties=(token,),
        )
    else:
        keep, send, parts = own_d_norm()
        sent = lax.ppermute(send, "gy", swap)
        _, back = over_cores(keep, parts)
        input_grad, _ = input_gradient(*scale(keep, sent, back))
        total, passing = [
            lax.psum_scatter(p.astype(F32), "gx", scatter_dimension=0, tiled=True) for p in partial
        ]
        passed = lax.ppermute(passing.astype(BF16), "groups", swap)
        up_grad = call(place_halves_kernel, (total, passed), up_grad_of)
    return (input_grad[None], up_grad)


def solution(mesh):
    placed = (
        P(("groups", "gx"), None, None),
        P(("groups", "gx"), None, None),
        P(),
        P("gx", "gy"),
        P("gx", "gy"),
        P("groups"),
    )
    return jax.shard_map(
        shards,
        mesh=mesh,
        in_specs=placed,
        out_specs=(P(("groups", "gx"), None, "gy"), P(("groups", "gx"), "gy")),
        check_vma=False,
    )
```

```python
import functools

import jax
import jax.numpy as jnp
from jax import lax
from jax.experimental import pallas as pl
from jax.experimental.pallas import tpu as pltpu
from jax.sharding import PartitionSpec as P

BF16, F32 = jnp.bfloat16, jnp.float32
VMEM = pl.BlockSpec(memory_space=pltpu.VMEM)
HBM = pl.BlockSpec(memory_space=pltpu.HBM)
ANY = pl.BlockSpec(memory_space=pl.ANY)
SMEM = pl.BlockSpec(memory_space=pltpu.SMEM)


def shape(dims, kind):
    return jax.ShapeDtypeStruct(dims, kind)


def call(kernel, ins, out_shape, scratch=(), vmem=16, flops=1, left=(), pinned=(), out=VMEM, ties=()):
    count = len(ins)

    def body(*refs):
        kernel(*refs[:count], *refs[count + len(ties) :])

    moved = sum(x.size * x.dtype.itemsize for x in list(ins) + jax.tree.leaves(out_shape))
    return pl.pallas_call(
        body if ties else kernel,
        out_shape=out_shape,
        in_specs=[
            SMEM if x.dtype == jnp.int32 else ANY if i in left else HBM if i in pinned else VMEM
            for i, x in enumerate(ins)
        ]
        + [ANY] * len(ties),
        out_specs=jax.tree.map(lambda _: out, out_shape),
        scratch_shapes=list(scratch),
        compiler_params=pltpu.CompilerParams(vmem_limit_bytes=vmem << 20),
        cost_estimate=pl.CostEstimate(flops=flops, bytes_accessed=moved, transcendentals=0),
    )(*ins, *ties)


def hold(array, *ties):
    return pl.pallas_call(
        lambda *refs: None,
        out_shape=shape(array.shape, array.dtype),
        in_specs=[ANY] * (1 + len(ties)),
        out_specs=ANY,
        input_output_aliases={0: 0},
        compiler_params=pltpu.CompilerParams(vmem_limit_bytes=1 << 20),
        cost_estimate=pl.CostEstimate(flops=1, bytes_accessed=1, transcendentals=0),
    )(array, *ties)


def dot(left, right, left_dim=1, right_dim=0):
    return lax.dot_general(
        left, right, (((left_dim,), (right_dim,)), ((), ())), preferred_element_type=F32
    )


def gelu_slope(values):
    return (
        0.5 * (1.0 + lax.erf(values * 0.7071067811865476))
        + values * jnp.exp(-0.5 * values * values) * 0.3989422804014327
    )


def block_rows(step, peers, depth):
    own = lax.axis_index("gx")
    place = jnp.where(lax.rem(own, 2) == 0, lax.div(own, 2), peers - 1 - lax.div(own, 2))
    place = lax.rem(place + (step + peers), peers)
    member = jnp.where(place < peers // 2, 2 * place, 2 * (peers - 1 - place) + 1)
    return pl.ds(pl.multiple_of(member * depth, depth), depth)


def norm_rows(rows, gain):
    values = rows.astype(F32)
    centre = jnp.mean(values, axis=-1, keepdims=True)
    shifted = values - centre
    variance = jnp.mean(shifted * shifted, axis=-1, keepdims=True)
    inv_std = lax.rsqrt(variance + 1e-05)
    return (shifted * inv_std * gain[...][None]).astype(BF16), centre, inv_std


def mask_rows(rows, start, length):
    index = start + lax.broadcasted_iota(jnp.int32, (rows.shape[0], 1), 0)
    return jnp.where(index < length, rows.astype(F32), 0.0).astype(BF16)


def first_kernel(lengths, frames, out_grad, gain_from, w_up, w_down, *refs):
    passing, mine_up, mine_down, rows, grads, normed, gain, sems = refs
    half, quarter = rows.shape[0], mine_up.shape[1]
    start = pl.multiple_of(lax.axis_index("gy") * half, half)
    columns = pl.ds(pl.multiple_of(lax.axis_index("groups") * quarter, quarter), quarter)
    moves = (
        (gain_from, gain),
        (frames.at[pl.ds(start, half)], rows),
        (out_grad.at[pl.ds(start, half)], grads),
        (w_up.at[:, columns], mine_up),
        (w_down.at[:, columns], mine_down),
        (normed, passing.at[0]),
        (grads, passing.at[1]),
    )
    copies = [pltpu.make_async_copy(*move, sems.at[i]) for i, move in enumerate(moves)]
    for copy in copies[:5]:
        copy.start()
    copies[2].wait()
    grads[...] = mask_rows(grads[...], start, lengths[lax.axis_index("gx")])
    copies[6].start()
    copies[0].wait()
    copies[1].wait()
    normed[...] = norm_rows(rows[...], gain)[0]
    copies[5].start()
    for copy in copies[3:]:
        copy.wait()


def norm_kernel(lengths, frames, out_grad, gain, normed, grads, stats):
    value, centre, inv_std = norm_rows(frames[...], gain)
    normed[...] = value
    stats[:, 0:1] = centre
    stats[:, 1:2] = inv_std
    grads[...] = mask_rows(out_grad[...], 0, lengths[lax.axis_index("gx")])


def back_through(normed, grads, up, down, d_pre, partial):
    pre_act = dot(normed[...], up[...])
    d_act = dot(grads[...], down[...])
    d_pre[...] = (d_act * gelu_slope(pre_act)).astype(BF16)
    partial[...] = dot(normed[...], d_pre[...], 0, 0).astype(BF16)


def place_kernel(places, peers, *refs):
    blocks, (up, down, sems) = refs[:-3], refs[-3:]
    copies = []
    for i, ((step, which), block) in enumerate(zip(places, blocks)):
        rows = block_rows(step, peers, block.shape[0])
        copies.append(pltpu.make_async_copy(block, (up, down)[which].at[rows], sems.at[i]))
    for copy in copies:
        copy.start()
    for copy in copies:
        copy.wait()


def own_kernel(places, sends, peers, normed, grads, near_up, near_down, *refs):
    late, refs = refs[: len(places)], refs[len(places) :]
    (d_pre, partial, up, down), blocks = refs[:4], refs[4:]
    up[...] = near_up[...]
    down[...] = near_down[...]
    for (step, which), block in zip(places, late):
        (up, down)[which][block_rows(step, peers, block.shape[0]), :] = block[...]
    back_through(normed, grads, up, down, d_pre, partial)
    for step, block in zip(sends, blocks):
        block[...] = partial[block_rows(step, peers, block.shape[0]), :]


def other_kernel(sends, peers, first, second, up, down, d_pre, partial, *refs):
    blocks, (normed, grads) = refs[:-2], refs[-2:]
    half = first.shape[1]
    for at, part in ((0, first), (half, second)):
        normed[at : at + half, :] = part[0]
        grads[at : at + half, :] = part[1]
    back_through(normed, grads, up, down, d_pre, partial)
    for step, block in zip(sends, blocks):
        block[...] = partial[block_rows(step, peers, block.shape[0]), :]


def d_norm_kernel(d_pre_own, d_pre_other, up, keep, send_own, *sends):
    core = lax.axis_index("gy")
    rows, width = keep.shape[1:]
    mine = up[pl.ds(pl.multiple_of(core * width, width), width), :]
    theirs = up[pl.ds(pl.multiple_of((1 - core) * width, width), width), :]
    keep[0] = dot(d_pre_own[...], mine, 1, 1).astype(BF16)
    keep[1] = dot(d_pre_other[...], mine, 1, 1).astype(BF16)
    send_own[...] = dot(d_pre_own[...], theirs, 1, 1).astype(BF16)
    sent = dot(d_pre_other[...], theirs, 1, 1).astype(BF16)
    sent = jnp.concatenate([sent[rows // 2 :], sent[: rows // 2]])
    step = rows // len(sends)
    for i, send in enumerate(sends):
        send[...] = sent[i * step : (i + 1) * step]


def over_kernel(keep, *refs):
    parts, over = refs[:-1], refs[-1]
    half = over.shape[0] // 2
    value = jnp.concatenate([part[...].astype(F32) for part in parts])
    value = (keep[1].astype(F32) + value).astype(BF16)
    for i in range(2):
        at = lax.rem(i + lax.axis_index("gy"), 2) * half
        over[pl.ds(pl.multiple_of(at, half), half), :] = value[i * half : (i + 1) * half]


def own_columns(ref, width):
    return ref[:, pl.ds(pl.multiple_of(lax.axis_index("gy") * width, width), width)]


def scale_kernel(keep, came, back, frames, gain, grads, stats, base, factor, sums):
    width = base.shape[1]
    d_norm = keep[0].astype(F32) + came[...].astype(F32) + back[...].astype(F32)
    scaled = d_norm * own_columns(gain, width)
    rows = own_columns(frames, width).astype(F32)
    inv_std = stats[:, 1:2]
    centred = (rows - stats[:, 0:1]) * inv_std
    sums[:, 0:1] = jnp.sum(scaled, axis=-1, keepdims=True)
    sums[:, 1:2] = jnp.sum(scaled * centred, axis=-1, keepdims=True)
    base[...] = own_columns(grads, width).astype(F32) + inv_std * scaled
    factor[...] = inv_std * centred


def input_rows(base, factor, sums, came, stats):
    means = (sums[...] + came[...]) * (0.5 / base.shape[1])
    value = base[...] - stats[:, 1:2] * means[:, 0:1] - factor[...] * means[:, 1:2]
    return value.astype(BF16)


def input_kernel(base, factor, sums, came, stats, out):
    out[...] = input_rows(base, factor, sums, came, stats)


def hop_kernel(places, peers, partial, *refs):
    count = len(places)
    for step, came, out in zip(places, refs[:count], refs[count:]):
        value = partial[block_rows(step, peers, out.shape[0]), :].astype(F32)
        out[...] = (value + came[...].astype(F32)).astype(BF16)


def total_kernel(peers, partial, up, down, total):
    value = partial[block_rows(0, peers, total.shape[0]), :].astype(F32)
    total[...] = (value + up[...].astype(F32) + down[...].astype(F32)).astype(BF16)


def last_kernel(peers, base, factor, sums, came, stats, partial, up, down, passed, *outs):
    input_grad, up_grad = outs
    input_grad[...] = input_rows(base, factor, sums, came, stats)
    depth, width = passed.shape
    side = lax.axis_index("groups")
    value = partial[block_rows(0, peers, depth), :].astype(F32)
    value = value + up[...].astype(F32) + down[...].astype(F32)
    up_grad[:, pl.ds(pl.multiple_of(side * width, width), width)] = value
    other = pl.ds(pl.multiple_of((1 - side) * width, width), width)
    up_grad[:, other] = passed[...].astype(F32)


def place_halves_kernel(own, passed, out):
    width = own.shape[1]
    side = lax.axis_index("groups")
    out[:, pl.ds(pl.multiple_of(side * width, width), width)] = own[...]
    other = pl.ds(pl.multiple_of((1 - side) * width, width), width)
    out[:, other] = passed[...].astype(F32)


def shards(frames, out_grad, ln_gain, w_up, w_down, lengths):
    peers = lax.axis_size("gx")
    half = peers // 2
    frame_len, width = frames.shape[1:]
    depth, hidden = w_up.shape
    quarter = hidden // 2
    half_width = width // 2
    half_rows = frame_len // 2
    ringed = peers <= 16 and peers % 2 == 0 and depth % 16 == 0

    order = list(range(0, peers, 2)) + list(range(peers - 1, 0, -2))
    ahead = [(order[i], order[(i + 1) % peers]) for i in range(peers)]
    behind = [(b, a) for a, b in ahead]
    swap = [(0, 1), (1, 0)]

    frames, out_grad = frames[0], out_grad[0]
    rows_of = shape((frame_len, width), BF16)
    block_of = shape((depth, quarter), BF16)
    passing, *mine = call(
        first_kernel,
        (lengths, frames, out_grad, ln_gain, w_up, w_down),
        (shape((2, half_rows, width), BF16), block_of, block_of),
        [pltpu.VMEM((half_rows, width), BF16)] * 3
        + [pltpu.VMEM((width,), F32), pltpu.SemaphoreType.DMA((7,))],
        flops=5 * frame_len * width,
        vmem=60,
        left=range(1, 6),
        out=ANY,
    )
    first = lax.ppermute(passing, "groups", swap)
    normed, grads, stats = call(
        norm_kernel,
        (lengths, frames, out_grad, ln_gain),
        (rows_of, rows_of, shape((frame_len, 2), F32)),
        flops=10 * frame_len * width,
    )

    weight = shape((width, quarter), BF16)
    if ringed:
        blocks = {(0, 0): mine[0], (0, 1): mine[1]}
        up, down = list(mine), list(mine)
        for step in range(1, half):
            for i in range(2):
                up[i] = lax.ppermute(up[i], "gx", ahead)
                down[i] = lax.ppermute(down[i], "gx", behind)
            if step == 1:
                up[0] = hold(up[0], normed)
            for i in range(2):
                blocks[-step, i], blocks[step, i] = up[i], down[i]
        late = {
            (half - 1, 0): blocks.pop((half - 1, 0)),
            (1 - half, 1): blocks.pop((1 - half, 1)),
            (half, 0): lax.ppermute(up[0], "gx", ahead),
            (half, 1): lax.ppermute(down[1], "gx", behind),
        }
        near = call(
            functools.partial(place_kernel, tuple(blocks), peers),
            list(blocks.values()),
            (weight, weight),
            [pltpu.SemaphoreType.DMA((len(blocks),))],
            pinned=range(len(blocks)),
        )
        first = hold(first, *late.values(), near[0])
        sends = ((half - 1, -half), (half, 1 - half))
    else:
        near = [lax.all_gather(block, "gx", axis=0, tiled=True) for block in mine]
        late, sends = {}, ((), ())
    second = lax.ppermute(first, "gy", swap)

    d_pre_of, partial_of = shape((frame_len, quarter), BF16), shape((width, quarter), BF16)
    d_pre_own, partial_own, full_up, full_down, *blocks_own = call(
        functools.partial(own_kernel, tuple(late), sends[1], peers),
        (normed, grads, *near, *late.values()),
        (d_pre_of, partial_of, weight, weight, *[block_of] * len(sends[1])),
        flops=6 * frame_len * width * quarter,
    )
    d_pre_other, partial_other, *blocks_other = call(
        functools.partial(other_kernel, sends[0], peers),
        (first, second, full_up, full_down),
        (d_pre_of, partial_of, *[block_of] * len(sends[0])),
        [pltpu.VMEM((frame_len, width), BF16)] * 2,
        flops=6 * frame_len * width * quarter,
    )
    partial = [partial_own, partial_other]

    half_rows_of = shape((frame_len, half_width), BF16)
    parts_of = [half_rows_of]

    def own_d_norm(*ties):
        keep, send, *parts = call(
            d_norm_kernel,
            (d_pre_own, d_pre_other, full_up),
            (shape((2, frame_len, half_width), BF16), half_rows_of, *parts_of),
            flops=4 * frame_len * width * quarter,
            ties=ties,
        )
        return keep, send, [lax.ppermute(part, "gy", swap) for part in parts]

    def over_cores(keep, parts, *ties):
        over = call(over_kernel, (keep, *parts), half_rows_of, ties=ties)
        return over, lax.ppermute(over, "groups", swap)

    def scale(keep, came, back, *ties):
        return call(
            scale_kernel,
            (keep, came, back, frames, ln_gain[None], grads, stats),
            (
                shape((frame_len, half_width), F32),
                shape((frame_len, half_width), F32),
                shape((frame_len, 2), F32),
            ),
            ties=ties,
        )

    up_grad_of = shape((depth, hidden), F32)
    if ringed:
        came, kept = [{}, {}], []

        def send_on(i, blocks, names):
            for block, name in zip(blocks, names):
                came[i][name] = lax.ppermute(block, "gx", ahead if name == "up" else behind)

        def hop(i, turn, *ties):
            ways = [("up", half - turn - i), ("down", turn + 1 - i - half)]
            ways = [way for way in ways if way[1] != 0]
            names = [name for name, _ in ways]
            ties += tuple(came[i][name] for name in came[i] if name not in names)
            blocks = call(
                functools.partial(hop_kernel, tuple(step for _, step in ways), peers),
                (partial[i], *[came[i][name] for name in names]),
                [block_of] * len(ways),
                ties=ties,
            )
            if (i, turn) == (0, half - 2):
                kept.append(blocks[1])
                blocks, names = blocks[:1], names[:1]
            send_on(i, blocks, names)
            return blocks[0]

        send_on(0, blocks_own, ("up", "down"))
        send_on(1, blocks_other, ("up", "down"))
        keep, send, parts = own_d_norm(*came[0].values())
        tie = hop(1, 1, keep)
        tie = hop(0, 1, tie)
        tie = hop(1, 2, tie)
        tie, back = over_cores(keep, parts, tie)
        tie = hop(0, 2, tie)
        for turn in range(3, half):
            tie = hop(0, turn, hop(1, turn, tie))
        sent = lax.ppermute(send, "gy", swap)
        passing = call(
            functools.partial(total_kernel, peers),
            (partial[1], came[1]["up"], came[1]["down"]),
            block_of,
            ties=(tie,),
        )
        passed = lax.ppermute(passing, "groups", swap)
        send_on(0, [hold(kept[0], passing)], ["down"])
        base, factor, sums = scale(keep, sent, back, passing)
        input_grad, up_grad = call(
            functools.partial(last_kernel, peers),
            (base, factor, sums, lax.ppermute(sums, "gy", swap), stats)
            + (partial[0], came[0]["up"], came[0]["down"], passed),
            (half_rows_of, up_grad_of),
        )
    else:
        keep, send, parts = own_d_norm()
        sent = lax.ppermute(send, "gy", swap)
        _, back = over_cores(keep, parts)
        base, factor, sums = scale(keep, sent, back)
        came = lax.ppermute(sums, "gy", swap)
        input_grad = call(input_kernel, (base, factor, sums, came, stats), half_rows_of)
        total, passing = [
            lax.psum_scatter(p.astype(F32), "gx", scatter_dimension=0, tiled=True) for p in partial
        ]
        passed = lax.ppermute(passing.astype(BF16), "groups", swap)
        up_grad = call(place_halves_kernel, (total, passed), up_grad_of)
    return (input_grad[None], up_grad)


def solution(mesh):
    placed = (
        P(("groups", "gx"), None, None),
        P(("groups", "gx"), None, None),
        P(),
        P("gx", "gy"),
        P("gx", "gy"),
        P("groups"),
    )
    return jax.shard_map(
        shards,
        mesh=mesh,
        in_specs=placed,
        out_specs=(P(("groups", "gx"), None, "gy"), P(("groups", "gx"), "gy")),
        check_vma=False,
    )
```

```python
import functools

import jax
import jax.numpy as jnp
from jax import lax
from jax.experimental import pallas as pl
from jax.experimental.pallas import tpu as pltpu
from jax.sharding import PartitionSpec as P

BF16, F32 = jnp.bfloat16, jnp.float32
VMEM = pl.BlockSpec(memory_space=pltpu.VMEM)
HBM = pl.BlockSpec(memory_space=pltpu.HBM)
ANY = pl.BlockSpec(memory_space=pl.ANY)
SMEM = pl.BlockSpec(memory_space=pltpu.SMEM)


def shape(dims, kind):
    return jax.ShapeDtypeStruct(dims, kind)


def call(kernel, ins, out_shape, scratch=(), vmem=16, flops=1, left=(), pinned=(), out=None, ties=()):
    count = len(ins)

    def body(*refs):
        kernel(*refs[:count], *refs[count + len(ties) :])

    moved = sum(x.size * x.dtype.itemsize for x in list(ins) + jax.tree.leaves(out_shape))
    return pl.pallas_call(
        body if ties else kernel,
        out_shape=out_shape,
        in_specs=[
            SMEM if x.dtype == jnp.int32 else ANY if i in left else HBM if i in pinned else VMEM
            for i, x in enumerate(ins)
        ]
        + [ANY] * len(ties),
        out_specs=out or jax.tree.map(lambda _: VMEM, out_shape),
        scratch_shapes=list(scratch),
        compiler_params=pltpu.CompilerParams(vmem_limit_bytes=vmem << 20),
        cost_estimate=pl.CostEstimate(flops=flops, bytes_accessed=moved, transcendentals=0),
    )(*ins, *ties)


def hold(array, *ties):
    return pl.pallas_call(
        lambda *refs: None,
        out_shape=shape(array.shape, array.dtype),
        in_specs=[ANY] * (1 + len(ties)),
        out_specs=ANY,
        input_output_aliases={0: 0},
        compiler_params=pltpu.CompilerParams(vmem_limit_bytes=1 << 20),
        cost_estimate=pl.CostEstimate(flops=1, bytes_accessed=1, transcendentals=0),
    )(array, *ties)


def dot(left, right, left_dim=1, right_dim=0):
    return lax.dot_general(
        left, right, (((left_dim,), (right_dim,)), ((), ())), preferred_element_type=F32
    )


def gelu_slope(values):
    return (
        0.5 * (1.0 + lax.erf(values * 0.7071067811865476))
        + values * jnp.exp(-0.5 * values * values) * 0.3989422804014327
    )


def block_rows(step, peers, depth):
    own = lax.axis_index("gx")
    place = jnp.where(lax.rem(own, 2) == 0, lax.div(own, 2), peers - 1 - lax.div(own, 2))
    place = lax.rem(place + (step + peers), peers)
    member = jnp.where(place < peers // 2, 2 * place, 2 * (peers - 1 - place) + 1)
    return pl.ds(pl.multiple_of(member * depth, depth), depth)


def norm_rows(rows, gain):
    values = rows.astype(F32)
    centre = jnp.mean(values, axis=-1, keepdims=True)
    shifted = values - centre
    variance = jnp.mean(shifted * shifted, axis=-1, keepdims=True)
    inv_std = lax.rsqrt(variance + 1e-05)
    return (shifted * inv_std * gain[...][None]).astype(BF16), centre, inv_std


def mask_rows(rows, start, length):
    index = start + lax.broadcasted_iota(jnp.int32, (rows.shape[0], 1), 0)
    return jnp.where(index < length, rows.astype(F32), 0.0).astype(BF16)


def first_kernel(lengths, frames, out_grad, gain_from, w_up, w_down, *refs):
    passing, mine_up, mine_down, rows, grads, normed, gain, sems = refs
    half, quarter = rows.shape[0], mine_up.shape[1]
    start = pl.multiple_of(lax.axis_index("gy") * half, half)
    columns = pl.ds(pl.multiple_of(lax.axis_index("groups") * quarter, quarter), quarter)
    moves = (
        (gain_from, gain),
        (frames.at[pl.ds(start, half)], rows),
        (out_grad.at[pl.ds(start, half)], grads),
        (w_up.at[:, columns], mine_up),
        (w_down.at[:, columns], mine_down),
        (normed, passing.at[0]),
        (grads, passing.at[1]),
    )
    copies = [pltpu.make_async_copy(*move, sems.at[i]) for i, move in enumerate(moves)]
    for copy in copies[:5]:
        copy.start()
    copies[2].wait()
    grads[...] = mask_rows(grads[...], start, lengths[lax.axis_index("gx")])
    copies[6].start()
    copies[0].wait()
    copies[1].wait()
    normed[...] = norm_rows(rows[...], gain)[0]
    copies[5].start()
    for copy in copies[3:]:
        copy.wait()


def norm_kernel(lengths, frames, out_grad, gain, normed, grads, stats):
    value, centre, inv_std = norm_rows(frames[...], gain)
    normed[...] = value
    stats[:, 0:1] = centre
    stats[:, 1:2] = inv_std
    grads[...] = mask_rows(out_grad[...], 0, lengths[lax.axis_index("gx")])


def back_through(normed, grads, up, down, d_pre, partial):
    pre_act = dot(normed[...], up[...])
    d_act = dot(grads[...], down[...])
    d_pre[...] = (d_act * gelu_slope(pre_act)).astype(BF16)
    partial[...] = dot(normed[...], d_pre[...], 0, 0).astype(BF16)


def place_kernel(places, peers, *refs):
    blocks, (up, down, sems) = refs[:-3], refs[-3:]
    copies = []
    for i, ((step, which), block) in enumerate(zip(places, blocks)):
        rows = block_rows(step, peers, block.shape[0])
        copies.append(pltpu.make_async_copy(block, (up, down)[which].at[rows], sems.at[i]))
    for copy in copies:
        copy.start()
    for copy in copies:
        copy.wait()


def own_kernel(places, sends, peers, normed, grads, near_up, near_down, *refs):
    late, refs = refs[: len(places)], refs[len(places) :]
    (d_pre, partial, up, down), blocks = refs[:4], refs[4:]
    up[...] = near_up[...]
    down[...] = near_down[...]
    for (step, which), block in zip(places, late):
        (up, down)[which][block_rows(step, peers, block.shape[0]), :] = block[...]
    back_through(normed, grads, up, down, d_pre, partial)
    for step, block in zip(sends, blocks):
        block[...] = partial[block_rows(step, peers, block.shape[0]), :]


def other_kernel(sends, peers, first, second, up, down, d_pre, partial, *refs):
    blocks, (normed, grads) = refs[:-2], refs[-2:]
    half = first.shape[1]
    for at, part in ((0, first), (half, second)):
        normed[at : at + half, :] = part[0]
        grads[at : at + half, :] = part[1]
    back_through(normed, grads, up, down, d_pre, partial)
    for step, block in zip(sends, blocks):
        block[...] = partial[block_rows(step, peers, block.shape[0]), :]


def d_norm_kernel(d_pre_own, d_pre_other, up, keep, send_own, *sends):
    core = lax.axis_index("gy")
    rows, width = keep.shape[1:]
    mine = up[pl.ds(pl.multiple_of(core * width, width), width), :]
    theirs = up[pl.ds(pl.multiple_of((1 - core) * width, width), width), :]
    keep[0] = dot(d_pre_own[...], mine, 1, 1).astype(BF16)
    keep[1] = dot(d_pre_other[...], mine, 1, 1).astype(BF16)
    send_own[...] = dot(d_pre_own[...], theirs, 1, 1).astype(BF16)
    sent = dot(d_pre_other[...], theirs, 1, 1).astype(BF16)
    sent = jnp.concatenate([sent[rows // 2 :], sent[: rows // 2]])
    step = rows // len(sends)
    for i, send in enumerate(sends):
        send[...] = sent[i * step : (i + 1) * step]


def over_kernel(keep, *refs):
    parts, over = refs[:-1], refs[-1]
    half = over.shape[0] // 2
    value = jnp.concatenate([part[...].astype(F32) for part in parts])
    value = (keep[1].astype(F32) + value).astype(BF16)
    for i in range(2):
        at = lax.rem(i + lax.axis_index("gy"), 2) * half
        over[pl.ds(pl.multiple_of(at, half), half), :] = value[i * half : (i + 1) * half]


def own_columns(ref, width):
    return ref[:, pl.ds(pl.multiple_of(lax.axis_index("gy") * width, width), width)]


def scale_kernel(keep, came, back, frames, gain, grads, stats, base, factor, sums):
    width = base.shape[1]
    d_norm = keep[0].astype(F32) + came[...].astype(F32) + back[...].astype(F32)
    scaled = d_norm * own_columns(gain, width)
    rows = own_columns(frames, width).astype(F32)
    inv_std = stats[:, 1:2]
    centred = (rows - stats[:, 0:1]) * inv_std
    sums[:, 0:1] = jnp.sum(scaled, axis=-1, keepdims=True)
    sums[:, 1:2] = jnp.sum(scaled * centred, axis=-1, keepdims=True)
    base[...] = own_columns(grads, width).astype(F32) + inv_std * scaled
    factor[...] = inv_std * centred


def input_rows(base, factor, sums, came, stats):
    means = (sums[...] + came[...]) * (0.5 / base.shape[1])
    value = base[...] - stats[:, 1:2] * means[:, 0:1] - factor[...] * means[:, 1:2]
    return value.astype(BF16)


def input_kernel(base, factor, sums, came, stats, out):
    out[...] = input_rows(base, factor, sums, came, stats)


def hop_kernel(places, peers, partial, *refs):
    count = len(places)
    for step, came, out in zip(places, refs[:count], refs[count:]):
        value = partial[block_rows(step, peers, out.shape[0]), :].astype(F32)
        out[...] = (value + came[...].astype(F32)).astype(BF16)


def total_kernel(peers, partial, up, down, total):
    value = partial[block_rows(0, peers, total.shape[0]), :].astype(F32)
    total[...] = (value + up[...].astype(F32) + down[...].astype(F32)).astype(BF16)


def last_kernel(peers, base, factor, sums, came, stats, partial, up, down, passed, *outs):
    input_grad, up_grad = outs
    input_grad[...] = input_rows(base, factor, sums, came, stats)
    depth, width = passed.shape
    side = lax.axis_index("groups")
    value = partial[block_rows(0, peers, depth), :].astype(F32)
    value = value + up[...].astype(F32) + down[...].astype(F32)
    up_grad[:, pl.ds(pl.multiple_of(side * width, width), width)] = value
    other = pl.ds(pl.multiple_of((1 - side) * width, width), width)
    up_grad[:, other] = passed[...].astype(F32)


def place_halves_kernel(own, passed, out):
    width = own.shape[1]
    side = lax.axis_index("groups")
    out[:, pl.ds(pl.multiple_of(side * width, width), width)] = own[...]
    other = pl.ds(pl.multiple_of((1 - side) * width, width), width)
    out[:, other] = passed[...].astype(F32)


def shards(frames, out_grad, ln_gain, w_up, w_down, lengths):
    peers = lax.axis_size("gx")
    half = peers // 2
    frame_len, width = frames.shape[1:]
    depth, hidden = w_up.shape
    quarter = hidden // 2
    half_width = width // 2
    half_rows = frame_len // 2
    ringed = peers <= 16 and peers % 2 == 0 and depth % 16 == 0

    order = list(range(0, peers, 2)) + list(range(peers - 1, 0, -2))
    ahead = [(order[i], order[(i + 1) % peers]) for i in range(peers)]
    behind = [(b, a) for a, b in ahead]
    swap = [(0, 1), (1, 0)]

    frames, out_grad = frames[0], out_grad[0]
    rows_of = shape((frame_len, width), BF16)
    block_of = shape((depth, quarter), BF16)
    passing, *mine = call(
        first_kernel,
        (lengths, frames, out_grad, ln_gain, w_up, w_down),
        (shape((2, half_rows, width), BF16), block_of, block_of),
        [pltpu.VMEM((half_rows, width), BF16)] * 3
        + [pltpu.VMEM((width,), F32), pltpu.SemaphoreType.DMA((7,))],
        flops=5 * frame_len * width,
        vmem=60,
        left=range(1, 6),
        out=(ANY, VMEM, VMEM),
    )
    first = lax.ppermute(passing, "groups", swap)
    normed, grads, stats = call(
        norm_kernel,
        (lengths, frames, out_grad, ln_gain),
        (rows_of, rows_of, shape((frame_len, 2), F32)),
        flops=10 * frame_len * width,
    )

    weight = shape((width, quarter), BF16)
    if ringed:
        blocks = {(0, 0): mine[0], (0, 1): mine[1]}
        up, down = list(mine), list(mine)
        for step in range(1, half):
            for i in range(2):
                up[i] = lax.ppermute(up[i], "gx", ahead)
                down[i] = lax.ppermute(down[i], "gx", behind)
            if step == 1:
                up[0] = hold(up[0], normed)
            for i in range(2):
                blocks[-step, i], blocks[step, i] = up[i], down[i]
        late = {
            (half - 1, 0): blocks.pop((half - 1, 0)),
            (1 - half, 1): blocks.pop((1 - half, 1)),
            (half, 0): lax.ppermute(up[0], "gx", ahead),
            (half, 1): lax.ppermute(down[1], "gx", behind),
        }
        near = call(
            functools.partial(place_kernel, tuple(blocks), peers),
            list(blocks.values()),
            (weight, weight),
            [pltpu.SemaphoreType.DMA((len(blocks),))],
            pinned=range(len(blocks)),
        )
        first = hold(first, *late.values(), near[0])
        sends = ((half - 1, -half), (half, 1 - half))
    else:
        near = [lax.all_gather(block, "gx", axis=0, tiled=True) for block in mine]
        late, sends = {}, ((), ())
    second = lax.ppermute(first, "gy", swap)

    d_pre_of, partial_of = shape((frame_len, quarter), BF16), shape((width, quarter), BF16)
    d_pre_own, partial_own, full_up, full_down, *blocks_own = call(
        functools.partial(own_kernel, tuple(late), sends[1], peers),
        (normed, grads, *near, *late.values()),
        (d_pre_of, partial_of, weight, weight, *[block_of] * len(sends[1])),
        flops=6 * frame_len * width * quarter,
    )
    d_pre_other, partial_other, *blocks_other = call(
        functools.partial(other_kernel, sends[0], peers),
        (first, second, full_up, full_down),
        (d_pre_of, partial_of, *[block_of] * len(sends[0])),
        [pltpu.VMEM((frame_len, width), BF16)] * 2,
        flops=6 * frame_len * width * quarter,
    )
    partial = [partial_own, partial_other]

    half_rows_of = shape((frame_len, half_width), BF16)
    parts_of = [half_rows_of]

    def own_d_norm(*ties):
        keep, send, *parts = call(
            d_norm_kernel,
            (d_pre_own, d_pre_other, full_up),
            (shape((2, frame_len, half_width), BF16), half_rows_of, *parts_of),
            flops=4 * frame_len * width * quarter,
            ties=ties,
        )
        return keep, send, [lax.ppermute(part, "gy", swap) for part in parts]

    def over_cores(keep, parts, *ties):
        over = call(over_kernel, (keep, *parts), half_rows_of, ties=ties)
        return over, lax.ppermute(over, "groups", swap)

    def scale(keep, came, back, *ties):
        return call(
            scale_kernel,
            (keep, came, back, frames, ln_gain[None], grads, stats),
            (
                shape((frame_len, half_width), F32),
                shape((frame_len, half_width), F32),
                shape((frame_len, 2), F32),
            ),
            ties=ties,
        )

    up_grad_of = shape((depth, hidden), F32)
    if ringed:
        came, kept = [{}, {}], []

        def send_on(i, blocks, names):
            for block, name in zip(blocks, names):
                came[i][name] = lax.ppermute(block, "gx", ahead if name == "up" else behind)

        def hop(i, turn, *ties):
            ways = [("up", half - turn - i), ("down", turn + 1 - i - half)]
            ways = [way for way in ways if way[1] != 0]
            names = [name for name, _ in ways]
            ties += tuple(came[i][name] for name in came[i] if name not in names)
            blocks = call(
                functools.partial(hop_kernel, tuple(step for _, step in ways), peers),
                (partial[i], *[came[i][name] for name in names]),
                [block_of] * len(ways),
                ties=ties,
            )
            if (i, turn) == (0, half - 2):
                kept.append(blocks[1])
                blocks, names = blocks[:1], names[:1]
            send_on(i, blocks, names)
            return blocks[0]

        send_on(0, blocks_own, ("up", "down"))
        send_on(1, blocks_other, ("up", "down"))
        keep, send, parts = own_d_norm(*came[0].values())
        tie = hop(1, 1, keep)
        tie = hop(0, 1, tie)
        tie = hop(1, 2, tie)
        tie, back = over_cores(keep, parts, tie)
        tie = hop(0, 2, tie)
        for turn in range(3, half):
            tie = hop(0, turn, hop(1, turn, tie))
        sent = lax.ppermute(send, "gy", swap)
        passing = call(
            functools.partial(total_kernel, peers),
            (partial[1], came[1]["up"], came[1]["down"]),
            block_of,
            ties=(tie,),
        )
        passed = lax.ppermute(passing, "groups", swap)
        send_on(0, [hold(kept[0], passing)], ["down"])
        base, factor, sums = scale(keep, sent, back, passing)
        input_grad, up_grad = call(
            functools.partial(last_kernel, peers),
            (base, factor, sums, lax.ppermute(sums, "gy", swap), stats)
            + (partial[0], came[0]["up"], came[0]["down"], passed),
            (half_rows_of, up_grad_of),
        )
    else:
        keep, send, parts = own_d_norm()
        sent = lax.ppermute(send, "gy", swap)
        _, back = over_cores(keep, parts)
        base, factor, sums = scale(keep, sent, back)
        came = lax.ppermute(sums, "gy", swap)
        input_grad = call(input_kernel, (base, factor, sums, came, stats), half_rows_of)
        total, passing = [
            lax.psum_scatter(p.astype(F32), "gx", scatter_dimension=0, tiled=True) for p in partial
        ]
        passed = lax.ppermute(passing.astype(BF16), "groups", swap)
        up_grad = call(place_halves_kernel, (total, passed), up_grad_of)
    return (input_grad[None], up_grad)


def solution(mesh):
    placed = (
        P(("groups", "gx"), None, None),
        P(("groups", "gx"), None, None),
        P(),
        P("gx", "gy"),
        P("gx", "gy"),
        P("groups"),
    )
    return jax.shard_map(
        shards,
        mesh=mesh,
        in_specs=placed,
        out_specs=(P(("groups", "gx"), None, "gy"), P(("groups", "gx"), "gy")),
        check_vma=False,
    )
```

```python
import functools

import jax
import jax.numpy as jnp
from jax import lax
from jax.experimental import pallas as pl
from jax.experimental.pallas import tpu as pltpu
from jax.sharding import PartitionSpec as P

BF16, F32 = jnp.bfloat16, jnp.float32
VMEM = pl.BlockSpec(memory_space=pltpu.VMEM)
HBM = pl.BlockSpec(memory_space=pltpu.HBM)
ANY = pl.BlockSpec(memory_space=pl.ANY)
SMEM = pl.BlockSpec(memory_space=pltpu.SMEM)


def shape(dims, kind):
    return jax.ShapeDtypeStruct(dims, kind)


def call(kernel, ins, out_shape, scratch=(), vmem=16, flops=1, left=(), pinned=(), ties=()):
    count = len(ins)

    def body(*refs):
        kernel(*refs[:count], *refs[count + len(ties) :])

    moved = sum(x.size * x.dtype.itemsize for x in list(ins) + jax.tree.leaves(out_shape))
    return pl.pallas_call(
        body if ties else kernel,
        out_shape=out_shape,
        in_specs=[
            SMEM if x.dtype == jnp.int32 else ANY if i in left else HBM if i in pinned else VMEM
            for i, x in enumerate(ins)
        ]
        + [ANY] * len(ties),
        out_specs=jax.tree.map(lambda _: VMEM, out_shape),
        scratch_shapes=list(scratch),
        compiler_params=pltpu.CompilerParams(vmem_limit_bytes=vmem << 20),
        cost_estimate=pl.CostEstimate(flops=flops, bytes_accessed=moved, transcendentals=0),
    )(*ins, *ties)


def hold(array, *ties):
    return pl.pallas_call(
        lambda *refs: None,
        out_shape=shape(array.shape, array.dtype),
        in_specs=[ANY] * (1 + len(ties)),
        out_specs=ANY,
        input_output_aliases={0: 0},
        compiler_params=pltpu.CompilerParams(vmem_limit_bytes=1 << 20),
        cost_estimate=pl.CostEstimate(flops=1, bytes_accessed=1, transcendentals=0),
    )(array, *ties)


def dot(left, right, left_dim=1, right_dim=0):
    return lax.dot_general(
        left, right, (((left_dim,), (right_dim,)), ((), ())), preferred_element_type=F32
    )


def gelu_slope(values):
    return (
        0.5 * (1.0 + lax.erf(values * 0.7071067811865476))
        + values * jnp.exp(-0.5 * values * values) * 0.3989422804014327
    )


def block_rows(step, peers, depth):
    own = lax.axis_index("gx")
    place = jnp.where(lax.rem(own, 2) == 0, lax.div(own, 2), peers - 1 - lax.div(own, 2))
    place = lax.rem(place + (step + peers), peers)
    member = jnp.where(place < peers // 2, 2 * place, 2 * (peers - 1 - place) + 1)
    return pl.ds(pl.multiple_of(member * depth, depth), depth)


def norm_rows(rows, gain):
    values = rows.astype(F32)
    centre = jnp.mean(values, axis=-1, keepdims=True)
    shifted = values - centre
    variance = jnp.mean(shifted * shifted, axis=-1, keepdims=True)
    inv_std = lax.rsqrt(variance + 1e-05)
    return (shifted * inv_std * gain[...][None]).astype(BF16), centre, inv_std


def mask_rows(rows, start, length):
    index = start + lax.broadcasted_iota(jnp.int32, (rows.shape[0], 1), 0)
    return jnp.where(index < length, rows.astype(F32), 0.0).astype(BF16)


def first_kernel(
    lengths, frames, out_grad, gain, w_up, w_down, passing, mine_up, mine_down, sems, rows, grads
):
    half, quarter = rows.shape[0], mine_up.shape[1]
    start = pl.multiple_of(lax.axis_index("gy") * half, half)
    columns = pl.ds(pl.multiple_of(lax.axis_index("groups") * quarter, quarter), quarter)
    moves = (
        (frames.at[pl.ds(start, half)], rows),
        (out_grad.at[pl.ds(start, half)], grads),
        (w_up.at[:, columns], mine_up),
        (w_down.at[:, columns], mine_down),
    )
    copies = [pltpu.make_async_copy(*move, sems.at[i]) for i, move in enumerate(moves)]
    for copy in copies:
        copy.start()
    copies[0].wait()
    passing[0] = norm_rows(rows[...], gain)[0]
    copies[1].wait()
    passing[1] = mask_rows(grads[...], start, lengths[lax.axis_index("gx")])
    copies[2].wait()
    copies[3].wait()


def norm_kernel(lengths, frames, out_grad, gain, normed, grads, stats):
    value, centre, inv_std = norm_rows(frames[...], gain)
    normed[...] = value
    stats[:, 0:1] = centre
    stats[:, 1:2] = inv_std
    grads[...] = mask_rows(out_grad[...], 0, lengths[lax.axis_index("gx")])


def back_through(normed, grads, up, down, d_pre, partial):
    pre_act = dot(normed[...], up[...])
    d_act = dot(grads[...], down[...])
    d_pre[...] = (d_act * gelu_slope(pre_act)).astype(BF16)
    partial[...] = dot(normed[...], d_pre[...], 0, 0).astype(BF16)


def place_kernel(places, peers, *refs):
    blocks, (up, down, sems) = refs[:-3], refs[-3:]
    copies = []
    for i, ((step, which), block) in enumerate(zip(places, blocks)):
        rows = block_rows(step, peers, block.shape[0])
        copies.append(pltpu.make_async_copy(block, (up, down)[which].at[rows], sems.at[i]))
    for copy in copies:
        copy.start()
    for copy in copies:
        copy.wait()


def own_kernel(places, sends, peers, normed, grads, near_up, near_down, *refs):
    late, refs = refs[: len(places)], refs[len(places) :]
    (d_pre, partial, up, down), blocks = refs[:4], refs[4:]
    up[...] = near_up[...]
    down[...] = near_down[...]
    for (step, which), block in zip(places, late):
        (up, down)[which][block_rows(step, peers, block.shape[0]), :] = block[...]
    back_through(normed, grads, up, down, d_pre, partial)
    for step, block in zip(sends, blocks):
        block[...] = partial[block_rows(step, peers, block.shape[0]), :]


def other_kernel(sends, peers, first, second, up, down, d_pre, partial, *refs):
    blocks, (normed, grads) = refs[:-2], refs[-2:]
    half = first.shape[1]
    for at, part in ((0, first), (half, second)):
        normed[at : at + half, :] = part[0]
        grads[at : at + half, :] = part[1]
    back_through(normed, grads, up, down, d_pre, partial)
    for step, block in zip(sends, blocks):
        block[...] = partial[block_rows(step, peers, block.shape[0]), :]


def d_norm_kernel(d_pre_own, d_pre_other, up, keep, send_own, *sends):
    core = lax.axis_index("gy")
    rows, width = keep.shape[1:]
    mine = up[pl.ds(pl.multiple_of(core * width, width), width), :]
    theirs = up[pl.ds(pl.multiple_of((1 - core) * width, width), width), :]
    keep[0] = dot(d_pre_own[...], mine, 1, 1).astype(BF16)
    keep[1] = dot(d_pre_other[...], mine, 1, 1).astype(BF16)
    send_own[...] = dot(d_pre_own[...], theirs, 1, 1).astype(BF16)
    sent = dot(d_pre_other[...], theirs, 1, 1).astype(BF16)
    sent = jnp.concatenate([sent[rows // 2 :], sent[: rows // 2]])
    step = rows // len(sends)
    for i, send in enumerate(sends):
        send[...] = sent[i * step : (i + 1) * step]


def over_kernel(keep, *refs):
    parts, over = refs[:-1], refs[-1]
    half = over.shape[0] // 2
    value = jnp.concatenate([part[...].astype(F32) for part in parts])
    value = (keep[1].astype(F32) + value).astype(BF16)
    for i in range(2):
        at = lax.rem(i + lax.axis_index("gy"), 2) * half
        over[pl.ds(pl.multiple_of(at, half), half), :] = value[i * half : (i + 1) * half]


def own_columns(ref, width):
    return ref[:, pl.ds(pl.multiple_of(lax.axis_index("gy") * width, width), width)]


def scale_kernel(keep, came, back, frames, gain, grads, stats, base, factor, sums):
    width = base.shape[1]
    d_norm = keep[0].astype(F32) + came[...].astype(F32) + back[...].astype(F32)
    scaled = d_norm * own_columns(gain, width)
    rows = own_columns(frames, width).astype(F32)
    inv_std = stats[:, 1:2]
    centred = (rows - stats[:, 0:1]) * inv_std
    sums[:, 0:1] = jnp.sum(scaled, axis=-1, keepdims=True)
    sums[:, 1:2] = jnp.sum(scaled * centred, axis=-1, keepdims=True)
    base[...] = own_columns(grads, width).astype(F32) + inv_std * scaled
    factor[...] = inv_std * centred


def input_rows(base, factor, sums, came, stats):
    means = (sums[...] + came[...]) * (0.5 / base.shape[1])
    value = base[...] - stats[:, 1:2] * means[:, 0:1] - factor[...] * means[:, 1:2]
    return value.astype(BF16)


def input_kernel(base, factor, sums, came, stats, out):
    out[...] = input_rows(base, factor, sums, came, stats)


def hop_kernel(places, peers, partial, *refs):
    count = len(places)
    for step, came, out in zip(places, refs[:count], refs[count:]):
        value = partial[block_rows(step, peers, out.shape[0]), :].astype(F32)
        out[...] = (value + came[...].astype(F32)).astype(BF16)


def total_kernel(peers, partial, up, down, total):
    value = partial[block_rows(0, peers, total.shape[0]), :].astype(F32)
    total[...] = (value + up[...].astype(F32) + down[...].astype(F32)).astype(BF16)


def last_kernel(peers, base, factor, sums, came, stats, partial, up, down, passed, *outs):
    input_grad, up_grad = outs
    input_grad[...] = input_rows(base, factor, sums, came, stats)
    depth, width = passed.shape
    side = lax.axis_index("groups")
    value = partial[block_rows(0, peers, depth), :].astype(F32)
    value = value + up[...].astype(F32) + down[...].astype(F32)
    up_grad[:, pl.ds(pl.multiple_of(side * width, width), width)] = value
    other = pl.ds(pl.multiple_of((1 - side) * width, width), width)
    up_grad[:, other] = passed[...].astype(F32)


def place_halves_kernel(own, passed, out):
    width = own.shape[1]
    side = lax.axis_index("groups")
    out[:, pl.ds(pl.multiple_of(side * width, width), width)] = own[...]
    other = pl.ds(pl.multiple_of((1 - side) * width, width), width)
    out[:, other] = passed[...].astype(F32)


def shards(frames, out_grad, ln_gain, w_up, w_down, lengths):
    peers = lax.axis_size("gx")
    half = peers // 2
    frame_len, width = frames.shape[1:]
    depth, hidden = w_up.shape
    quarter = hidden // 2
    half_width = width // 2
    half_rows = frame_len // 2
    ringed = peers <= 16 and peers % 2 == 0 and depth % 16 == 0

    order = list(range(0, peers, 2)) + list(range(peers - 1, 0, -2))
    ahead = [(order[i], order[(i + 1) % peers]) for i in range(peers)]
    behind = [(b, a) for a, b in ahead]
    swap = [(0, 1), (1, 0)]

    frames, out_grad = frames[0], out_grad[0]
    rows_of = shape((frame_len, width), BF16)
    block_of = shape((depth, quarter), BF16)
    passing, *mine = call(
        first_kernel,
        (lengths, frames, out_grad, ln_gain, w_up, w_down),
        (shape((2, half_rows, width), BF16), block_of, block_of),
        [pltpu.SemaphoreType.DMA((4,))] + [pltpu.VMEM((half_rows, width), BF16)] * 2,
        flops=5 * frame_len * width,
        vmem=60,
        left=(1, 2, 4, 5),
    )
    first = lax.ppermute(passing, "groups", swap)
    normed, grads, stats = call(
        norm_kernel,
        (lengths, frames, out_grad, ln_gain),
        (rows_of, rows_of, shape((frame_len, 2), F32)),
        flops=10 * frame_len * width,
    )

    weight = shape((width, quarter), BF16)
    if ringed:
        blocks = {(0, 0): mine[0], (0, 1): mine[1]}
        up, down = list(mine), list(mine)
        for step in range(1, half):
            for i in range(2):
                up[i] = lax.ppermute(up[i], "gx", ahead)
                down[i] = lax.ppermute(down[i], "gx", behind)
            if step == 1:
                up[0] = hold(up[0], normed)
            for i in range(2):
                blocks[-step, i], blocks[step, i] = up[i], down[i]
        late = {
            (half - 1, 0): blocks.pop((half - 1, 0)),
            (1 - half, 1): blocks.pop((1 - half, 1)),
            (half, 0): lax.ppermute(up[0], "gx", ahead),
            (half, 1): lax.ppermute(down[1], "gx", behind),
        }
        near = call(
            functools.partial(place_kernel, tuple(blocks), peers),
            list(blocks.values()),
            (weight, weight),
            [pltpu.SemaphoreType.DMA((len(blocks),))],
            pinned=range(len(blocks)),
        )
        first = hold(first, *late.values(), near[0])
        sends = ((half - 1, -half), (half, 1 - half))
    else:
        near = [lax.all_gather(block, "gx", axis=0, tiled=True) for block in mine]
        late, sends = {}, ((), ())
    second = lax.ppermute(first, "gy", swap)

    d_pre_of, partial_of = shape((frame_len, quarter), BF16), shape((width, quarter), BF16)
    d_pre_own, partial_own, full_up, full_down, *blocks_own = call(
        functools.partial(own_kernel, tuple(late), sends[1], peers),
        (normed, grads, *near, *late.values()),
        (d_pre_of, partial_of, weight, weight, *[block_of] * len(sends[1])),
        flops=6 * frame_len * width * quarter,
    )
    d_pre_other, partial_other, *blocks_other = call(
        functools.partial(other_kernel, sends[0], peers),
        (first, second, full_up, full_down),
        (d_pre_of, partial_of, *[block_of] * len(sends[0])),
        [pltpu.VMEM((frame_len, width), BF16)] * 2,
        flops=6 * frame_len * width * quarter,
    )
    partial = [partial_own, partial_other]

    half_rows_of = shape((frame_len, half_width), BF16)
    parts_of = [half_rows_of]

    def own_d_norm(*ties):
        keep, send, *parts = call(
            d_norm_kernel,
            (d_pre_own, d_pre_other, full_up),
            (shape((2, frame_len, half_width), BF16), half_rows_of, *parts_of),
            flops=4 * frame_len * width * quarter,
            ties=ties,
        )
        return keep, send, [lax.ppermute(part, "gy", swap) for part in parts]

    def over_cores(keep, parts, *ties):
        over = call(over_kernel, (keep, *parts), half_rows_of, ties=ties)
        return over, lax.ppermute(over, "groups", swap)

    def scale(keep, came, back, *ties):
        return call(
            scale_kernel,
            (keep, came, back, frames, ln_gain[None], grads, stats),
            (
                shape((frame_len, half_width), F32),
                shape((frame_len, half_width), F32),
                shape((frame_len, 2), F32),
            ),
            ties=ties,
        )

    up_grad_of = shape((depth, hidden), F32)
    if ringed:
        came, kept = [{}, {}], []

        def send_on(i, blocks, names):
            for block, name in zip(blocks, names):
                came[i][name] = lax.ppermute(block, "gx", ahead if name == "up" else behind)

        def hop(i, turn, *ties):
            ways = [("up", half - turn - i), ("down", turn + 1 - i - half)]
            ways = [way for way in ways if way[1] != 0]
            names = [name for name, _ in ways]
            ties += tuple(came[i][name] for name in came[i] if name not in names)
            blocks = call(
                functools.partial(hop_kernel, tuple(step for _, step in ways), peers),
                (partial[i], *[came[i][name] for name in names]),
                [block_of] * len(ways),
                ties=ties,
            )
            if (i, turn) == (0, half - 2):
                kept.append(blocks[1])
                blocks, names = blocks[:1], names[:1]
            send_on(i, blocks, names)
            return blocks[0]

        send_on(1, blocks_other, ("up", "down"))
        keep, send, parts = own_d_norm()
        send_on(0, [hold(block, keep) for block in blocks_own], ("up", "down"))
        tie = hop(1, 1, keep)
        tie = hop(0, 1, tie)
        tie = hop(1, 2, tie)
        tie, back = over_cores(keep, parts, tie)
        tie = hop(0, 2, tie)
        for turn in range(3, half):
            tie = hop(0, turn, hop(1, turn, tie))
        sent = lax.ppermute(send, "gy", swap)
        passing = call(
            functools.partial(total_kernel, peers),
            (partial[1], came[1]["up"], came[1]["down"]),
            block_of,
            ties=(tie,),
        )
        passed = lax.ppermute(passing, "groups", swap)
        send_on(0, [hold(kept[0], passing)], ["down"])
        base, factor, sums = scale(keep, sent, back, passing)
        input_grad, up_grad = call(
            functools.partial(last_kernel, peers),
            (base, factor, sums, lax.ppermute(sums, "gy", swap), stats)
            + (partial[0], came[0]["up"], came[0]["down"], passed),
            (half_rows_of, up_grad_of),
        )
    else:
        keep, send, parts = own_d_norm()
        sent = lax.ppermute(send, "gy", swap)
        _, back = over_cores(keep, parts)
        base, factor, sums = scale(keep, sent, back)
        came = lax.ppermute(sums, "gy", swap)
        input_grad = call(input_kernel, (base, factor, sums, came, stats), half_rows_of)
        total, passing = [
            lax.psum_scatter(p.astype(F32), "gx", scatter_dimension=0, tiled=True) for p in partial
        ]
        passed = lax.ppermute(passing.astype(BF16), "groups", swap)
        up_grad = call(place_halves_kernel, (total, passed), up_grad_of)
    return (input_grad[None], up_grad)


def solution(mesh):
    placed = (
        P(("groups", "gx"), None, None),
        P(("groups", "gx"), None, None),
        P(),
        P("gx", "gy"),
        P("gx", "gy"),
        P("groups"),
    )
    return jax.shard_map(
        shards,
        mesh=mesh,
        in_specs=placed,
        out_specs=(P(("groups", "gx"), None, "gy"), P(("groups", "gx"), "gy")),
        check_vma=False,
    )
```

```python
import functools

import jax
import jax.numpy as jnp
from jax import lax
from jax.experimental import pallas as pl
from jax.experimental.pallas import tpu as pltpu
from jax.sharding import PartitionSpec as P

BF16, F32 = jnp.bfloat16, jnp.float32
VMEM = pl.BlockSpec(memory_space=pltpu.VMEM)
HBM = pl.BlockSpec(memory_space=pltpu.HBM)
ANY = pl.BlockSpec(memory_space=pl.ANY)
SMEM = pl.BlockSpec(memory_space=pltpu.SMEM)


def shape(dims, kind):
    return jax.ShapeDtypeStruct(dims, kind)


def call(kernel, ins, out_shape, scratch=(), vmem=16, flops=1, left=(), pinned=(), ties=()):
    count = len(ins)

    def body(*refs):
        kernel(*refs[:count], *refs[count + len(ties) :])

    moved = sum(x.size * x.dtype.itemsize for x in list(ins) + jax.tree.leaves(out_shape))
    return pl.pallas_call(
        body if ties else kernel,
        out_shape=out_shape,
        in_specs=[
            SMEM if x.dtype == jnp.int32 else ANY if i in left else HBM if i in pinned else VMEM
            for i, x in enumerate(ins)
        ]
        + [ANY] * len(ties),
        out_specs=jax.tree.map(lambda _: VMEM, out_shape),
        scratch_shapes=list(scratch),
        compiler_params=pltpu.CompilerParams(vmem_limit_bytes=vmem << 20),
        cost_estimate=pl.CostEstimate(flops=flops, bytes_accessed=moved, transcendentals=0),
    )(*ins, *ties)


def hold(array, *ties):
    return pl.pallas_call(
        lambda *refs: None,
        out_shape=shape(array.shape, array.dtype),
        in_specs=[ANY] * (1 + len(ties)),
        out_specs=ANY,
        input_output_aliases={0: 0},
        compiler_params=pltpu.CompilerParams(vmem_limit_bytes=1 << 20),
        cost_estimate=pl.CostEstimate(flops=1, bytes_accessed=1, transcendentals=0),
    )(array, *ties)


def dot(left, right, left_dim=1, right_dim=0):
    return lax.dot_general(
        left, right, (((left_dim,), (right_dim,)), ((), ())), preferred_element_type=F32
    )


def gelu_slope(values):
    return (
        0.5 * (1.0 + lax.erf(values * 0.7071067811865476))
        + values * jnp.exp(-0.5 * values * values) * 0.3989422804014327
    )


def block_rows(step, peers, depth):
    own = lax.axis_index("gx")
    place = jnp.where(lax.rem(own, 2) == 0, lax.div(own, 2), peers - 1 - lax.div(own, 2))
    place = lax.rem(place + (step + peers), peers)
    member = jnp.where(place < peers // 2, 2 * place, 2 * (peers - 1 - place) + 1)
    return pl.ds(pl.multiple_of(member * depth, depth), depth)


def norm_rows(rows, gain):
    values = rows.astype(F32)
    centre = jnp.mean(values, axis=-1, keepdims=True)
    shifted = values - centre
    variance = jnp.mean(shifted * shifted, axis=-1, keepdims=True)
    inv_std = lax.rsqrt(variance + 1e-05)
    return (shifted * inv_std * gain[...][None]).astype(BF16), centre, inv_std


def mask_rows(rows, start, length):
    index = start + lax.broadcasted_iota(jnp.int32, (rows.shape[0], 1), 0)
    return jnp.where(index < length, rows.astype(F32), 0.0).astype(BF16)


def first_kernel(
    lengths, frames, out_grad, gain, w_up, w_down, passing, mine_up, mine_down, sems, rows, grads
):
    half, quarter = rows.shape[0], mine_up.shape[1]
    start = pl.multiple_of(lax.axis_index("gy") * half, half)
    columns = pl.ds(pl.multiple_of(lax.axis_index("groups") * quarter, quarter), quarter)
    moves = (
        (frames.at[pl.ds(start, half)], rows),
        (out_grad.at[pl.ds(start, half)], grads),
        (w_up.at[:, columns], mine_up),
        (w_down.at[:, columns], mine_down),
    )
    copies = [pltpu.make_async_copy(*move, sems.at[i]) for i, move in enumerate(moves)]
    for copy in copies:
        copy.start()
    copies[0].wait()
    passing[0] = norm_rows(rows[...], gain)[0]
    copies[1].wait()
    passing[1] = mask_rows(grads[...], start, lengths[lax.axis_index("gx")])
    copies[2].wait()
    copies[3].wait()


def norm_kernel(lengths, frames, out_grad, gain, normed, grads, stats):
    value, centre, inv_std = norm_rows(frames[...], gain)
    normed[...] = value
    stats[:, 0:1] = centre
    stats[:, 1:2] = inv_std
    grads[...] = mask_rows(out_grad[...], 0, lengths[lax.axis_index("gx")])


def back_through(normed, grads, up, down, d_pre, partial):
    pre_act = dot(normed[...], up[...])
    d_act = dot(grads[...], down[...])
    d_pre[...] = (d_act * gelu_slope(pre_act)).astype(BF16)
    partial[...] = dot(normed[...], d_pre[...], 0, 0).astype(BF16)


def place_kernel(places, peers, *refs):
    blocks, (up, down, sems) = refs[:-3], refs[-3:]
    copies = []
    for i, ((step, which), block) in enumerate(zip(places, blocks)):
        rows = block_rows(step, peers, block.shape[0])
        copies.append(pltpu.make_async_copy(block, (up, down)[which].at[rows], sems.at[i]))
    for copy in copies:
        copy.start()
    for copy in copies:
        copy.wait()


def own_kernel(places, sends, peers, normed, grads, near_up, near_down, *refs):
    late, refs = refs[: len(places)], refs[len(places) :]
    (d_pre, partial, up, down), blocks = refs[:4], refs[4:]
    up[...] = near_up[...]
    down[...] = near_down[...]
    for (step, which), block in zip(places, late):
        (up, down)[which][block_rows(step, peers, block.shape[0]), :] = block[...]
    back_through(normed, grads, up, down, d_pre, partial)
    for step, block in zip(sends, blocks):
        block[...] = partial[block_rows(step, peers, block.shape[0]), :]


def other_kernel(sends, peers, first, second, up, down, d_pre, partial, *refs):
    blocks, (normed, grads) = refs[:-2], refs[-2:]
    half = first.shape[1]
    for at, part in ((0, first), (half, second)):
        normed[at : at + half, :] = part[0]
        grads[at : at + half, :] = part[1]
    back_through(normed, grads, up, down, d_pre, partial)
    for step, block in zip(sends, blocks):
        block[...] = partial[block_rows(step, peers, block.shape[0]), :]


def d_norm_kernel(d_pre_own, d_pre_other, up, keep, send_other, *sends):
    core = lax.axis_index("gy")
    rows, width = keep.shape[1:]
    mine = up[pl.ds(pl.multiple_of(core * width, width), width), :]
    theirs = up[pl.ds(pl.multiple_of((1 - core) * width, width), width), :]
    keep[0] = dot(d_pre_own[...], mine, 1, 1).astype(BF16)
    keep[1] = dot(d_pre_other[...], mine, 1, 1).astype(BF16)
    sent = dot(d_pre_other[...], theirs, 1, 1).astype(BF16)
    send_other[: rows // 2, :] = sent[rows // 2 :]
    send_other[rows // 2 :, :] = sent[: rows // 2]
    sent = dot(d_pre_own[...], theirs, 1, 1).astype(BF16)
    step = rows // len(sends)
    for i, send in enumerate(sends):
        send[...] = sent[i * step : (i + 1) * step]


def over_kernel(keep, came, over):
    half = over.shape[0] // 2
    value = (keep[1].astype(F32) + came[...].astype(F32)).astype(BF16)
    for i in range(2):
        at = lax.rem(i + lax.axis_index("gy"), 2) * half
        over[pl.ds(pl.multiple_of(at, half), half), :] = value[i * half : (i + 1) * half]


def own_columns(ref, width):
    return ref[:, pl.ds(pl.multiple_of(lax.axis_index("gy") * width, width), width)]


def scale_kernel(keep, back, frames, gain, grads, stats, *refs):
    came, (base, factor, sums) = refs[:-3], refs[-3:]
    width = base.shape[1]
    d_norm = jnp.concatenate([part[...].astype(F32) for part in came])
    d_norm = keep[0].astype(F32) + d_norm + back[...].astype(F32)
    scaled = d_norm * own_columns(gain, width)
    rows = own_columns(frames, width).astype(F32)
    inv_std = stats[:, 1:2]
    centred = (rows - stats[:, 0:1]) * inv_std
    sums[:, 0:1] = jnp.sum(scaled, axis=-1, keepdims=True)
    sums[:, 1:2] = jnp.sum(scaled * centred, axis=-1, keepdims=True)
    base[...] = own_columns(grads, width).astype(F32) + inv_std * scaled
    factor[...] = inv_std * centred


def input_rows(base, factor, sums, came, stats):
    means = (sums[...] + came[...]) * (0.5 / base.shape[1])
    value = base[...] - stats[:, 1:2] * means[:, 0:1] - factor[...] * means[:, 1:2]
    return value.astype(BF16)


def input_kernel(base, factor, sums, came, stats, out):
    out[...] = input_rows(base, factor, sums, came, stats)


def hop_kernel(places, peers, partial, *refs):
    count = len(places)
    for step, came, out in zip(places, refs[:count], refs[count:]):
        value = partial[block_rows(step, peers, out.shape[0]), :].astype(F32)
        out[...] = (value + came[...].astype(F32)).astype(BF16)


def total_kernel(peers, partial, up, down, total):
    value = partial[block_rows(0, peers, total.shape[0]), :].astype(F32)
    total[...] = (value + up[...].astype(F32) + down[...].astype(F32)).astype(BF16)


def last_kernel(peers, base, factor, sums, came, stats, partial, up, down, passed, *outs):
    input_grad, up_grad = outs
    input_grad[...] = input_rows(base, factor, sums, came, stats)
    depth, width = passed.shape
    side = lax.axis_index("groups")
    value = partial[block_rows(0, peers, depth), :].astype(F32)
    value = value + up[...].astype(F32) + down[...].astype(F32)
    up_grad[:, pl.ds(pl.multiple_of(side * width, width), width)] = value
    other = pl.ds(pl.multiple_of((1 - side) * width, width), width)
    up_grad[:, other] = passed[...].astype(F32)


def place_halves_kernel(own, passed, out):
    width = own.shape[1]
    side = lax.axis_index("groups")
    out[:, pl.ds(pl.multiple_of(side * width, width), width)] = own[...]
    other = pl.ds(pl.multiple_of((1 - side) * width, width), width)
    out[:, other] = passed[...].astype(F32)


def shards(frames, out_grad, ln_gain, w_up, w_down, lengths):
    peers = lax.axis_size("gx")
    half = peers // 2
    frame_len, width = frames.shape[1:]
    depth, hidden = w_up.shape
    quarter = hidden // 2
    half_width = width // 2
    half_rows = frame_len // 2
    ringed = peers <= 16 and peers % 2 == 0 and depth % 16 == 0

    order = list(range(0, peers, 2)) + list(range(peers - 1, 0, -2))
    ahead = [(order[i], order[(i + 1) % peers]) for i in range(peers)]
    behind = [(b, a) for a, b in ahead]
    swap = [(0, 1), (1, 0)]

    frames, out_grad = frames[0], out_grad[0]
    rows_of = shape((frame_len, width), BF16)
    block_of = shape((depth, quarter), BF16)
    passing, *mine = call(
        first_kernel,
        (lengths, frames, out_grad, ln_gain, w_up, w_down),
        (shape((2, half_rows, width), BF16), block_of, block_of),
        [pltpu.SemaphoreType.DMA((4,))] + [pltpu.VMEM((half_rows, width), BF16)] * 2,
        flops=5 * frame_len * width,
        vmem=60,
        left=(1, 2, 4, 5),
    )
    first = lax.ppermute(passing, "groups", swap)
    normed, grads, stats = call(
        norm_kernel,
        (lengths, frames, out_grad, ln_gain),
        (rows_of, rows_of, shape((frame_len, 2), F32)),
        flops=10 * frame_len * width,
    )

    weight = shape((width, quarter), BF16)
    if ringed:
        blocks = {(0, 0): mine[0], (0, 1): mine[1]}
        up, down = list(mine), list(mine)
        for step in range(1, half):
            for i in range(2):
                up[i] = lax.ppermute(up[i], "gx", ahead)
                down[i] = lax.ppermute(down[i], "gx", behind)
            if step == 1:
                up[0] = hold(up[0], normed)
            for i in range(2):
                blocks[-step, i], blocks[step, i] = up[i], down[i]
        late = {
            (half - 1, 0): blocks.pop((half - 1, 0)),
            (1 - half, 1): blocks.pop((1 - half, 1)),
            (half, 0): lax.ppermute(up[0], "gx", ahead),
            (half, 1): lax.ppermute(down[1], "gx", behind),
        }
        near = call(
            functools.partial(place_kernel, tuple(blocks), peers),
            list(blocks.values()),
            (weight, weight),
            [pltpu.SemaphoreType.DMA((len(blocks),))],
            pinned=range(len(blocks)),
        )
        first = hold(first, *late.values(), near[0])
        sends = ((half - 1, -half), (half, 1 - half))
    else:
        near = [lax.all_gather(block, "gx", axis=0, tiled=True) for block in mine]
        late, sends = {}, ((), ())
    second = lax.ppermute(first, "gy", swap)

    d_pre_of, partial_of = shape((frame_len, quarter), BF16), shape((width, quarter), BF16)
    d_pre_own, partial_own, full_up, full_down, *blocks_own = call(
        functools.partial(own_kernel, tuple(late), sends[1], peers),
        (normed, grads, *near, *late.values()),
        (d_pre_of, partial_of, weight, weight, *[block_of] * len(sends[1])),
        flops=6 * frame_len * width * quarter,
    )
    d_pre_other, partial_other, *blocks_other = call(
        functools.partial(other_kernel, sends[0], peers),
        (first, second, full_up, full_down),
        (d_pre_of, partial_of, *[block_of] * len(sends[0])),
        [pltpu.VMEM((frame_len, width), BF16)] * 2,
        flops=6 * frame_len * width * quarter,
    )
    partial = [partial_own, partial_other]

    half_rows_of = shape((frame_len, half_width), BF16)
    parts_of = [shape((frame_len // 3, half_width), BF16)] * 3

    def own_d_norm(*ties):
        keep, send, *parts = call(
            d_norm_kernel,
            (d_pre_own, d_pre_other, full_up),
            (shape((2, frame_len, half_width), BF16), half_rows_of, *parts_of),
            flops=4 * frame_len * width * quarter,
            ties=ties,
        )
        sent = [lax.ppermute(part, "gy", swap) for part in parts]
        return keep, lax.ppermute(send, "gy", swap), sent

    def over_cores(keep, came, *ties):
        over = call(over_kernel, (keep, came), half_rows_of, ties=ties)
        return over, lax.ppermute(over, "groups", swap)

    def scale(keep, came, back, *ties):
        return call(
            scale_kernel,
            (keep, back, frames, ln_gain[None], grads, stats, *came),
            (
                shape((frame_len, half_width), F32),
                shape((frame_len, half_width), F32),
                shape((frame_len, 2), F32),
            ),
            ties=ties,
        )

    up_grad_of = shape((depth, hidden), F32)
    if ringed:
        came, kept = [{}, {}], []

        def send_on(i, blocks, names):
            for block, name in zip(blocks, names):
                came[i][name] = lax.ppermute(block, "gx", ahead if name == "up" else behind)

        def hop(i, turn, *ties):
            ways = [("up", half - turn - i), ("down", turn + 1 - i - half)]
            ways = [way for way in ways if way[1] != 0]
            names = [name for name, _ in ways]
            ties += tuple(came[i][name] for name in came[i] if name not in names)
            blocks = call(
                functools.partial(hop_kernel, tuple(step for _, step in ways), peers),
                (partial[i], *[came[i][name] for name in names]),
                [block_of] * len(ways),
                ties=ties,
            )
            if (i, turn) == (0, half - 2):
                kept.append(blocks[1])
                blocks, names = blocks[:1], names[:1]
            send_on(i, blocks, names)
            return blocks[0]

        send_on(1, blocks_other, ("up", "down"))
        keep, came_other, sent = own_d_norm()
        send_on(0, [hold(block, keep) for block in blocks_own], ("up", "down"))
        tie = hop(1, 1, keep)
        tie = hop(0, 1, tie)
        tie = hop(1, 2, tie)
        tie, back = over_cores(keep, came_other, tie)
        tie = hop(0, 2, tie)
        for turn in range(3, half):
            tie = hop(0, turn, hop(1, turn, tie))
        passing = call(
            functools.partial(total_kernel, peers),
            (partial[1], came[1]["up"], came[1]["down"]),
            block_of,
            ties=(tie,),
        )
        passed = lax.ppermute(passing, "groups", swap)
        send_on(0, [hold(kept[0], passing)], ["down"])
        base, factor, sums = scale(keep, sent, back, passing)
        input_grad, up_grad = call(
            functools.partial(last_kernel, peers),
            (base, factor, sums, lax.ppermute(sums, "gy", swap), stats)
            + (partial[0], came[0]["up"], came[0]["down"], passed),
            (half_rows_of, up_grad_of),
        )
    else:
        keep, came_other, sent = own_d_norm()
        _, back = over_cores(keep, came_other)
        base, factor, sums = scale(keep, sent, back)
        came = lax.ppermute(sums, "gy", swap)
        input_grad = call(input_kernel, (base, factor, sums, came, stats), half_rows_of)
        total, passing = [
            lax.psum_scatter(p.astype(F32), "gx", scatter_dimension=0, tiled=True) for p in partial
        ]
        passed = lax.ppermute(passing.astype(BF16), "groups", swap)
        up_grad = call(place_halves_kernel, (total, passed), up_grad_of)
    return (input_grad[None], up_grad)


def solution(mesh):
    placed = (
        P(("groups", "gx"), None, None),
        P(("groups", "gx"), None, None),
        P(),
        P("gx", "gy"),
        P("gx", "gy"),
        P("groups"),
    )
    return jax.shard_map(
        shards,
        mesh=mesh,
        in_specs=placed,
        out_specs=(P(("groups", "gx"), None, "gy"), P(("groups", "gx"), "gy")),
        check_vma=False,
    )
```

```python
import functools

import jax
import jax.numpy as jnp
from jax import lax
from jax.experimental import pallas as pl
from jax.experimental.pallas import tpu as pltpu
from jax.sharding import PartitionSpec as P

BF16, F32 = jnp.bfloat16, jnp.float32
VMEM = pl.BlockSpec(memory_space=pltpu.VMEM)
HBM = pl.BlockSpec(memory_space=pltpu.HBM)
ANY = pl.BlockSpec(memory_space=pl.ANY)
SMEM = pl.BlockSpec(memory_space=pltpu.SMEM)


def shape(dims, kind):
    return jax.ShapeDtypeStruct(dims, kind)


def call(kernel, ins, out_shape, scratch=(), vmem=16, flops=1, left=(), pinned=(), ties=()):
    count = len(ins)

    def body(*refs):
        kernel(*refs[:count], *refs[count + len(ties) :])

    moved = sum(x.size * x.dtype.itemsize for x in list(ins) + jax.tree.leaves(out_shape))
    return pl.pallas_call(
        body if ties else kernel,
        out_shape=out_shape,
        in_specs=[
            SMEM if x.dtype == jnp.int32 else ANY if i in left else HBM if i in pinned else VMEM
            for i, x in enumerate(ins)
        ]
        + [ANY] * len(ties),
        out_specs=jax.tree.map(lambda _: VMEM, out_shape),
        scratch_shapes=list(scratch),
        compiler_params=pltpu.CompilerParams(vmem_limit_bytes=vmem << 20),
        cost_estimate=pl.CostEstimate(flops=flops, bytes_accessed=moved, transcendentals=0),
    )(*ins, *ties)


def hold(array, *ties):
    return pl.pallas_call(
        lambda *refs: None,
        out_shape=shape(array.shape, array.dtype),
        in_specs=[ANY] * (1 + len(ties)),
        out_specs=ANY,
        input_output_aliases={0: 0},
        compiler_params=pltpu.CompilerParams(vmem_limit_bytes=1 << 20),
        cost_estimate=pl.CostEstimate(flops=1, bytes_accessed=1, transcendentals=0),
    )(array, *ties)


def dot(left, right, left_dim=1, right_dim=0):
    return lax.dot_general(
        left, right, (((left_dim,), (right_dim,)), ((), ())), preferred_element_type=F32
    )


def gelu_slope(values):
    return (
        0.5 * (1.0 + lax.erf(values * 0.7071067811865476))
        + values * jnp.exp(-0.5 * values * values) * 0.3989422804014327
    )


def block_rows(step, peers, depth):
    own = lax.axis_index("gx")
    place = jnp.where(lax.rem(own, 2) == 0, lax.div(own, 2), peers - 1 - lax.div(own, 2))
    place = lax.rem(place + (step + peers), peers)
    member = jnp.where(place < peers // 2, 2 * place, 2 * (peers - 1 - place) + 1)
    return pl.ds(pl.multiple_of(member * depth, depth), depth)


def norm_rows(rows, gain):
    values = rows.astype(F32)
    centre = jnp.mean(values, axis=-1, keepdims=True)
    shifted = values - centre
    variance = jnp.mean(shifted * shifted, axis=-1, keepdims=True)
    inv_std = lax.rsqrt(variance + 1e-05)
    return (shifted * inv_std * gain[...][None]).astype(BF16), centre, inv_std


def mask_rows(rows, start, length):
    index = start + lax.broadcasted_iota(jnp.int32, (rows.shape[0], 1), 0)
    return jnp.where(index < length, rows.astype(F32), 0.0).astype(BF16)


def first_kernel(
    lengths, frames, out_grad, gain, w_up, w_down, passing, mine_up, mine_down, sems, rows, grads
):
    half, quarter = rows.shape[0], mine_up.shape[1]
    start = pl.multiple_of(lax.axis_index("gy") * half, half)
    columns = pl.ds(pl.multiple_of(lax.axis_index("groups") * quarter, quarter), quarter)
    moves = (
        (frames.at[pl.ds(start, half)], rows),
        (out_grad.at[pl.ds(start, half)], grads),
        (w_up.at[:, columns], mine_up),
        (w_down.at[:, columns], mine_down),
    )
    copies = [pltpu.make_async_copy(*move, sems.at[i]) for i, move in enumerate(moves)]
    for copy in copies:
        copy.start()
    copies[0].wait()
    passing[0] = norm_rows(rows[...], gain)[0]
    copies[1].wait()
    passing[1] = mask_rows(grads[...], start, lengths[lax.axis_index("gx")])
    copies[2].wait()
    copies[3].wait()


def norm_kernel(lengths, frames, out_grad, gain, normed, grads, stats):
    value, centre, inv_std = norm_rows(frames[...], gain)
    normed[...] = value
    stats[:, 0:1] = centre
    stats[:, 1:2] = inv_std
    grads[...] = mask_rows(out_grad[...], 0, lengths[lax.axis_index("gx")])


def back_through(normed, grads, up, down, d_pre, partial):
    tile = 256
    for at in range(0, d_pre.shape[1], tile):
        columns = slice(at, min(at + tile, d_pre.shape[1]))
        pre_act = dot(normed[...], up[:, columns])
        d_act = dot(grads[...], down[:, columns])
        d_pre[:, columns] = (d_act * gelu_slope(pre_act)).astype(BF16)
    partial[...] = dot(normed[...], d_pre[...], 0, 0).astype(BF16)


def place_kernel(places, peers, *refs):
    blocks, (up, down, sems) = refs[:-3], refs[-3:]
    copies = []
    for i, ((step, which), block) in enumerate(zip(places, blocks)):
        rows = block_rows(step, peers, block.shape[0])
        copies.append(pltpu.make_async_copy(block, (up, down)[which].at[rows], sems.at[i]))
    for copy in copies:
        copy.start()
    for copy in copies:
        copy.wait()


def own_kernel(places, sends, peers, normed, grads, near_up, near_down, *refs):
    late, refs = refs[: len(places)], refs[len(places) :]
    (d_pre, partial, up, down), blocks = refs[:4], refs[4:]
    up[...] = near_up[...]
    down[...] = near_down[...]
    for (step, which), block in zip(places, late):
        (up, down)[which][block_rows(step, peers, block.shape[0]), :] = block[...]
    back_through(normed, grads, up, down, d_pre, partial)
    for step, block in zip(sends, blocks):
        block[...] = partial[block_rows(step, peers, block.shape[0]), :]


def other_kernel(sends, peers, first, second, up, down, d_pre, partial, *refs):
    blocks, (normed, grads) = refs[:-2], refs[-2:]
    half = first.shape[1]
    for at, part in ((0, first), (half, second)):
        normed[at : at + half, :] = part[0]
        grads[at : at + half, :] = part[1]
    back_through(normed, grads, up, down, d_pre, partial)
    for step, block in zip(sends, blocks):
        block[...] = partial[block_rows(step, peers, block.shape[0]), :]


def d_norm_kernel(d_pre_own, d_pre_other, up, keep, send_other, *sends):
    core = lax.axis_index("gy")
    rows, width = keep.shape[1:]
    mine = up[pl.ds(pl.multiple_of(core * width, width), width), :]
    theirs = up[pl.ds(pl.multiple_of((1 - core) * width, width), width), :]
    keep[0] = dot(d_pre_own[...], mine, 1, 1).astype(BF16)
    keep[1] = dot(d_pre_other[...], mine, 1, 1).astype(BF16)
    sent = dot(d_pre_other[...], theirs, 1, 1).astype(BF16)
    send_other[: rows // 2, :] = sent[rows // 2 :]
    send_other[rows // 2 :, :] = sent[: rows // 2]
    sent = dot(d_pre_own[...], theirs, 1, 1).astype(BF16)
    step = rows // len(sends)
    for i, send in enumerate(sends):
        send[...] = sent[i * step : (i + 1) * step]


def over_kernel(keep, came, over):
    half = over.shape[0] // 2
    value = (keep[1].astype(F32) + came[...].astype(F32)).astype(BF16)
    for i in range(2):
        at = lax.rem(i + lax.axis_index("gy"), 2) * half
        over[pl.ds(pl.multiple_of(at, half), half), :] = value[i * half : (i + 1) * half]


def own_columns(ref, width):
    return ref[:, pl.ds(pl.multiple_of(lax.axis_index("gy") * width, width), width)]


def scale_kernel(keep, back, frames, gain, grads, stats, *refs):
    came, (base, factor, sums) = refs[:-3], refs[-3:]
    width = base.shape[1]
    d_norm = jnp.concatenate([part[...].astype(F32) for part in came])
    d_norm = keep[0].astype(F32) + d_norm + back[...].astype(F32)
    scaled = d_norm * own_columns(gain, width)
    rows = own_columns(frames, width).astype(F32)
    inv_std = stats[:, 1:2]
    centred = (rows - stats[:, 0:1]) * inv_std
    sums[:, 0:1] = jnp.sum(scaled, axis=-1, keepdims=True)
    sums[:, 1:2] = jnp.sum(scaled * centred, axis=-1, keepdims=True)
    base[...] = own_columns(grads, width).astype(F32) + inv_std * scaled
    factor[...] = inv_std * centred


def input_rows(base, factor, sums, came, stats):
    means = (sums[...] + came[...]) * (0.5 / base.shape[1])
    value = base[...] - stats[:, 1:2] * means[:, 0:1] - factor[...] * means[:, 1:2]
    return value.astype(BF16)


def input_kernel(base, factor, sums, came, stats, out):
    out[...] = input_rows(base, factor, sums, came, stats)


def hop_kernel(places, peers, partial, *refs):
    count = len(places)
    for step, came, out in zip(places, refs[:count], refs[count:]):
        value = partial[block_rows(step, peers, out.shape[0]), :].astype(F32)
        out[...] = (value + came[...].astype(F32)).astype(BF16)


def total_kernel(peers, partial, up, down, total):
    value = partial[block_rows(0, peers, total.shape[0]), :].astype(F32)
    total[...] = (value + up[...].astype(F32) + down[...].astype(F32)).astype(BF16)


def last_kernel(peers, base, factor, sums, came, stats, partial, up, down, passed, *outs):
    input_grad, up_grad = outs
    input_grad[...] = input_rows(base, factor, sums, came, stats)
    depth, width = passed.shape
    side = lax.axis_index("groups")
    value = partial[block_rows(0, peers, depth), :].astype(F32)
    value = value + up[...].astype(F32) + down[...].astype(F32)
    up_grad[:, pl.ds(pl.multiple_of(side * width, width), width)] = value
    other = pl.ds(pl.multiple_of((1 - side) * width, width), width)
    up_grad[:, other] = passed[...].astype(F32)


def place_halves_kernel(own, passed, out):
    width = own.shape[1]
    side = lax.axis_index("groups")
    out[:, pl.ds(pl.multiple_of(side * width, width), width)] = own[...]
    other = pl.ds(pl.multiple_of((1 - side) * width, width), width)
    out[:, other] = passed[...].astype(F32)


def shards(frames, out_grad, ln_gain, w_up, w_down, lengths):
    peers = lax.axis_size("gx")
    half = peers // 2
    frame_len, width = frames.shape[1:]
    depth, hidden = w_up.shape
    quarter = hidden // 2
    half_width = width // 2
    half_rows = frame_len // 2
    ringed = peers <= 16 and peers % 2 == 0 and depth % 16 == 0

    order = list(range(0, peers, 2)) + list(range(peers - 1, 0, -2))
    ahead = [(order[i], order[(i + 1) % peers]) for i in range(peers)]
    behind = [(b, a) for a, b in ahead]
    swap = [(0, 1), (1, 0)]

    frames, out_grad = frames[0], out_grad[0]
    rows_of = shape((frame_len, width), BF16)
    block_of = shape((depth, quarter), BF16)
    passing, *mine = call(
        first_kernel,
        (lengths, frames, out_grad, ln_gain, w_up, w_down),
        (shape((2, half_rows, width), BF16), block_of, block_of),
        [pltpu.SemaphoreType.DMA((4,))] + [pltpu.VMEM((half_rows, width), BF16)] * 2,
        flops=5 * frame_len * width,
        vmem=60,
        left=(1, 2, 4, 5),
    )
    first = lax.ppermute(passing, "groups", swap)
    normed, grads, stats = call(
        norm_kernel,
        (lengths, frames, out_grad, ln_gain),
        (rows_of, rows_of, shape((frame_len, 2), F32)),
        flops=10 * frame_len * width,
    )

    weight = shape((width, quarter), BF16)
    if ringed:
        blocks = {(0, 0): mine[0], (0, 1): mine[1]}
        up, down = list(mine), list(mine)
        for step in range(1, half):
            for i in range(2):
                up[i] = lax.ppermute(up[i], "gx", ahead)
                down[i] = lax.ppermute(down[i], "gx", behind)
            if step == 1:
                up[0] = hold(up[0], normed)
            for i in range(2):
                blocks[-step, i], blocks[step, i] = up[i], down[i]
        late = {
            (half - 1, 0): blocks.pop((half - 1, 0)),
            (1 - half, 1): blocks.pop((1 - half, 1)),
            (half, 0): lax.ppermute(up[0], "gx", ahead),
            (half, 1): lax.ppermute(down[1], "gx", behind),
        }
        near = call(
            functools.partial(place_kernel, tuple(blocks), peers),
            list(blocks.values()),
            (weight, weight),
            [pltpu.SemaphoreType.DMA((len(blocks),))],
            pinned=range(len(blocks)),
        )
        first = hold(first, *late.values(), near[0])
        sends = ((half - 1, -half), (half, 1 - half))
    else:
        near = [lax.all_gather(block, "gx", axis=0, tiled=True) for block in mine]
        late, sends = {}, ((), ())
    second = lax.ppermute(first, "gy", swap)

    d_pre_of, partial_of = shape((frame_len, quarter), BF16), shape((width, quarter), BF16)
    d_pre_own, partial_own, full_up, full_down, *blocks_own = call(
        functools.partial(own_kernel, tuple(late), sends[1], peers),
        (normed, grads, *near, *late.values()),
        (d_pre_of, partial_of, weight, weight, *[block_of] * len(sends[1])),
        flops=6 * frame_len * width * quarter,
    )
    d_pre_other, partial_other, *blocks_other = call(
        functools.partial(other_kernel, sends[0], peers),
        (first, second, full_up, full_down),
        (d_pre_of, partial_of, *[block_of] * len(sends[0])),
        [pltpu.VMEM((frame_len, width), BF16)] * 2,
        flops=6 * frame_len * width * quarter,
    )
    partial = [partial_own, partial_other]

    half_rows_of = shape((frame_len, half_width), BF16)
    parts_of = [shape((frame_len // 3, half_width), BF16)] * 3

    def own_d_norm(*ties):
        keep, send, *parts = call(
            d_norm_kernel,
            (d_pre_own, d_pre_other, full_up),
            (shape((2, frame_len, half_width), BF16), half_rows_of, *parts_of),
            flops=4 * frame_len * width * quarter,
            ties=ties,
        )
        sent = [lax.ppermute(part, "gy", swap) for part in parts]
        return keep, lax.ppermute(send, "gy", swap), sent

    def over_cores(keep, came, *ties):
        over = call(over_kernel, (keep, came), half_rows_of, ties=ties)
        return over, lax.ppermute(over, "groups", swap)

    def scale(keep, came, back, *ties):
        return call(
            scale_kernel,
            (keep, back, frames, ln_gain[None], grads, stats, *came),
            (
                shape((frame_len, half_width), F32),
                shape((frame_len, half_width), F32),
                shape((frame_len, 2), F32),
            ),
            ties=ties,
        )

    up_grad_of = shape((depth, hidden), F32)
    if ringed:
        came, kept = [{}, {}], []

        def send_on(i, blocks, names):
            for block, name in zip(blocks, names):
                came[i][name] = lax.ppermute(block, "gx", ahead if name == "up" else behind)

        def hop(i, turn, *ties):
            ways = [("up", half - turn - i), ("down", turn + 1 - i - half)]
            ways = [way for way in ways if way[1] != 0]
            names = [name for name, _ in ways]
            ties += tuple(came[i][name] for name in came[i] if name not in names)
            blocks = call(
                functools.partial(hop_kernel, tuple(step for _, step in ways), peers),
                (partial[i], *[came[i][name] for name in names]),
                [block_of] * len(ways),
                ties=ties,
            )
            if (i, turn) == (0, half - 2):
                kept.append(blocks[1])
                blocks, names = blocks[:1], names[:1]
            send_on(i, blocks, names)
            return blocks[0]

        send_on(1, blocks_other, ("up", "down"))
        keep, came_other, sent = own_d_norm()
        send_on(0, [hold(block, keep) for block in blocks_own], ("up", "down"))
        tie = hop(1, 1, keep)
        tie = hop(0, 1, tie)
        tie = hop(1, 2, tie)
        tie, back = over_cores(keep, came_other, tie)
        tie = hop(0, 2, tie)
        for turn in range(3, half):
            tie = hop(0, turn, hop(1, turn, tie))
        passing = call(
            functools.partial(total_kernel, peers),
            (partial[1], came[1]["up"], came[1]["down"]),
            block_of,
            ties=(tie,),
        )
        passed = lax.ppermute(passing, "groups", swap)
        send_on(0, [hold(kept[0], passing)], ["down"])
        base, factor, sums = scale(keep, sent, back, passing)
        input_grad, up_grad = call(
            functools.partial(last_kernel, peers),
            (base, factor, sums, lax.ppermute(sums, "gy", swap), stats)
            + (partial[0], came[0]["up"], came[0]["down"], passed),
            (half_rows_of, up_grad_of),
        )
    else:
        keep, came_other, sent = own_d_norm()
        _, back = over_cores(keep, came_other)
        base, factor, sums = scale(keep, sent, back)
        came = lax.ppermute(sums, "gy", swap)
        input_grad = call(input_kernel, (base, factor, sums, came, stats), half_rows_of)
        total, passing = [
            lax.psum_scatter(p.astype(F32), "gx", scatter_dimension=0, tiled=True) for p in partial
        ]
        passed = lax.ppermute(passing.astype(BF16), "groups", swap)
        up_grad = call(place_halves_kernel, (total, passed), up_grad_of)
    return (input_grad[None], up_grad)


def solution(mesh):
    placed = (
        P(("groups", "gx"), None, None),
        P(("groups", "gx"), None, None),
        P(),
        P("gx", "gy"),
        P("gx", "gy"),
        P("groups"),
    )
    return jax.shard_map(
        shards,
        mesh=mesh,
        in_specs=placed,
        out_specs=(P(("groups", "gx"), None, "gy"), P(("groups", "gx"), "gy")),
        check_vma=False,
    )
```

```python
import functools

import jax
import jax.numpy as jnp
from jax import lax
from jax.experimental import pallas as pl
from jax.experimental.pallas import tpu as pltpu
from jax.sharding import PartitionSpec as P

BF16, F32 = jnp.bfloat16, jnp.float32
VMEM = pl.BlockSpec(memory_space=pltpu.VMEM)
HBM = pl.BlockSpec(memory_space=pltpu.HBM)
ANY = pl.BlockSpec(memory_space=pl.ANY)
SMEM = pl.BlockSpec(memory_space=pltpu.SMEM)


def shape(dims, kind):
    return jax.ShapeDtypeStruct(dims, kind)


def call(kernel, ins, out_shape, scratch=(), vmem=16, flops=1, left=(), pinned=(), ties=()):
    count = len(ins)

    def body(*refs):
        kernel(*refs[:count], *refs[count + len(ties) :])

    moved = sum(x.size * x.dtype.itemsize for x in list(ins) + jax.tree.leaves(out_shape))
    return pl.pallas_call(
        body if ties else kernel,
        out_shape=out_shape,
        in_specs=[
            SMEM if x.dtype == jnp.int32 else ANY if i in left else HBM if i in pinned else VMEM
            for i, x in enumerate(ins)
        ]
        + [ANY] * len(ties),
        out_specs=jax.tree.map(lambda _: VMEM, out_shape),
        scratch_shapes=list(scratch),
        compiler_params=pltpu.CompilerParams(vmem_limit_bytes=vmem << 20),
        cost_estimate=pl.CostEstimate(flops=flops, bytes_accessed=moved, transcendentals=0),
    )(*ins, *ties)


def hold(array, *ties):
    return pl.pallas_call(
        lambda *refs: None,
        out_shape=shape(array.shape, array.dtype),
        in_specs=[ANY] * (1 + len(ties)),
        out_specs=ANY,
        input_output_aliases={0: 0},
        compiler_params=pltpu.CompilerParams(vmem_limit_bytes=1 << 20),
        cost_estimate=pl.CostEstimate(flops=1, bytes_accessed=1, transcendentals=0),
    )(array, *ties)


def dot(left, right, left_dim=1, right_dim=0):
    return lax.dot_general(
        left, right, (((left_dim,), (right_dim,)), ((), ())), preferred_element_type=F32
    )


def gelu_slope(values):
    return (
        0.5 * (1.0 + lax.erf(values * 0.7071067811865476))
        + values * jnp.exp(-0.5 * values * values) * 0.3989422804014327
    )


def block_rows(step, peers, depth):
    own = lax.axis_index("gx")
    place = jnp.where(lax.rem(own, 2) == 0, lax.div(own, 2), peers - 1 - lax.div(own, 2))
    place = lax.rem(place + (step + peers), peers)
    member = jnp.where(place < peers // 2, 2 * place, 2 * (peers - 1 - place) + 1)
    return pl.ds(pl.multiple_of(member * depth, depth), depth)


def norm_rows(rows, gain):
    values = rows.astype(F32)
    centre = jnp.mean(values, axis=-1, keepdims=True)
    shifted = values - centre
    variance = jnp.mean(shifted * shifted, axis=-1, keepdims=True)
    inv_std = lax.rsqrt(variance + 1e-05)
    return (shifted * inv_std * gain[...][None]).astype(BF16), centre, inv_std


def mask_rows(rows, start, length):
    index = start + lax.broadcasted_iota(jnp.int32, (rows.shape[0], 1), 0)
    return jnp.where(index < length, rows.astype(F32), 0.0).astype(BF16)


def first_kernel(
    lengths, frames, out_grad, gain, w_up, w_down, passing, mine_up, mine_down, sems, rows, grads
):
    half, quarter = rows.shape[0], mine_up.shape[1]
    start = pl.multiple_of(lax.axis_index("gy") * half, half)
    columns = pl.ds(pl.multiple_of(lax.axis_index("groups") * quarter, quarter), quarter)
    moves = (
        (frames.at[pl.ds(start, half)], rows),
        (out_grad.at[pl.ds(start, half)], grads),
        (w_up.at[:, columns], mine_up),
        (w_down.at[:, columns], mine_down),
    )
    copies = [pltpu.make_async_copy(*move, sems.at[i]) for i, move in enumerate(moves)]
    for copy in copies:
        copy.start()
    copies[0].wait()
    passing[0] = norm_rows(rows[...], gain)[0]
    copies[1].wait()
    passing[1] = mask_rows(grads[...], start, lengths[lax.axis_index("gx")])
    copies[2].wait()
    copies[3].wait()


def norm_kernel(lengths, frames, out_grad, gain, normed, grads, stats):
    value, centre, inv_std = norm_rows(frames[...], gain)
    normed[...] = value
    stats[:, 0:1] = centre
    stats[:, 1:2] = inv_std
    grads[...] = mask_rows(out_grad[...], 0, lengths[lax.axis_index("gx")])


def back_through(normed, grads, up, down, d_pre, partial):
    tile = 256
    for at in range(0, d_pre.shape[1], tile):
        columns = slice(at, min(at + tile, d_pre.shape[1]))
        pre_act = dot(normed[...], up[:, columns])
        d_act = dot(grads[...], down[:, columns])
        d_pre[:, columns] = (d_act * gelu_slope(pre_act)).astype(BF16)
    partial[...] = dot(normed[...], d_pre[...], 0, 0).astype(BF16)


def place_kernel(places, peers, *refs):
    blocks, (up, down, sems) = refs[:-3], refs[-3:]
    copies = []
    for i, ((step, which), block) in enumerate(zip(places, blocks)):
        rows = block_rows(step, peers, block.shape[0])
        copies.append(pltpu.make_async_copy(block, (up, down)[which].at[rows], sems.at[i]))
    for copy in copies:
        copy.start()
    for copy in copies:
        copy.wait()


def own_kernel(places, sends, peers, normed, grads, near_up, near_down, *refs):
    late, refs = refs[: len(places)], refs[len(places) :]
    (d_pre, partial, up, down), blocks = refs[:4], refs[4:]
    up[...] = near_up[...]
    down[...] = near_down[...]
    for (step, which), block in zip(places, late):
        (up, down)[which][block_rows(step, peers, block.shape[0]), :] = block[...]
    back_through(normed, grads, up, down, d_pre, partial)
    for step, block in zip(sends, blocks):
        block[...] = partial[block_rows(step, peers, block.shape[0]), :]


def other_kernel(sends, peers, first, second, up, down, d_pre, partial, *refs):
    blocks, (normed, grads) = refs[:-2], refs[-2:]
    half = first.shape[1]
    for at, part in ((0, first), (half, second)):
        normed[at : at + half, :] = part[0]
        grads[at : at + half, :] = part[1]
    back_through(normed, grads, up, down, d_pre, partial)
    for step, block in zip(sends, blocks):
        block[...] = partial[block_rows(step, peers, block.shape[0]), :]


def d_norm_kernel(d_pre_own, d_pre_other, up, keep, send_other, *sends):
    core = lax.axis_index("gy")
    rows, width = keep.shape[1:]
    mine = up[pl.ds(pl.multiple_of(core * width, width), width), :]
    theirs = up[pl.ds(pl.multiple_of((1 - core) * width, width), width), :]
    keep[0] = dot(d_pre_own[...], mine, 1, 1).astype(BF16)
    keep[1] = dot(d_pre_other[...], mine, 1, 1).astype(BF16)
    sent = dot(d_pre_other[...], theirs, 1, 1).astype(BF16)
    send_other[: rows // 2, :] = sent[rows // 2 :]
    send_other[rows // 2 :, :] = sent[: rows // 2]
    sent = dot(d_pre_own[...], theirs, 1, 1).astype(BF16)
    step = rows // len(sends)
    for i, send in enumerate(sends):
        send[...] = sent[i * step : (i + 1) * step]


def over_kernel(keep, came, over):
    half = over.shape[0] // 2
    value = (keep[1].astype(F32) + came[...].astype(F32)).astype(BF16)
    for i in range(2):
        at = lax.rem(i + lax.axis_index("gy"), 2) * half
        over[pl.ds(pl.multiple_of(at, half), half), :] = value[i * half : (i + 1) * half]


def own_columns(ref, width):
    return ref[:, pl.ds(pl.multiple_of(lax.axis_index("gy") * width, width), width)]


def scale_kernel(keep, back, frames, gain, grads, stats, *refs):
    came, (base, factor, sums) = refs[:-3], refs[-3:]
    width = base.shape[1]
    d_norm = jnp.concatenate([part[...].astype(F32) for part in came])
    d_norm = keep[0].astype(F32) + d_norm + back[...].astype(F32)
    scaled = d_norm * own_columns(gain, width)
    rows = own_columns(frames, width).astype(F32)
    inv_std = stats[:, 1:2]
    centred = (rows - stats[:, 0:1]) * inv_std
    sums[:, 0:1] = jnp.sum(scaled, axis=-1, keepdims=True)
    sums[:, 1:2] = jnp.sum(scaled * centred, axis=-1, keepdims=True)
    base[...] = own_columns(grads, width).astype(F32) + inv_std * scaled
    factor[...] = inv_std * centred


def input_rows(base, factor, sums, came, stats):
    means = (sums[...] + came[...]) * (0.5 / base.shape[1])
    value = base[...] - stats[:, 1:2] * means[:, 0:1] - factor[...] * means[:, 1:2]
    return value.astype(BF16)


def input_kernel(base, factor, sums, came, stats, out, token):
    out[...] = input_rows(base, factor, sums, came, stats)
    token[...] = jnp.zeros_like(token)


def hop_kernel(places, peers, partial, *refs):
    count = len(places)
    for step, came, out in zip(places, refs[:count], refs[count:]):
        value = partial[block_rows(step, peers, out.shape[0]), :].astype(F32)
        out[...] = (value + came[...].astype(F32)).astype(BF16)


def total_kernel(peers, partial, up, down, total):
    value = partial[block_rows(0, peers, total.shape[0]), :].astype(F32)
    total[...] = (value + up[...].astype(F32) + down[...].astype(F32)).astype(BF16)


def last_kernel(peers, partial, up, down, passed, up_grad):
    depth, width = passed.shape
    side = lax.axis_index("groups")
    value = partial[block_rows(0, peers, depth), :].astype(F32)
    value = value + up[...].astype(F32) + down[...].astype(F32)
    up_grad[:, pl.ds(pl.multiple_of(side * width, width), width)] = value
    other = pl.ds(pl.multiple_of((1 - side) * width, width), width)
    up_grad[:, other] = passed[...].astype(F32)


def place_halves_kernel(own, passed, out):
    width = own.shape[1]
    side = lax.axis_index("groups")
    out[:, pl.ds(pl.multiple_of(side * width, width), width)] = own[...]
    other = pl.ds(pl.multiple_of((1 - side) * width, width), width)
    out[:, other] = passed[...].astype(F32)


def shards(frames, out_grad, ln_gain, w_up, w_down, lengths):
    peers = lax.axis_size("gx")
    half = peers // 2
    frame_len, width = frames.shape[1:]
    depth, hidden = w_up.shape
    quarter = hidden // 2
    half_width = width // 2
    half_rows = frame_len // 2
    ringed = peers <= 16 and peers % 2 == 0 and depth % 16 == 0

    order = list(range(0, peers, 2)) + list(range(peers - 1, 0, -2))
    ahead = [(order[i], order[(i + 1) % peers]) for i in range(peers)]
    behind = [(b, a) for a, b in ahead]
    swap = [(0, 1), (1, 0)]

    frames, out_grad = frames[0], out_grad[0]
    rows_of = shape((frame_len, width), BF16)
    block_of = shape((depth, quarter), BF16)
    passing, *mine = call(
        first_kernel,
        (lengths, frames, out_grad, ln_gain, w_up, w_down),
        (shape((2, half_rows, width), BF16), block_of, block_of),
        [pltpu.SemaphoreType.DMA((4,))] + [pltpu.VMEM((half_rows, width), BF16)] * 2,
        flops=5 * frame_len * width,
        vmem=60,
        left=(1, 2, 4, 5),
    )
    first = lax.ppermute(passing, "groups", swap)
    normed, grads, stats = call(
        norm_kernel,
        (lengths, frames, out_grad, ln_gain),
        (rows_of, rows_of, shape((frame_len, 2), F32)),
        flops=10 * frame_len * width,
    )

    weight = shape((width, quarter), BF16)
    if ringed:
        blocks = {(0, 0): mine[0], (0, 1): mine[1]}
        up, down = list(mine), list(mine)
        for step in range(1, half):
            for i in range(2):
                up[i] = lax.ppermute(up[i], "gx", ahead)
                down[i] = lax.ppermute(down[i], "gx", behind)
            if step == 1:
                up[0] = hold(up[0], normed)
            for i in range(2):
                blocks[-step, i], blocks[step, i] = up[i], down[i]
        late = {
            (half - 1, 0): blocks.pop((half - 1, 0)),
            (1 - half, 1): blocks.pop((1 - half, 1)),
            (half, 0): lax.ppermute(up[0], "gx", ahead),
            (half, 1): lax.ppermute(down[1], "gx", behind),
        }
        near = call(
            functools.partial(place_kernel, tuple(blocks), peers),
            list(blocks.values()),
            (weight, weight),
            [pltpu.SemaphoreType.DMA((len(blocks),))],
            pinned=range(len(blocks)),
        )
        first = hold(first, *late.values(), near[0])
        sends = ((half - 1, -half), (half, 1 - half))
    else:
        near = [lax.all_gather(block, "gx", axis=0, tiled=True) for block in mine]
        late, sends = {}, ((), ())
    second = lax.ppermute(first, "gy", swap)

    d_pre_of, partial_of = shape((frame_len, quarter), BF16), shape((width, quarter), BF16)
    d_pre_own, partial_own, full_up, full_down, *blocks_own = call(
        functools.partial(own_kernel, tuple(late), sends[1], peers),
        (normed, grads, *near, *late.values()),
        (d_pre_of, partial_of, weight, weight, *[block_of] * len(sends[1])),
        flops=6 * frame_len * width * quarter,
    )
    d_pre_other, partial_other, *blocks_other = call(
        functools.partial(other_kernel, sends[0], peers),
        (first, second, full_up, full_down),
        (d_pre_of, partial_of, *[block_of] * len(sends[0])),
        [pltpu.VMEM((frame_len, width), BF16)] * 2,
        flops=6 * frame_len * width * quarter,
    )
    partial = [partial_own, partial_other]

    half_rows_of = shape((frame_len, half_width), BF16)
    parts_of = [shape((frame_len // 3, half_width), BF16)] * 3

    def own_d_norm(*ties):
        keep, send, *parts = call(
            d_norm_kernel,
            (d_pre_own, d_pre_other, full_up),
            (shape((2, frame_len, half_width), BF16), half_rows_of, *parts_of),
            flops=4 * frame_len * width * quarter,
            ties=ties,
        )
        sent = [lax.ppermute(part, "gy", swap) for part in parts]
        return keep, lax.ppermute(send, "gy", swap), sent

    def over_cores(keep, came, *ties):
        over = call(over_kernel, (keep, came), half_rows_of, ties=ties)
        return over, lax.ppermute(over, "groups", swap)

    def scale(keep, came, back, *ties):
        return call(
            scale_kernel,
            (keep, back, frames, ln_gain[None], grads, stats, *came),
            (
                shape((frame_len, half_width), F32),
                shape((frame_len, half_width), F32),
                shape((frame_len, 2), F32),
            ),
            ties=ties,
        )

    def input_gradient(base, factor, sums):
        return call(
            input_kernel,
            (base, factor, sums, lax.ppermute(sums, "gy", swap), stats),
            (half_rows_of, shape((8, 128), F32)),
        )

    up_grad_of = shape((depth, hidden), F32)
    if ringed:
        came, kept = [{}, {}], []

        def send_on(i, blocks, names):
            for block, name in zip(blocks, names):
                came[i][name] = lax.ppermute(block, "gx", ahead if name == "up" else behind)

        def hop(i, turn, *ties):
            ways = [("up", half - turn - i), ("down", turn + 1 - i - half)]
            ways = [way for way in ways if way[1] != 0]
            names = [name for name, _ in ways]
            ties += tuple(came[i][name] for name in came[i] if name not in names)
            blocks = call(
                functools.partial(hop_kernel, tuple(step for _, step in ways), peers),
                (partial[i], *[came[i][name] for name in names]),
                [block_of] * len(ways),
                ties=ties,
            )
            if (i, turn) == (0, half - 2):
                kept.append(blocks[1])
                blocks, names = blocks[:1], names[:1]
            send_on(i, blocks, names)
            return blocks[0]

        send_on(1, blocks_other, ("up", "down"))
        keep, came_other, sent = own_d_norm()
        send_on(0, [hold(block, keep) for block in blocks_own], ("up", "down"))
        tie = hop(1, 1, keep)
        tie = hop(0, 1, tie)
        tie = hop(1, 2, tie)
        tie, back = over_cores(keep, came_other, tie)
        tie = hop(0, 2, tie)
        for turn in range(3, half):
            tie = hop(0, turn, hop(1, turn, tie))
        passing = call(
            functools.partial(total_kernel, peers),
            (partial[1], came[1]["up"], came[1]["down"]),
            block_of,
            ties=(tie,),
        )
        passed = lax.ppermute(passing, "groups", swap)
        send_on(0, [hold(kept[0], passing)], ["down"])
        input_grad, token = input_gradient(*scale(keep, sent, back, passing))
        up_grad = call(
            functools.partial(last_kernel, peers),
            (partial[0], came[0]["up"], came[0]["down"], passed),
            up_grad_of,
            ties=(token,),
        )
    else:
        keep, came_other, sent = own_d_norm()
        _, back = over_cores(keep, came_other)
        input_grad, _ = input_gradient(*scale(keep, sent, back))
        total, passing = [
            lax.psum_scatter(p.astype(F32), "gx", scatter_dimension=0, tiled=True) for p in partial
        ]
        passed = lax.ppermute(passing.astype(BF16), "groups", swap)
        up_grad = call(place_halves_kernel, (total, passed), up_grad_of)
    return (input_grad[None], up_grad)


def solution(mesh):
    placed = (
        P(("groups", "gx"), None, None),
        P(("groups", "gx"), None, None),
        P(),
        P("gx", "gy"),
        P("gx", "gy"),
        P("groups"),
    )
    return jax.shard_map(
        shards,
        mesh=mesh,
        in_specs=placed,
        out_specs=(P(("groups", "gx"), None, "gy"), P(("groups", "gx"), "gy")),
        check_vma=False,
    )
```

```python
import functools

import jax
import jax.numpy as jnp
from jax import lax
from jax.experimental import pallas as pl
from jax.experimental.pallas import tpu as pltpu
from jax.sharding import PartitionSpec as P

BF16, F32 = jnp.bfloat16, jnp.float32
VMEM = pl.BlockSpec(memory_space=pltpu.VMEM)
HBM = pl.BlockSpec(memory_space=pltpu.HBM)
ANY = pl.BlockSpec(memory_space=pl.ANY)
SMEM = pl.BlockSpec(memory_space=pltpu.SMEM)


def shape(dims, kind):
    return jax.ShapeDtypeStruct(dims, kind)


def call(kernel, ins, out_shape, scratch=(), vmem=16, flops=1, left=(), pinned=(), ties=()):
    count = len(ins)

    def body(*refs):
        kernel(*refs[:count], *refs[count + len(ties) :])

    moved = sum(x.size * x.dtype.itemsize for x in list(ins) + jax.tree.leaves(out_shape))
    return pl.pallas_call(
        body if ties else kernel,
        out_shape=out_shape,
        in_specs=[
            SMEM if x.dtype == jnp.int32 else ANY if i in left else HBM if i in pinned else VMEM
            for i, x in enumerate(ins)
        ]
        + [ANY] * len(ties),
        out_specs=jax.tree.map(lambda _: VMEM, out_shape),
        scratch_shapes=list(scratch),
        compiler_params=pltpu.CompilerParams(vmem_limit_bytes=vmem << 20),
        cost_estimate=pl.CostEstimate(flops=flops, bytes_accessed=moved, transcendentals=0),
    )(*ins, *ties)


def hold(array, *ties):
    return pl.pallas_call(
        lambda *refs: None,
        out_shape=shape(array.shape, array.dtype),
        in_specs=[ANY] * (1 + len(ties)),
        out_specs=ANY,
        input_output_aliases={0: 0},
        compiler_params=pltpu.CompilerParams(vmem_limit_bytes=1 << 20),
        cost_estimate=pl.CostEstimate(flops=1, bytes_accessed=1, transcendentals=0),
    )(array, *ties)


def dot(left, right, left_dim=1, right_dim=0):
    return lax.dot_general(
        left, right, (((left_dim,), (right_dim,)), ((), ())), preferred_element_type=F32
    )


def gelu_slope(values):
    return (
        0.5 * (1.0 + lax.erf(values * 0.7071067811865476))
        + values * jnp.exp(-0.5 * values * values) * 0.3989422804014327
    )


def block_rows(step, peers, depth):
    own = lax.axis_index("gx")
    place = jnp.where(lax.rem(own, 2) == 0, lax.div(own, 2), peers - 1 - lax.div(own, 2))
    place = lax.rem(place + (step + peers), peers)
    member = jnp.where(place < peers // 2, 2 * place, 2 * (peers - 1 - place) + 1)
    return pl.ds(pl.multiple_of(member * depth, depth), depth)


def norm_rows(rows, gain):
    values = rows.astype(F32)
    centre = jnp.mean(values, axis=-1, keepdims=True)
    shifted = values - centre
    variance = jnp.mean(shifted * shifted, axis=-1, keepdims=True)
    inv_std = lax.rsqrt(variance + 1e-05)
    return (shifted * inv_std * gain[...][None]).astype(BF16), centre, inv_std


def mask_rows(rows, start, length):
    index = start + lax.broadcasted_iota(jnp.int32, (rows.shape[0], 1), 0)
    return jnp.where(index < length, rows.astype(F32), 0.0).astype(BF16)


def first_kernel(
    lengths, frames, out_grad, gain, w_up, w_down, passing, mine_up, mine_down, sems, rows, grads
):
    half, quarter = rows.shape[0], mine_up.shape[1]
    start = pl.multiple_of(lax.axis_index("gy") * half, half)
    columns = pl.ds(pl.multiple_of(lax.axis_index("groups") * quarter, quarter), quarter)
    moves = (
        (frames.at[pl.ds(start, half)], rows),
        (out_grad.at[pl.ds(start, half)], grads),
        (w_up.at[:, columns], mine_up),
        (w_down.at[:, columns], mine_down),
    )
    copies = [pltpu.make_async_copy(*move, sems.at[i]) for i, move in enumerate(moves)]
    for copy in copies:
        copy.start()
    copies[0].wait()
    passing[0] = norm_rows(rows[...], gain)[0]
    copies[1].wait()
    passing[1] = mask_rows(grads[...], start, lengths[lax.axis_index("gx")])
    copies[2].wait()
    copies[3].wait()


def norm_kernel(lengths, frames, out_grad, gain, normed, grads, stats):
    value, centre, inv_std = norm_rows(frames[...], gain)
    normed[...] = value
    stats[:, 0:1] = centre
    stats[:, 1:2] = inv_std
    grads[...] = mask_rows(out_grad[...], 0, lengths[lax.axis_index("gx")])


def back_through(normed, grads, up, down, d_pre, partial):
    tile = 256
    for at in range(0, d_pre.shape[1], tile):
        columns = slice(at, min(at + tile, d_pre.shape[1]))
        pre_act = dot(normed[...], up[:, columns])
        d_act = dot(grads[...], down[:, columns])
        d_pre[:, columns] = (d_act * gelu_slope(pre_act)).astype(BF16)
    partial[...] = dot(normed[...], d_pre[...], 0, 0).astype(BF16)


def place_kernel(places, peers, *refs):
    blocks, (up, down, sems) = refs[:-3], refs[-3:]
    copies = []
    for i, ((step, which), block) in enumerate(zip(places, blocks)):
        rows = block_rows(step, peers, block.shape[0])
        copies.append(pltpu.make_async_copy(block, (up, down)[which].at[rows], sems.at[i]))
    for copy in copies:
        copy.start()
    for copy in copies:
        copy.wait()


def own_kernel(places, sends, peers, normed, grads, near_up, near_down, *refs):
    late, refs = refs[: len(places)], refs[len(places) :]
    (d_pre, partial, up, down), blocks = refs[:4], refs[4:]
    up[...] = near_up[...]
    down[...] = near_down[...]
    for (step, which), block in zip(places, late):
        (up, down)[which][block_rows(step, peers, block.shape[0]), :] = block[...]
    back_through(normed, grads, up, down, d_pre, partial)
    for step, block in zip(sends, blocks):
        block[...] = partial[block_rows(step, peers, block.shape[0]), :]


def other_kernel(sends, peers, first, second, up, down, d_pre, partial, *refs):
    blocks, (normed, grads) = refs[:-2], refs[-2:]
    half = first.shape[1]
    for at, part in ((0, first), (half, second)):
        normed[at : at + half, :] = part[0]
        grads[at : at + half, :] = part[1]
    back_through(normed, grads, up, down, d_pre, partial)
    for step, block in zip(sends, blocks):
        block[...] = partial[block_rows(step, peers, block.shape[0]), :]


def d_norm_kernel(d_pre_own, d_pre_other, up, keep, send_other, *sends):
    core = lax.axis_index("gy")
    rows, width = keep.shape[1:]
    mine = up[pl.ds(pl.multiple_of(core * width, width), width), :]
    theirs = up[pl.ds(pl.multiple_of((1 - core) * width, width), width), :]
    keep[0] = dot(d_pre_own[...], mine, 1, 1).astype(BF16)
    keep[1] = dot(d_pre_other[...], mine, 1, 1).astype(BF16)
    sent = dot(d_pre_other[...], theirs, 1, 1).astype(BF16)
    send_other[: rows // 2, :] = sent[rows // 2 :]
    send_other[rows // 2 :, :] = sent[: rows // 2]
    sent = dot(d_pre_own[...], theirs, 1, 1).astype(BF16)
    step = rows // len(sends)
    for i, send in enumerate(sends):
        send[...] = sent[i * step : (i + 1) * step]


def over_kernel(keep, came, over):
    half = over.shape[0] // 2
    value = (keep[1].astype(F32) + came[...].astype(F32)).astype(BF16)
    for i in range(2):
        at = lax.rem(i + lax.axis_index("gy"), 2) * half
        over[pl.ds(pl.multiple_of(at, half), half), :] = value[i * half : (i + 1) * half]


def own_columns(ref, width):
    return ref[:, pl.ds(pl.multiple_of(lax.axis_index("gy") * width, width), width)]


def scale_kernel(keep, back, frames, gain, grads, stats, *refs):
    came, (base, factor, sums) = refs[:-3], refs[-3:]
    width = base.shape[1]
    d_norm = jnp.concatenate([part[...].astype(F32) for part in came])
    d_norm = keep[0].astype(F32) + d_norm + back[...].astype(F32)
    scaled = d_norm * own_columns(gain, width)
    rows = own_columns(frames, width).astype(F32)
    inv_std = stats[:, 1:2]
    centred = (rows - stats[:, 0:1]) * inv_std
    sums[:, 0:1] = jnp.sum(scaled, axis=-1, keepdims=True)
    sums[:, 1:2] = jnp.sum(scaled * centred, axis=-1, keepdims=True)
    base[...] = own_columns(grads, width).astype(F32) + inv_std * scaled
    factor[...] = inv_std * centred


def input_rows(base, factor, sums, came, stats):
    means = (sums[...] + came[...]) * (0.5 / base.shape[1])
    value = base[...] - stats[:, 1:2] * means[:, 0:1] - factor[...] * means[:, 1:2]
    return value.astype(BF16)


def input_kernel(base, factor, sums, came, stats, out, token):
    out[...] = input_rows(base, factor, sums, came, stats)
    token[...] = jnp.zeros_like(token)


def hop_kernel(places, peers, partial, *refs):
    count = len(places)
    for step, came, out in zip(places, refs[:count], refs[count:]):
        value = partial[block_rows(step, peers, out.shape[0]), :].astype(F32)
        out[...] = (value + came[...].astype(F32)).astype(BF16)


def total_kernel(peers, partial, up, down, total):
    value = partial[block_rows(0, peers, total.shape[0]), :].astype(F32)
    total[...] = (value + up[...].astype(F32) + down[...].astype(F32)).astype(BF16)


def last_kernel(peers, partial, up, down, passed, up_grad):
    depth, width = passed.shape
    side = lax.axis_index("groups")
    value = partial[block_rows(0, peers, depth), :].astype(F32)
    value = value + up[...].astype(F32) + down[...].astype(F32)
    up_grad[:, pl.ds(pl.multiple_of(side * width, width), width)] = value
    other = pl.ds(pl.multiple_of((1 - side) * width, width), width)
    up_grad[:, other] = passed[...].astype(F32)


def place_halves_kernel(own, passed, out):
    width = own.shape[1]
    side = lax.axis_index("groups")
    out[:, pl.ds(pl.multiple_of(side * width, width), width)] = own[...]
    other = pl.ds(pl.multiple_of((1 - side) * width, width), width)
    out[:, other] = passed[...].astype(F32)


def shards(frames, out_grad, ln_gain, w_up, w_down, lengths):
    peers = lax.axis_size("gx")
    half = peers // 2
    frame_len, width = frames.shape[1:]
    depth, hidden = w_up.shape
    quarter = hidden // 2
    half_width = width // 2
    half_rows = frame_len // 2
    ringed = peers <= 16 and peers % 2 == 0 and depth % 16 == 0

    order = list(range(0, peers, 2)) + list(range(peers - 1, 0, -2))
    ahead = [(order[i], order[(i + 1) % peers]) for i in range(peers)]
    behind = [(b, a) for a, b in ahead]
    swap = [(0, 1), (1, 0)]

    frames, out_grad = frames[0], out_grad[0]
    rows_of = shape((frame_len, width), BF16)
    block_of = shape((depth, quarter), BF16)
    passing, *mine = call(
        first_kernel,
        (lengths, frames, out_grad, ln_gain, w_up, w_down),
        (shape((2, half_rows, width), BF16), block_of, block_of),
        [pltpu.SemaphoreType.DMA((4,))] + [pltpu.VMEM((half_rows, width), BF16)] * 2,
        flops=5 * frame_len * width,
        vmem=60,
        left=(1, 2, 4, 5),
    )
    first = lax.ppermute(passing, "groups", swap)
    normed, grads, stats = call(
        norm_kernel,
        (lengths, frames, out_grad, ln_gain),
        (rows_of, rows_of, shape((frame_len, 2), F32)),
        flops=10 * frame_len * width,
    )

    weight = shape((width, quarter), BF16)
    if ringed:
        blocks = {(0, 0): mine[0], (0, 1): mine[1]}
        up, down = list(mine), list(mine)
        for step in range(1, half):
            for i in range(2):
                up[i] = lax.ppermute(up[i], "gx", ahead)
                down[i] = lax.ppermute(down[i], "gx", behind)
            if step == 1:
                up[0] = hold(up[0], normed)
            for i in range(2):
                blocks[-step, i], blocks[step, i] = up[i], down[i]
        late = {
            (half - 1, 0): blocks.pop((half - 1, 0)),
            (1 - half, 1): blocks.pop((1 - half, 1)),
            (half, 0): lax.ppermute(up[0], "gx", ahead),
            (half, 1): lax.ppermute(down[1], "gx", behind),
        }
        near = call(
            functools.partial(place_kernel, tuple(blocks), peers),
            list(blocks.values()),
            (weight, weight),
            [pltpu.SemaphoreType.DMA((len(blocks),))],
            pinned=range(len(blocks)),
        )
        first = hold(first, *late.values(), near[0])
        sends = ((half - 1, -half), (half, 1 - half))
    else:
        near = [lax.all_gather(block, "gx", axis=0, tiled=True) for block in mine]
        late, sends = {}, ((), ())
    second = lax.ppermute(first, "gy", swap)

    d_pre_of, partial_of = shape((frame_len, quarter), BF16), shape((width, quarter), BF16)
    d_pre_own, partial_own, full_up, full_down, *blocks_own = call(
        functools.partial(own_kernel, tuple(late), sends[1], peers),
        (normed, grads, *near, *late.values()),
        (d_pre_of, partial_of, weight, weight, *[block_of] * len(sends[1])),
        flops=6 * frame_len * width * quarter,
    )
    d_pre_other, partial_other, *blocks_other = call(
        functools.partial(other_kernel, sends[0], peers),
        (first, second, full_up, full_down),
        (d_pre_of, partial_of, *[block_of] * len(sends[0])),
        [pltpu.VMEM((frame_len, width), BF16)] * 2,
        flops=6 * frame_len * width * quarter,
    )
    partial = [partial_own, partial_other]

    half_rows_of = shape((frame_len, half_width), BF16)
    parts_of = [shape((frame_len // 3, half_width), BF16)] * 3

    def own_d_norm(*ties):
        keep, send, *parts = call(
            d_norm_kernel,
            (d_pre_own, d_pre_other, full_up),
            (shape((2, frame_len, half_width), BF16), half_rows_of, *parts_of),
            flops=4 * frame_len * width * quarter,
            ties=ties,
        )
        sent = [lax.ppermute(part, "gy", swap) for part in parts]
        return keep, lax.ppermute(send, "gy", swap), sent

    def over_cores(keep, came, *ties):
        over = call(over_kernel, (keep, came), half_rows_of, ties=ties)
        return over, lax.ppermute(over, "groups", swap)

    def scale(keep, came, back, *ties):
        return call(
            scale_kernel,
            (keep, back, frames, ln_gain[None], grads, stats, *came),
            (
                shape((frame_len, half_width), F32),
                shape((frame_len, half_width), F32),
                shape((frame_len, 2), F32),
            ),
            ties=ties,
        )

    def input_gradient(base, factor, sums):
        return call(
            input_kernel,
            (base, factor, sums, lax.ppermute(sums, "gy", swap), stats),
            (half_rows_of, shape((8, 128), F32)),
        )

    up_grad_of = shape((depth, hidden), F32)
    if ringed:
        came, kept = [{}, {}], []

        def send_on(i, blocks, names):
            for block, name in zip(blocks, names):
                came[i][name] = lax.ppermute(block, "gx", ahead if name == "up" else behind)

        def hop(i, turn, *ties):
            ways = [("up", half - turn - i), ("down", turn + 1 - i - half)]
            ways = [way for way in ways if way[1] != 0]
            names = [name for name, _ in ways]
            blocks = call(
                functools.partial(hop_kernel, tuple(step for _, step in ways), peers),
                (partial[i], *[came[i][name] for name in names]),
                [block_of] * len(ways),
                ties=ties,
            )
            if (i, turn) == (0, half - 2):
                kept.append(blocks[1])
                blocks, names = blocks[:1], names[:1]
            send_on(i, blocks, names)
            return blocks[0]

        send_on(1, blocks_other, ("up", "down"))
        keep, came_other, sent = own_d_norm()
        send_on(0, [hold(block, keep) for block in blocks_own], ("up", "down"))
        tie = hop(1, 1, keep)
        tie = hop(0, 1, tie)
        tie = hop(1, 2, tie)
        tie, back = over_cores(keep, came_other, tie)
        tie = hop(0, 2, tie)
        for turn in range(3, half):
            tie = hop(0, turn, hop(1, turn, tie), came[1]["up"])
        passing = call(
            functools.partial(total_kernel, peers),
            (partial[1], came[1]["up"], came[1]["down"]),
            block_of,
            ties=(tie,),
        )
        passed = lax.ppermute(passing, "groups", swap)
        send_on(0, [hold(kept[0], passing)], ["down"])
        input_grad, token = input_gradient(*scale(keep, sent, back, passing))
        up_grad = call(
            functools.partial(last_kernel, peers),
            (partial[0], came[0]["up"], came[0]["down"], passed),
            up_grad_of,
            ties=(token,),
        )
    else:
        keep, came_other, sent = own_d_norm()
        _, back = over_cores(keep, came_other)
        input_grad, _ = input_gradient(*scale(keep, sent, back))
        total, passing = [
            lax.psum_scatter(p.astype(F32), "gx", scatter_dimension=0, tiled=True) for p in partial
        ]
        passed = lax.ppermute(passing.astype(BF16), "groups", swap)
        up_grad = call(place_halves_kernel, (total, passed), up_grad_of)
    return (input_grad[None], up_grad)


def solution(mesh):
    placed = (
        P(("groups", "gx"), None, None),
        P(("groups", "gx"), None, None),
        P(),
        P("gx", "gy"),
        P("gx", "gy"),
        P("groups"),
    )
    return jax.shard_map(
        shards,
        mesh=mesh,
        in_specs=placed,
        out_specs=(P(("groups", "gx"), None, "gy"), P(("groups", "gx"), "gy")),
        check_vma=False,
    )
```

```python
import functools

import jax
import jax.numpy as jnp
from jax import lax
from jax.experimental import pallas as pl
from jax.experimental.pallas import tpu as pltpu
from jax.sharding import PartitionSpec as P

BF16, F32 = jnp.bfloat16, jnp.float32
VMEM = pl.BlockSpec(memory_space=pltpu.VMEM)
HBM = pl.BlockSpec(memory_space=pltpu.HBM)
ANY = pl.BlockSpec(memory_space=pl.ANY)
SMEM = pl.BlockSpec(memory_space=pltpu.SMEM)


def shape(dims, kind):
    return jax.ShapeDtypeStruct(dims, kind)


def call(kernel, ins, out_shape, scratch=(), vmem=16, flops=1, left=(), pinned=(), ties=()):
    count = len(ins)

    def body(*refs):
        kernel(*refs[:count], *refs[count + len(ties) :])

    moved = sum(x.size * x.dtype.itemsize for x in list(ins) + jax.tree.leaves(out_shape))
    return pl.pallas_call(
        body if ties else kernel,
        out_shape=out_shape,
        in_specs=[
            SMEM if x.dtype == jnp.int32 else ANY if i in left else HBM if i in pinned else VMEM
            for i, x in enumerate(ins)
        ]
        + [ANY] * len(ties),
        out_specs=jax.tree.map(lambda _: VMEM, out_shape),
        scratch_shapes=list(scratch),
        compiler_params=pltpu.CompilerParams(vmem_limit_bytes=vmem << 20),
        cost_estimate=pl.CostEstimate(flops=flops, bytes_accessed=moved, transcendentals=0),
    )(*ins, *ties)


def hold(array, *ties):
    return pl.pallas_call(
        lambda *refs: None,
        out_shape=shape(array.shape, array.dtype),
        in_specs=[ANY] * (1 + len(ties)),
        out_specs=ANY,
        input_output_aliases={0: 0},
        compiler_params=pltpu.CompilerParams(vmem_limit_bytes=1 << 20),
        cost_estimate=pl.CostEstimate(flops=1, bytes_accessed=1, transcendentals=0),
    )(array, *ties)


def dot(left, right, left_dim=1, right_dim=0):
    return lax.dot_general(
        left, right, (((left_dim,), (right_dim,)), ((), ())), preferred_element_type=F32
    )


def gelu_slope(values):
    return (
        0.5 * (1.0 + lax.erf(values * 0.7071067811865476))
        + values * jnp.exp(-0.5 * values * values) * 0.3989422804014327
    )


def block_rows(step, peers, depth):
    own = lax.axis_index("gx")
    place = jnp.where(lax.rem(own, 2) == 0, lax.div(own, 2), peers - 1 - lax.div(own, 2))
    place = lax.rem(place + (step + peers), peers)
    member = jnp.where(place < peers // 2, 2 * place, 2 * (peers - 1 - place) + 1)
    return pl.ds(pl.multiple_of(member * depth, depth), depth)


def norm_rows(rows, gain):
    values = rows.astype(F32)
    centre = jnp.mean(values, axis=-1, keepdims=True)
    shifted = values - centre
    variance = jnp.mean(shifted * shifted, axis=-1, keepdims=True)
    inv_std = lax.rsqrt(variance + 1e-05)
    return (shifted * inv_std * gain[...][None]).astype(BF16), centre, inv_std


def mask_rows(rows, start, length):
    index = start + lax.broadcasted_iota(jnp.int32, (rows.shape[0], 1), 0)
    return jnp.where(index < length, rows.astype(F32), 0.0).astype(BF16)


def first_kernel(
    lengths, frames, out_grad, gain, w_up, w_down, passing, mine_up, mine_down, sems, rows, grads
):
    half, quarter = rows.shape[0], mine_up.shape[1]
    start = pl.multiple_of(lax.axis_index("gy") * half, half)
    columns = pl.ds(pl.multiple_of(lax.axis_index("groups") * quarter, quarter), quarter)
    moves = (
        (frames.at[pl.ds(start, half)], rows),
        (out_grad.at[pl.ds(start, half)], grads),
        (w_up.at[:, columns], mine_up),
        (w_down.at[:, columns], mine_down),
    )
    copies = [pltpu.make_async_copy(*move, sems.at[i]) for i, move in enumerate(moves)]
    for copy in copies:
        copy.start()
    copies[0].wait()
    passing[0] = norm_rows(rows[...], gain)[0]
    copies[1].wait()
    passing[1] = mask_rows(grads[...], start, lengths[lax.axis_index("gx")])
    copies[2].wait()
    copies[3].wait()


def norm_kernel(lengths, frames, out_grad, gain, normed, grads, stats):
    value, centre, inv_std = norm_rows(frames[...], gain)
    normed[...] = value
    stats[:, 0:1] = centre
    stats[:, 1:2] = inv_std
    grads[...] = mask_rows(out_grad[...], 0, lengths[lax.axis_index("gx")])


def back_through(normed, grads, up, down, d_pre, partial):
    tile = 256
    for at in range(0, d_pre.shape[1], tile):
        columns = slice(at, min(at + tile, d_pre.shape[1]))
        pre_act = dot(normed[...], up[:, columns])
        d_act = dot(grads[...], down[:, columns])
        d_pre[:, columns] = (d_act * gelu_slope(pre_act)).astype(BF16)
    partial[...] = dot(normed[...], d_pre[...], 0, 0).astype(BF16)


def place_kernel(places, peers, *refs):
    blocks, (up, down, sems) = refs[:-3], refs[-3:]
    copies = []
    for i, ((step, which), block) in enumerate(zip(places, blocks)):
        rows = block_rows(step, peers, block.shape[0])
        copies.append(pltpu.make_async_copy(block, (up, down)[which].at[rows], sems.at[i]))
    for copy in copies:
        copy.start()
    for copy in copies:
        copy.wait()


def own_kernel(places, sends, peers, normed, grads, near_up, near_down, *refs):
    late, refs = refs[: len(places)], refs[len(places) :]
    (d_pre, partial, up, down), blocks = refs[:4], refs[4:]
    up[...] = near_up[...]
    down[...] = near_down[...]
    for (step, which), block in zip(places, late):
        (up, down)[which][block_rows(step, peers, block.shape[0]), :] = block[...]
    back_through(normed, grads, up, down, d_pre, partial)
    for step, block in zip(sends, blocks):
        block[...] = partial[block_rows(step, peers, block.shape[0]), :]


def other_kernel(sends, peers, first, second, up, down, d_pre, partial, *refs):
    blocks, (normed, grads) = refs[:-2], refs[-2:]
    half = first.shape[1]
    for at, part in ((0, first), (half, second)):
        normed[at : at + half, :] = part[0]
        grads[at : at + half, :] = part[1]
    back_through(normed, grads, up, down, d_pre, partial)
    for step, block in zip(sends, blocks):
        block[...] = partial[block_rows(step, peers, block.shape[0]), :]


def d_norm_kernel(d_pre_own, d_pre_other, up, keep, send_other, *sends):
    core = lax.axis_index("gy")
    rows, width = keep.shape[1:]
    mine = up[pl.ds(pl.multiple_of(core * width, width), width), :]
    theirs = up[pl.ds(pl.multiple_of((1 - core) * width, width), width), :]
    keep[0] = dot(d_pre_own[...], mine, 1, 1).astype(BF16)
    keep[1] = dot(d_pre_other[...], mine, 1, 1).astype(BF16)
    sent = dot(d_pre_other[...], theirs, 1, 1).astype(BF16)
    send_other[: rows // 2, :] = sent[rows // 2 :]
    send_other[rows // 2 :, :] = sent[: rows // 2]
    sent = dot(d_pre_own[...], theirs, 1, 1).astype(BF16)
    step = rows // len(sends)
    for i, send in enumerate(sends):
        send[...] = sent[i * step : (i + 1) * step]


def over_kernel(keep, came, over):
    half = over.shape[0] // 2
    value = (keep[1].astype(F32) + came[...].astype(F32)).astype(BF16)
    for i in range(2):
        at = lax.rem(i + lax.axis_index("gy"), 2) * half
        over[pl.ds(pl.multiple_of(at, half), half), :] = value[i * half : (i + 1) * half]


def own_columns(ref, width):
    return ref[:, pl.ds(pl.multiple_of(lax.axis_index("gy") * width, width), width)]


def scale_kernel(keep, back, frames, gain, grads, stats, *refs):
    came, (base, factor, sums) = refs[:-3], refs[-3:]
    width = base.shape[1]
    d_norm = jnp.concatenate([part[...].astype(F32) for part in came])
    d_norm = keep[0].astype(F32) + d_norm + back[...].astype(F32)
    scaled = d_norm * own_columns(gain, width)
    rows = own_columns(frames, width).astype(F32)
    inv_std = stats[:, 1:2]
    centred = (rows - stats[:, 0:1]) * inv_std
    sums[:, 0:1] = jnp.sum(scaled, axis=-1, keepdims=True)
    sums[:, 1:2] = jnp.sum(scaled * centred, axis=-1, keepdims=True)
    base[...] = own_columns(grads, width).astype(F32) + inv_std * scaled
    factor[...] = inv_std * centred


def input_rows(base, factor, sums, came, stats):
    means = (sums[...] + came[...]) * (0.5 / base.shape[1])
    value = base[...] - stats[:, 1:2] * means[:, 0:1] - factor[...] * means[:, 1:2]
    return value.astype(BF16)


def input_kernel(base, factor, sums, came, stats, out, token):
    out[...] = input_rows(base, factor, sums, came, stats)
    token[...] = jnp.zeros_like(token)


def hop_kernel(places, peers, partial, *refs):
    count = len(places)
    for step, came, out in zip(places, refs[:count], refs[count:]):
        value = partial[block_rows(step, peers, out.shape[0]), :].astype(F32)
        out[...] = (value + came[...].astype(F32)).astype(BF16)


def total_kernel(peers, partial, up, down, total):
    value = partial[block_rows(0, peers, total.shape[0]), :].astype(F32)
    total[...] = (value + up[...].astype(F32) + down[...].astype(F32)).astype(BF16)


def last_kernel(peers, partial, up, down, passed, up_grad):
    depth, width = passed.shape
    side = lax.axis_index("groups")
    value = partial[block_rows(0, peers, depth), :].astype(F32)
    value = value + up[...].astype(F32) + down[...].astype(F32)
    up_grad[:, pl.ds(pl.multiple_of(side * width, width), width)] = value
    other = pl.ds(pl.multiple_of((1 - side) * width, width), width)
    up_grad[:, other] = passed[...].astype(F32)


def place_halves_kernel(own, passed, out):
    width = own.shape[1]
    side = lax.axis_index("groups")
    out[:, pl.ds(pl.multiple_of(side * width, width), width)] = own[...]
    other = pl.ds(pl.multiple_of((1 - side) * width, width), width)
    out[:, other] = passed[...].astype(F32)


def shards(frames, out_grad, ln_gain, w_up, w_down, lengths):
    peers = lax.axis_size("gx")
    half = peers // 2
    frame_len, width = frames.shape[1:]
    depth, hidden = w_up.shape
    quarter = hidden // 2
    half_width = width // 2
    half_rows = frame_len // 2
    ringed = peers <= 16 and peers % 2 == 0 and depth % 16 == 0

    order = list(range(0, peers, 2)) + list(range(peers - 1, 0, -2))
    ahead = [(order[i], order[(i + 1) % peers]) for i in range(peers)]
    behind = [(b, a) for a, b in ahead]
    swap = [(0, 1), (1, 0)]

    frames, out_grad = frames[0], out_grad[0]
    rows_of = shape((frame_len, width), BF16)
    block_of = shape((depth, quarter), BF16)
    passing, *mine = call(
        first_kernel,
        (lengths, frames, out_grad, ln_gain, w_up, w_down),
        (shape((2, half_rows, width), BF16), block_of, block_of),
        [pltpu.SemaphoreType.DMA((4,))] + [pltpu.VMEM((half_rows, width), BF16)] * 2,
        flops=5 * frame_len * width,
        vmem=60,
        left=(1, 2, 4, 5),
    )
    first = lax.ppermute(passing, "groups", swap)
    normed, grads, stats = call(
        norm_kernel,
        (lengths, frames, out_grad, ln_gain),
        (rows_of, rows_of, shape((frame_len, 2), F32)),
        flops=10 * frame_len * width,
    )

    weight = shape((width, quarter), BF16)
    if ringed:
        blocks = {(0, 0): mine[0], (0, 1): mine[1]}
        up, down = list(mine), list(mine)
        for step in range(1, half):
            for i in range(2):
                up[i] = lax.ppermute(up[i], "gx", ahead)
                down[i] = lax.ppermute(down[i], "gx", behind)
            if step == 1:
                up[0] = hold(up[0], normed)
            for i in range(2):
                blocks[-step, i], blocks[step, i] = up[i], down[i]
        late = {
            (half - 1, 0): blocks.pop((half - 1, 0)),
            (1 - half, 1): blocks.pop((1 - half, 1)),
            (half, 0): lax.ppermute(up[0], "gx", ahead),
            (half, 1): lax.ppermute(down[1], "gx", behind),
        }
        near = call(
            functools.partial(place_kernel, tuple(blocks), peers),
            list(blocks.values()),
            (weight, weight),
            [pltpu.SemaphoreType.DMA((len(blocks),))],
            pinned=range(len(blocks)),
        )
        first = hold(first, *late.values(), near[0])
        sends = ((half - 1, -half), (half, 1 - half))
    else:
        near = [lax.all_gather(block, "gx", axis=0, tiled=True) for block in mine]
        late, sends = {}, ((), ())
    second = lax.ppermute(first, "gy", swap)

    d_pre_of, partial_of = shape((frame_len, quarter), BF16), shape((width, quarter), BF16)
    d_pre_own, partial_own, full_up, full_down, *blocks_own = call(
        functools.partial(own_kernel, tuple(late), sends[1], peers),
        (normed, grads, *near, *late.values()),
        (d_pre_of, partial_of, weight, weight, *[block_of] * len(sends[1])),
        flops=6 * frame_len * width * quarter,
    )
    d_pre_other, partial_other, *blocks_other = call(
        functools.partial(other_kernel, sends[0], peers),
        (first, second, full_up, full_down),
        (d_pre_of, partial_of, *[block_of] * len(sends[0])),
        [pltpu.VMEM((frame_len, width), BF16)] * 2,
        flops=6 * frame_len * width * quarter,
    )
    partial = [partial_own, partial_other]

    half_rows_of = shape((frame_len, half_width), BF16)
    parts_of = [shape((frame_len // 3, half_width), BF16)] * 3

    def own_d_norm(*ties):
        keep, send, *parts = call(
            d_norm_kernel,
            (d_pre_own, d_pre_other, full_up),
            (shape((2, frame_len, half_width), BF16), half_rows_of, *parts_of),
            flops=4 * frame_len * width * quarter,
            ties=ties,
        )
        sent = [lax.ppermute(part, "gy", swap) for part in parts]
        return keep, lax.ppermute(send, "gy", swap), sent

    def over_cores(keep, came, *ties):
        over = call(over_kernel, (keep, came), half_rows_of, ties=ties)
        return over, lax.ppermute(over, "groups", swap)

    def scale(keep, came, back, *ties):
        return call(
            scale_kernel,
            (keep, back, frames, ln_gain[None], grads, stats, *came),
            (
                shape((frame_len, half_width), F32),
                shape((frame_len, half_width), F32),
                shape((frame_len, 2), F32),
            ),
            ties=ties,
        )

    def input_gradient(base, factor, sums):
        return call(
            input_kernel,
            (base, factor, sums, lax.ppermute(sums, "gy", swap), stats),
            (half_rows_of, shape((8, 128), F32)),
        )

    up_grad_of = shape((depth, hidden), F32)
    if ringed:
        came, kept = [{}, {}], []

        def send_on(i, blocks, names):
            for block, name in zip(blocks, names):
                came[i][name] = lax.ppermute(block, "gx", ahead if name == "up" else behind)

        def hop(i, turn, *ties):
            ways = [("up", half - turn - i), ("down", turn + 1 - i - half)]
            ways = [way for way in ways if way[1] != 0]
            names = [name for name, _ in ways]
            blocks = call(
                functools.partial(hop_kernel, tuple(step for _, step in ways), peers),
                (partial[i], *[came[i][name] for name in names]),
                [block_of] * len(ways),
                ties=ties,
            )
            if (i, turn) == (0, half - 2):
                kept.append(blocks[1])
                blocks, names = blocks[:1], names[:1]
            send_on(i, blocks, names)
            return blocks[0]

        send_on(1, blocks_other, ("up", "down"))
        keep, came_other, sent = own_d_norm()
        send_on(0, [hold(block, keep) for block in blocks_own], ("up", "down"))
        tie = hop(1, 1, keep)
        tie = hop(0, 1, tie)
        tie = hop(1, 2, tie)
        tie, back = over_cores(keep, came_other, tie)
        tie = hop(0, 2, tie)
        for turn in range(3, half):
            tie = hop(0, turn, hop(1, turn, tie), came[1]["up"])
        passing = call(
            functools.partial(total_kernel, peers),
            (partial[1], came[1]["up"], came[1]["down"]),
            block_of,
            ties=(tie,),
        )
        passed = lax.ppermute(passing, "groups", swap)
        send_on(0, [hold(kept[0], passing, sent[0], sent[1])], ["down"])
        input_grad, token = input_gradient(*scale(keep, sent, back, passing))
        up_grad = call(
            functools.partial(last_kernel, peers),
            (partial[0], came[0]["up"], came[0]["down"], passed),
            up_grad_of,
            ties=(token,),
        )
    else:
        keep, came_other, sent = own_d_norm()
        _, back = over_cores(keep, came_other)
        input_grad, _ = input_gradient(*scale(keep, sent, back))
        total, passing = [
            lax.psum_scatter(p.astype(F32), "gx", scatter_dimension=0, tiled=True) for p in partial
        ]
        passed = lax.ppermute(passing.astype(BF16), "groups", swap)
        up_grad = call(place_halves_kernel, (total, passed), up_grad_of)
    return (input_grad[None], up_grad)


def solution(mesh):
    placed = (
        P(("groups", "gx"), None, None),
        P(("groups", "gx"), None, None),
        P(),
        P("gx", "gy"),
        P("gx", "gy"),
        P("groups"),
    )
    return jax.shard_map(
        shards,
        mesh=mesh,
        in_specs=placed,
        out_specs=(P(("groups", "gx"), None, "gy"), P(("groups", "gx"), "gy")),
        check_vma=False,
    )
```
